32 devices in a mesh: ctx: 8 (over z, x), fsdp: 4 (over y, core).
Axes of the slice: x: 2, y: 2, z: 4, core: 2. Of those that a mesh axis runs over, the one named last changes fastest.
Arguments:
- projected: bfloat16 [3, 2048, 8192], P(None, 'ctx', 'fsdp'), may hold values from -6 to 6
- short_weight: bfloat16 [3, 3, 8192], P(None, None, 'fsdp'), may hold values from -3 to 3
- rates: float32 [512, 16], P('fsdp'), may hold values from 0.00014648438 to 0.03
- residues: float32 [512, 16], P('fsdp'), may hold values from -0.12 to 0.12
- skip: float32 [8192], P('fsdp'), may hold values from -1 to 1
- residual: bfloat16 [2048, 8192], P('ctx', 'fsdp'), may hold values from -40 to 40
- gain: float32 [8192], P('fsdp'), may hold values from 0.5 to 1.5
Outputs:
- new_residual: bfloat16 [2048, 8192], P('ctx', 'fsdp')
- normed: bfloat16 [2048, 8192], P('ctx', 'fsdp')
The draws below stay inside these ranges and needn't reach their ends.
All inputs are finite; a program needn't handle non-finite values.
Results may differ from the reference program's by a relative error of at most 0.0047.
Values may be sent and summed in bfloat16 or wider, within the bound.
No kernel may reach another device: no remote copies, remote signals or barrier semaphores. Data moves between devices by JAX's collectives and lax.ppermute only.
A program may use at most 64 MiB of HBM per device.

```python
import math
import jax
import jax.numpy as jnp
from jax import lax

D = 8192
CHANNELS_PER_GRP = 16
FILTER_MODES = 16
TAPS = 3
SEQ = 2048
GROUPS = 512


def draw_residual(key, part):
    columns = jnp.arange(D).astype(jnp.float32) / D
    column_scale = 10.0 ** (columns - 0.5)
    row_draw = jax.random.uniform(jax.random.fold_in(key, 1), (SEQ, 1), jnp.float32)
    row_scale = 10.0 ** (row_draw - 0.5)
    base = jnp.clip(jax.random.normal(jax.random.fold_in(key, 4), (SEQ, D), jnp.float32), -4.0, 4.0)
    return (base * row_scale * column_scale[None, :]).astype(jnp.bfloat16)


def shard_levels(stream_key, extent, shards, least, top_value):
    def one(dim, parts):
        heights = jax.random.uniform(jax.random.fold_in(jax.random.fold_in(stream_key, 6), dim), (parts,), jnp.float32, least / len(shards), top_value / len(shards))
        return jnp.repeat(jnp.exp(heights), extent[dim] // parts).reshape((-1,) + (1,) * (len(extent) - dim - 1))

    factor_of = one(*shards[0])
    for cut in shards[1:]:
        factor_of = factor_of * one(*cut)
    return factor_of


def scatter_about(key, dims, spread, most, cuts=(), dtype=jnp.bfloat16):
    array = jax.random.normal(key, dims, jnp.float32) * spread
    if len(cuts) > 0:
        array = shard_levels(key, dims, cuts, -0.22, 0.18) * array
    return jnp.clip(array, min=-most, max=most).astype(dtype)


def setup_inputs(seed: int = 0) -> dict:
    key_of = jax.random.split(jax.random.key(seed), 8)
    return {
        "projected": scatter_about(key_of[0], (3, SEQ, D), 1.0, 6.0, ((1, 8), (2, 4))),
        "short_weight": scatter_about(key_of[1], (TAPS, 3, D), 0.6, 3.0, ((2, 4),)),
        "rates": jnp.clip(jnp.exp(math.log(0.03) - 5.322034 * jax.random.uniform(key_of[2], (GROUPS, FILTER_MODES), jnp.float32) ** shard_levels(key_of[2], (GROUPS, FILTER_MODES), ((0, 4),), -0.2, 0.2)), 0.00014648438, 0.03),
        "residues": scatter_about(key_of[3], (GROUPS, FILTER_MODES), 0.02, 0.12, ((0, 4),), jnp.float32),
        "skip": jnp.clip(jax.random.uniform(key_of[4], (D,), jnp.float32, -1.0, 1.0) * shard_levels(key_of[4], (D,), ((0, 4),), -0.4, 0.0), -1.0, 1.0),
        "residual": draw_residual(jax.random.fold_in(key_of[7], 71), 0),
        "gain": jnp.clip(1.0 + 0.1 * jax.random.normal(key_of[6], (D,), jnp.float32), 0.5, 1.5),
    }


def reference(projected, short_weight, rates, residues, skip, residual, gain):
    times_axis = jnp.arange(SEQ).astype(jnp.float32)
    filter_taps = jnp.zeros((GROUPS, SEQ), jnp.float32)
    for mode in range(FILTER_MODES):
        filter_taps = filter_taps + residues[:, mode:mode + 1] * jnp.exp(-rates[:, mode:mode + 1] * times_axis[None, :])
    column_block = min(D, 1024)
    pieces = []
    for block in range(D // column_block):
        lower = block * column_block
        upper = lower + column_block
        inputs = projected[:, :, lower:upper].astype(jnp.float32)
        weights = short_weight[:, :, lower:upper].astype(jnp.float32)
        padded_input = jnp.pad(inputs, ((0, 0), (TAPS - 1, 0), (0, 0)))
        filtered = jnp.zeros_like(inputs)
        for shift_amount in range(TAPS):
            lead = TAPS - 1 - shift_amount
            filtered = filtered + weights[shift_amount][:, None, :] * padded_input[:, lead:lead + SEQ, :]
        query_part = filtered[0]
        product = (filtered[1] * filtered[2]).astype(jnp.bfloat16)
        product_wide = product.astype(jnp.float32)
        channel_taps = jnp.repeat(filter_taps[lower // CHANNELS_PER_GRP:upper // CHANNELS_PER_GRP], CHANNELS_PER_GRP, axis=0).T
        spectrum = jnp.fft.rfft(product_wide, n=2 * SEQ, axis=0) * jnp.fft.rfft(channel_taps, n=2 * SEQ, axis=0)
        conv = jnp.fft.irfft(spectrum, n=2 * SEQ, axis=0)[:SEQ]
        summed_block = residual[:, lower:upper].astype(jnp.float32) + query_part * (conv + skip[None, lower:upper] * product_wide)
        pieces.append(summed_block)
    summed = jnp.concatenate(pieces, axis=1)
    new_residual = summed.astype(jnp.bfloat16)
    squares = lax.optimization_barrier(jnp.sum(summed * summed, axis=1, keepdims=True))
    normed = (summed * lax.rsqrt(squares / D + 1e-05) * gain[None, :]).astype(jnp.bfloat16)
    return (new_residual, normed)
```

```python
import jax
import jax.numpy as jnp
from jax import lax
from jax.experimental import pallas as pl
from jax.experimental.pallas import tpu as pltpu
from jax.sharding import PartitionSpec as P

CHANNELS_PER_GRP = 16
MODES = 16
CHUNK = 32
LANES = 128
WIDE = 256
VMEM_LIMIT = 48 * 1024 * 1024
F32 = jnp.float32
BF16 = jnp.bfloat16


def index_of(shape, dim):
    return lax.broadcasted_iota(jnp.int32, shape, dim)


def mode_column(table):
    count = table.shape[0]
    rows = jnp.broadcast_to(table[:, None, :], (count, MODES, MODES)).reshape(count * MODES, MODES)
    own = (index_of(rows.shape, 0) & (MODES - 1)) == index_of(rows.shape, 1)
    return jnp.sum(jnp.where(own, rows, 0.0), axis=1, keepdims=True)


def as_row(column):
    size = column.shape[0]
    own = index_of((size, size), 0) == index_of((size, size), 1)
    return jnp.sum(jnp.where(own, column, 0.0), axis=0, keepdims=True)


def same_group(size, lanes, per_group):
    return index_of((size, lanes), 0) // MODES == index_of((size, lanes), 1) // per_group


def per_mode(masked):
    size, lanes = masked.shape
    return jnp.sum(masked.reshape(size // MODES, MODES, lanes), axis=0)


def spread(rows, groups):
    size, lanes = rows.shape
    copies = jnp.broadcast_to(rows[None], (groups, size, lanes))
    own = index_of(copies.shape, 0) == index_of(copies.shape, 2) // CHANNELS_PER_GRP
    return jnp.where(own, copies, jnp.zeros_like(copies)).reshape(groups * size, lanes)


def short_conv(block, before, weights):
    one = pltpu.roll(block, 1, 0)
    two = pltpu.roll(block, 2, 0)
    first = index_of((8, block.shape[1]), 0)
    head_one = jnp.where(first == 0, before[1:2], one[:8])
    head_two = jnp.where(first == 0, before[0:1], jnp.where(first == 1, before[1:2], two[:8]))
    one = jnp.concatenate([head_one, one[8:]], axis=0)
    two = jnp.concatenate([head_two, two[8:]], axis=0)
    return weights[0] * block + weights[1] * one + weights[2] * two


def state_kernel(key_ref, value_ref, before_ref, weight_ref, rate_ref, product_ref, state_ref, decay_ref):
    rows, lanes = product_ref.shape
    weights = weight_ref[...].astype(F32)
    before = before_ref[...].astype(F32)
    for tile in range(lanes // WIDE):
        here = slice(tile * WIDE, (tile + 1) * WIDE)
        parts = [
            short_conv(
                ref[0, :, here].astype(F32),
                before[c, :, here],
                [weights[tap, c : c + 1, here] for tap in range(3)],
            )
            for c, ref in ((1, key_ref), (2, value_ref))
        ]
        product = (parts[0] * parts[1]).astype(BF16)
        product_ref[:, here] = product
        groups = WIDE // CHANNELS_PER_GRP
        rate = mode_column(rate_ref[tile * groups : (tile + 1) * groups, :])
        left = (rows - 1 - index_of((1, rows), 1)).astype(F32)
        ending = jnp.exp(-rate * left).astype(BF16)
        every = jnp.dot(ending, product, preferred_element_type=F32)
        own = same_group(WIDE, WIDE, CHANNELS_PER_GRP)
        state = per_mode(jnp.where(own, every, 0.0)).astype(BF16)
        decay = jnp.exp(-float(rows) * per_mode(jnp.where(own, rate, 0.0)))
        for half in range(WIDE // LANES):
            cut = slice(half * LANES, (half + 1) * LANES)
            state_ref[tile * (WIDE // LANES) + half] = state[:, cut]
            decay_ref[tile * (WIDE // LANES) + half] = decay[:, cut]


def scan_kernel(states_ref, decay_ref, entry_ref):
    decay = decay_ref[...]
    entry = jnp.zeros(decay.shape, F32)
    for k in range(states_ref.shape[0]):
        entry_ref[k] = entry.astype(BF16)
        entry = decay * entry + states_ref[k].astype(F32)


def split(x):
    high = x.astype(BF16)
    return high, (x - high.astype(F32)).astype(BF16)


def local_kernel(
    query_ref, before_ref, weight_ref, product_ref, residual_ref, rate_ref, residue_ref, skip_ref, base_ref, gate_ref
):
    rows, lanes = product_ref.shape
    groups = LANES // CHANNELS_PER_GRP
    modes = groups * MODES
    weights = weight_ref[...].astype(F32)
    before = before_ref[...].astype(F32)
    for tile in range(lanes // LANES):
        here = slice(tile * LANES, (tile + 1) * LANES)
        mine = slice(tile * groups, (tile + 1) * groups)
        rate = mode_column(rate_ref[mine, :])
        rate_row = as_row(rate)
        residue_row = as_row(mode_column(residue_ref[mine, :]))
        step = index_of((CHUNK, modes), 0).astype(F32)
        falling = residue_row * jnp.exp(-rate_row * step)
        source = (index_of((modes, groups * CHUNK), 1) & (CHUNK - 1)).astype(F32)
        rising = jnp.where(same_group(modes, groups * CHUNK, CHUNK), jnp.exp(rate * source), 0.0)
        fall_high, fall_low = split(falling)
        rise_high, rise_low = split(rising)
        taps = (
            jnp.dot(fall_high, rise_high, preferred_element_type=F32)
            + jnp.dot(fall_low, rise_high, preferred_element_type=F32)
            + jnp.dot(fall_high, rise_low, preferred_element_type=F32)
        )
        target = index_of(taps.shape, 0)
        taps = jnp.where((index_of(taps.shape, 1) & (CHUNK - 1)) <= target, taps, 0.0)
        ending = per_mode(rising * jnp.exp(-float(CHUNK - 1) * rate))
        table = jnp.concatenate([taps.astype(BF16), ending.astype(BF16)], axis=0)
        entering = (falling * jnp.exp(-rate_row)).astype(BF16)
        mode_rate = per_mode(jnp.where(same_group(modes, LANES, CHANNELS_PER_GRP), rate, 0.0))
        decay = jnp.exp(-float(CHUNK) * mode_rate)

        query = short_conv(
            query_ref[0, :, here].astype(F32),
            before[0, :, here],
            [weights[tap, 0:1, here] for tap in range(3)],
        )
        state = jnp.zeros((MODES, LANES), F32)
        skip = skip_ref[:, here]
        for pair in range(rows // (2 * CHUNK)):
            spans = [slice((2 * pair + k) * CHUNK, (2 * pair + k + 1) * CHUNK) for k in (0, 1)]
            pieces = [product_ref[span, here] for span in spans]
            sources = jnp.concatenate([spread(piece, groups) for piece in pieces], axis=1)
            inner = jnp.dot(table, sources, preferred_element_type=F32)
            states = []
            for k in (0, 1):
                states.append(spread(state.astype(BF16), groups))
                state = decay * state + inner[CHUNK:, k * LANES : (k + 1) * LANES]
            outer = jnp.dot(entering, jnp.concatenate(states, axis=1), preferred_element_type=F32)
            conv = inner[:CHUNK] + outer
            for k in (0, 1):
                span = spans[k]
                whole = conv[:, k * LANES : (k + 1) * LANES] + skip * pieces[k].astype(F32)
                base_ref[span, here] = residual_ref[span, here].astype(F32) + query[span] * whole
        gate_ref[:, here] = query


def carry_kernel(base_ref, gate_ref, entry_ref, rate_ref, residue_ref, summed_ref, new_ref, squares_ref):
    rows, lanes = base_ref.shape
    groups = WIDE // CHANNELS_PER_GRP
    total = jnp.zeros((rows, LANES), F32)
    for tile in range(lanes // WIDE):
        here = slice(tile * WIDE, (tile + 1) * WIDE)
        mine = slice(tile * groups, (tile + 1) * groups)
        rate_row = as_row(mode_column(rate_ref[mine, :]))
        residue_row = as_row(mode_column(residue_ref[mine, :]))
        step = (index_of((rows, WIDE), 0) + 1).astype(F32)
        table = (residue_row * jnp.exp(-rate_row * step)).astype(BF16)
        per = WIDE // LANES
        entry = jnp.concatenate([entry_ref[per * tile + k] for k in range(per)], axis=1)
        carry = jnp.dot(table, spread(entry, groups), preferred_element_type=F32)
        summed = base_ref[:, here] + gate_ref[:, here] * carry
        summed_ref[:, here] = summed
        new_ref[:, here] = summed.astype(BF16)
        square = summed * summed
        for k in range(per):
            total = total + square[:, k * LANES : (k + 1) * LANES]

    @pl.when(pl.program_id(0) == 0)
    def _():
        squares_ref[...] = jnp.zeros_like(squares_ref)

    squares_ref[...] += lax.dot_general(
        jnp.ones((8, LANES), F32),
        total,
        (((1,), (1,)), ((), ())),
        precision=lax.Precision.HIGHEST,
        preferred_element_type=F32,
    )


def norm_kernel(width, summed_ref, squares_ref, gain_ref, normed_ref):
    squares = jnp.transpose(squares_ref[...])[:, 0:1]
    scale = lax.rsqrt(squares / width + 1e-05)
    normed_ref[...] = (summed_ref[...] * scale * gain_ref[...]).astype(BF16)


def params():
    return pltpu.CompilerParams(vmem_limit_bytes=VMEM_LIMIT)


def per_device(projected, short_weight, rates, residues, skip, residual, gain):
    rows, width = projected.shape[1:]
    taps = short_weight.shape[0]
    peers = lax.axis_size("ctx")
    full_width = width * lax.axis_size("fsdp")
    span = min(512, width)
    grid = (width // span,)
    span_groups = span // CHANNELS_PER_GRP
    span_tiles = span // LANES
    tiles = width // LANES

    route = [(i, i + 1) for i in range(peers - 1)]
    before = lax.ppermute(projected[:, rows - (taps - 1) :, :], "ctx", route)

    token_spec = pl.BlockSpec((rows, span), lambda i: (0, i))
    row_spec = pl.BlockSpec((1, span), lambda i: (0, i))
    before_spec = pl.BlockSpec((3, taps - 1, span), lambda i: (0, 0, i))
    weight_spec = pl.BlockSpec((taps, 3, span), lambda i: (0, 0, i))
    mode_spec = pl.BlockSpec((span_groups, MODES), lambda i: (i, 0))
    state_spec = pl.BlockSpec((span_tiles, MODES, LANES), lambda i: (i, 0, 0))

    def feature(c):
        return pl.BlockSpec((1, rows, span), lambda i: (c, 0, i))

    product, state, decay = pl.pallas_call(
        state_kernel,
        grid=grid,
        in_specs=[feature(1), feature(2), before_spec, weight_spec, mode_spec],
        out_specs=[token_spec, state_spec, state_spec],
        out_shape=[
            jax.ShapeDtypeStruct((rows, width), BF16),
            jax.ShapeDtypeStruct((tiles, MODES, LANES), BF16),
            jax.ShapeDtypeStruct((tiles, MODES, LANES), F32),
        ],
        compiler_params=params(),
        name="block_state",
    )(projected, projected, before, short_weight, rates)

    state_rows = tiles * MODES
    share = -(-state_rows // peers)
    padding = ((0, share * peers - state_rows), (0, 0))
    shares = jnp.pad(state.reshape(state_rows, LANES), padding).reshape(peers, share, LANES)
    decays = jnp.pad(decay.reshape(state_rows, LANES), padding).reshape(peers, share, LANES)
    own_decay = lax.dynamic_index_in_dim(decays, lax.axis_index("ctx"), 0, keepdims=False)
    everyone = lax.all_to_all(shares, "ctx", 0, 0, tiled=True)
    entries = pl.pallas_call(
        scan_kernel,
        out_shape=jax.ShapeDtypeStruct((peers, share, LANES), BF16),
        name="block_scan",
    )(everyone, own_decay)
    entry = lax.all_to_all(entries, "ctx", 0, 0, tiled=True)
    entry = entry.reshape(peers * share, LANES)[:state_rows].reshape(tiles, MODES, LANES)

    base, gate = pl.pallas_call(
        local_kernel,
        grid=grid,
        in_specs=[
            feature(0),
            before_spec,
            weight_spec,
            token_spec,
            token_spec,
            mode_spec,
            mode_spec,
            row_spec,
        ],
        out_specs=[token_spec, token_spec],
        out_shape=[jax.ShapeDtypeStruct((rows, width), F32)] * 2,
        compiler_params=params(),
        name="local_conv",
    )(projected, before, short_weight, product, residual, rates, residues, skip[None])

    summed, new_residual, squares = pl.pallas_call(
        carry_kernel,
        grid=grid,
        in_specs=[token_spec, token_spec, state_spec, mode_spec, mode_spec],
        out_specs=[token_spec, token_spec, pl.BlockSpec((8, rows), lambda i: (0, 0))],
        out_shape=[
            jax.ShapeDtypeStruct((rows, width), F32),
            jax.ShapeDtypeStruct((rows, width), BF16),
            jax.ShapeDtypeStruct((8, rows), F32),
        ],
        compiler_params=params(),
        name="add_carry",
    )(base, gate, entry, rates, residues)

    squares = lax.psum(squares, "fsdp")

    def norm(*refs):
        norm_kernel(full_width, *refs)

    normed = pl.pallas_call(
        norm,
        grid=grid,
        in_specs=[token_spec, pl.BlockSpec((8, rows), lambda i: (0, 0)), row_spec],
        out_specs=token_spec,
        out_shape=jax.ShapeDtypeStruct((rows, width), BF16),
        compiler_params=params(),
        name="norm",
    )(summed, squares, gain[None])
    return (new_residual, normed)


def solution(mesh):
    return jax.shard_map(
        per_device,
        mesh=mesh,
        in_specs=(
            P(None, "ctx", "fsdp"),
            P(None, None, "fsdp"),
            P("fsdp", None),
            P("fsdp", None),
            P("fsdp"),
            P("ctx", "fsdp"),
            P("fsdp"),
        ),
        out_specs=(P("ctx", "fsdp"), P("ctx", "fsdp")),
        check_vma=False,
    )
```

```python
import jax
import jax.numpy as jnp
from jax import lax
from jax.experimental import pallas as pl
from jax.experimental.pallas import tpu as pltpu
from jax.sharding import PartitionSpec as P

CHANNELS_PER_GRP = 16
MODES = 16
CHUNK = 32
LANES = 128
WIDE = 256
GROUPS = LANES // CHANNELS_PER_GRP
VMEM_LIMIT = 16 * 1024 * 1024
F32 = jnp.float32
BF16 = jnp.bfloat16


def index_of(shape, dim):
    return lax.broadcasted_iota(jnp.int32, shape, dim)


def lanes_of(tile, width=LANES):
    return slice(tile * width, (tile + 1) * width)


def per_channel(table):
    groups = table.shape[1]
    width = groups * CHANNELS_PER_GRP
    high = table.astype(BF16)
    rest = table - high.astype(F32)
    middle = rest.astype(BF16)
    low = (rest - middle.astype(F32)).astype(BF16)
    terms = jnp.concatenate([high, middle, low], axis=0)
    parts = []
    for tile in range(width // WIDE):
        shape = (groups, WIDE)
        own = index_of(shape, 0) == index_of(shape, 1) // CHANNELS_PER_GRP + tile * (WIDE // CHANNELS_PER_GRP)
        three = jnp.dot(terms, jnp.where(own, 1.0, 0.0).astype(BF16), preferred_element_type=F32)
        parts.append(three[:MODES] + three[MODES : 2 * MODES] + three[2 * MODES :])
    return jnp.concatenate(parts, axis=1)


def mode_row(channel_table):
    own = index_of(channel_table.shape, 0) == (index_of(channel_table.shape, 1) & (MODES - 1))
    return jnp.sum(jnp.where(own, channel_table, 0.0), axis=0, keepdims=True)


def mode_column(row):
    return jnp.transpose(jnp.broadcast_to(row, (LANES, LANES)))


def group_mask(dtype):
    shape = (GROUPS, MODES, LANES)
    own = index_of(shape, 0) == index_of(shape, 2) // CHANNELS_PER_GRP
    return jnp.where(own, 1.0, 0.0).astype(dtype)


def spread(rows, mask):
    size = rows.shape[0]
    copies = rows.reshape(1, size // MODES, MODES, LANES) * mask.reshape(GROUPS, 1, MODES, LANES)
    return copies.reshape(GROUPS * size, LANES)


def shifted(block, before):
    one = pltpu.roll(block, 1, 0)
    two = pltpu.roll(block, 2, 0)
    first = index_of((8, block.shape[1]), 0)
    near, far = (0.0, 0.0) if before is None else (before[1:2], before[0:1])
    head_one = jnp.where(first == 0, near, one[:8])
    head_two = jnp.where(first == 0, far, jnp.where(first == 1, near, two[:8]))
    if block.shape[0] == 8:
        return head_one, head_two
    return jnp.concatenate([head_one, one[8:]], axis=0), jnp.concatenate([head_two, two[8:]], axis=0)


def short_conv(block, before, weights):
    one, two = shifted(block, before)
    return weights[0] * block + weights[1] * one + weights[2] * two


def taps_of(weights, feature, lanes):
    return [weights[tap, feature : feature + 1, lanes] for tap in range(weights.shape[0])]


def state_kernel(
    projected_ref, weight_ref, rate_ref, product_ref, state_ref, mode_rate_ref, head_ref, buffer_ref, sems
):
    rows, width = product_ref.shape
    copies = []
    for tile in range(width // WIDE):
        here = pl.ds(tile * WIDE, WIDE)
        copies.append(
            pltpu.make_async_copy(projected_ref.at[pl.ds(1, 2), :, here], buffer_ref.at[:, :, here], sems.at[tile])
        )
        copies[-1].start()
    weights = weight_ref[...].astype(F32)
    mode_rate = per_channel(rate_ref[...])
    mode_rate_ref[...] = mode_rate
    mask = group_mask(F32)
    left = (rows - 1 - index_of((1, rows), 1)).astype(F32)
    left = jnp.where(left > rows - 2.5, 1e30, left)
    for tile in range(width // WIDE):
        here = lanes_of(tile, WIDE)
        row = mode_row(mode_rate[:, here])
        pieces = []
        for half in range(WIDE // LANES):
            rate = mode_column(row[:, lanes_of(half)])
            rate = jnp.concatenate([rate] * (rows // LANES), axis=1)
            pieces.append(jnp.exp(-rate * left).astype(BF16))
        ending = jnp.concatenate(pieces, axis=0)
        copies[tile].wait()
        parts = []
        for c in (0, 1):
            block = buffer_ref[c, :, here].astype(F32)
            head_ref[c, :, here] = block[:8]
            parts.append(short_conv(block, None, taps_of(weights, c + 1, here)))
        product = (parts[0] * parts[1]).astype(BF16)
        product_ref[:, here] = product
        every = jnp.dot(ending, product, preferred_element_type=F32)
        for half in range(WIDE // LANES):
            own = every[lanes_of(half), lanes_of(half)].reshape(GROUPS, MODES, LANES)
            state_ref[:, lanes_of((WIDE // LANES) * tile + half)] = jnp.sum(own * mask, axis=0)


def head_kernel(rows, before_ref, head_ref, weight_ref, state_ref, mode_rate_ref, full_ref, first_ref):
    weights = weight_ref[...].astype(F32)
    before = before_ref[...].astype(F32)
    everything = slice(0, head_ref.shape[2])
    parts = [short_conv(head_ref[c], before[c + 1], taps_of(weights, c + 1, everything)) for c in (0, 1)]
    first = (parts[0] * parts[1]).astype(BF16).astype(F32)
    first_ref[...] = first
    rate = mode_rate_ref[...]
    early = jnp.exp(-float(rows - 1) * rate) * first[0:1] + jnp.exp(-float(rows - 2) * rate) * first[1:2]
    full_ref[...] = (state_ref[...] + early).astype(BF16)


def split(x):
    high = x.astype(BF16)
    return high, (x - high.astype(F32)).astype(BF16)


def table_kernel(rows, mode_rate_ref, residue_ref, inner_ref, entering_ref, carry_ref):
    width = mode_rate_ref.shape[1]
    residue = per_channel(residue_ref[...])
    wide = GROUPS * CHUNK
    step = index_of((CHUNK, LANES), 0).astype(F32)
    source = (index_of((LANES, wide), 1) & (CHUNK - 1)).astype(F32)
    own = index_of((LANES, wide), 0) // MODES == index_of((LANES, wide), 1) // CHUNK
    causal = (index_of((CHUNK, wide), 1) & (CHUNK - 1)) <= index_of((CHUNK, wide), 0)
    for tile in range(width // LANES):
        here = lanes_of(tile)
        rate_row = mode_row(mode_rate_ref[:, here])
        rate = mode_column(rate_row)
        rate = jnp.concatenate([rate] * (wide // LANES), axis=1)
        falling = mode_row(residue[:, here]) * jnp.exp(-rate_row * step)
        rising = jnp.where(own, jnp.exp(rate * source), 0.0)
        fall_high, fall_low = split(falling)
        rise_high, rise_low = split(rising)
        taps = jnp.dot(jnp.concatenate([fall_high, fall_low], axis=0), rise_high, preferred_element_type=F32)
        taps = taps[:CHUNK] + taps[CHUNK:] + jnp.dot(fall_high, rise_low, preferred_element_type=F32)
        taps = jnp.where(causal, taps, 0.0)
        ending = rising * jnp.exp(-float(CHUNK - 1) * rate)
        ending = jnp.sum(ending.reshape(GROUPS, MODES, wide), axis=0)
        inner_ref[tile] = jnp.concatenate([taps.astype(BF16), ending.astype(BF16)], axis=0)
        half = tile % (WIDE // LANES)
        for chunk in range(rows // CHUNK):
            entering = (falling * jnp.exp(-float(CHUNK * chunk + 1) * rate_row)).astype(BF16)
            carry_ref[tile // (WIDE // LANES), chunk * CHUNK : (chunk + 1) * CHUNK, lanes_of(half)] = entering
            if chunk == 0:
                entering_ref[tile] = entering


def local_kernel(
    projected_ref,
    residual_hbm,
    before_ref,
    weight_ref,
    product_ref,
    first_ref,
    mode_rate_ref,
    inner_ref,
    entering_ref,
    skip_ref,
    base_ref,
    gate_ref,
    query_ref,
    residual_ref,
    sems,
):
    rows, width = product_ref.shape
    copies = []
    for part in range(width // WIDE):
        here = pl.ds(part * WIDE, WIDE)
        copies.append(
            (
                pltpu.make_async_copy(projected_ref.at[0, :, here], query_ref.at[:, here], sems.at[0, part]),
                pltpu.make_async_copy(residual_hbm.at[:, here], residual_ref.at[:, here], sems.at[1, part]),
            )
        )
        for copy in copies[-1]:
            copy.start()
    weights = weight_ref[...].astype(F32)
    before = before_ref[0].astype(F32)
    mask = group_mask(BF16)
    top = index_of((8, LANES), 0) < 2
    for tile in range(width // LANES):
        here = lanes_of(tile)
        if tile % (WIDE // LANES) == 0:
            for copy in copies[tile // (WIDE // LANES)]:
                copy.wait()
        pieces = []
        for chunk in range(rows // CHUNK):
            piece = product_ref[chunk * CHUNK : (chunk + 1) * CHUNK, here]
            if chunk == 0:
                wide = piece.astype(F32)
                head = jnp.where(top, first_ref[:, here], wide[:8])
                piece = jnp.concatenate([head, wide[8:]], axis=0).astype(BF16)
            pieces.append(piece)
        table = inner_ref[tile]
        inner = []
        for pair in range(rows // (2 * CHUNK)):
            sources = jnp.concatenate([spread(pieces[2 * pair + k], mask) for k in (0, 1)], axis=1)
            inner.append(jnp.dot(table, sources, preferred_element_type=F32))
        query = short_conv(query_ref[:, here].astype(F32), before[:, here], taps_of(weights, 0, here))
        gate_ref[:, here] = query
        decay = jnp.exp(-float(CHUNK) * mode_rate_ref[:, here])
        state = jnp.zeros((MODES, LANES), F32)
        states = []
        for chunk in range(rows // CHUNK):
            states.append(spread(state.astype(BF16), mask))
            state = decay * state + inner[chunk // 2][CHUNK:, lanes_of(chunk % 2)]
        entering = entering_ref[tile]
        skip = skip_ref[:, here]
        for pair in range(rows // (2 * CHUNK)):
            two = jnp.concatenate(states[2 * pair : 2 * pair + 2], axis=1)
            conv = inner[pair][:CHUNK] + jnp.dot(entering, two, preferred_element_type=F32)
            for k in (0, 1):
                chunk = 2 * pair + k
                span = slice(chunk * CHUNK, (chunk + 1) * CHUNK)
                whole = conv[:, lanes_of(k)] + skip * pieces[chunk].astype(F32)
                base_ref[span, here] = residual_ref[span, here].astype(F32) + query[span] * whole


def carry_kernel(stride, received, place_ref, base_ref, gate_ref, carry_ref, mode_rate_ref, inner_entry_ref, *refs):
    entry_refs, (summed_ref, squares_ref) = refs[:received], refs[received:]
    rows, width = base_ref.shape
    place = place_ref[0].astype(F32) * float(rows)
    mask = group_mask(BF16)
    total = jnp.zeros((rows, LANES), F32)
    nothing = jnp.zeros((LANES, LANES), BF16)
    for tile in range(width // WIDE):
        here = lanes_of(tile, WIDE)
        rate = mode_rate_ref[:, here]
        decay = jnp.exp(-float(rows * stride) * rate)
        outer = entry_refs[-1][:, here].astype(F32)
        for ref in entry_refs[-2::-1]:
            outer = decay * outer + ref[:, here].astype(F32)
        entry = (inner_entry_ref[:, here].astype(F32) + jnp.exp(-place * rate) * outer).astype(BF16)
        left, right = spread(entry[:, :LANES], mask), spread(entry[:, LANES:], mask)
        both = jnp.concatenate(
            [jnp.concatenate([left, nothing], axis=1), jnp.concatenate([nothing, right], axis=1)], axis=0
        )
        carry = jnp.dot(carry_ref[tile], both, preferred_element_type=F32)
        summed = base_ref[:, here] + gate_ref[:, here] * carry
        summed_ref[:, here] = summed
        square = summed * summed
        total = total + (square[:, :LANES] + square[:, LANES:])
    squares = lax.dot_general(
        jnp.ones((8, LANES), F32),
        total,
        (((1,), (1,)), ((), ())),
        precision=lax.Precision.HIGHEST,
        preferred_element_type=F32,
    )
    squares_ref[...] = squares[0:1]


def params():
    return pltpu.CompilerParams(vmem_limit_bytes=VMEM_LIMIT)


def cost(microseconds):
    return pl.CostEstimate(flops=0, bytes_accessed=int(microseconds * 3.0e6), transcendentals=0)


def radices(count):
    found = []
    for radix in (2, 4, 4, 4):
        if count % radix == 0 and count > 1:
            found.append(radix)
            count //= radix
    for radix in (3, 2, 5, 7):
        while count % radix == 0 and count > 1:
            found.append(radix)
            count //= radix
    return found + ([count] if count > 1 else [])


def decayed(value, rate, tokens):
    return jnp.exp(-tokens * rate) * value


def per_device(projected, short_weight, rates, residues, skip, residual, gain):
    rows, width = projected.shape[1:]
    taps = short_weight.shape[0]
    peers = lax.axis_size("ctx")
    here = lax.axis_index("ctx")
    full_width = width * lax.axis_size("fsdp")
    any_spec = pl.BlockSpec(memory_space=pl.ANY)
    vmem_spec = pl.BlockSpec(memory_space=pltpu.VMEM)
    smem_spec = pl.BlockSpec(memory_space=pltpu.SMEM)
    tiles = width // LANES
    wides = width // WIDE

    route = [(i, i + 1) for i in range(peers - 1)]
    before = lax.ppermute(projected[:, rows - (taps - 1) :, :], "ctx", route)

    product, state, mode_rate, head = pl.pallas_call(
        state_kernel,
        in_specs=[any_spec, vmem_spec, vmem_spec],
        out_shape=[
            jax.ShapeDtypeStruct((rows, width), BF16),
            jax.ShapeDtypeStruct((MODES, width), F32),
            jax.ShapeDtypeStruct((MODES, width), F32),
            jax.ShapeDtypeStruct((2, 8, width), F32),
        ],
        scratch_shapes=[pltpu.VMEM((2, rows, width), BF16), pltpu.SemaphoreType.DMA((wides,))],
        compiler_params=params(),
        cost_estimate=cost(3),
        name="block_state",
    )(projected, short_weight, rates.T)

    inner, entering, carry_table = pl.pallas_call(
        lambda *refs: table_kernel(rows, *refs),
        out_shape=[
            jax.ShapeDtypeStruct((tiles, CHUNK + MODES, GROUPS * CHUNK), BF16),
            jax.ShapeDtypeStruct((tiles, CHUNK, LANES), BF16),
            jax.ShapeDtypeStruct((wides, rows, WIDE), BF16),
        ],
        compiler_params=params(),
        cost_estimate=cost(3),
        name="tables",
    )(mode_rate, residues.T)

    full_state, first = pl.pallas_call(
        lambda *refs: head_kernel(rows, *refs),
        out_shape=[jax.ShapeDtypeStruct((MODES, width), BF16), jax.ShapeDtypeStruct((8, width), F32)],
        compiler_params=params(),
        cost_estimate=cost(1),
        name="head_tokens",
    )(before, head, short_weight, state, mode_rate)

    base, gate = pl.pallas_call(
        local_kernel,
        in_specs=[any_spec, any_spec] + [vmem_spec] * 8,
        out_shape=[jax.ShapeDtypeStruct((rows, width), F32)] * 2,
        scratch_shapes=[
            pltpu.VMEM((rows, width), BF16),
            pltpu.VMEM((rows, width), BF16),
            pltpu.SemaphoreType.DMA((2, wides)),
        ],
        compiler_params=params(),
        cost_estimate=cost(6),
        name="local_conv",
    )(projected, residual, before, short_weight, product, first, mode_rate, inner, entering, skip[None])

    group, entry, stride = full_state, jnp.zeros((MODES, width), F32), 1
    levels = radices(peers)
    for level, radix in enumerate(levels):
        last = level == len(levels) - 1
        size = stride * radix
        if last:
            shifts = [[(i, i + stride * k) for i in range(peers - stride * k)] for k in range(1, radix)]
            received = [lax.ppermute(group, "ctx", shift) for shift in shifts]
            break
        cycles = [
            [(i, i // size * size + (i + stride * k) % size) for i in range(peers)] for k in range(1, radix)
        ]
        others = [lax.ppermute(group, "ctx", cycle).astype(F32) for cycle in cycles]
        run = here % size // stride
        own = group.astype(F32)
        found = jnp.zeros_like(own)
        span = float(rows * stride)
        for k, other in enumerate(others, 1):
            earlier = run >= k
            lag = jnp.where(earlier, k - 1, 0).astype(F32) * span
            found = found + jnp.where(earlier, decayed(other, mode_rate, lag), 0.0)
        total = decayed(own, mode_rate, (radix - 1 - run).astype(F32) * span)
        for k, other in enumerate(others, 1):
            source = (run - k) % radix
            total = total + decayed(other, mode_rate, (radix - 1 - source).astype(F32) * span)
        entry = entry + decayed(found, mode_rate, (here % stride).astype(F32) * float(rows))
        group, stride = total.astype(BF16), size

    place = (here % stride).astype(jnp.int32).reshape(1)
    summed, squares = pl.pallas_call(
        lambda *refs: carry_kernel(stride, len(received), *refs),
        in_specs=[smem_spec] + [vmem_spec] * (5 + len(received)),
        out_shape=[jax.ShapeDtypeStruct((rows, width), F32), jax.ShapeDtypeStruct((1, rows), F32)],
        compiler_params=params(),
        cost_estimate=cost(2),
        name="add_carry",
    )(place, base, gate, carry_table, mode_rate, entry, *received)

    peers = lax.axis_size("fsdp")
    rings = [[(i, (i + k) % peers) for i in range(peers)] for k in range(1, peers)]
    parts = [lax.ppermute(squares, "fsdp", ring) for ring in rings]
    new_residual = summed.astype(BF16)
    for part in parts:
        squares = squares + part
    scale = lax.rsqrt(squares[0][:, None] / full_width + 1e-05)
    normed = (summed * scale * gain[None, :]).astype(BF16)
    return (new_residual, normed)


def solution(mesh):
    return jax.shard_map(
        per_device,
        mesh=mesh,
        in_specs=(
            P(None, "ctx", "fsdp"),
            P(None, None, "fsdp"),
            P("fsdp", None),
            P("fsdp", None),
            P("fsdp"),
            P("ctx", "fsdp"),
            P("fsdp"),
        ),
        out_specs=(P("ctx", "fsdp"), P("ctx", "fsdp")),
        check_vma=False,
    )
```

```python
import jax
import jax.numpy as jnp
from jax import lax
from jax.experimental import pallas as pl
from jax.experimental.pallas import tpu as pltpu
from jax.sharding import PartitionSpec as P

CHANNELS_PER_GRP = 16
MODES = 16
CHUNK = 32
LANES = 128
WIDE = 256
GROUPS = LANES // CHANNELS_PER_GRP
VMEM_LIMIT = 16 * 1024 * 1024
F32 = jnp.float32
BF16 = jnp.bfloat16


def index_of(shape, dim):
    return lax.broadcasted_iota(jnp.int32, shape, dim)


def lanes_of(tile, width=LANES):
    return slice(tile * width, (tile + 1) * width)


def per_channel(table):
    groups = table.shape[1]
    width = groups * CHANNELS_PER_GRP
    high = table.astype(BF16)
    rest = table - high.astype(F32)
    middle = rest.astype(BF16)
    low = (rest - middle.astype(F32)).astype(BF16)
    terms = jnp.concatenate([high, middle, low], axis=0)
    parts = []
    for tile in range(width // WIDE):
        shape = (groups, WIDE)
        own = index_of(shape, 0) == index_of(shape, 1) // CHANNELS_PER_GRP + tile * (WIDE // CHANNELS_PER_GRP)
        three = jnp.dot(terms, jnp.where(own, 1.0, 0.0).astype(BF16), preferred_element_type=F32)
        parts.append(three[:MODES] + three[MODES : 2 * MODES] + three[2 * MODES :])
    return jnp.concatenate(parts, axis=1)


def mode_row(channel_table):
    own = index_of(channel_table.shape, 0) == (index_of(channel_table.shape, 1) & (MODES - 1))
    return jnp.sum(jnp.where(own, channel_table, 0.0), axis=0, keepdims=True)


def mode_column(row):
    return jnp.transpose(jnp.broadcast_to(row, (LANES, LANES)))


def group_mask(dtype):
    shape = (GROUPS, MODES, LANES)
    own = index_of(shape, 0) == index_of(shape, 2) // CHANNELS_PER_GRP
    return jnp.where(own, 1.0, 0.0).astype(dtype)


def spread(rows, mask):
    size = rows.shape[0]
    copies = rows.reshape(1, size // MODES, MODES, LANES) * mask.reshape(GROUPS, 1, MODES, LANES)
    return copies.reshape(GROUPS * size, LANES)


def shifted(block, before):
    one = pltpu.roll(block, 1, 0)
    two = pltpu.roll(block, 2, 0)
    first = index_of((8, block.shape[1]), 0)
    near, far = (0.0, 0.0) if before is None else (before[1:2], before[0:1])
    head_one = jnp.where(first == 0, near, one[:8])
    head_two = jnp.where(first == 0, far, jnp.where(first == 1, near, two[:8]))
    if block.shape[0] == 8:
        return head_one, head_two
    return jnp.concatenate([head_one, one[8:]], axis=0), jnp.concatenate([head_two, two[8:]], axis=0)


def short_conv(block, before, weights):
    one, two = shifted(block, before)
    return weights[0] * block + weights[1] * one + weights[2] * two


def taps_of(weights, feature, lanes):
    return [weights[tap, feature : feature + 1, lanes] for tap in range(weights.shape[0])]


def state_kernel(
    projected_ref,
    weight_hbm,
    rate_hbm,
    product_ref,
    state_ref,
    mode_rate_ref,
    head_ref,
    weight_ref,
    buffer_ref,
    ending_ref,
    short_ref,
    rate_ref,
    sems,
    small_sems,
):
    rows, width = product_ref.shape
    wides = width // WIDE
    rate_copy = pltpu.make_async_copy(rate_hbm, rate_ref, small_sems.at[0])
    rate_copy.start()
    weight_copy = pltpu.make_async_copy(weight_hbm, short_ref, small_sems.at[1])
    weight_copy.start()
    copies = []
    for tile in range(wides):
        here = pl.ds(tile * WIDE, WIDE)
        copies.append(
            pltpu.make_async_copy(projected_ref.at[pl.ds(1, 2), :, here], buffer_ref.at[:, :, here], sems.at[tile])
        )
        copies[-1].start()
    rate_copy.wait()
    mode_rate = per_channel(rate_ref[...])
    mode_rate_ref[...] = mode_rate
    left = (rows - 1 - index_of((1, rows), 1)).astype(F32)
    left = jnp.where(left > rows - 2.5, 1e30, left)
    for tile in range(width // LANES):
        rate = mode_column(mode_row(mode_rate[:, lanes_of(tile)]))
        rate = jnp.concatenate([rate] * (rows // LANES), axis=1)
        ending_ref[tile // 2, lanes_of(tile % 2), :] = jnp.exp(-rate * left).astype(BF16)
    weight_copy.wait()
    weights = short_ref[...].astype(F32)
    weight_ref[...] = weights
    mask = group_mask(F32)

    def leave_state(tile, product):
        every = jnp.dot(ending_ref[tile], product, preferred_element_type=F32)
        for half in range(WIDE // LANES):
            own = every[lanes_of(half), lanes_of(half)].reshape(GROUPS, MODES, LANES)
            state_ref[:, lanes_of((WIDE // LANES) * tile + half)] = jnp.sum(own * mask, axis=0)

    previous = None
    for tile in range(wides):
        here = lanes_of(tile, WIDE)
        copies[tile].wait()
        if previous is not None:
            leave_state(tile - 1, previous)
        parts = []
        for c in (0, 1):
            block = buffer_ref[c, :, here].astype(F32)
            head_ref[c, :, here] = block[:8]
            parts.append(short_conv(block, None, taps_of(weights, c + 1, here)))
        previous = (parts[0] * parts[1]).astype(BF16)
        product_ref[:, here] = previous
    leave_state(wides - 1, previous)


def halo(before_ref, place_ref):
    return jnp.where(place_ref[0] > 0, before_ref[...].astype(F32), 0.0)


def head_kernel(rows, place_ref, before_ref, head_ref, weight_ref, state_ref, mode_rate_ref, full_ref, first_ref):
    before = halo(before_ref, place_ref)
    everything = slice(0, head_ref.shape[2])
    parts = [short_conv(head_ref[c], before[c + 1], taps_of(weight_ref, c + 1, everything)) for c in (0, 1)]
    first = (parts[0] * parts[1]).astype(BF16).astype(F32)
    first_ref[...] = first
    rate = mode_rate_ref[...]
    early = jnp.exp(-float(rows - 1) * rate) * first[0:1] + jnp.exp(-float(rows - 2) * rate) * first[1:2]
    full_ref[...] = (state_ref[...] + early).astype(BF16)


def split(x):
    high = x.astype(BF16)
    return high, (x - high.astype(F32)).astype(BF16)


def prepare_kernel(
    place_ref,
    projected_ref,
    residual_hbm,
    residue_hbm,
    before_ref,
    weight_ref,
    mode_rate_ref,
    inner_ref,
    entering_ref,
    carry_ref,
    gate_ref,
    residual_ref,
    query_ref,
    residue_ref,
    sems,
):
    rows, width = gate_ref.shape
    copies = [
        pltpu.make_async_copy(residue_hbm, residue_ref, sems.at[0]),
        pltpu.make_async_copy(projected_ref.at[0], query_ref, sems.at[1]),
        pltpu.make_async_copy(residual_hbm, residual_ref, sems.at[2]),
    ]
    for copy in copies:
        copy.start()
    copies[0].wait()
    residue = per_channel(residue_ref[...])
    wide = GROUPS * CHUNK
    step = index_of((CHUNK, LANES), 0).astype(F32)
    source = (index_of((LANES, wide), 1) & (CHUNK - 1)).astype(F32)
    own = index_of((LANES, wide), 0) // MODES == index_of((LANES, wide), 1) // CHUNK
    causal = (index_of((CHUNK, wide), 1) & (CHUNK - 1)) <= index_of((CHUNK, wide), 0)
    for tile in range(width // LANES):
        here = lanes_of(tile)
        rate_row = mode_row(mode_rate_ref[:, here])
        rate = mode_column(rate_row)
        rate = jnp.concatenate([rate] * (wide // LANES), axis=1)
        falling = mode_row(residue[:, here]) * jnp.exp(-rate_row * step)
        rising = jnp.where(own, jnp.exp(rate * source), 0.0)
        fall_high, fall_low = split(falling)
        rise_high, rise_low = split(rising)
        taps = jnp.dot(jnp.concatenate([fall_high, fall_low], axis=0), rise_high, preferred_element_type=F32)
        taps = taps[:CHUNK] + taps[CHUNK:] + jnp.dot(fall_high, rise_low, preferred_element_type=F32)
        taps = jnp.where(causal, taps, 0.0)
        ending = rising * jnp.exp(-float(CHUNK - 1) * rate)
        ending = jnp.sum(ending.reshape(GROUPS, MODES, wide), axis=0)
        inner_ref[tile] = jnp.concatenate([taps.astype(BF16), ending.astype(BF16)], axis=0)
        half = tile % (WIDE // LANES)
        for chunk in range(rows // CHUNK):
            entering = (falling * jnp.exp(-float(CHUNK * chunk + 1) * rate_row)).astype(BF16)
            carry_ref[tile // (WIDE // LANES), chunk * CHUNK : (chunk + 1) * CHUNK, lanes_of(half)] = entering
            if chunk == 0:
                entering_ref[tile] = entering
    before = halo(before_ref, place_ref)
    copies[1].wait()
    for tile in range(width // LANES):
        here = lanes_of(tile)
        gate_ref[:, here] = short_conv(
            query_ref[:, here].astype(F32), before[0, :, here], taps_of(weight_ref, 0, here)
        )
    copies[2].wait()


def local_kernel(
    gate_ref,
    residual_ref,
    product_ref,
    first_ref,
    mode_rate_ref,
    inner_ref,
    entering_ref,
    skip_ref,
    base_ref,
):
    rows, width = product_ref.shape
    mask = group_mask(BF16)
    top = index_of((8, LANES), 0) < 2
    for tile in range(width // LANES):
        here = lanes_of(tile)
        pieces = []
        for chunk in range(rows // CHUNK):
            piece = product_ref[chunk * CHUNK : (chunk + 1) * CHUNK, here]
            if chunk == 0:
                wide = piece.astype(F32)
                head = jnp.where(top, first_ref[:, here], wide[:8])
                piece = jnp.concatenate([head, wide[8:]], axis=0).astype(BF16)
            pieces.append(piece)
        table = inner_ref[tile]
        inner = []
        for pair in range(rows // (2 * CHUNK)):
            sources = jnp.concatenate([spread(pieces[2 * pair + k], mask) for k in (0, 1)], axis=1)
            inner.append(jnp.dot(table, sources, preferred_element_type=F32))
        decay = jnp.exp(-float(CHUNK) * mode_rate_ref[:, here])
        state = jnp.zeros((MODES, LANES), F32)
        states = []
        for chunk in range(rows // CHUNK):
            states.append(spread(state.astype(BF16), mask))
            state = decay * state + inner[chunk // 2][CHUNK:, lanes_of(chunk % 2)]
        entering = entering_ref[tile]
        skip = skip_ref[:, here]
        for pair in range(rows // (2 * CHUNK)):
            two = jnp.concatenate(states[2 * pair : 2 * pair + 2], axis=1)
            conv = inner[pair][:CHUNK] + jnp.dot(entering, two, preferred_element_type=F32)
            for k in (0, 1):
                chunk = 2 * pair + k
                span = slice(chunk * CHUNK, (chunk + 1) * CHUNK)
                whole = conv[:, lanes_of(k)] + skip * pieces[chunk].astype(F32)
                base_ref[span, here] = residual_ref[span, here].astype(F32) + gate_ref[span, here] * whole


def join_kernel(tokens, radix, stride, place_ref, own_ref, mode_rate_ref, entry_ref, *refs):
    others, (found_ref, group_ref) = refs[: radix - 1], refs[radix - 1 :]
    rate = mode_rate_ref[...]
    run = lax.rem(place_ref[0] // stride, radix)
    step = float(tokens * stride)

    def decayed(value, runs):
        return jnp.exp(-step * runs.astype(F32) * rate) * value

    found = jnp.zeros_like(rate)
    total = decayed(own_ref[...].astype(F32), radix - 1 - run)
    for k, ref in enumerate(others, 1):
        other = ref[...].astype(F32)
        found = found + jnp.where(run >= k, decayed(other, jnp.full((), k - 1, jnp.int32)), 0.0)
        source = lax.rem(run - k + radix, radix)
        total = total + decayed(other, radix - 1 - source)
    within = lax.rem(place_ref[0], stride).astype(F32) * float(tokens)
    found_ref[...] = entry_ref[...] + jnp.exp(-within * rate) * found
    group_ref[...] = total.astype(BF16)


def carry_kernel(stride, received, place_ref, base_ref, gate_ref, carry_ref, mode_rate_ref, inner_entry_ref, *refs):
    entry_refs, (summed_ref, squares_ref) = refs[:received], refs[received:]
    rows, width = base_ref.shape
    run = place_ref[0] // stride
    within = lax.rem(place_ref[0], stride).astype(F32) * float(rows)
    mask = group_mask(BF16)
    total = jnp.zeros((rows, LANES), F32)
    nothing = jnp.zeros((LANES, LANES), BF16)
    for tile in range(width // WIDE):
        here = lanes_of(tile, WIDE)
        rate = mode_rate_ref[:, here]
        decay = jnp.exp(-float(rows * stride) * rate)
        outer = jnp.zeros_like(rate)
        for k in range(received, 0, -1):
            outer = decay * outer + jnp.where(run >= k, entry_refs[k - 1][:, here].astype(F32), 0.0)
        entry = (inner_entry_ref[:, here] + jnp.exp(-within * rate) * outer).astype(BF16)
        left, right = spread(entry[:, :LANES], mask), spread(entry[:, LANES:], mask)
        both = jnp.concatenate(
            [jnp.concatenate([left, nothing], axis=1), jnp.concatenate([nothing, right], axis=1)], axis=0
        )
        carry = jnp.dot(carry_ref[tile], both, preferred_element_type=F32)
        summed = base_ref[:, here] + gate_ref[:, here] * carry
        summed_ref[:, here] = summed
        square = summed * summed
        total = total + (square[:, :LANES] + square[:, LANES:])
    squares = lax.dot_general(
        jnp.ones((8, LANES), F32),
        total,
        (((1,), (1,)), ((), ())),
        precision=lax.Precision.HIGHEST,
        preferred_element_type=F32,
    )
    squares_ref[...] = squares[0:1]


def write_kernel(summed_ref, out_hbm, rounded_ref, sems):
    width = summed_ref.shape[1]
    copies = []
    for tile in range(width // WIDE):
        here = lanes_of(tile, WIDE)
        rounded_ref[:, here] = summed_ref[:, here].astype(BF16)
        span = pl.ds(tile * WIDE, WIDE)
        copies.append(pltpu.make_async_copy(rounded_ref.at[:, span], out_hbm.at[:, span], sems.at[tile]))
        copies[-1].start()
    for copy in copies:
        copy.wait()


def norm_kernel(full_width, parts, summed_ref, gain_ref, *refs):
    squares_refs, (out_hbm, rounded_ref, sems) = refs[:parts], refs[parts:]
    rows, width = summed_ref.shape
    squares = squares_refs[0][...]
    for ref in squares_refs[1:]:
        squares = squares + ref[...]
    scale_row = lax.rsqrt(squares / full_width + 1e-05)
    scale = jnp.concatenate([mode_column(scale_row[:, lanes_of(k)]) for k in range(rows // LANES)], axis=0)
    copies = []
    for tile in range(width // WIDE):
        for half in range(WIDE // LANES):
            here = lanes_of(tile * (WIDE // LANES) + half)
            rounded_ref[:, here] = (summed_ref[:, here] * scale * gain_ref[:, here]).astype(BF16)
        span = pl.ds(tile * WIDE, WIDE)
        copies.append(pltpu.make_async_copy(rounded_ref.at[:, span], out_hbm.at[:, span], sems.at[tile]))
        copies[-1].start()
    for copy in copies:
        copy.wait()


def params():
    return pltpu.CompilerParams(vmem_limit_bytes=VMEM_LIMIT)


def cost(microseconds):
    return pl.CostEstimate(flops=0, bytes_accessed=int(microseconds * 3.0e6), transcendentals=0)


def radices(count):
    found = []
    for radix in (2, 4, 4, 4):
        if count % radix == 0 and count > 1:
            found.append(radix)
            count //= radix
    for radix in (3, 2, 5, 7):
        while count % radix == 0 and count > 1:
            found.append(radix)
            count //= radix
    return found + ([count] if count > 1 else [])


def ring(count, shift):
    return [(i, (i + shift) % count) for i in range(count)]


def per_device(projected, short_weight, rates, residues, skip, residual, gain):
    rows, width = projected.shape[1:]
    taps = short_weight.shape[0]
    peers = lax.axis_size("ctx")
    full_width = width * lax.axis_size("fsdp")
    place = lax.axis_index("ctx").astype(jnp.int32).reshape(1)
    hbm_spec = pl.BlockSpec(memory_space=pltpu.HBM)
    vmem_spec = pl.BlockSpec(memory_space=pltpu.VMEM)
    smem_spec = pl.BlockSpec(memory_space=pltpu.SMEM)
    tiles = width // LANES
    wides = width // WIDE

    def kept(array):
        return pltpu.with_memory_space_constraint(array, pltpu.HBM)

    def f32(*shape):
        return jax.ShapeDtypeStruct(shape, F32)

    def bf16(*shape):
        return jax.ShapeDtypeStruct(shape, BF16)

    before = lax.ppermute(projected[:, rows - (taps - 1) :, :], "ctx", ring(peers, 1))

    product, state, mode_rate, head, weights = pl.pallas_call(
        state_kernel,
        in_specs=[hbm_spec] * 3,
        out_shape=[
            bf16(rows, width),
            f32(MODES, width),
            f32(MODES, width),
            f32(2, 8, width),
            f32(*short_weight.shape),
        ],
        scratch_shapes=[
            pltpu.VMEM((2, rows, width), BF16),
            pltpu.VMEM((wides, WIDE, rows), BF16),
            pltpu.VMEM(short_weight.shape, BF16),
            pltpu.VMEM((MODES, rates.shape[0]), F32),
            pltpu.SemaphoreType.DMA((wides,)),
            pltpu.SemaphoreType.DMA((2,)),
        ],
        compiler_params=params(),
        cost_estimate=cost(3),
        name="block_state",
    )(kept(projected), kept(short_weight), kept(rates.T))

    full_state, first = pl.pallas_call(
        lambda *refs: head_kernel(rows, *refs),
        in_specs=[smem_spec] + [vmem_spec] * 5,
        out_shape=[bf16(MODES, width), f32(8, width)],
        compiler_params=params(),
        cost_estimate=cost(0.2),
        name="head_tokens",
    )(place, before, head, weights, state, mode_rate)

    inner, entering, carry_table, gate, residual_here = pl.pallas_call(
        prepare_kernel,
        in_specs=[smem_spec] + [hbm_spec] * 3 + [vmem_spec] * 3,
        out_shape=[
            bf16(tiles, CHUNK + MODES, GROUPS * CHUNK),
            bf16(tiles, CHUNK, LANES),
            bf16(wides, rows, WIDE),
            f32(rows, width),
            bf16(rows, width),
        ],
        scratch_shapes=[
            pltpu.VMEM((rows, width), BF16),
            pltpu.VMEM((MODES, rates.shape[0]), F32),
            pltpu.SemaphoreType.DMA((3,)),
        ],
        compiler_params=params(),
        cost_estimate=cost(2),
        name="prepare",
    )(place, kept(projected), kept(residual), kept(residues.T), before, weights, mode_rate)

    group, entry, stride = full_state, jnp.zeros((MODES, width), F32), 1
    levels = radices(peers)
    for level, radix in enumerate(levels):
        size = stride * radix
        if level == len(levels) - 1:
            break
        cycles = [
            [(i, i // size * size + (i + stride * k) % size) for i in range(peers)] for k in range(1, radix)
        ]
        others = [lax.ppermute(group, "ctx", cycle) for cycle in cycles]
        if level == 0:
            others[0], inner = lax.optimization_barrier((others[0], inner))
        entry, group = pl.pallas_call(
            lambda *refs, radix=radix, stride=stride: join_kernel(rows, radix, stride, *refs),
            in_specs=[smem_spec] + [vmem_spec] * (2 + radix),
            out_shape=[f32(MODES, width), bf16(MODES, width)],
            compiler_params=params(),
            cost_estimate=cost(0.2),
            name="join",
        )(place, group, mode_rate, entry, *others)
        stride = size
    received = [lax.ppermute(group, "ctx", ring(peers, stride * k)) for k in range(1, levels[-1])]

    base = pl.pallas_call(
        local_kernel,
        out_shape=f32(rows, width),
        compiler_params=params(),
        cost_estimate=cost(5),
        name="local_conv",
    )(gate, residual_here, product, first, mode_rate, inner, entering, skip[None])

    summed, squares = pl.pallas_call(
        lambda *refs: carry_kernel(stride, len(received), *refs),
        in_specs=[smem_spec] + [vmem_spec] * (5 + len(received)),
        out_shape=[f32(rows, width), f32(1, rows)],
        compiler_params=params(),
        cost_estimate=cost(1),
        name="add_carry",
    )(place, base, gate, carry_table, mode_rate, entry, *received)

    count = lax.axis_size("fsdp")
    parts = [lax.ppermute(squares, "fsdp", ring(count, k)) for k in range(1, count)]

    def write(kernel, operands, name):
        return pl.pallas_call(
            kernel,
            out_specs=hbm_spec,
            out_shape=bf16(rows, width),
            scratch_shapes=[pltpu.VMEM((rows, width), BF16), pltpu.SemaphoreType.DMA((wides,))],
            compiler_params=params(),
            cost_estimate=cost(1),
            name=name,
        )(*operands)

    new_residual = write(write_kernel, (summed,), "new_residual")
    normed = write(
        lambda *refs: norm_kernel(full_width, count, *refs), (summed, gain[None], squares, *parts), "normed"
    )
    return (new_residual, normed)


def solution(mesh):
    return jax.shard_map(
        per_device,
        mesh=mesh,
        in_specs=(
            P(None, "ctx", "fsdp"),
            P(None, None, "fsdp"),
            P("fsdp", None),
            P("fsdp", None),
            P("fsdp"),
            P("ctx", "fsdp"),
            P("fsdp"),
        ),
        out_specs=(P("ctx", "fsdp"), P("ctx", "fsdp")),
        check_vma=False,
    )
```

```python
import jax
import jax.numpy as jnp
from jax import lax
from jax.experimental import pallas as pl
from jax.experimental.pallas import tpu as pltpu
from jax.sharding import PartitionSpec as P

CHANNELS_PER_GRP = 16
MODES = 16
CHUNK = 32
PIECE = 64
LANES = 128
WIDE = 256
GROUPS = LANES // CHANNELS_PER_GRP
VMEM_LIMIT = 16 * 1024 * 1024
F32 = jnp.float32
BF16 = jnp.bfloat16


def index_of(shape, dim):
    return lax.broadcasted_iota(jnp.int32, shape, dim)


def lanes_of(tile, width=LANES):
    return slice(tile * width, (tile + 1) * width)


def per_channel(table):
    groups = table.shape[1]
    width = groups * CHANNELS_PER_GRP
    high = table.astype(BF16)
    rest = table - high.astype(F32)
    middle = rest.astype(BF16)
    low = (rest - middle.astype(F32)).astype(BF16)
    terms = jnp.concatenate([high, middle, low], axis=0)
    parts = []
    for tile in range(width // WIDE):
        shape = (groups, WIDE)
        own = index_of(shape, 0) == index_of(shape, 1) // CHANNELS_PER_GRP + tile * (WIDE // CHANNELS_PER_GRP)
        three = jnp.dot(terms, jnp.where(own, 1.0, 0.0).astype(BF16), preferred_element_type=F32)
        parts.append(three[:MODES] + three[MODES : 2 * MODES] + three[2 * MODES :])
    return jnp.concatenate(parts, axis=1)


def mode_row(channel_table):
    own = index_of(channel_table.shape, 0) == (index_of(channel_table.shape, 1) & (MODES - 1))
    return jnp.sum(jnp.where(own, channel_table, 0.0), axis=0, keepdims=True)


def as_column(row):
    return jnp.transpose(jnp.broadcast_to(row, (LANES, LANES)))


def own_mode(dtype):
    shape = (GROUPS, MODES, LANES)
    own = index_of(shape, 0) * MODES + index_of(shape, 1) == index_of(shape, 2)
    return jnp.where(own, 1.0, 0.0).astype(dtype)


def split(x):
    high = x.astype(BF16)
    return high, (x - high.astype(F32)).astype(BF16)


def group_mask(dtype):
    shape = (GROUPS, MODES, LANES)
    own = index_of(shape, 0) == index_of(shape, 2) // CHANNELS_PER_GRP
    return jnp.where(own, 1.0, 0.0).astype(dtype)


def spread(rows, mask):
    size = rows.shape[0]
    copies = rows.reshape(1, size // MODES, MODES, LANES) * mask.reshape(GROUPS, 1, MODES, LANES)
    return copies.reshape(GROUPS * size, LANES)


def shifted(block, before):
    one = pltpu.roll(block, 1, 0)
    two = pltpu.roll(block, 2, 0)
    first = index_of((8, block.shape[1]), 0)
    near, far = (0.0, 0.0) if before is None else (before[1:2], before[0:1])
    head_one = jnp.where(first == 0, near, one[:8])
    head_two = jnp.where(first == 0, far, jnp.where(first == 1, near, two[:8]))
    if block.shape[0] == 8:
        return head_one, head_two
    return jnp.concatenate([head_one, one[8:]], axis=0), jnp.concatenate([head_two, two[8:]], axis=0)


def short_conv(block, before, weights):
    one, two = shifted(block, before)
    return weights[0] * block + weights[1] * one + weights[2] * two


def conv_piece(load, start, before, weights):
    if start == 0:
        return short_conv(load(0, PIECE), before, weights)
    block = load(start - 16, start + PIECE)[8:]
    one = pltpu.roll(block, 1, 0)[8:]
    two = pltpu.roll(block, 2, 0)[8:]
    return weights[0] * block[8:] + weights[1] * one + weights[2] * two


def taps_of(weights, feature, lanes):
    return [weights[tap, feature : feature + 1, lanes] for tap in range(weights.shape[0])]


def state_kernel(
    projected_ref,
    weight_hbm,
    rate_hbm,
    product_ref,
    state_ref,
    mode_rate_ref,
    head_ref,
    weight_ref,
    buffer_ref,
    ending_ref,
    short_ref,
    rate_ref,
    sems,
    small_sems,
):
    rows, width = product_ref.shape
    wides = width // WIDE
    rate_copy = pltpu.make_async_copy(rate_hbm, rate_ref, small_sems.at[0])
    rate_copy.start()
    weight_copy = pltpu.make_async_copy(weight_hbm, short_ref, small_sems.at[1])
    weight_copy.start()
    copies = []
    for tile in range(wides):
        here = pl.ds(tile * WIDE, WIDE)
        copies.append(
            pltpu.make_async_copy(projected_ref.at[pl.ds(1, 2), :, here], buffer_ref.at[:, :, here], sems.at[tile])
        )
        copies[-1].start()
    rate_copy.wait()
    mode_rate = per_channel(rate_ref[...])
    mode_rate_ref[...] = mode_rate
    eye = own_mode(BF16)
    token = index_of((2 * LANES, rows), 1)
    left = jnp.where(token < 2, -1e30, (token - (rows - 1)).astype(F32)).astype(BF16)
    for tile in range(width // LANES):
        high, low = split(mode_rate[:, lanes_of(tile)])
        diagonal = jnp.concatenate([spread(high, eye), spread(low, eye)], axis=1)
        exponent = jnp.dot(diagonal, left, preferred_element_type=F32)
        ending_ref[tile // 2, lanes_of(tile % 2), :] = jnp.exp(exponent).astype(BF16)
    weight_copy.wait()
    weights = short_ref[...].astype(F32)
    weight_ref[...] = weights
    mask = group_mask(F32)

    def leave_state(tile):
        every = jnp.dot(ending_ref[tile], product_ref[:, lanes_of(tile, WIDE)], preferred_element_type=F32)
        for half in range(WIDE // LANES):
            own = every[lanes_of(half), lanes_of(half)].reshape(GROUPS, MODES, LANES)
            state_ref[:, lanes_of((WIDE // LANES) * tile + half)] = jnp.sum(own * mask, axis=0)

    for wide in range(wides):
        copies[wide].wait()
        if wide > 0:
            leave_state(wide - 1)
        for tile in range(wide * (WIDE // LANES), (wide + 1) * (WIDE // LANES)):
            here = lanes_of(tile)
            for c in (0, 1):
                head_ref[c, :, here] = buffer_ref[c, 0:16, here].astype(F32)[:8]
            for start in range(0, rows, PIECE):
                parts = []
                for c in (0, 1):

                    def load(first, last):
                        return buffer_ref[c, first:last, here].astype(F32)

                    parts.append(conv_piece(load, start, None, taps_of(weights, c + 1, here)))
                product_ref[start : start + PIECE, here] = (parts[0] * parts[1]).astype(BF16)
    leave_state(wides - 1)


def halo(before_ref, place_ref):
    return jnp.where(place_ref[0] > 0, before_ref[...].astype(F32), 0.0)


def head_kernel(rows, place_ref, before_ref, head_ref, weight_ref, state_ref, mode_rate_ref, full_ref, first_ref):
    before = halo(before_ref, place_ref)
    everything = slice(0, head_ref.shape[2])
    parts = [short_conv(head_ref[c], before[c + 1], taps_of(weight_ref, c + 1, everything)) for c in (0, 1)]
    first = (parts[0] * parts[1]).astype(BF16).astype(F32)
    first_ref[...] = first
    rate = mode_rate_ref[...]
    early = jnp.exp(-float(rows - 1) * rate) * first[0:1] + jnp.exp(-float(rows - 2) * rate) * first[1:2]
    full_ref[...] = (state_ref[...] + early).astype(BF16)


def prepare_kernel(
    place_ref,
    projected_ref,
    residual_hbm,
    residue_hbm,
    before_ref,
    weight_ref,
    mode_rate_ref,
    inner_ref,
    entering_ref,
    carry_ref,
    gate_ref,
    residual_ref,
    query_ref,
    residue_ref,
    sems,
):
    rows, width = gate_ref.shape
    copies = [
        pltpu.make_async_copy(residue_hbm, residue_ref, sems.at[0]),
        pltpu.make_async_copy(projected_ref.at[0], query_ref, sems.at[1]),
        pltpu.make_async_copy(residual_hbm, residual_ref, sems.at[2]),
    ]
    for copy in copies:
        copy.start()
    copies[0].wait()
    residue = per_channel(residue_ref[...])
    wide = GROUPS * CHUNK
    step = index_of((CHUNK, LANES), 0).astype(F32)
    causal = (index_of((CHUNK, wide), 1) & (CHUNK - 1)) <= index_of((CHUNK, wide), 0)
    eye = own_mode(BF16)
    flat_eye = jnp.where((index_of((MODES, LANES), 1) & (MODES - 1)) == index_of((MODES, LANES), 0), 1.0, 0.0)
    flat_eye = flat_eye.astype(BF16)
    shape = (2 * LANES, wide)
    source = (index_of(shape, 1) & (CHUNK - 1)).astype(F32)
    own = (index_of(shape, 0) & (LANES - 1)) // MODES == index_of(shape, 1) // CHUNK
    risen = jnp.where(own, source, -1e30).astype(BF16)
    left = jnp.where(own, source - (CHUNK - 1), 0.0).astype(BF16)
    for tile in range(width // LANES):
        here = lanes_of(tile)
        rate = mode_rate_ref[:, here]
        high, low = split(rate)
        diagonal = jnp.concatenate([spread(high, eye), spread(low, eye)], axis=1)
        rising = jnp.exp(jnp.dot(diagonal, risen, preferred_element_type=F32))
        each = jnp.concatenate([high * flat_eye, low * flat_eye], axis=1)
        ending = jnp.exp(jnp.dot(each, left, preferred_element_type=F32))
        rate_row = mode_row(rate)
        falling = mode_row(residue[:, here]) * jnp.exp(-rate_row * step)
        fall_high, fall_low = split(falling)
        rise_high, rise_low = split(rising)
        taps = jnp.dot(jnp.concatenate([fall_high, fall_low], axis=0), rise_high, preferred_element_type=F32)
        taps = taps[:CHUNK] + taps[CHUNK:] + jnp.dot(fall_high, rise_low, preferred_element_type=F32)
        taps = jnp.where(causal, taps, 0.0)
        inner_ref[tile] = jnp.concatenate([taps.astype(BF16), ending.astype(BF16)], axis=0)
        half = tile % (WIDE // LANES)
        for chunk in range(rows // CHUNK):
            entering = (falling * jnp.exp(-float(CHUNK * chunk + 1) * rate_row)).astype(BF16)
            carry_ref[tile // (WIDE // LANES), chunk * CHUNK : (chunk + 1) * CHUNK, lanes_of(half)] = entering
            if chunk == 0:
                entering_ref[tile] = entering
    before = halo(before_ref, place_ref)
    copies[1].wait()
    for tile in range(width // LANES):
        here = lanes_of(tile)

        def load(first, last):
            return query_ref[first:last, here].astype(F32)

        for start in range(0, rows, PIECE):
            gate_ref[start : start + PIECE, here] = conv_piece(
                load, start, before[0, :, here], taps_of(weight_ref, 0, here)
            )
    copies[2].wait()


def local_kernel(
    gate_ref,
    residual_ref,
    product_ref,
    first_ref,
    mode_rate_ref,
    inner_ref,
    entering_ref,
    skip_ref,
    base_ref,
):
    rows, width = product_ref.shape
    mask = group_mask(BF16)
    top = index_of((8, LANES), 0) < 2
    for tile in range(width // LANES):
        here = lanes_of(tile)
        pieces = []
        for chunk in range(rows // CHUNK):
            piece = product_ref[chunk * CHUNK : (chunk + 1) * CHUNK, here]
            if chunk == 0:
                wide = piece.astype(F32)
                head = jnp.where(top, first_ref[:, here], wide[:8])
                piece = jnp.concatenate([head, wide[8:]], axis=0).astype(BF16)
            pieces.append(piece)
        table = inner_ref[tile]
        inner = []
        for pair in range(rows // (2 * CHUNK)):
            sources = jnp.concatenate([spread(pieces[2 * pair + k], mask) for k in (0, 1)], axis=1)
            inner.append(jnp.dot(table, sources, preferred_element_type=F32))
        decay = jnp.exp(-float(CHUNK) * mode_rate_ref[:, here])
        state = jnp.zeros((MODES, LANES), F32)
        states = []
        for chunk in range(rows // CHUNK):
            states.append(spread(state.astype(BF16), mask))
            state = decay * state + inner[chunk // 2][CHUNK:, lanes_of(chunk % 2)]
        entering = entering_ref[tile]
        skip = skip_ref[:, here]
        for pair in range(rows // (2 * CHUNK)):
            two = jnp.concatenate(states[2 * pair : 2 * pair + 2], axis=1)
            conv = inner[pair][:CHUNK] + jnp.dot(entering, two, preferred_element_type=F32)
            for k in (0, 1):
                chunk = 2 * pair + k
                span = slice(chunk * CHUNK, (chunk + 1) * CHUNK)
                whole = conv[:, lanes_of(k)] + skip * pieces[chunk].astype(F32)
                base_ref[span, here] = residual_ref[span, here].astype(F32) + gate_ref[span, here] * whole


def join_kernel(tokens, radix, stride, place_ref, own_ref, mode_rate_ref, entry_ref, *refs):
    others, (found_ref, group_ref) = refs[: radix - 1], refs[radix - 1 :]
    own = own_ref[0] if len(own_ref.shape) == 3 else own_ref[...]
    rate = mode_rate_ref[...]
    run = lax.rem(place_ref[0] // stride, radix)
    step = float(tokens * stride)

    def decayed(value, runs):
        return jnp.exp(-step * runs.astype(F32) * rate) * value

    found = jnp.zeros_like(rate)
    total = decayed(own.astype(F32), radix - 1 - run)
    for k, ref in enumerate(others, 1):
        other = ref[...].reshape(rate.shape).astype(F32)
        found = found + jnp.where(run >= k, decayed(other, jnp.full((), k - 1, jnp.int32)), 0.0)
        source = lax.rem(run - k + radix, radix)
        total = total + decayed(other, radix - 1 - source)
    within = lax.rem(place_ref[0], stride).astype(F32) * float(tokens)
    found_ref[...] = entry_ref[...] + jnp.exp(-within * rate) * found
    for copy in range(group_ref.shape[0]):
        group_ref[copy] = total.astype(BF16)


def carry_kernel(
    stride,
    place_ref,
    base_ref,
    gate_ref,
    carry_ref,
    mode_rate_ref,
    inner_entry_ref,
    received_ref,
    summed_ref,
    squares_ref,
):
    rows, width = base_ref.shape
    run = place_ref[0] // stride
    within = lax.rem(place_ref[0], stride).astype(F32) * float(rows)
    mask = group_mask(BF16)
    total = jnp.zeros((rows, LANES), F32)
    nothing = jnp.zeros((LANES, LANES), BF16)
    for tile in range(width // WIDE):
        here = lanes_of(tile, WIDE)
        rate = mode_rate_ref[:, here]
        decay = jnp.exp(-float(rows * stride) * rate)
        outer = jnp.zeros_like(rate)
        for k in range(received_ref.shape[0] - 1):
            outer = jnp.where(k < run, decay * outer + received_ref[k, :, here].astype(F32), outer)
        entry = (inner_entry_ref[:, here] + jnp.exp(-within * rate) * outer).astype(BF16)
        left, right = spread(entry[:, :LANES], mask), spread(entry[:, LANES:], mask)
        both = jnp.concatenate(
            [jnp.concatenate([left, nothing], axis=1), jnp.concatenate([nothing, right], axis=1)], axis=0
        )
        carry = jnp.dot(carry_ref[tile], both, preferred_element_type=F32)
        summed = base_ref[:, here] + gate_ref[:, here] * carry
        summed_ref[:, here] = summed
        square = summed * summed
        total = total + (square[:, :LANES] + square[:, LANES:])
    squares = lax.dot_general(
        jnp.ones((8, LANES), F32),
        total,
        (((1,), (1,)), ((), ())),
        precision=lax.Precision.HIGHEST,
        preferred_element_type=F32,
    )
    for copy in range(squares_ref.shape[0]):
        squares_ref[copy] = squares[0:1]


def write_kernel(summed_ref, out_hbm, rounded_ref, sems):
    width = summed_ref.shape[1]
    copies = []
    for tile in range(width // WIDE):
        here = lanes_of(tile, WIDE)
        rounded_ref[:, here] = summed_ref[:, here].astype(BF16)
        span = pl.ds(tile * WIDE, WIDE)
        copies.append(pltpu.make_async_copy(rounded_ref.at[:, span], out_hbm.at[:, span], sems.at[tile]))
        copies[-1].start()
    for copy in copies:
        copy.wait()


def norm_kernel(full_width, summed_ref, gain_ref, squares_ref, out_hbm, rounded_ref, sems):
    rows, width = summed_ref.shape
    squares = squares_ref[0]
    for part in range(1, squares_ref.shape[0]):
        squares = squares + squares_ref[part]
    scale_row = lax.rsqrt(squares / full_width + 1e-05)
    scale = jnp.concatenate([as_column(scale_row[:, lanes_of(k)]) for k in range(rows // LANES)], axis=0)
    copies = []
    for tile in range(width // WIDE):
        for half in range(WIDE // LANES):
            here = lanes_of(tile * (WIDE // LANES) + half)
            rounded_ref[:, here] = (summed_ref[:, here] * scale * gain_ref[:, here]).astype(BF16)
        span = pl.ds(tile * WIDE, WIDE)
        copies.append(pltpu.make_async_copy(rounded_ref.at[:, span], out_hbm.at[:, span], sems.at[tile]))
        copies[-1].start()
    for copy in copies:
        copy.wait()


def params():
    return pltpu.CompilerParams(vmem_limit_bytes=VMEM_LIMIT)


def cost(microseconds):
    return pl.CostEstimate(flops=0, bytes_accessed=int(microseconds * 3.0e6), transcendentals=0)


def radices(count):
    found = []
    for radix in (2, 4, 4, 4):
        if count % radix == 0 and count > 1:
            found.append(radix)
            count //= radix
    for radix in (3, 2, 5, 7):
        while count % radix == 0 and count > 1:
            found.append(radix)
            count //= radix
    return found + ([count] if count > 1 else [])


def ring(count, shift):
    return [(i, (i + shift) % count) for i in range(count)]


def per_device(projected, short_weight, rates, residues, skip, residual, gain):
    rows, width = projected.shape[1:]
    taps = short_weight.shape[0]
    peers = lax.axis_size("ctx")
    full_width = width * lax.axis_size("fsdp")
    place = lax.axis_index("ctx").astype(jnp.int32).reshape(1)
    hbm_spec = pl.BlockSpec(memory_space=pltpu.HBM)
    vmem_spec = pl.BlockSpec(memory_space=pltpu.VMEM)
    smem_spec = pl.BlockSpec(memory_space=pltpu.SMEM)
    tiles = width // LANES
    wides = width // WIDE

    def kept(array):
        return pltpu.with_memory_space_constraint(array, pltpu.HBM)

    def f32(*shape):
        return jax.ShapeDtypeStruct(shape, F32)

    def bf16(*shape):
        return jax.ShapeDtypeStruct(shape, BF16)

    before = lax.ppermute(projected[:, rows - (taps - 1) :, :], "ctx", ring(peers, 1))

    product, state, mode_rate, head, weights = pl.pallas_call(
        state_kernel,
        in_specs=[hbm_spec] * 3,
        out_shape=[
            bf16(rows, width),
            f32(MODES, width),
            f32(MODES, width),
            f32(2, 8, width),
            f32(*short_weight.shape),
        ],
        scratch_shapes=[
            pltpu.VMEM((2, rows, width), BF16),
            pltpu.VMEM((wides, WIDE, rows), BF16),
            pltpu.VMEM(short_weight.shape, BF16),
            pltpu.VMEM((MODES, rates.shape[0]), F32),
            pltpu.SemaphoreType.DMA((wides,)),
            pltpu.SemaphoreType.DMA((2,)),
        ],
        compiler_params=params(),
        cost_estimate=cost(3),
        name="block_state",
    )(kept(projected), kept(short_weight), kept(rates.T))

    full_state, first = pl.pallas_call(
        lambda *refs: head_kernel(rows, *refs),
        in_specs=[smem_spec] + [vmem_spec] * 5,
        out_shape=[bf16(MODES, width), f32(8, width)],
        compiler_params=params(),
        cost_estimate=cost(0.2),
        name="head_tokens",
    )(place, before, head, weights, state, mode_rate)

    inner, entering, carry_table, gate, residual_here = pl.pallas_call(
        prepare_kernel,
        in_specs=[smem_spec] + [hbm_spec] * 3 + [vmem_spec] * 3,
        out_shape=[
            bf16(tiles, CHUNK + MODES, GROUPS * CHUNK),
            bf16(tiles, CHUNK, LANES),
            bf16(wides, rows, WIDE),
            f32(rows, width),
            bf16(rows, width),
        ],
        scratch_shapes=[
            pltpu.VMEM((rows, width), BF16),
            pltpu.VMEM((MODES, rates.shape[0]), F32),
            pltpu.SemaphoreType.DMA((3,)),
        ],
        compiler_params=params(),
        cost_estimate=cost(2),
        name="prepare",
    )(place, kept(projected), kept(residual), kept(residues.T), before, weights, mode_rate)

    group, entry, stride = full_state, jnp.zeros((MODES, width), F32), 1
    levels = radices(peers)
    for level, radix in enumerate(levels):
        size = stride * radix
        if level == len(levels) - 1:
            break
        cycles = [
            [(i, i // size * size + (i + stride * k) % size) for i in range(peers)] for k in range(1, radix)
        ]
        others = [lax.ppermute(group, "ctx", cycle) for cycle in cycles]
        if level == 0:
            others[0], inner = lax.optimization_barrier((others[0], inner))
        copies = levels[-1] if level == len(levels) - 2 else 1
        entry, group = pl.pallas_call(
            lambda *refs, radix=radix, stride=stride: join_kernel(rows, radix, stride, *refs),
            in_specs=[smem_spec] + [vmem_spec] * (2 + radix),
            out_shape=[f32(MODES, width), bf16(copies, MODES, width)],
            compiler_params=params(),
            cost_estimate=cost(0.2),
            name="join",
        )(place, group, mode_rate, entry, *others)
        stride = size
    if len(levels) == 1:
        group = jnp.broadcast_to(group[None], (levels[0], MODES, width))
    runs = [[first + stride * k for k in range(levels[-1])] for first in range(stride)]
    received = lax.all_to_all(group, "ctx", 0, 0, axis_index_groups=runs, tiled=True)

    base = pl.pallas_call(
        local_kernel,
        out_shape=f32(rows, width),
        compiler_params=params(),
        cost_estimate=cost(5),
        name="local_conv",
    )(gate, residual_here, product, first, mode_rate, inner, entering, skip[None])

    count = lax.axis_size("fsdp")
    summed, squares = pl.pallas_call(
        lambda *refs: carry_kernel(stride, *refs),
        in_specs=[smem_spec] + [vmem_spec] * 6,
        out_shape=[f32(rows, width), f32(count, 1, rows)],
        compiler_params=params(),
        cost_estimate=cost(1),
        name="add_carry",
    )(place, base, gate, carry_table, mode_rate, entry, received)

    squares = lax.all_to_all(squares, "fsdp", 0, 0, tiled=True)

    def write(kernel, operands, name):
        return pl.pallas_call(
            kernel,
            out_specs=hbm_spec,
            out_shape=bf16(rows, width),
            scratch_shapes=[pltpu.VMEM((rows, width), BF16), pltpu.SemaphoreType.DMA((wides,))],
            compiler_params=params(),
            cost_estimate=cost(1),
            name=name,
        )(*operands)

    new_residual = write(write_kernel, (summed,), "new_residual")
    normed = write(
        lambda *refs: norm_kernel(full_width, *refs), (summed, gain[None], squares), "normed"
    )
    return (new_residual, normed)


def solution(mesh):
    return jax.shard_map(
        per_device,
        mesh=mesh,
        in_specs=(
            P(None, "ctx", "fsdp"),
            P(None, None, "fsdp"),
            P("fsdp", None),
            P("fsdp", None),
            P("fsdp"),
            P("ctx", "fsdp"),
            P("fsdp"),
        ),
        out_specs=(P("ctx", "fsdp"), P("ctx", "fsdp")),
        check_vma=False,
    )
```

```python
import jax
import jax.numpy as jnp
from jax import lax
from jax.experimental import pallas as pl
from jax.experimental.pallas import tpu as pltpu
from jax.sharding import PartitionSpec as P

CHANNELS_PER_GRP = 16
MODES = 16
CHUNK = 32
LANES = 128
WIDE = 256
GROUPS = LANES // CHANNELS_PER_GRP
VMEM_LIMIT = 16 * 1024 * 1024
F32 = jnp.float32
BF16 = jnp.bfloat16


def index_of(shape, dim):
    return lax.broadcasted_iota(jnp.int32, shape, dim)


def lanes_of(tile, width=LANES):
    return slice(tile * width, (tile + 1) * width)


def per_channel(table):
    groups = table.shape[1]
    width = groups * CHANNELS_PER_GRP
    high = table.astype(BF16)
    rest = table - high.astype(F32)
    middle = rest.astype(BF16)
    low = (rest - middle.astype(F32)).astype(BF16)
    terms = jnp.concatenate([high, middle, low], axis=0)
    parts = []
    for tile in range(width // WIDE):
        shape = (groups, WIDE)
        own = index_of(shape, 0) == index_of(shape, 1) // CHANNELS_PER_GRP + tile * (WIDE // CHANNELS_PER_GRP)
        three = jnp.dot(terms, jnp.where(own, 1.0, 0.0).astype(BF16), preferred_element_type=F32)
        parts.append(three[:MODES] + three[MODES : 2 * MODES] + three[2 * MODES :])
    return jnp.concatenate(parts, axis=1)


def mode_row(channel_table):
    own = index_of(channel_table.shape, 0) == (index_of(channel_table.shape, 1) & (MODES - 1))
    return jnp.sum(jnp.where(own, channel_table, 0.0), axis=0, keepdims=True)


def as_column(row):
    return jnp.transpose(jnp.broadcast_to(row, (LANES, LANES)))


def own_mode(dtype):
    shape = (GROUPS, MODES, LANES)
    own = index_of(shape, 0) * MODES + index_of(shape, 1) == index_of(shape, 2)
    return jnp.where(own, 1.0, 0.0).astype(dtype)


def split(x):
    high = x.astype(BF16)
    return high, (x - high.astype(F32)).astype(BF16)


def group_mask(dtype):
    shape = (GROUPS, MODES, LANES)
    own = index_of(shape, 0) == index_of(shape, 2) // CHANNELS_PER_GRP
    return jnp.where(own, 1.0, 0.0).astype(dtype)


def spread(rows, mask):
    size = rows.shape[0]
    copies = rows.reshape(1, size // MODES, MODES, LANES) * mask.reshape(GROUPS, 1, MODES, LANES)
    return copies.reshape(GROUPS * size, LANES)


def shifted(block, before):
    one = pltpu.roll(block, 1, 0)
    two = pltpu.roll(block, 2, 0)
    first = index_of((8, block.shape[1]), 0)
    near, far = (0.0, 0.0) if before is None else (before[1:2], before[0:1])
    head_one = jnp.where(first == 0, near, one[:8])
    head_two = jnp.where(first == 0, far, jnp.where(first == 1, near, two[:8]))
    if block.shape[0] == 8:
        return head_one, head_two
    return jnp.concatenate([head_one, one[8:]], axis=0), jnp.concatenate([head_two, two[8:]], axis=0)


def short_conv(block, before, weights):
    one, two = shifted(block, before)
    return weights[0] * block + weights[1] * one + weights[2] * two


def shift_matrix(rows):
    shape = (2 * rows, rows)
    target = index_of(shape, 0)
    source = index_of(shape, 1)
    taken = jnp.where(target < rows, target - 1, target - (rows + 2))
    return jnp.where(source == taken, 1.0, 0.0).astype(BF16)


def wide_conv(block, shift, weights):
    rows = block.shape[0]
    earlier = jnp.dot(shift, block, preferred_element_type=F32)
    return weights[0] * block.astype(F32) + weights[1] * earlier[:rows] + weights[2] * earlier[rows:]


def taps_of(weights, feature, lanes):
    return [weights[tap, feature : feature + 1, lanes] for tap in range(weights.shape[0])]


def state_kernel(
    projected_ref,
    weight_hbm,
    rate_hbm,
    product_ref,
    state_ref,
    mode_rate_ref,
    head_ref,
    weight_ref,
    buffer_ref,
    ending_ref,
    shift_ref,
    short_ref,
    rate_ref,
    sems,
    small_sems,
):
    rows, width = product_ref.shape
    wides = width // WIDE
    rate_copy = pltpu.make_async_copy(rate_hbm, rate_ref, small_sems.at[0])
    rate_copy.start()
    weight_copy = pltpu.make_async_copy(weight_hbm, short_ref, small_sems.at[1])
    weight_copy.start()
    copies = []
    for tile in range(wides):
        here = pl.ds(tile * WIDE, WIDE)
        copies.append(
            pltpu.make_async_copy(projected_ref.at[pl.ds(1, 2), :, here], buffer_ref.at[:, :, here], sems.at[tile])
        )
        copies[-1].start()
    shift_ref[...] = shift_matrix(rows)
    rate_copy.wait()
    mode_rate = per_channel(rate_ref[...])
    mode_rate_ref[...] = mode_rate
    eye = own_mode(BF16)
    token = index_of((2 * LANES, rows), 1)
    left = jnp.where(token < 2, -1e30, (token - (rows - 1)).astype(F32)).astype(BF16)
    for tile in range(width // LANES):
        high, low = split(mode_rate[:, lanes_of(tile)])
        diagonal = jnp.concatenate([spread(high, eye), spread(low, eye)], axis=1)
        exponent = jnp.dot(diagonal, left, preferred_element_type=F32)
        ending_ref[tile // 2, lanes_of(tile % 2), :] = jnp.exp(exponent).astype(BF16)
    weight_copy.wait()
    weights = short_ref[...].astype(F32)
    weight_ref[...] = weights
    mask = group_mask(F32)

    def leave_state(tile):
        every = jnp.dot(ending_ref[tile], product_ref[:, lanes_of(tile, WIDE)], preferred_element_type=F32)
        for half in range(WIDE // LANES):
            own = every[lanes_of(half), lanes_of(half)].reshape(GROUPS, MODES, LANES)
            state_ref[:, lanes_of((WIDE // LANES) * tile + half)] = jnp.sum(own * mask, axis=0)

    for wide in range(wides):
        copies[wide].wait()
        if wide > 0:
            leave_state(wide - 1)
        here = lanes_of(wide, WIDE)
        parts = []
        for c in (0, 1):
            head_ref[c, :, here] = buffer_ref[c, 0:16, here].astype(F32)[:8]
            parts.append(wide_conv(buffer_ref[c, :, here], shift_ref[...], taps_of(weights, c + 1, here)))
        product_ref[:, here] = (parts[0] * parts[1]).astype(BF16)
    leave_state(wides - 1)


def halo(before_ref, place_ref):
    return jnp.where(place_ref[0] > 0, before_ref[...].astype(F32), 0.0)


def head_kernel(rows, place_ref, before_ref, head_ref, weight_ref, state_ref, mode_rate_ref, full_ref, first_ref):
    before = halo(before_ref, place_ref)
    everything = slice(0, head_ref.shape[2])
    parts = [short_conv(head_ref[c], before[c + 1], taps_of(weight_ref, c + 1, everything)) for c in (0, 1)]
    first = (parts[0] * parts[1]).astype(BF16).astype(F32)
    first_ref[...] = first
    rate = mode_rate_ref[...]
    early = jnp.exp(-float(rows - 1) * rate) * first[0:1] + jnp.exp(-float(rows - 2) * rate) * first[1:2]
    full_ref[...] = (state_ref[...] + early).astype(BF16)


def prepare_kernel(
    place_ref,
    projected_ref,
    residual_hbm,
    residue_hbm,
    before_ref,
    weight_ref,
    mode_rate_ref,
    inner_ref,
    entering_ref,
    carry_ref,
    gate_ref,
    residual_ref,
    query_ref,
    shift_ref,
    residue_ref,
    sems,
):
    rows, width = gate_ref.shape
    copies = [
        pltpu.make_async_copy(residue_hbm, residue_ref, sems.at[0]),
        pltpu.make_async_copy(projected_ref.at[0], query_ref, sems.at[1]),
        pltpu.make_async_copy(residual_hbm, residual_ref, sems.at[2]),
    ]
    for copy in copies:
        copy.start()
    copies[0].wait()
    residue = per_channel(residue_ref[...])
    wide = GROUPS * CHUNK
    step = index_of((CHUNK, LANES), 0).astype(F32)
    causal = (index_of((CHUNK, wide), 1) & (CHUNK - 1)) <= index_of((CHUNK, wide), 0)
    eye = own_mode(BF16)
    flat_eye = jnp.where((index_of((MODES, LANES), 1) & (MODES - 1)) == index_of((MODES, LANES), 0), 1.0, 0.0)
    flat_eye = flat_eye.astype(BF16)
    shape = (2 * LANES, wide)
    source = (index_of(shape, 1) & (CHUNK - 1)).astype(F32)
    own = (index_of(shape, 0) & (LANES - 1)) // MODES == index_of(shape, 1) // CHUNK
    risen = jnp.where(own, source, -1e30).astype(BF16)
    left = jnp.where(own, source - (CHUNK - 1), 0.0).astype(BF16)
    for tile in range(width // LANES):
        here = lanes_of(tile)
        rate = mode_rate_ref[:, here]
        high, low = split(rate)
        diagonal = jnp.concatenate([spread(high, eye), spread(low, eye)], axis=1)
        rising = jnp.exp(jnp.dot(diagonal, risen, preferred_element_type=F32))
        each = jnp.concatenate([high * flat_eye, low * flat_eye], axis=1)
        ending = jnp.exp(jnp.dot(each, left, preferred_element_type=F32))
        rate_row = mode_row(rate)
        falling = mode_row(residue[:, here]) * jnp.exp(-rate_row * step)
        fall_high, fall_low = split(falling)
        rise_high, rise_low = split(rising)
        taps = jnp.dot(jnp.concatenate([fall_high, fall_low], axis=0), rise_high, preferred_element_type=F32)
        taps = taps[:CHUNK] + taps[CHUNK:] + jnp.dot(fall_high, rise_low, preferred_element_type=F32)
        taps = jnp.where(causal, taps, 0.0)
        inner_ref[tile] = jnp.concatenate([taps.astype(BF16), ending.astype(BF16)], axis=0)
        half = tile % (WIDE // LANES)
        for chunk in range(rows // CHUNK):
            entering = (falling * jnp.exp(-float(CHUNK * chunk + 1) * rate_row)).astype(BF16)
            carry_ref[tile // (WIDE // LANES), chunk * CHUNK : (chunk + 1) * CHUNK, lanes_of(half)] = entering
            if chunk == 0:
                entering_ref[tile] = entering
    before = halo(before_ref, place_ref)
    copies[1].wait()
    shift_ref[...] = shift_matrix(rows)
    for tile in range(width // WIDE):
        here = lanes_of(tile, WIDE)
        weights = taps_of(weight_ref, 0, here)
        gate_ref[:, here] = wide_conv(query_ref[:, here], shift_ref[...], weights)
        head = query_ref[0:16, here].astype(F32)[:8]
        gate_ref[0:8, here] = short_conv(head, before[0, :, here], weights)
    copies[2].wait()


def local_kernel(
    gate_ref,
    residual_ref,
    product_ref,
    first_ref,
    mode_rate_ref,
    inner_ref,
    entering_ref,
    skip_ref,
    base_ref,
):
    rows, width = product_ref.shape
    mask = group_mask(BF16)
    top = index_of((8, LANES), 0) < 2
    for tile in range(width // LANES):
        here = lanes_of(tile)
        pieces = []
        for chunk in range(rows // CHUNK):
            piece = product_ref[chunk * CHUNK : (chunk + 1) * CHUNK, here]
            if chunk == 0:
                wide = piece.astype(F32)
                head = jnp.where(top, first_ref[:, here], wide[:8])
                piece = jnp.concatenate([head, wide[8:]], axis=0).astype(BF16)
            pieces.append(piece)
        table = inner_ref[tile]
        inner = []
        for pair in range(rows // (2 * CHUNK)):
            sources = jnp.concatenate([spread(pieces[2 * pair + k], mask) for k in (0, 1)], axis=1)
            inner.append(jnp.dot(table, sources, preferred_element_type=F32))
        decay = jnp.exp(-float(CHUNK) * mode_rate_ref[:, here])
        state = jnp.zeros((MODES, LANES), F32)
        states = []
        for chunk in range(rows // CHUNK):
            states.append(spread(state.astype(BF16), mask))
            state = decay * state + inner[chunk // 2][CHUNK:, lanes_of(chunk % 2)]
        entering = entering_ref[tile]
        skip = skip_ref[:, here]
        for pair in range(rows // (2 * CHUNK)):
            two = jnp.concatenate(states[2 * pair : 2 * pair + 2], axis=1)
            conv = inner[pair][:CHUNK] + jnp.dot(entering, two, preferred_element_type=F32)
            for k in (0, 1):
                chunk = 2 * pair + k
                span = slice(chunk * CHUNK, (chunk + 1) * CHUNK)
                whole = conv[:, lanes_of(k)] + skip * pieces[chunk].astype(F32)
                base_ref[span, here] = residual_ref[span, here].astype(F32) + gate_ref[span, here] * whole


def join_kernel(tokens, radix, stride, place_ref, own_ref, mode_rate_ref, entry_ref, *refs):
    others, (found_ref, group_ref) = refs[: radix - 1], refs[radix - 1 :]
    rate = mode_rate_ref[...]
    run = lax.rem(place_ref[0] // stride, radix)
    step = float(tokens * stride)

    def decayed(value, runs):
        return jnp.exp(-step * runs.astype(F32) * rate) * value

    found = jnp.zeros_like(rate)
    total = decayed(own_ref[...].astype(F32), radix - 1 - run)
    for k, ref in enumerate(others, 1):
        other = ref[...].astype(F32)
        found = found + jnp.where(run >= k, decayed(other, jnp.full((), k - 1, jnp.int32)), 0.0)
        source = lax.rem(run - k + radix, radix)
        total = total + decayed(other, radix - 1 - source)
    within = lax.rem(place_ref[0], stride).astype(F32) * float(tokens)
    found_ref[...] = entry_ref[...] + jnp.exp(-within * rate) * found
    group_ref[...] = total.astype(BF16)


def carry_kernel(stride, place_ref, base_ref, gate_ref, carry_ref, mode_rate_ref, inner_entry_ref, *refs):
    entry_refs, (summed_ref, squares_ref) = refs[:-2], refs[-2:]
    rows, width = base_ref.shape
    run = place_ref[0] // stride
    within = lax.rem(place_ref[0], stride).astype(F32) * float(rows)
    mask = group_mask(BF16)
    total = jnp.zeros((rows, LANES), F32)
    nothing = jnp.zeros((LANES, LANES), BF16)
    for tile in range(width // WIDE):
        here = lanes_of(tile, WIDE)
        rate = mode_rate_ref[:, here]
        decay = jnp.exp(-float(rows * stride) * rate)
        outer = jnp.zeros_like(rate)
        for k in range(len(entry_refs), 0, -1):
            outer = decay * outer + jnp.where(run >= k, entry_refs[k - 1][:, here].astype(F32), 0.0)
        entry = (inner_entry_ref[:, here] + jnp.exp(-within * rate) * outer).astype(BF16)
        left, right = spread(entry[:, :LANES], mask), spread(entry[:, LANES:], mask)
        both = jnp.concatenate(
            [jnp.concatenate([left, nothing], axis=1), jnp.concatenate([nothing, right], axis=1)], axis=0
        )
        carry = jnp.dot(carry_ref[tile], both, preferred_element_type=F32)
        summed = base_ref[:, here] + gate_ref[:, here] * carry
        summed_ref[:, here] = summed
        square = summed * summed
        total = total + (square[:, :LANES] + square[:, LANES:])
    squares = lax.dot_general(
        jnp.ones((8, LANES), F32),
        total,
        (((1,), (1,)), ((), ())),
        precision=lax.Precision.HIGHEST,
        preferred_element_type=F32,
    )
    squares_ref[...] = squares[0:1]


def write_kernel(summed_ref, out_hbm, rounded_ref, sems):
    width = summed_ref.shape[1]
    copies = []
    for tile in range(width // WIDE):
        here = lanes_of(tile, WIDE)
        rounded_ref[:, here] = summed_ref[:, here].astype(BF16)
        span = pl.ds(tile * WIDE, WIDE)
        copies.append(pltpu.make_async_copy(rounded_ref.at[:, span], out_hbm.at[:, span], sems.at[tile]))
        copies[-1].start()
    for copy in copies:
        copy.wait()


def norm_kernel(full_width, summed_ref, gain_ref, *refs):
    squares_refs, (out_hbm, rounded_ref, sems) = refs[:-3], refs[-3:]
    rows, width = summed_ref.shape
    squares = squares_refs[0][...]
    for ref in squares_refs[1:]:
        squares = squares + ref[...]
    scale_row = lax.rsqrt(squares / full_width + 1e-05)
    scale = jnp.concatenate([as_column(scale_row[:, lanes_of(k)]) for k in range(rows // LANES)], axis=0)
    copies = []
    for tile in range(width // WIDE):
        for half in range(WIDE // LANES):
            here = lanes_of(tile * (WIDE // LANES) + half)
            rounded_ref[:, here] = (summed_ref[:, here] * scale * gain_ref[:, here]).astype(BF16)
        span = pl.ds(tile * WIDE, WIDE)
        copies.append(pltpu.make_async_copy(rounded_ref.at[:, span], out_hbm.at[:, span], sems.at[tile]))
        copies[-1].start()
    for copy in copies:
        copy.wait()


def params():
    return pltpu.CompilerParams(vmem_limit_bytes=VMEM_LIMIT)


def cost(microseconds):
    return pl.CostEstimate(flops=0, bytes_accessed=int(microseconds * 3.0e6), transcendentals=0)


def radices(count):
    found = []
    for radix in (2, 4, 4, 4):
        if count % radix == 0 and count > 1:
            found.append(radix)
            count //= radix
    for radix in (3, 2, 5, 7):
        while count % radix == 0 and count > 1:
            found.append(radix)
            count //= radix
    return found + ([count] if count > 1 else [])


def ring(count, shift):
    return [(i, (i + shift) % count) for i in range(count)]


def per_device(projected, short_weight, rates, residues, skip, residual, gain):
    rows, width = projected.shape[1:]
    taps = short_weight.shape[0]
    peers = lax.axis_size("ctx")
    full_width = width * lax.axis_size("fsdp")
    place = lax.axis_index("ctx").astype(jnp.int32).reshape(1)
    hbm_spec = pl.BlockSpec(memory_space=pltpu.HBM)
    vmem_spec = pl.BlockSpec(memory_space=pltpu.VMEM)
    smem_spec = pl.BlockSpec(memory_space=pltpu.SMEM)
    tiles = width // LANES
    wides = width // WIDE

    def kept(array):
        return pltpu.with_memory_space_constraint(array, pltpu.HBM)

    def f32(*shape):
        return jax.ShapeDtypeStruct(shape, F32)

    def bf16(*shape):
        return jax.ShapeDtypeStruct(shape, BF16)

    before = lax.ppermute(projected[:, rows - (taps - 1) :, :], "ctx", ring(peers, 1))

    product, state, mode_rate, head, weights = pl.pallas_call(
        state_kernel,
        in_specs=[hbm_spec] * 3,
        out_shape=[
            bf16(rows, width),
            f32(MODES, width),
            f32(MODES, width),
            f32(2, 8, width),
            f32(*short_weight.shape),
        ],
        scratch_shapes=[
            pltpu.VMEM((2, rows, width), BF16),
            pltpu.VMEM((wides, WIDE, rows), BF16),
            pltpu.VMEM((2 * rows, rows), BF16),
            pltpu.VMEM(short_weight.shape, BF16),
            pltpu.VMEM((MODES, rates.shape[0]), F32),
            pltpu.SemaphoreType.DMA((wides,)),
            pltpu.SemaphoreType.DMA((2,)),
        ],
        compiler_params=params(),
        cost_estimate=cost(3),
        name="block_state",
    )(kept(projected), kept(short_weight), kept(rates.T))

    full_state, first = pl.pallas_call(
        lambda *refs: head_kernel(rows, *refs),
        in_specs=[smem_spec] + [vmem_spec] * 5,
        out_shape=[bf16(MODES, width), f32(8, width)],
        compiler_params=params(),
        cost_estimate=cost(0.2),
        name="head_tokens",
    )(place, before, head, weights, state, mode_rate)

    inner, entering, carry_table, gate, residual_here = pl.pallas_call(
        prepare_kernel,
        in_specs=[smem_spec] + [hbm_spec] * 3 + [vmem_spec] * 3,
        out_shape=[
            bf16(tiles, CHUNK + MODES, GROUPS * CHUNK),
            bf16(tiles, CHUNK, LANES),
            bf16(wides, rows, WIDE),
            f32(rows, width),
            bf16(rows, width),
        ],
        scratch_shapes=[
            pltpu.VMEM((rows, width), BF16),
            pltpu.VMEM((2 * rows, rows), BF16),
            pltpu.VMEM((MODES, rates.shape[0]), F32),
            pltpu.SemaphoreType.DMA((3,)),
        ],
        compiler_params=params(),
        cost_estimate=cost(2),
        name="prepare",
    )(place, kept(projected), kept(residual), kept(residues.T), before, weights, mode_rate)

    group, entry, stride = full_state, jnp.zeros((MODES, width), F32), 1
    levels = radices(peers)
    for level, radix in enumerate(levels):
        size = stride * radix
        if level == len(levels) - 1:
            break
        cycles = [
            [(i, i // size * size + (i + stride * k) % size) for i in range(peers)] for k in range(1, radix)
        ]
        others = [lax.ppermute(group, "ctx", cycle) for cycle in cycles]
        if level == 0:
            others[0], inner = lax.optimization_barrier((others[0], inner))
        entry, group = pl.pallas_call(
            lambda *refs, radix=radix, stride=stride: join_kernel(rows, radix, stride, *refs),
            in_specs=[smem_spec] + [vmem_spec] * (2 + radix),
            out_shape=[f32(MODES, width), bf16(MODES, width)],
            compiler_params=params(),
            cost_estimate=cost(0.2),
            name="join",
        )(place, group, mode_rate, entry, *others)
        stride = size
    received = [lax.ppermute(group, "ctx", ring(peers, stride * k)) for k in range(1, levels[-1])]

    base = pl.pallas_call(
        local_kernel,
        out_shape=f32(rows, width),
        compiler_params=params(),
        cost_estimate=cost(5),
        name="local_conv",
    )(gate, residual_here, product, first, mode_rate, inner, entering, skip[None])

    count = lax.axis_size("fsdp")
    summed, squares = pl.pallas_call(
        lambda *refs: carry_kernel(stride, *refs),
        in_specs=[smem_spec] + [vmem_spec] * (5 + len(received)),
        out_shape=[f32(rows, width), f32(1, rows)],
        compiler_params=params(),
        cost_estimate=cost(1),
        name="add_carry",
    )(place, base, gate, carry_table, mode_rate, entry, *received)

    parts = [lax.ppermute(squares, "fsdp", ring(count, k)) for k in range(1, count)]

    def write(kernel, operands, name):
        return pl.pallas_call(
            kernel,
            out_specs=hbm_spec,
            out_shape=bf16(rows, width),
            scratch_shapes=[pltpu.VMEM((rows, width), BF16), pltpu.SemaphoreType.DMA((wides,))],
            compiler_params=params(),
            cost_estimate=cost(1),
            name=name,
        )(*operands)

    new_residual = write(write_kernel, (summed,), "new_residual")
    normed = write(
        lambda *refs: norm_kernel(full_width, *refs), (summed, gain[None], squares, *parts), "normed"
    )
    return (new_residual, normed)


def solution(mesh):
    return jax.shard_map(
        per_device,
        mesh=mesh,
        in_specs=(
            P(None, "ctx", "fsdp"),
            P(None, None, "fsdp"),
            P("fsdp", None),
            P("fsdp", None),
            P("fsdp"),
            P("ctx", "fsdp"),
            P("fsdp"),
        ),
        out_specs=(P("ctx", "fsdp"), P("ctx", "fsdp")),
        check_vma=False,
    )
```

```python
import jax
import jax.numpy as jnp
from jax import lax
from jax.experimental import pallas as pl
from jax.experimental.pallas import tpu as pltpu
from jax.sharding import PartitionSpec as P

CHANNELS_PER_GRP = 16
MODES = 16
CHUNK = 32
LANES = 128
WIDE = 256
GROUPS = LANES // CHANNELS_PER_GRP
VMEM_LIMIT = 16 * 1024 * 1024
F32 = jnp.float32
BF16 = jnp.bfloat16


def index_of(shape, dim):
    return lax.broadcasted_iota(jnp.int32, shape, dim)


def lanes_of(tile, width=LANES):
    return slice(tile * width, (tile + 1) * width)


def per_channel(table):
    groups = table.shape[1]
    width = groups * CHANNELS_PER_GRP
    high = table.astype(BF16)
    rest = table - high.astype(F32)
    middle = rest.astype(BF16)
    low = (rest - middle.astype(F32)).astype(BF16)
    terms = jnp.concatenate([high, middle, low], axis=0)
    parts = []
    for tile in range(width // WIDE):
        shape = (groups, WIDE)
        own = index_of(shape, 0) == index_of(shape, 1) // CHANNELS_PER_GRP + tile * (WIDE // CHANNELS_PER_GRP)
        three = jnp.dot(terms, jnp.where(own, 1.0, 0.0).astype(BF16), preferred_element_type=F32)
        parts.append(three[:MODES] + three[MODES : 2 * MODES] + three[2 * MODES :])
    return jnp.concatenate(parts, axis=1)


def mode_row(channel_table):
    own = index_of(channel_table.shape, 0) == (index_of(channel_table.shape, 1) & (MODES - 1))
    return jnp.sum(jnp.where(own, channel_table, 0.0), axis=0, keepdims=True)


def as_column(row):
    return jnp.transpose(jnp.broadcast_to(row, (LANES, LANES)))


def own_mode(dtype):
    shape = (GROUPS, MODES, LANES)
    own = index_of(shape, 0) * MODES + index_of(shape, 1) == index_of(shape, 2)
    return jnp.where(own, 1.0, 0.0).astype(dtype)


def split(x):
    high = x.astype(BF16)
    return high, (x - high.astype(F32)).astype(BF16)


def group_mask(dtype):
    shape = (GROUPS, MODES, LANES)
    own = index_of(shape, 0) == index_of(shape, 2) // CHANNELS_PER_GRP
    return jnp.where(own, 1.0, 0.0).astype(dtype)


def spread(rows, mask):
    size = rows.shape[0]
    copies = rows.reshape(1, size // MODES, MODES, LANES) * mask.reshape(GROUPS, 1, MODES, LANES)
    return copies.reshape(GROUPS * size, LANES)


def shifted(block, before):
    one = pltpu.roll(block, 1, 0)
    two = pltpu.roll(block, 2, 0)
    first = index_of((8, block.shape[1]), 0)
    near, far = (0.0, 0.0) if before is None else (before[1:2], before[0:1])
    head_one = jnp.where(first == 0, near, one[:8])
    head_two = jnp.where(first == 0, far, jnp.where(first == 1, near, two[:8]))
    if block.shape[0] == 8:
        return head_one, head_two
    return jnp.concatenate([head_one, one[8:]], axis=0), jnp.concatenate([head_two, two[8:]], axis=0)


def short_conv(block, before, weights):
    one, two = shifted(block, before)
    return weights[0] * block + weights[1] * one + weights[2] * two


def shift_matrix(rows):
    shape = (2 * rows, rows)
    target = index_of(shape, 0)
    source = index_of(shape, 1)
    taken = jnp.where(target < rows, target - 1, target - (rows + 2))
    return jnp.where(source == taken, 1.0, 0.0).astype(BF16)


def wide_conv(block, shift, weights):
    rows = block.shape[0]
    earlier = jnp.dot(shift, block, preferred_element_type=F32)
    return weights[0] * block.astype(F32) + weights[1] * earlier[:rows] + weights[2] * earlier[rows:]


def taps_of(weights, feature, lanes):
    return [weights[tap, feature : feature + 1, lanes] for tap in range(weights.shape[0])]


def fetch_kernel(
    projected_ref,
    weight_hbm,
    rate_hbm,
    block_ref,
    tail_ref,
    weight_ref,
    mode_rate_ref,
    ending_ref,
    shift_ref,
    last_ref,
    short_ref,
    rate_ref,
    sems,
):
    rows, width = block_ref.shape[1:]
    copies = [
        pltpu.make_async_copy(rate_hbm, rate_ref, sems.at[0]),
        pltpu.make_async_copy(projected_ref.at[:, pl.ds(rows - 16, 16), :], last_ref, sems.at[1]),
        pltpu.make_async_copy(weight_hbm, short_ref, sems.at[2]),
        pltpu.make_async_copy(projected_ref.at[1], block_ref.at[0], sems.at[3]),
        pltpu.make_async_copy(projected_ref.at[2], block_ref.at[1], sems.at[4]),
    ]
    for copy in copies:
        copy.start()
    shift_ref[...] = shift_matrix(rows)
    copies[0].wait()
    mode_rate = per_channel(rate_ref[...])
    mode_rate_ref[...] = mode_rate
    eye = own_mode(BF16)
    token = index_of((2 * LANES, rows), 1)
    left = jnp.where(token < 2, -1e30, (token - (rows - 1)).astype(F32)).astype(BF16)
    for tile in range(width // LANES):
        high, low = split(mode_rate[:, lanes_of(tile)])
        diagonal = jnp.concatenate([spread(high, eye), spread(low, eye)], axis=1)
        exponent = jnp.dot(diagonal, left, preferred_element_type=F32)
        ending_ref[tile // 2, lanes_of(tile % 2), :] = jnp.exp(exponent).astype(BF16)
    copies[1].wait()
    for c in range(3):
        tail_ref[c] = last_ref[c].astype(F32)[14:16].astype(BF16)
    copies[2].wait()
    weight_ref[...] = short_ref[...].astype(F32)
    copies[3].wait()
    copies[4].wait()


def state_kernel(block_ref, weight_ref, ending_ref, shift_ref, product_ref, state_ref):
    width = product_ref.shape[1]
    mask = group_mask(F32)

    def leave_state(wide, product):
        every = jnp.dot(ending_ref[wide], product, preferred_element_type=F32)
        for half in range(WIDE // LANES):
            own = every[lanes_of(half), lanes_of(half)].reshape(GROUPS, MODES, LANES)
            state_ref[:, lanes_of((WIDE // LANES) * wide + half)] = jnp.sum(own * mask, axis=0)

    previous = None
    for wide in range(width // WIDE):
        here = lanes_of(wide, WIDE)
        parts = [wide_conv(block_ref[c, :, here], shift_ref[...], taps_of(weight_ref, c + 1, here)) for c in (0, 1)]
        product = (parts[0] * parts[1]).astype(BF16)
        product_ref[:, here] = product
        if wide > 0:
            leave_state(wide - 1, previous)
        previous = product
    leave_state(width // WIDE - 1, previous)


def halo(before_ref, place_ref):
    return jnp.where(place_ref[0] > 0, before_ref[...].astype(F32), 0.0)


def head_kernel(place_ref, before_ref, block_ref, weight_ref, state_ref, mode_rate_ref, full_ref, first_ref):
    before = halo(before_ref, place_ref)
    rows, width = block_ref.shape[1:]
    everything = slice(0, width)
    heads = [block_ref[c, 0:16, :].astype(F32)[:8] for c in (0, 1)]
    parts = [short_conv(heads[c], before[c + 1], taps_of(weight_ref, c + 1, everything)) for c in (0, 1)]
    first = (parts[0] * parts[1]).astype(BF16).astype(F32)
    first_ref[...] = first
    rate = mode_rate_ref[...]
    early = jnp.exp(-float(rows - 1) * rate) * first[0:1] + jnp.exp(-float(rows - 2) * rate) * first[1:2]
    full_ref[...] = (state_ref[...] + early).astype(BF16)


def prepare_kernel(
    place_ref,
    projected_ref,
    residual_hbm,
    residue_hbm,
    before_ref,
    weight_ref,
    mode_rate_ref,
    shift_ref,
    inner_ref,
    entering_ref,
    carry_ref,
    gate_ref,
    residual_ref,
    query_ref,
    residue_ref,
    sems,
):
    rows, width = gate_ref.shape
    copies = [
        pltpu.make_async_copy(residue_hbm, residue_ref, sems.at[0]),
        pltpu.make_async_copy(projected_ref.at[0], query_ref, sems.at[1]),
        pltpu.make_async_copy(residual_hbm, residual_ref, sems.at[2]),
    ]
    for copy in copies:
        copy.start()
    copies[0].wait()
    residue = per_channel(residue_ref[...])
    wide = GROUPS * CHUNK
    step = index_of((CHUNK, LANES), 0).astype(F32)
    causal = (index_of((CHUNK, wide), 1) & (CHUNK - 1)) <= index_of((CHUNK, wide), 0)
    eye = own_mode(BF16)
    flat_eye = jnp.where((index_of((MODES, LANES), 1) & (MODES - 1)) == index_of((MODES, LANES), 0), 1.0, 0.0)
    flat_eye = flat_eye.astype(BF16)
    shape = (2 * LANES, wide)
    source = (index_of(shape, 1) & (CHUNK - 1)).astype(F32)
    own = (index_of(shape, 0) & (LANES - 1)) // MODES == index_of(shape, 1) // CHUNK
    risen = jnp.where(own, source, -1e30).astype(BF16)
    left = jnp.where(own, source - (CHUNK - 1), 0.0).astype(BF16)
    for tile in range(width // LANES):
        here = lanes_of(tile)
        rate = mode_rate_ref[:, here]
        high, low = split(rate)
        diagonal = jnp.concatenate([spread(high, eye), spread(low, eye)], axis=1)
        rising = jnp.exp(jnp.dot(diagonal, risen, preferred_element_type=F32))
        each = jnp.concatenate([high * flat_eye, low * flat_eye], axis=1)
        ending = jnp.exp(jnp.dot(each, left, preferred_element_type=F32))
        rate_row = mode_row(rate)
        falling = mode_row(residue[:, here]) * jnp.exp(-rate_row * step)
        fall_high, fall_low = split(falling)
        rise_high, rise_low = split(rising)
        taps = jnp.dot(jnp.concatenate([fall_high, fall_low], axis=0), rise_high, preferred_element_type=F32)
        taps = taps[:CHUNK] + taps[CHUNK:] + jnp.dot(fall_high, rise_low, preferred_element_type=F32)
        taps = jnp.where(causal, taps, 0.0)
        inner_ref[tile] = jnp.concatenate([taps.astype(BF16), ending.astype(BF16)], axis=0)
        half = tile % (WIDE // LANES)
        for chunk in range(rows // CHUNK):
            entering = (falling * jnp.exp(-float(CHUNK * chunk + 1) * rate_row)).astype(BF16)
            carry_ref[tile // (WIDE // LANES), chunk * CHUNK : (chunk + 1) * CHUNK, lanes_of(half)] = entering
            if chunk == 0:
                entering_ref[tile] = entering
    before = halo(before_ref, place_ref)
    copies[1].wait()
    for tile in range(width // WIDE):
        here = lanes_of(tile, WIDE)
        weights = taps_of(weight_ref, 0, here)
        gate_ref[:, here] = wide_conv(query_ref[:, here], shift_ref[...], weights)
        head = query_ref[0:16, here].astype(F32)[:8]
        gate_ref[0:8, here] = short_conv(head, before[0, :, here], weights)
    copies[2].wait()


def local_kernel(
    gate_ref,
    residual_ref,
    product_ref,
    first_ref,
    mode_rate_ref,
    inner_ref,
    entering_ref,
    skip_ref,
    base_ref,
):
    rows, width = product_ref.shape
    mask = group_mask(BF16)
    top = index_of((8, LANES), 0) < 2
    for tile in range(width // LANES):
        here = lanes_of(tile)
        pieces = []
        for chunk in range(rows // CHUNK):
            piece = product_ref[chunk * CHUNK : (chunk + 1) * CHUNK, here]
            if chunk == 0:
                wide = piece.astype(F32)
                head = jnp.where(top, first_ref[:, here], wide[:8])
                piece = jnp.concatenate([head, wide[8:]], axis=0).astype(BF16)
            pieces.append(piece)
        table = inner_ref[tile]
        inner = []
        for pair in range(rows // (2 * CHUNK)):
            sources = jnp.concatenate([spread(pieces[2 * pair + k], mask) for k in (0, 1)], axis=1)
            inner.append(jnp.dot(table, sources, preferred_element_type=F32))
        decay = jnp.exp(-float(CHUNK) * mode_rate_ref[:, here])
        state = jnp.zeros((MODES, LANES), F32)
        states = []
        for chunk in range(rows // CHUNK):
            states.append(spread(state.astype(BF16), mask))
            state = decay * state + inner[chunk // 2][CHUNK:, lanes_of(chunk % 2)]
        entering = entering_ref[tile]
        skip = skip_ref[:, here]
        for pair in range(rows // (2 * CHUNK)):
            two = jnp.concatenate(states[2 * pair : 2 * pair + 2], axis=1)
            conv = inner[pair][:CHUNK] + jnp.dot(entering, two, preferred_element_type=F32)
            for k in (0, 1):
                chunk = 2 * pair + k
                span = slice(chunk * CHUNK, (chunk + 1) * CHUNK)
                whole = conv[:, lanes_of(k)] + skip * pieces[chunk].astype(F32)
                base_ref[span, here] = residual_ref[span, here].astype(F32) + gate_ref[span, here] * whole


def join_kernel(tokens, radix, stride, place_ref, own_ref, mode_rate_ref, entry_ref, *refs):
    others, (found_ref, group_ref) = refs[: radix - 1], refs[radix - 1 :]
    rate = mode_rate_ref[...]
    run = lax.rem(place_ref[0] // stride, radix)
    step = float(tokens * stride)

    def decayed(value, runs):
        return jnp.exp(-step * runs.astype(F32) * rate) * value

    found = jnp.zeros_like(rate)
    total = decayed(own_ref[...].astype(F32), radix - 1 - run)
    for k, ref in enumerate(others, 1):
        other = ref[...].astype(F32)
        found = found + jnp.where(run >= k, decayed(other, jnp.full((), k - 1, jnp.int32)), 0.0)
        source = lax.rem(run - k + radix, radix)
        total = total + decayed(other, radix - 1 - source)
    within = lax.rem(place_ref[0], stride).astype(F32) * float(tokens)
    found_ref[...] = entry_ref[...] + jnp.exp(-within * rate) * found
    group_ref[...] = total.astype(BF16)


def carry_kernel(stride, place_ref, base_ref, gate_ref, carry_ref, mode_rate_ref, inner_entry_ref, *refs):
    entry_refs, (summed_ref, squares_ref) = refs[:-2], refs[-2:]
    rows, width = base_ref.shape
    run = place_ref[0] // stride
    within = lax.rem(place_ref[0], stride).astype(F32) * float(rows)
    mask = group_mask(BF16)
    total = jnp.zeros((rows, LANES), F32)
    nothing = jnp.zeros((LANES, LANES), BF16)
    for tile in range(width // WIDE):
        here = lanes_of(tile, WIDE)
        rate = mode_rate_ref[:, here]
        decay = jnp.exp(-float(rows * stride) * rate)
        outer = jnp.zeros_like(rate)
        for k in range(len(entry_refs), 0, -1):
            outer = decay * outer + jnp.where(run >= k, entry_refs[k - 1][:, here].astype(F32), 0.0)
        entry = (inner_entry_ref[:, here] + jnp.exp(-within * rate) * outer).astype(BF16)
        left, right = spread(entry[:, :LANES], mask), spread(entry[:, LANES:], mask)
        both = jnp.concatenate(
            [jnp.concatenate([left, nothing], axis=1), jnp.concatenate([nothing, right], axis=1)], axis=0
        )
        carry = jnp.dot(carry_ref[tile], both, preferred_element_type=F32)
        summed = base_ref[:, here] + gate_ref[:, here] * carry
        summed_ref[:, here] = summed
        square = summed * summed
        total = total + (square[:, :LANES] + square[:, LANES:])
    squares = lax.dot_general(
        jnp.ones((8, LANES), F32),
        total,
        (((1,), (1,)), ((), ())),
        precision=lax.Precision.HIGHEST,
        preferred_element_type=F32,
    )
    squares_ref[...] = squares[0:1]


def write_kernel(summed_ref, out_hbm, rounded_ref, sems):
    width = summed_ref.shape[1]
    copies = []
    for tile in range(width // WIDE):
        here = lanes_of(tile, WIDE)
        rounded_ref[:, here] = summed_ref[:, here].astype(BF16)
        span = pl.ds(tile * WIDE, WIDE)
        copies.append(pltpu.make_async_copy(rounded_ref.at[:, span], out_hbm.at[:, span], sems.at[tile]))
        copies[-1].start()
    for copy in copies:
        copy.wait()


def norm_kernel(full_width, summed_ref, gain_ref, *refs):
    squares_refs, (out_hbm, rounded_ref, sems) = refs[:-3], refs[-3:]
    rows, width = summed_ref.shape
    squares = squares_refs[0][...]
    for ref in squares_refs[1:]:
        squares = squares + ref[...]
    scale_row = lax.rsqrt(squares / full_width + 1e-05)
    scale = jnp.concatenate([as_column(scale_row[:, lanes_of(k)]) for k in range(rows // LANES)], axis=0)
    copies = []
    for tile in range(width // WIDE):
        for half in range(WIDE // LANES):
            here = lanes_of(tile * (WIDE // LANES) + half)
            rounded_ref[:, here] = (summed_ref[:, here] * scale * gain_ref[:, here]).astype(BF16)
        span = pl.ds(tile * WIDE, WIDE)
        copies.append(pltpu.make_async_copy(rounded_ref.at[:, span], out_hbm.at[:, span], sems.at[tile]))
        copies[-1].start()
    for copy in copies:
        copy.wait()


def params():
    return pltpu.CompilerParams(vmem_limit_bytes=VMEM_LIMIT)


def cost(microseconds):
    return pl.CostEstimate(flops=0, bytes_accessed=int(microseconds * 3.0e6), transcendentals=0)


def radices(count):
    found = []
    for radix in (2, 4, 4, 4):
        if count % radix == 0 and count > 1:
            found.append(radix)
            count //= radix
    for radix in (3, 2, 5, 7):
        while count % radix == 0 and count > 1:
            found.append(radix)
            count //= radix
    return found + ([count] if count > 1 else [])


def ring(count, shift):
    return [(i, (i + shift) % count) for i in range(count)]


def per_device(projected, short_weight, rates, residues, skip, residual, gain):
    rows, width = projected.shape[1:]
    taps = short_weight.shape[0]
    peers = lax.axis_size("ctx")
    full_width = width * lax.axis_size("fsdp")
    place = lax.axis_index("ctx").astype(jnp.int32).reshape(1)
    hbm_spec = pl.BlockSpec(memory_space=pltpu.HBM)
    vmem_spec = pl.BlockSpec(memory_space=pltpu.VMEM)
    smem_spec = pl.BlockSpec(memory_space=pltpu.SMEM)
    tiles = width // LANES
    wides = width // WIDE

    def kept(array):
        return pltpu.with_memory_space_constraint(array, pltpu.HBM)

    def f32(*shape):
        return jax.ShapeDtypeStruct(shape, F32)

    def bf16(*shape):
        return jax.ShapeDtypeStruct(shape, BF16)

    block, tail, weights, mode_rate, ending, shift = pl.pallas_call(
        fetch_kernel,
        in_specs=[hbm_spec] * 3,
        out_shape=[
            bf16(2, rows, width),
            bf16(3, taps - 1, width),
            f32(*short_weight.shape),
            f32(MODES, width),
            bf16(wides, WIDE, rows),
            bf16(2 * rows, rows),
        ],
        scratch_shapes=[
            pltpu.VMEM((3, 16, width), BF16),
            pltpu.VMEM(short_weight.shape, BF16),
            pltpu.VMEM((MODES, rates.shape[0]), F32),
            pltpu.SemaphoreType.DMA((5,)),
        ],
        compiler_params=params(),
        cost_estimate=cost(2),
        name="fetch",
    )(kept(projected), kept(short_weight), kept(rates.T))

    before = lax.ppermute(tail, "ctx", ring(peers, 1))

    product, state = pl.pallas_call(
        state_kernel,
        out_shape=[bf16(rows, width), f32(MODES, width)],
        compiler_params=params(),
        cost_estimate=cost(3),
        name="block_state",
    )(block, weights, ending, shift)

    full_state, first = pl.pallas_call(
        head_kernel,
        in_specs=[smem_spec] + [vmem_spec] * 5,
        out_shape=[bf16(MODES, width), f32(8, width)],
        compiler_params=params(),
        cost_estimate=cost(0.2),
        name="head_tokens",
    )(place, before, block, weights, state, mode_rate)

    inner, entering, carry_table, gate, residual_here = pl.pallas_call(
        prepare_kernel,
        in_specs=[smem_spec] + [hbm_spec] * 3 + [vmem_spec] * 4,
        out_shape=[
            bf16(tiles, CHUNK + MODES, GROUPS * CHUNK),
            bf16(tiles, CHUNK, LANES),
            bf16(wides, rows, WIDE),
            f32(rows, width),
            bf16(rows, width),
        ],
        scratch_shapes=[
            pltpu.VMEM((rows, width), BF16),
            pltpu.VMEM((MODES, rates.shape[0]), F32),
            pltpu.SemaphoreType.DMA((3,)),
        ],
        compiler_params=params(),
        cost_estimate=cost(2),
        name="prepare",
    )(place, kept(projected), kept(residual), kept(residues.T), before, weights, mode_rate, shift)

    group, entry, stride = full_state, jnp.zeros((MODES, width), F32), 1
    levels = radices(peers)
    for level, radix in enumerate(levels):
        size = stride * radix
        if level == len(levels) - 1:
            break
        cycles = [
            [(i, i // size * size + (i + stride * k) % size) for i in range(peers)] for k in range(1, radix)
        ]
        others = [lax.ppermute(group, "ctx", cycle) for cycle in cycles]
        if level == 0:
            others[0], inner = lax.optimization_barrier((others[0], inner))
        entry, group = pl.pallas_call(
            lambda *refs, radix=radix, stride=stride: join_kernel(rows, radix, stride, *refs),
            in_specs=[smem_spec] + [vmem_spec] * (2 + radix),
            out_shape=[f32(MODES, width), bf16(MODES, width)],
            compiler_params=params(),
            cost_estimate=cost(0.2),
            name="join",
        )(place, group, mode_rate, entry, *others)
        stride = size
    received = [lax.ppermute(group, "ctx", ring(peers, stride * k)) for k in range(1, levels[-1])]

    base = pl.pallas_call(
        local_kernel,
        out_shape=f32(rows, width),
        compiler_params=params(),
        cost_estimate=cost(5),
        name="local_conv",
    )(gate, residual_here, product, first, mode_rate, inner, entering, skip[None])

    count = lax.axis_size("fsdp")
    summed, squares = pl.pallas_call(
        lambda *refs: carry_kernel(stride, *refs),
        in_specs=[smem_spec] + [vmem_spec] * (5 + len(received)),
        out_shape=[f32(rows, width), f32(1, rows)],
        compiler_params=params(),
        cost_estimate=cost(1),
        name="add_carry",
    )(place, base, gate, carry_table, mode_rate, entry, *received)

    parts = [lax.ppermute(squares, "fsdp", ring(count, k)) for k in range(1, count)]

    def write(kernel, operands, name):
        return pl.pallas_call(
            kernel,
            out_specs=hbm_spec,
            out_shape=bf16(rows, width),
            scratch_shapes=[pltpu.VMEM((rows, width), BF16), pltpu.SemaphoreType.DMA((wides,))],
            compiler_params=params(),
            cost_estimate=cost(1),
            name=name,
        )(*operands)

    new_residual = write(write_kernel, (summed,), "new_residual")
    normed = write(
        lambda *refs: norm_kernel(full_width, *refs), (summed, gain[None], squares, *parts), "normed"
    )
    return (new_residual, normed)


def solution(mesh):
    return jax.shard_map(
        per_device,
        mesh=mesh,
        in_specs=(
            P(None, "ctx", "fsdp"),
            P(None, None, "fsdp"),
            P("fsdp", None),
            P("fsdp", None),
            P("fsdp"),
            P("ctx", "fsdp"),
            P("fsdp"),
        ),
        out_specs=(P("ctx", "fsdp"), P("ctx", "fsdp")),
        check_vma=False,
    )
```

```python
import jax
import jax.numpy as jnp
from jax import lax
from jax.experimental import pallas as pl
from jax.experimental.pallas import tpu as pltpu
from jax.sharding import PartitionSpec as P

CHANNELS_PER_GRP = 16
MODES = 16
CHUNK = 32
LANES = 128
WIDE = 256
GROUPS = LANES // CHANNELS_PER_GRP
VMEM_LIMIT = 16 * 1024 * 1024
F32 = jnp.float32
BF16 = jnp.bfloat16


def index_of(shape, dim):
    return lax.broadcasted_iota(jnp.int32, shape, dim)


def pipelined(count, *stages):
    held = {}
    for step in range(count + len(stages) - 1):
        for k, stage in enumerate(stages):
            item = step - k
            if 0 <= item < count:
                held[item] = stage(item, *held.get(item, ()))


def lanes_of(tile, width=LANES):
    return slice(tile * width, (tile + 1) * width)


def per_channel(table):
    groups = table.shape[1]
    width = groups * CHANNELS_PER_GRP
    high = table.astype(BF16)
    rest = table - high.astype(F32)
    middle = rest.astype(BF16)
    low = (rest - middle.astype(F32)).astype(BF16)
    terms = jnp.concatenate([high, middle, low], axis=0)
    parts = []
    for tile in range(width // WIDE):
        shape = (groups, WIDE)
        own = index_of(shape, 0) == index_of(shape, 1) // CHANNELS_PER_GRP + tile * (WIDE // CHANNELS_PER_GRP)
        three = jnp.dot(terms, jnp.where(own, 1.0, 0.0).astype(BF16), preferred_element_type=F32)
        parts.append(three[:MODES] + three[MODES : 2 * MODES] + three[2 * MODES :])
    return jnp.concatenate(parts, axis=1)


def mode_row(channel_table):
    own = index_of(channel_table.shape, 0) == (index_of(channel_table.shape, 1) & (MODES - 1))
    return jnp.sum(jnp.where(own, channel_table, 0.0), axis=0, keepdims=True)


def as_column(row):
    return jnp.transpose(jnp.broadcast_to(row, (LANES, LANES)))


def own_mode(dtype):
    shape = (GROUPS, MODES, LANES)
    own = index_of(shape, 0) * MODES + index_of(shape, 1) == index_of(shape, 2)
    return jnp.where(own, 1.0, 0.0).astype(dtype)


def split(x):
    high = x.astype(BF16)
    return high, (x - high.astype(F32)).astype(BF16)


def group_mask(dtype):
    shape = (GROUPS, MODES, LANES)
    own = index_of(shape, 0) == index_of(shape, 2) // CHANNELS_PER_GRP
    return jnp.where(own, 1.0, 0.0).astype(dtype)


def spread(rows, mask):
    size = rows.shape[0]
    copies = rows.reshape(1, size // MODES, MODES, LANES) * mask.reshape(GROUPS, 1, MODES, LANES)
    return copies.reshape(GROUPS * size, LANES)


def shifted(block, before):
    one = pltpu.roll(block, 1, 0)
    two = pltpu.roll(block, 2, 0)
    first = index_of((8, block.shape[1]), 0)
    near, far = (0.0, 0.0) if before is None else (before[1:2], before[0:1])
    head_one = jnp.where(first == 0, near, one[:8])
    head_two = jnp.where(first == 0, far, jnp.where(first == 1, near, two[:8]))
    if block.shape[0] == 8:
        return head_one, head_two
    return jnp.concatenate([head_one, one[8:]], axis=0), jnp.concatenate([head_two, two[8:]], axis=0)


def short_conv(block, before, weights):
    one, two = shifted(block, before)
    return weights[0] * block + weights[1] * one + weights[2] * two


def shift_matrix(rows):
    shape = (2 * rows, rows)
    target = index_of(shape, 0)
    source = index_of(shape, 1)
    taken = jnp.where(target < rows, target - 1, target - (rows + 2))
    return jnp.where(source == taken, 1.0, 0.0).astype(BF16)


def earlier_tokens(shift, block):
    return jnp.dot(shift, block, preferred_element_type=F32)


def wide_conv(block, earlier, weights):
    rows = block.shape[0]
    return weights[0] * block.astype(F32) + weights[1] * earlier[:rows] + weights[2] * earlier[rows:]


def taps_of(weights, feature, lanes):
    return [weights[tap, feature : feature + 1, lanes] for tap in range(weights.shape[0])]


def state_kernel(
    projected_ref,
    weight_hbm,
    rate_hbm,
    product_ref,
    state_ref,
    mode_rate_ref,
    head_ref,
    weight_ref,
    buffer_ref,
    ending_ref,
    shift_ref,
    short_ref,
    rate_ref,
    sems,
    small_sems,
):
    rows, width = product_ref.shape
    wides = width // WIDE
    rate_copy = pltpu.make_async_copy(rate_hbm, rate_ref, small_sems.at[0])
    rate_copy.start()
    weight_copy = pltpu.make_async_copy(weight_hbm, short_ref, small_sems.at[1])
    weight_copy.start()
    copies = [pltpu.make_async_copy(projected_ref.at[1 + c], buffer_ref.at[c], sems.at[c]) for c in (0, 1)]
    for copy in copies:
        copy.start()
    shift_ref[...] = shift_matrix(rows)
    rate_copy.wait()
    mode_rate = per_channel(rate_ref[...])
    mode_rate_ref[...] = mode_rate
    eye = own_mode(BF16)
    token = index_of((2 * LANES, rows), 1)
    left = jnp.where(token < 2, -1e30, (token - (rows - 1)).astype(F32)).astype(BF16)

    def exponents(tile):
        high, low = split(mode_rate[:, lanes_of(tile)])
        diagonal = jnp.concatenate([spread(high, eye), spread(low, eye)], axis=1)
        return (jnp.dot(diagonal, left, preferred_element_type=F32),)

    def endings(tile, exponent):
        ending_ref[tile // 2, lanes_of(tile % 2), :] = jnp.exp(exponent).astype(BF16)

    pipelined(width // LANES, exponents, endings)
    weight_copy.wait()
    weights = short_ref[...].astype(F32)
    weight_ref[...] = weights
    mask = group_mask(F32)
    for copy in copies:
        copy.wait()

    def fetch(wide):
        return [earlier_tokens(shift_ref[...], buffer_ref[c, :, lanes_of(wide, WIDE)]) for c in (0, 1)]

    def multiply(wide, *earlier):
        here = lanes_of(wide, WIDE)
        parts = []
        for c in (0, 1):
            head_ref[c, :, here] = buffer_ref[c, 0:16, here].astype(F32)[:8]
            parts.append(wide_conv(buffer_ref[c, :, here], earlier[c], taps_of(weights, c + 1, here)))
        product = (parts[0] * parts[1]).astype(BF16)
        product_ref[:, here] = product
        return (jnp.dot(ending_ref[wide], product, preferred_element_type=F32),)

    def leave(wide, every):
        for half in range(WIDE // LANES):
            own = every[lanes_of(half), lanes_of(half)].reshape(GROUPS, MODES, LANES)
            state_ref[:, lanes_of((WIDE // LANES) * wide + half)] = jnp.sum(own * mask, axis=0)

    pipelined(wides, fetch, multiply, leave)


def halo(before_ref, place_ref):
    return jnp.where(place_ref[0] > 0, before_ref[...].astype(F32), 0.0)


def head_kernel(rows, place_ref, before_ref, head_ref, weight_ref, state_ref, mode_rate_ref, full_ref, first_ref):
    before = halo(before_ref, place_ref)
    everything = slice(0, head_ref.shape[2])
    parts = [short_conv(head_ref[c], before[c + 1], taps_of(weight_ref, c + 1, everything)) for c in (0, 1)]
    first = (parts[0] * parts[1]).astype(BF16).astype(F32)
    first_ref[...] = first
    rate = mode_rate_ref[...]
    early = jnp.exp(-float(rows - 1) * rate) * first[0:1] + jnp.exp(-float(rows - 2) * rate) * first[1:2]
    full_ref[...] = (state_ref[...] + early).astype(BF16)


def prepare_kernel(
    place_ref,
    projected_ref,
    residual_hbm,
    residue_hbm,
    before_ref,
    weight_ref,
    mode_rate_ref,
    inner_ref,
    entering_ref,
    carry_ref,
    gate_ref,
    residual_ref,
    query_ref,
    shift_ref,
    residue_ref,
    sems,
):
    rows, width = gate_ref.shape
    copies = [
        pltpu.make_async_copy(residue_hbm, residue_ref, sems.at[0]),
        pltpu.make_async_copy(projected_ref.at[0], query_ref, sems.at[1]),
        pltpu.make_async_copy(residual_hbm, residual_ref, sems.at[2]),
    ]
    for copy in copies:
        copy.start()
    copies[0].wait()
    residue = per_channel(residue_ref[...])
    wide = GROUPS * CHUNK
    step = index_of((CHUNK, LANES), 0).astype(F32)
    causal = (index_of((CHUNK, wide), 1) & (CHUNK - 1)) <= index_of((CHUNK, wide), 0)
    eye = own_mode(BF16)
    flat_eye = jnp.where((index_of((MODES, LANES), 1) & (MODES - 1)) == index_of((MODES, LANES), 0), 1.0, 0.0)
    flat_eye = flat_eye.astype(BF16)
    shape = (2 * LANES, wide)
    source = (index_of(shape, 1) & (CHUNK - 1)).astype(F32)
    own = (index_of(shape, 0) & (LANES - 1)) // MODES == index_of(shape, 1) // CHUNK
    own_chunk = jnp.where(own[:LANES], 1.0, 0.0).astype(BF16)
    risen = source[:, :LANES].astype(BF16)
    left = jnp.where(own, source - (CHUNK - 1), 0.0).astype(BF16)

    def exponents(tile):
        rate = mode_rate_ref[:, lanes_of(tile)]
        high, low = split(rate)
        diagonal = jnp.concatenate([spread(high, eye), spread(low, eye)], axis=1)
        each = jnp.concatenate([high * flat_eye, low * flat_eye], axis=1)
        return (
            jnp.dot(diagonal, risen, preferred_element_type=F32),
            jnp.dot(each, left, preferred_element_type=F32),
        )

    def products(tile, rise, end):
        here = lanes_of(tile)
        rise_high, rise_low = [
            jnp.concatenate([part] * (wide // LANES), axis=1) * own_chunk for part in split(jnp.exp(rise))
        ]
        rate_row = mode_row(mode_rate_ref[:, here])
        falling = mode_row(residue[:, here]) * jnp.exp(-rate_row * step)
        fall_high, fall_low = split(falling)
        half = tile % (WIDE // LANES)
        for chunk in range(rows // CHUNK):
            entering = (falling * jnp.exp(-float(CHUNK * chunk + 1) * rate_row)).astype(BF16)
            carry_ref[tile // (WIDE // LANES), chunk * CHUNK : (chunk + 1) * CHUNK, lanes_of(half)] = entering
            if chunk == 0:
                entering_ref[tile] = entering
        return (
            jnp.dot(jnp.concatenate([fall_high, fall_low], axis=0), rise_high, preferred_element_type=F32),
            jnp.dot(fall_high, rise_low, preferred_element_type=F32),
            jnp.exp(end),
        )

    def finish(tile, taps, rest, ending):
        taps = jnp.where(causal, taps[:CHUNK] + taps[CHUNK:] + rest, 0.0)
        inner_ref[tile] = jnp.concatenate([taps.astype(BF16), ending.astype(BF16)], axis=0)

    pipelined(width // LANES, exponents, products, finish)
    before = halo(before_ref, place_ref)
    copies[1].wait()
    shift_ref[...] = shift_matrix(rows)

    def fetch(part):
        return (earlier_tokens(shift_ref[...], query_ref[:, lanes_of(part, WIDE)]),)

    def convolve(part, earlier):
        here = lanes_of(part, WIDE)
        weights = taps_of(weight_ref, 0, here)
        gate_ref[:, here] = wide_conv(query_ref[:, here], earlier, weights)
        head = query_ref[0:16, here].astype(F32)[:8]
        gate_ref[0:8, here] = short_conv(head, before[0, :, here], weights)

    pipelined(width // WIDE, fetch, convolve)
    copies[2].wait()


def local_kernel(
    gate_ref,
    residual_ref,
    product_ref,
    first_ref,
    mode_rate_ref,
    inner_ref,
    entering_ref,
    skip_ref,
    base_ref,
):
    rows, width = product_ref.shape
    mask = group_mask(BF16)
    top = index_of((8, LANES), 0) < 2
    chunks = range(rows // CHUNK)

    def inside(tile):
        here = lanes_of(tile)
        pieces = []
        for chunk in chunks:
            piece = product_ref[chunk * CHUNK : (chunk + 1) * CHUNK, here]
            if chunk == 0:
                wide = piece.astype(F32)
                head = jnp.where(top, first_ref[:, here], wide[:8])
                piece = jnp.concatenate([head, wide[8:]], axis=0).astype(BF16)
            pieces.append(piece)
        found = []
        for pair in chunks[::2]:
            sources = jnp.concatenate([spread(pieces[pair + k], mask) for k in (0, 1)], axis=1)
            found.append(jnp.dot(inner_ref[tile], sources, preferred_element_type=F32))
        return found, pieces[0]

    def across(tile, inner, first):
        decay = jnp.exp(-float(CHUNK) * mode_rate_ref[:, lanes_of(tile)])
        state = jnp.zeros((MODES, LANES), F32)
        states = []
        for chunk in chunks:
            states.append(spread(state.astype(BF16), mask))
            state = decay * state + inner[chunk // 2][CHUNK:, lanes_of(chunk % 2)]
        outer = []
        for pair in chunks[::2]:
            two = jnp.concatenate(states[pair : pair + 2], axis=1)
            outer.append(jnp.dot(entering_ref[tile], two, preferred_element_type=F32))
        return [part[:CHUNK] for part in inner], outer, first

    def finish(tile, inner, outer, first):
        here = lanes_of(tile)
        skip = skip_ref[:, here]
        for chunk in chunks:
            span = slice(chunk * CHUNK, (chunk + 1) * CHUNK)
            piece = first if chunk == 0 else product_ref[span, here]
            conv = (inner[chunk // 2] + outer[chunk // 2])[:, lanes_of(chunk % 2)]
            whole = conv + skip * piece.astype(F32)
            base_ref[span, here] = residual_ref[span, here].astype(F32) + gate_ref[span, here] * whole

    pipelined(width // LANES, inside, across, finish)


def join_kernel(tokens, radix, stride, place_ref, own_ref, mode_rate_ref, entry_ref, *refs):
    others, (found_ref, group_ref) = refs[: radix - 1], refs[radix - 1 :]
    rate = mode_rate_ref[...]
    run = lax.rem(place_ref[0] // stride, radix)
    step = float(tokens * stride)

    def decayed(value, runs):
        return jnp.exp(-step * runs.astype(F32) * rate) * value

    found = jnp.zeros_like(rate)
    total = decayed(own_ref[...].astype(F32), radix - 1 - run)
    for k, ref in enumerate(others, 1):
        other = ref[...].astype(F32)
        found = found + jnp.where(run >= k, decayed(other, jnp.full((), k - 1, jnp.int32)), 0.0)
        source = lax.rem(run - k + radix, radix)
        total = total + decayed(other, radix - 1 - source)
    within = lax.rem(place_ref[0], stride).astype(F32) * float(tokens)
    found_ref[...] = entry_ref[...] + jnp.exp(-within * rate) * found
    group_ref[...] = total.astype(BF16)


def carry_kernel(stride, place_ref, base_ref, gate_ref, carry_ref, mode_rate_ref, inner_entry_ref, *refs):
    entry_refs, (summed_ref, squares_ref) = refs[:-2], refs[-2:]
    rows, width = base_ref.shape
    run = place_ref[0] // stride
    within = lax.rem(place_ref[0], stride).astype(F32) * float(rows)
    mask = group_mask(BF16)
    totals = [jnp.zeros((rows, LANES), F32)]
    nothing = jnp.zeros((LANES, LANES), BF16)

    def enter(tile):
        here = lanes_of(tile, WIDE)
        rate = mode_rate_ref[:, here]
        decay = jnp.exp(-float(rows * stride) * rate)
        outer = jnp.zeros_like(rate)
        for k in range(len(entry_refs), 0, -1):
            outer = decay * outer + jnp.where(run >= k, entry_refs[k - 1][:, here].astype(F32), 0.0)
        entry = (inner_entry_ref[:, here] + jnp.exp(-within * rate) * outer).astype(BF16)
        left, right = spread(entry[:, :LANES], mask), spread(entry[:, LANES:], mask)
        both = jnp.concatenate(
            [jnp.concatenate([left, nothing], axis=1), jnp.concatenate([nothing, right], axis=1)], axis=0
        )
        return (jnp.dot(carry_ref[tile], both, preferred_element_type=F32),)

    def add(tile, carry):
        here = lanes_of(tile, WIDE)
        summed = base_ref[:, here] + gate_ref[:, here] * carry
        summed_ref[:, here] = summed
        square = summed * summed
        totals[0] = totals[0] + (square[:, :LANES] + square[:, LANES:])

    pipelined(width // WIDE, enter, add)
    total = totals[0]
    squares = lax.dot_general(
        jnp.ones((8, LANES), F32),
        total,
        (((1,), (1,)), ((), ())),
        precision=lax.Precision.HIGHEST,
        preferred_element_type=F32,
    )
    squares_ref[...] = squares[0:1]


def write_kernel(summed_ref, out_hbm, rounded_ref, sems):
    width = summed_ref.shape[1]
    copies = []
    for tile in range(width // WIDE):
        here = lanes_of(tile, WIDE)
        rounded_ref[:, here] = summed_ref[:, here].astype(BF16)
        span = pl.ds(tile * WIDE, WIDE)
        copies.append(pltpu.make_async_copy(rounded_ref.at[:, span], out_hbm.at[:, span], sems.at[tile]))
        copies[-1].start()
    for copy in copies:
        copy.wait()


def norm_kernel(full_width, summed_ref, gain_ref, *refs):
    squares_refs, (out_hbm, rounded_ref, sems) = refs[:-3], refs[-3:]
    rows, width = summed_ref.shape
    squares = squares_refs[0][...]
    for ref in squares_refs[1:]:
        squares = squares + ref[...]
    scale_row = lax.rsqrt(squares / full_width + 1e-05)
    scale = jnp.concatenate([as_column(scale_row[:, lanes_of(k)]) for k in range(rows // LANES)], axis=0)
    copies = []
    for tile in range(width // WIDE):
        for half in range(WIDE // LANES):
            here = lanes_of(tile * (WIDE // LANES) + half)
            rounded_ref[:, here] = (summed_ref[:, here] * scale * gain_ref[:, here]).astype(BF16)
        span = pl.ds(tile * WIDE, WIDE)
        copies.append(pltpu.make_async_copy(rounded_ref.at[:, span], out_hbm.at[:, span], sems.at[tile]))
        copies[-1].start()
    for copy in copies:
        copy.wait()


def params():
    return pltpu.CompilerParams(vmem_limit_bytes=VMEM_LIMIT)


def cost(microseconds):
    return pl.CostEstimate(flops=0, bytes_accessed=int(microseconds * 3.0e6), transcendentals=0)


def radices(count):
    found = []
    for radix in (2, 4, 4, 4):
        if count % radix == 0 and count > 1:
            found.append(radix)
            count //= radix
    for radix in (3, 2, 5, 7):
        while count % radix == 0 and count > 1:
            found.append(radix)
            count //= radix
    return found + ([count] if count > 1 else [])


def ring(count, shift):
    return [(i, (i + shift) % count) for i in range(count)]


def per_device(projected, short_weight, rates, residues, skip, residual, gain):
    rows, width = projected.shape[1:]
    taps = short_weight.shape[0]
    peers = lax.axis_size("ctx")
    full_width = width * lax.axis_size("fsdp")
    place = lax.axis_index("ctx").astype(jnp.int32).reshape(1)
    hbm_spec = pl.BlockSpec(memory_space=pltpu.HBM)
    vmem_spec = pl.BlockSpec(memory_space=pltpu.VMEM)
    smem_spec = pl.BlockSpec(memory_space=pltpu.SMEM)
    tiles = width // LANES
    wides = width // WIDE

    def kept(array):
        return pltpu.with_memory_space_constraint(array, pltpu.HBM)

    def f32(*shape):
        return jax.ShapeDtypeStruct(shape, F32)

    def bf16(*shape):
        return jax.ShapeDtypeStruct(shape, BF16)

    before = lax.ppermute(projected[:, rows - (taps - 1) :, :], "ctx", ring(peers, 1))

    product, state, mode_rate, head, weights = pl.pallas_call(
        state_kernel,
        in_specs=[hbm_spec] * 3,
        out_shape=[
            bf16(rows, width),
            f32(MODES, width),
            f32(MODES, width),
            f32(2, 8, width),
            f32(*short_weight.shape),
        ],
        scratch_shapes=[
            pltpu.VMEM((2, rows, width), BF16),
            pltpu.VMEM((wides, WIDE, rows), BF16),
            pltpu.VMEM((2 * rows, rows), BF16),
            pltpu.VMEM(short_weight.shape, BF16),
            pltpu.VMEM((MODES, rates.shape[0]), F32),
            pltpu.SemaphoreType.DMA((2,)),
            pltpu.SemaphoreType.DMA((2,)),
        ],
        compiler_params=params(),
        cost_estimate=cost(3),
        name="block_state",
    )(kept(projected), kept(short_weight), kept(rates.T))

    full_state, first = pl.pallas_call(
        lambda *refs: head_kernel(rows, *refs),
        in_specs=[smem_spec] + [vmem_spec] * 5,
        out_shape=[bf16(MODES, width), f32(8, width)],
        compiler_params=params(),
        cost_estimate=cost(0.2),
        name="head_tokens",
    )(place, before, head, weights, state, mode_rate)

    inner, entering, carry_table, gate, residual_here = pl.pallas_call(
        prepare_kernel,
        in_specs=[smem_spec] + [hbm_spec] * 3 + [vmem_spec] * 3,
        out_shape=[
            bf16(tiles, CHUNK + MODES, GROUPS * CHUNK),
            bf16(tiles, CHUNK, LANES),
            bf16(wides, rows, WIDE),
            f32(rows, width),
            bf16(rows, width),
        ],
        scratch_shapes=[
            pltpu.VMEM((rows, width), BF16),
            pltpu.VMEM((2 * rows, rows), BF16),
            pltpu.VMEM((MODES, rates.shape[0]), F32),
            pltpu.SemaphoreType.DMA((3,)),
        ],
        compiler_params=params(),
        cost_estimate=cost(2),
        name="prepare",
    )(place, kept(projected), kept(residual), kept(residues.T), before, weights, mode_rate)

    group, entry, stride = full_state, jnp.zeros((MODES, width), F32), 1
    levels = radices(peers)
    for level, radix in enumerate(levels):
        size = stride * radix
        if level == len(levels) - 1:
            break
        cycles = [
            [(i, i // size * size + (i + stride * k) % size) for i in range(peers)] for k in range(1, radix)
        ]
        others = [lax.ppermute(group, "ctx", cycle) for cycle in cycles]
        if level == 0:
            others[0], inner = lax.optimization_barrier((others[0], inner))
        entry, group = pl.pallas_call(
            lambda *refs, radix=radix, stride=stride: join_kernel(rows, radix, stride, *refs),
            in_specs=[smem_spec] + [vmem_spec] * (2 + radix),
            out_shape=[f32(MODES, width), bf16(MODES, width)],
            compiler_params=params(),
            cost_estimate=cost(0.2),
            name="join",
        )(place, group, mode_rate, entry, *others)
        stride = size
    received = [lax.ppermute(group, "ctx", ring(peers, stride * k)) for k in range(1, levels[-1])]

    base = pl.pallas_call(
        local_kernel,
        out_shape=f32(rows, width),
        compiler_params=params(),
        cost_estimate=cost(5),
        name="local_conv",
    )(gate, residual_here, product, first, mode_rate, inner, entering, skip[None])

    count = lax.axis_size("fsdp")
    summed, squares = pl.pallas_call(
        lambda *refs: carry_kernel(stride, *refs),
        in_specs=[smem_spec] + [vmem_spec] * (5 + len(received)),
        out_shape=[f32(rows, width), f32(1, rows)],
        compiler_params=params(),
        cost_estimate=cost(1),
        name="add_carry",
    )(place, base, gate, carry_table, mode_rate, entry, *received)

    parts = [lax.ppermute(squares, "fsdp", ring(count, k)) for k in range(1, count)]

    def write(kernel, operands, name):
        return pl.pallas_call(
            kernel,
            out_specs=hbm_spec,
            out_shape=bf16(rows, width),
            scratch_shapes=[pltpu.VMEM((rows, width), BF16), pltpu.SemaphoreType.DMA((wides,))],
            compiler_params=params(),
            cost_estimate=cost(1),
            name=name,
        )(*operands)

    new_residual = write(write_kernel, (summed,), "new_residual")
    normed = write(
        lambda *refs: norm_kernel(full_width, *refs), (summed, gain[None], squares, *parts), "normed"
    )
    return (new_residual, normed)


def solution(mesh):
    return jax.shard_map(
        per_device,
        mesh=mesh,
        in_specs=(
            P(None, "ctx", "fsdp"),
            P(None, None, "fsdp"),
            P("fsdp", None),
            P("fsdp", None),
            P("fsdp"),
            P("ctx", "fsdp"),
            P("fsdp"),
        ),
        out_specs=(P("ctx", "fsdp"), P("ctx", "fsdp")),
        check_vma=False,
    )
```

```python
import jax
import jax.numpy as jnp
from jax import lax
from jax.experimental import pallas as pl
from jax.experimental.pallas import tpu as pltpu
from jax.sharding import PartitionSpec as P

CHANNELS_PER_GRP = 16
MODES = 16
CHUNK = 32
LANES = 128
WIDE = 256
GROUPS = LANES // CHANNELS_PER_GRP
VMEM_LIMIT = 16 * 1024 * 1024
F32 = jnp.float32
BF16 = jnp.bfloat16


def index_of(shape, dim):
    return lax.broadcasted_iota(jnp.int32, shape, dim)


def pipelined(count, *stages):
    held = {}
    for step in range(count + len(stages) - 1):
        for k, stage in enumerate(stages):
            item = step - k
            if 0 <= item < count:
                held[item] = stage(item, *held.get(item, ()))


def lanes_of(tile, width=LANES):
    return slice(tile * width, (tile + 1) * width)


def per_channel(table):
    groups = table.shape[1]
    width = groups * CHANNELS_PER_GRP
    high = table.astype(BF16)
    rest = table - high.astype(F32)
    middle = rest.astype(BF16)
    low = (rest - middle.astype(F32)).astype(BF16)
    terms = jnp.concatenate([high, middle, low], axis=0)
    parts = []
    for tile in range(width // WIDE):
        shape = (groups, WIDE)
        own = index_of(shape, 0) == index_of(shape, 1) // CHANNELS_PER_GRP + tile * (WIDE // CHANNELS_PER_GRP)
        three = jnp.dot(terms, jnp.where(own, 1.0, 0.0).astype(BF16), preferred_element_type=F32)
        parts.append(three[:MODES] + three[MODES : 2 * MODES] + three[2 * MODES :])
    return jnp.concatenate(parts, axis=1)


def mode_row(channel_table):
    own = index_of(channel_table.shape, 0) == (index_of(channel_table.shape, 1) & (MODES - 1))
    return jnp.sum(jnp.where(own, channel_table, 0.0), axis=0, keepdims=True)


def as_column(row):
    return jnp.transpose(jnp.broadcast_to(row, (LANES, LANES)))


def own_mode(dtype):
    shape = (GROUPS, MODES, LANES)
    own = index_of(shape, 0) * MODES + index_of(shape, 1) == index_of(shape, 2)
    return jnp.where(own, 1.0, 0.0).astype(dtype)


def split(x):
    high = x.astype(BF16)
    return high, (x - high.astype(F32)).astype(BF16)


def group_mask(dtype):
    shape = (GROUPS, MODES, LANES)
    own = index_of(shape, 0) == index_of(shape, 2) // CHANNELS_PER_GRP
    return jnp.where(own, 1.0, 0.0).astype(dtype)


def spread(rows, mask):
    size = rows.shape[0]
    copies = rows.reshape(1, size // MODES, MODES, LANES) * mask.reshape(GROUPS, 1, MODES, LANES)
    return copies.reshape(GROUPS * size, LANES)


def shifted(block, before):
    one = pltpu.roll(block, 1, 0)
    two = pltpu.roll(block, 2, 0)
    first = index_of((8, block.shape[1]), 0)
    near, far = (0.0, 0.0) if before is None else (before[1:2], before[0:1])
    head_one = jnp.where(first == 0, near, one[:8])
    head_two = jnp.where(first == 0, far, jnp.where(first == 1, near, two[:8]))
    if block.shape[0] == 8:
        return head_one, head_two
    return jnp.concatenate([head_one, one[8:]], axis=0), jnp.concatenate([head_two, two[8:]], axis=0)


def short_conv(block, before, weights):
    one, two = shifted(block, before)
    return weights[0] * block + weights[1] * one + weights[2] * two


def shift_matrix(rows):
    shape = (2 * rows, rows)
    target = index_of(shape, 0)
    source = index_of(shape, 1)
    taken = jnp.where(target < rows, target - 1, target - (rows + 2))
    return jnp.where(source == taken, 1.0, 0.0).astype(BF16)


def earlier_tokens(shift, block):
    return jnp.dot(shift, block, preferred_element_type=F32)


def wide_conv(block, earlier, weights):
    rows = block.shape[0]
    return weights[0] * block.astype(F32) + weights[1] * earlier[:rows] + weights[2] * earlier[rows:]


def taps_of(weights, feature, lanes):
    return [weights[tap, feature : feature + 1, lanes] for tap in range(weights.shape[0])]


def state_kernel(
    projected_ref,
    weight_hbm,
    rate_hbm,
    residue_hbm,
    residual_hbm,
    product_ref,
    state_ref,
    mode_rate_ref,
    head_ref,
    weight_ref,
    query_ref,
    residue_ref,
    residual_ref,
    buffer_ref,
    ending_ref,
    shift_ref,
    short_ref,
    rate_ref,
    sems,
    small_sems,
):
    rows, width = product_ref.shape
    wides = width // WIDE
    rate_copy = pltpu.make_async_copy(rate_hbm, rate_ref, small_sems.at[0])
    rate_copy.start()
    weight_copy = pltpu.make_async_copy(weight_hbm, short_ref, small_sems.at[1])
    weight_copy.start()
    copies = [pltpu.make_async_copy(projected_ref.at[1 + c], buffer_ref.at[c], sems.at[c]) for c in (0, 1)]
    later = [
        pltpu.make_async_copy(residue_hbm, residue_ref, sems.at[2]),
        pltpu.make_async_copy(projected_ref.at[0], query_ref, sems.at[3]),
        pltpu.make_async_copy(residual_hbm, residual_ref, sems.at[4]),
    ]
    for copy in copies + later:
        copy.start()
    shift_ref[...] = shift_matrix(rows)
    rate_copy.wait()
    mode_rate = per_channel(rate_ref[...])
    mode_rate_ref[...] = mode_rate
    eye = own_mode(BF16)
    token = index_of((2 * LANES, rows), 1)
    left = jnp.where(token < 2, -1e30, (token - (rows - 1)).astype(F32)).astype(BF16)

    def exponents(tile):
        high, low = split(mode_rate[:, lanes_of(tile)])
        diagonal = jnp.concatenate([spread(high, eye), spread(low, eye)], axis=1)
        return (jnp.dot(diagonal, left, preferred_element_type=F32),)

    def endings(tile, exponent):
        ending_ref[tile // 2, lanes_of(tile % 2), :] = jnp.exp(exponent).astype(BF16)

    pipelined(width // LANES, exponents, endings)
    weight_copy.wait()
    weights = short_ref[...].astype(F32)
    weight_ref[...] = weights
    mask = group_mask(F32)
    for copy in copies:
        copy.wait()

    def fetch(wide):
        return [earlier_tokens(shift_ref[...], buffer_ref[c, :, lanes_of(wide, WIDE)]) for c in (0, 1)]

    def multiply(wide, *earlier):
        here = lanes_of(wide, WIDE)
        parts = []
        for c in (0, 1):
            head_ref[c, :, here] = buffer_ref[c, 0:16, here].astype(F32)[:8]
            parts.append(wide_conv(buffer_ref[c, :, here], earlier[c], taps_of(weights, c + 1, here)))
        product = (parts[0] * parts[1]).astype(BF16)
        product_ref[:, here] = product
        return (jnp.dot(ending_ref[wide], product, preferred_element_type=F32),)

    def leave(wide, every):
        for half in range(WIDE // LANES):
            own = every[lanes_of(half), lanes_of(half)].reshape(GROUPS, MODES, LANES)
            state_ref[:, lanes_of((WIDE // LANES) * wide + half)] = jnp.sum(own * mask, axis=0)

    pipelined(wides, fetch, multiply, leave)
    for copy in later:
        copy.wait()


def halo(before_ref, place_ref):
    return jnp.where(place_ref[0] > 0, before_ref[...].astype(F32), 0.0)


def halves(table, place_ref):
    half = table.shape[1] // 2
    left, right = table[:, :half], table[:, half:]
    even = lax.rem(place_ref[0], 2) == 0
    return jnp.where(even, left, right), jnp.where(even, right, left)


def head_kernel(rows, place_ref, before_ref, head_ref, weight_ref, state_ref, mode_rate_ref, keep_ref, send_ref, first_ref):
    before = halo(before_ref, place_ref)
    everything = slice(0, head_ref.shape[2])
    parts = [short_conv(head_ref[c], before[c + 1], taps_of(weight_ref, c + 1, everything)) for c in (0, 1)]
    first = (parts[0] * parts[1]).astype(BF16).astype(F32)
    first_ref[...] = first
    rate = mode_rate_ref[...]
    early = jnp.exp(-float(rows - 1) * rate) * first[0:1] + jnp.exp(-float(rows - 2) * rate) * first[1:2]
    keep, send = halves(state_ref[...] + early, place_ref)
    keep_ref[...] = keep
    send_ref[...] = send.astype(BF16)


def prepare_kernel(
    place_ref,
    query_ref,
    residue_ref,
    before_ref,
    weight_ref,
    mode_rate_ref,
    inner_ref,
    entering_ref,
    carry_ref,
    gate_ref,
    shift_ref,
):
    rows, width = gate_ref.shape
    shift_ref[...] = shift_matrix(rows)
    residue = per_channel(residue_ref[...])
    wide = GROUPS * CHUNK
    step = index_of((CHUNK, LANES), 0).astype(F32)
    causal = (index_of((CHUNK, wide), 1) & (CHUNK - 1)) <= index_of((CHUNK, wide), 0)
    eye = own_mode(BF16)
    flat_eye = jnp.where((index_of((MODES, LANES), 1) & (MODES - 1)) == index_of((MODES, LANES), 0), 1.0, 0.0)
    flat_eye = flat_eye.astype(BF16)
    shape = (2 * LANES, wide)
    source = (index_of(shape, 1) & (CHUNK - 1)).astype(F32)
    own = (index_of(shape, 0) & (LANES - 1)) // MODES == index_of(shape, 1) // CHUNK
    own_chunk = jnp.where(own[:LANES], 1.0, 0.0).astype(BF16)
    risen = source[:, :LANES].astype(BF16)
    left = jnp.where(own, source - (CHUNK - 1), 0.0).astype(BF16)

    def exponents(tile):
        rate = mode_rate_ref[:, lanes_of(tile)]
        high, low = split(rate)
        diagonal = jnp.concatenate([spread(high, eye), spread(low, eye)], axis=1)
        each = jnp.concatenate([high * flat_eye, low * flat_eye], axis=1)
        return (
            jnp.dot(diagonal, risen, preferred_element_type=F32),
            jnp.dot(each, left, preferred_element_type=F32),
        )

    def products(tile, rise, end):
        here = lanes_of(tile)
        rise_high, rise_low = [
            jnp.concatenate([part] * (wide // LANES), axis=1) * own_chunk for part in split(jnp.exp(rise))
        ]
        rate_row = mode_row(mode_rate_ref[:, here])
        falling = mode_row(residue[:, here]) * jnp.exp(-rate_row * step)
        fall_high, fall_low = split(falling)
        half = tile % (WIDE // LANES)
        for chunk in range(rows // CHUNK):
            entering = (falling * jnp.exp(-float(CHUNK * chunk + 1) * rate_row)).astype(BF16)
            carry_ref[tile // (WIDE // LANES), chunk * CHUNK : (chunk + 1) * CHUNK, lanes_of(half)] = entering
            if chunk == 0:
                entering_ref[tile] = entering
        return (
            jnp.dot(jnp.concatenate([fall_high, fall_low], axis=0), rise_high, preferred_element_type=F32),
            jnp.dot(fall_high, rise_low, preferred_element_type=F32),
            jnp.exp(end),
        )

    def finish(tile, taps, rest, ending):
        taps = jnp.where(causal, taps[:CHUNK] + taps[CHUNK:] + rest, 0.0)
        inner_ref[tile] = jnp.concatenate([taps.astype(BF16), ending.astype(BF16)], axis=0)

    pipelined(width // LANES, exponents, products, finish)
    before = halo(before_ref, place_ref)

    def fetch(part):
        return (earlier_tokens(shift_ref[...], query_ref[:, lanes_of(part, WIDE)]),)

    def convolve(part, earlier):
        here = lanes_of(part, WIDE)
        weights = taps_of(weight_ref, 0, here)
        gate_ref[:, here] = wide_conv(query_ref[:, here], earlier, weights)
        head = query_ref[0:16, here].astype(F32)[:8]
        gate_ref[0:8, here] = short_conv(head, before[0, :, here], weights)

    pipelined(width // WIDE, fetch, convolve)


def local_kernel(
    start,
    gate_ref,
    residual_ref,
    product_ref,
    first_ref,
    mode_rate_ref,
    inner_ref,
    entering_ref,
    skip_ref,
    base_ref,
):
    rows, width = base_ref.shape
    mask = group_mask(BF16)
    top = index_of((8, LANES), 0) < 2
    chunks = range(rows // CHUNK)

    def inside(item):
        tile = start + item
        here = lanes_of(tile)
        pieces = []
        for chunk in chunks:
            piece = product_ref[chunk * CHUNK : (chunk + 1) * CHUNK, here]
            if chunk == 0:
                wide = piece.astype(F32)
                head = jnp.where(top, first_ref[:, here], wide[:8])
                piece = jnp.concatenate([head, wide[8:]], axis=0).astype(BF16)
            pieces.append(piece)
        found = []
        for pair in chunks[::2]:
            sources = jnp.concatenate([spread(pieces[pair + k], mask) for k in (0, 1)], axis=1)
            found.append(jnp.dot(inner_ref[tile], sources, preferred_element_type=F32))
        return found, pieces[0]

    def across(item, inner, first):
        tile = start + item
        decay = jnp.exp(-float(CHUNK) * mode_rate_ref[:, lanes_of(tile)])
        state = jnp.zeros((MODES, LANES), F32)
        states = []
        for chunk in chunks:
            states.append(spread(state.astype(BF16), mask))
            state = decay * state + inner[chunk // 2][CHUNK:, lanes_of(chunk % 2)]
        outer = []
        for pair in chunks[::2]:
            two = jnp.concatenate(states[pair : pair + 2], axis=1)
            outer.append(jnp.dot(entering_ref[tile], two, preferred_element_type=F32))
        return [part[:CHUNK] for part in inner], outer, first

    def finish(item, inner, outer, first):
        here = lanes_of(start + item)
        skip = skip_ref[:, here]
        for chunk in chunks:
            span = slice(chunk * CHUNK, (chunk + 1) * CHUNK)
            piece = first if chunk == 0 else product_ref[span, here]
            conv = (inner[chunk // 2] + outer[chunk // 2])[:, lanes_of(chunk % 2)]
            whole = conv + skip * piece.astype(F32)
            base_ref[span, lanes_of(item)] = residual_ref[span, here].astype(F32) + gate_ref[span, here] * whole

    pipelined(width // LANES, inside, across, finish)


def pair_kernel(tokens, place_ref, keep_ref, got_ref, mode_rate_ref, even_ref, group_ref):
    rate, _ = halves(mode_rate_ref[...], place_ref)
    first = lax.rem(place_ref[0], 2) == 0
    keep, got = keep_ref[...], got_ref[...].astype(F32)
    even, odd = jnp.where(first, keep, got), jnp.where(first, got, keep)
    even_ref[...] = even
    group_ref[...] = (jnp.exp(-float(tokens) * rate) * even + odd).astype(BF16)


def join_kernel(tokens, radix, stride, place_ref, own_ref, mode_rate_ref, entry_ref, *refs):
    others, (found_ref, group_ref) = refs[: radix - 1], refs[radix - 1 :]
    rate, _ = halves(mode_rate_ref[...], place_ref)
    run = lax.rem(place_ref[0] // stride, radix)
    step = float(tokens * stride)

    def decayed(value, runs):
        return jnp.exp(-step * runs.astype(F32) * rate) * value

    found = jnp.zeros_like(rate)
    total = decayed(own_ref[...].astype(F32), radix - 1 - run)
    for k, ref in enumerate(others, 1):
        other = ref[...].astype(F32)
        found = found + jnp.where(run >= k, decayed(other, jnp.full((), k - 1, jnp.int32)), 0.0)
        source = lax.rem(run - k + radix, radix)
        total = total + decayed(other, radix - 1 - source)
    found_ref[...] = entry_ref[...] + jnp.exp(-before_pair(stride, tokens, place_ref) * rate) * found
    group_ref[...] = total.astype(BF16)


def before_pair(stride, tokens, place_ref):
    within = lax.rem(place_ref[0], stride)
    return (within - lax.rem(within, 2)).astype(F32) * float(tokens)


def hand_kernel(tokens, stride, place_ref, mode_rate_ref, entry_ref, even_ref, *refs):
    received, (keep_ref, send_ref) = refs[:-2], refs[-2:]
    rate, _ = halves(mode_rate_ref[...], place_ref)
    run = place_ref[0] // stride
    decay = jnp.exp(-float(tokens * stride) * rate)
    outer = jnp.zeros_like(rate)
    for k in range(len(received), 0, -1):
        outer = decay * outer + jnp.where(run >= k, received[k - 1][...].astype(F32), 0.0)
    entry = entry_ref[...] + jnp.exp(-before_pair(stride, tokens, place_ref) * rate) * outer
    second = jnp.exp(-float(tokens) * rate) * entry + even_ref[...]
    first = lax.rem(place_ref[0], 2) == 0
    keep_ref[...] = jnp.where(first, entry, second).astype(BF16)
    send_ref[...] = jnp.where(first, second, entry).astype(BF16)


def carry_kernel(
    place_ref, left_ref, right_ref, gate_ref, carry_ref, keep_ref, got_ref, summed_ref, squares_ref
):
    rows, width = gate_ref.shape
    half = width // 2
    even = lax.rem(place_ref[0], 2) == 0
    mask = group_mask(BF16)
    totals = [jnp.zeros((rows, LANES), F32)]
    nothing = jnp.zeros((LANES, LANES), BF16)

    def enter(tile):
        there = lanes_of(tile % (half // WIDE), WIDE)
        keep, got = keep_ref[:, there].astype(F32), got_ref[:, there].astype(F32)
        own_half = even if tile < half // WIDE else jnp.logical_not(even)
        entry = jnp.where(own_half, keep, got).astype(BF16)
        left, right = spread(entry[:, :LANES], mask), spread(entry[:, LANES:], mask)
        both = jnp.concatenate(
            [jnp.concatenate([left, nothing], axis=1), jnp.concatenate([nothing, right], axis=1)], axis=0
        )
        return (jnp.dot(carry_ref[tile], both, preferred_element_type=F32),)

    def add(tile, carry):
        here = lanes_of(tile, WIDE)
        base_ref = left_ref if tile < half // WIDE else right_ref
        base = base_ref[:, lanes_of(tile % (half // WIDE), WIDE)]
        summed = base + gate_ref[:, here] * carry
        summed_ref[:, here] = summed
        square = summed * summed
        totals[0] = totals[0] + (square[:, :LANES] + square[:, LANES:])

    pipelined(width // WIDE, enter, add)
    total = totals[0]
    squares = lax.dot_general(
        jnp.ones((8, 2 * LANES), BF16),
        jnp.concatenate(split(total), axis=1),
        (((1,), (1,)), ((), ())),
        preferred_element_type=F32,
    )
    squares_ref[...] = squares[0:1]


def write_kernel(summed_ref, out_hbm, rounded_ref, sems):
    width = summed_ref.shape[1]
    copies = []
    for tile in range(width // WIDE):
        here = lanes_of(tile, WIDE)
        rounded_ref[:, here] = summed_ref[:, here].astype(BF16)
        span = pl.ds(tile * WIDE, WIDE)
        copies.append(pltpu.make_async_copy(rounded_ref.at[:, span], out_hbm.at[:, span], sems.at[tile]))
        copies[-1].start()
    for copy in copies:
        copy.wait()


def norm_kernel(full_width, summed_ref, gain_ref, *refs):
    squares_refs, (out_hbm, rounded_ref, sems) = refs[:-3], refs[-3:]
    rows, width = summed_ref.shape
    squares = squares_refs[0][...]
    for ref in squares_refs[1:]:
        squares = squares + ref[...]
    scale_row = lax.rsqrt(squares / full_width + 1e-05)
    scale = jnp.concatenate([as_column(scale_row[:, lanes_of(k)]) for k in range(rows // LANES)], axis=0)
    copies = []
    for tile in range(width // WIDE):
        for half in range(WIDE // LANES):
            here = lanes_of(tile * (WIDE // LANES) + half)
            rounded_ref[:, here] = (summed_ref[:, here] * scale * gain_ref[:, here]).astype(BF16)
        span = pl.ds(tile * WIDE, WIDE)
        copies.append(pltpu.make_async_copy(rounded_ref.at[:, span], out_hbm.at[:, span], sems.at[tile]))
        copies[-1].start()
    for copy in copies:
        copy.wait()


def params():
    return pltpu.CompilerParams(vmem_limit_bytes=VMEM_LIMIT)


def cost(microseconds):
    return pl.CostEstimate(flops=0, bytes_accessed=int(microseconds * 3.0e6), transcendentals=0)


def radices(count):
    found = []
    for radix in (4, 3, 2, 5, 7):
        while count % radix == 0:
            found.append(radix)
            count //= radix
    return found + ([count] if count > 1 else [])


def ring(count, shift):
    return [(i, (i + shift) % count) for i in range(count)]


def per_device(projected, short_weight, rates, residues, skip, residual, gain):
    rows, width = projected.shape[1:]
    taps = short_weight.shape[0]
    peers = lax.axis_size("ctx")
    full_width = width * lax.axis_size("fsdp")
    place = lax.axis_index("ctx").astype(jnp.int32).reshape(1)
    hbm_spec = pl.BlockSpec(memory_space=pltpu.HBM)
    vmem_spec = pl.BlockSpec(memory_space=pltpu.VMEM)
    smem_spec = pl.BlockSpec(memory_space=pltpu.SMEM)
    tiles = width // LANES
    wides = width // WIDE

    def kept(array):
        return pltpu.with_memory_space_constraint(array, pltpu.HBM)

    def f32(*shape):
        return jax.ShapeDtypeStruct(shape, F32)

    def bf16(*shape):
        return jax.ShapeDtypeStruct(shape, BF16)

    before = lax.ppermute(projected[:, rows - (taps - 1) :, :], "ctx", ring(peers, 1))

    product, state, mode_rate, head, weights, query, residue, residual_here = pl.pallas_call(
        state_kernel,
        in_specs=[hbm_spec] * 5,
        out_shape=[
            bf16(rows, width),
            f32(MODES, width),
            f32(MODES, width),
            f32(2, 8, width),
            f32(*short_weight.shape),
            bf16(rows, width),
            f32(MODES, residues.shape[0]),
            bf16(rows, width),
        ],
        scratch_shapes=[
            pltpu.VMEM((2, rows, width), BF16),
            pltpu.VMEM((wides, WIDE, rows), BF16),
            pltpu.VMEM((2 * rows, rows), BF16),
            pltpu.VMEM(short_weight.shape, BF16),
            pltpu.VMEM((MODES, rates.shape[0]), F32),
            pltpu.SemaphoreType.DMA((5,)),
            pltpu.SemaphoreType.DMA((2,)),
        ],
        compiler_params=params(),
        cost_estimate=cost(3),
        name="block_state",
    )(kept(projected), kept(short_weight), kept(rates.T), kept(residues.T), kept(residual))

    half = width // 2

    def place_call(kernel, count, out_shape, microseconds, name, scratch=()):
        return pl.pallas_call(
            kernel,
            in_specs=[smem_spec] + [vmem_spec] * count,
            out_shape=out_shape,
            scratch_shapes=scratch,
            compiler_params=params(),
            cost_estimate=cost(microseconds),
            name=name,
        )

    keep, send, first = place_call(
        lambda *refs: head_kernel(rows, *refs),
        5,
        [f32(MODES, half), bf16(MODES, half), f32(8, width)],
        0.2,
        "head_tokens",
    )(place, before, head, weights, state, mode_rate)

    inner, entering, carry_table, gate = place_call(
        prepare_kernel,
        5,
        [
            bf16(tiles, CHUNK + MODES, GROUPS * CHUNK),
            bf16(tiles, CHUNK, LANES),
            bf16(wides, rows, WIDE),
            f32(rows, width),
        ],
        2,
        "prepare",
        [pltpu.VMEM((2 * rows, rows), BF16)],
    )(place, query, residue, before, weights, mode_rate)

    swap = [(i, i ^ 1) for i in range(peers)]
    got = lax.ppermute(send, "ctx", swap)
    got, inner = lax.optimization_barrier((got, inner))
    even, group = place_call(
        lambda *refs: pair_kernel(rows, *refs), 3, [f32(MODES, half), bf16(MODES, half)], 0.2, "pair"
    )(place, keep, got, mode_rate)

    entry, stride = jnp.zeros((MODES, half), F32), 2
    levels = radices(peers // 2)
    for radix in levels[:-1]:
        size = stride * radix
        cycles = [
            [(i, i // size * size + (i + stride * k) % size) for i in range(peers)] for k in range(1, radix)
        ]
        others = [lax.ppermute(group, "ctx", cycle) for cycle in cycles]
        entry, group = place_call(
            lambda *refs, radix=radix, stride=stride: join_kernel(rows, radix, stride, *refs),
            2 + radix,
            [f32(MODES, half), bf16(MODES, half)],
            0.2,
            "join",
        )(place, group, mode_rate, entry, *others)
        stride = size
    received = [lax.ppermute(group, "ctx", ring(peers, stride * k)) for k in range(1, levels[-1])]

    def local(start, entering):
        return pl.pallas_call(
            lambda *refs: local_kernel(start, *refs),
            out_shape=f32(rows, half),
            compiler_params=params(),
            cost_estimate=cost(1.3),
            name="local_conv",
        )(gate, residual_here, product, first, mode_rate, inner, entering, skip[None])

    left = local(0, entering)
    received[0], left = lax.optimization_barrier((received[0], left))
    keep, send = place_call(
        lambda *refs: hand_kernel(rows, stride, *refs), 3 + len(received), [bf16(MODES, half)] * 2, 0.2, "hand"
    )(place, mode_rate, entry, even, *received)
    got = lax.ppermute(send, "ctx", swap)
    keep, entering = lax.optimization_barrier((keep, entering))
    right = local(tiles // 2, entering)

    summed, squares = place_call(carry_kernel, 6, [f32(rows, width), f32(1, rows)], 1, "add_carry")(
        place, left, right, gate, carry_table, keep, got
    )

    count = lax.axis_size("fsdp")
    paired = count & (count - 1) == 0
    routes = [[(i, i ^ k if paired else (i + k) % count) for i in range(count)] for k in range(1, count)]
    parts = [lax.ppermute(squares, "fsdp", route) for route in routes]

    def write(kernel, operands, name):
        return pl.pallas_call(
            kernel,
            out_specs=hbm_spec,
            out_shape=bf16(rows, width),
            scratch_shapes=[pltpu.VMEM((rows, width), BF16), pltpu.SemaphoreType.DMA((wides,))],
            compiler_params=params(),
            cost_estimate=cost(1),
            name=name,
        )(*operands)

    new_residual = write(write_kernel, (summed,), "new_residual")
    normed = write(
        lambda *refs: norm_kernel(full_width, *refs), (summed, gain[None], squares, *parts), "normed"
    )
    return (new_residual, normed)


def solution(mesh):
    return jax.shard_map(
        per_device,
        mesh=mesh,
        in_specs=(
            P(None, "ctx", "fsdp"),
            P(None, None, "fsdp"),
            P("fsdp", None),
            P("fsdp", None),
            P("fsdp"),
            P("ctx", "fsdp"),
            P("fsdp"),
        ),
        out_specs=(P("ctx", "fsdp"), P("ctx", "fsdp")),
        check_vma=False,
    )
```

```python
import jax
import jax.numpy as jnp
from jax import lax
from jax.experimental import pallas as pl
from jax.experimental.pallas import tpu as pltpu
from jax.sharding import PartitionSpec as P

CHANNELS_PER_GRP = 16
MODES = 16
CHUNK = 32
LANES = 128
WIDE = 256
GROUPS = LANES // CHANNELS_PER_GRP
VMEM_LIMIT = 16 * 1024 * 1024
F32 = jnp.float32
BF16 = jnp.bfloat16


def index_of(shape, dim):
    return lax.broadcasted_iota(jnp.int32, shape, dim)


def pipelined(count, *stages):
    held = {}
    for step in range(count + len(stages) - 1):
        for k, stage in enumerate(stages):
            item = step - k
            if 0 <= item < count:
                held[item] = stage(item, *held.get(item, ()))


def lanes_of(tile, width=LANES):
    return slice(tile * width, (tile + 1) * width)


def per_channel(table):
    groups = table.shape[1]
    width = groups * CHANNELS_PER_GRP
    high = table.astype(BF16)
    rest = table - high.astype(F32)
    middle = rest.astype(BF16)
    low = (rest - middle.astype(F32)).astype(BF16)
    terms = jnp.concatenate([high, middle, low], axis=0)
    parts = []
    for tile in range(width // WIDE):
        shape = (groups, WIDE)
        own = index_of(shape, 0) == index_of(shape, 1) // CHANNELS_PER_GRP + tile * (WIDE // CHANNELS_PER_GRP)
        three = jnp.dot(terms, jnp.where(own, 1.0, 0.0).astype(BF16), preferred_element_type=F32)
        parts.append(three[:MODES] + three[MODES : 2 * MODES] + three[2 * MODES :])
    return jnp.concatenate(parts, axis=1)


def mode_row(channel_table):
    own = index_of(channel_table.shape, 0) == (index_of(channel_table.shape, 1) & (MODES - 1))
    return jnp.sum(jnp.where(own, channel_table, 0.0), axis=0, keepdims=True)


def as_column(row):
    return jnp.transpose(jnp.broadcast_to(row, (LANES, LANES)))


def own_mode(dtype):
    shape = (GROUPS, MODES, LANES)
    own = index_of(shape, 0) * MODES + index_of(shape, 1) == index_of(shape, 2)
    return jnp.where(own, 1.0, 0.0).astype(dtype)


def split(x):
    high = x.astype(BF16)
    return high, (x - high.astype(F32)).astype(BF16)


def group_mask(dtype):
    shape = (GROUPS, MODES, LANES)
    own = index_of(shape, 0) == index_of(shape, 2) // CHANNELS_PER_GRP
    return jnp.where(own, 1.0, 0.0).astype(dtype)


def spread(rows, mask):
    size = rows.shape[0]
    copies = rows.reshape(1, size // MODES, MODES, LANES) * mask.reshape(GROUPS, 1, MODES, LANES)
    return copies.reshape(GROUPS * size, LANES)


def shifted(block, before):
    one = pltpu.roll(block, 1, 0)
    two = pltpu.roll(block, 2, 0)
    first = index_of((8, block.shape[1]), 0)
    near, far = (0.0, 0.0) if before is None else (before[1:2], before[0:1])
    head_one = jnp.where(first == 0, near, one[:8])
    head_two = jnp.where(first == 0, far, jnp.where(first == 1, near, two[:8]))
    if block.shape[0] == 8:
        return head_one, head_two
    return jnp.concatenate([head_one, one[8:]], axis=0), jnp.concatenate([head_two, two[8:]], axis=0)


def short_conv(block, before, weights):
    one, two = shifted(block, before)
    return weights[0] * block + weights[1] * one + weights[2] * two


def shift_matrix(rows):
    shape = (2 * rows, rows)
    target = index_of(shape, 0)
    source = index_of(shape, 1)
    taken = jnp.where(target < rows, target - 1, target - (rows + 2))
    return jnp.where(source == taken, 1.0, 0.0).astype(BF16)


def earlier_tokens(shift, block):
    return jnp.dot(shift, block, preferred_element_type=F32)


def wide_conv(block, earlier, weights):
    rows = block.shape[0]
    return weights[0] * block.astype(F32) + weights[1] * earlier[:rows] + weights[2] * earlier[rows:]


def taps_of(weights, feature, lanes):
    return [weights[tap, feature : feature + 1, lanes] for tap in range(weights.shape[0])]


def state_kernel(
    projected_ref,
    weight_hbm,
    rate_hbm,
    residue_hbm,
    residual_hbm,
    product_ref,
    state_ref,
    mode_rate_ref,
    head_ref,
    weight_ref,
    query_ref,
    residue_ref,
    residual_ref,
    buffer_ref,
    ending_ref,
    shift_ref,
    short_ref,
    rate_ref,
    sems,
    small_sems,
):
    rows, width = product_ref.shape
    wides = width // WIDE
    rate_copy = pltpu.make_async_copy(rate_hbm, rate_ref, small_sems.at[0])
    rate_copy.start()
    weight_copy = pltpu.make_async_copy(weight_hbm, short_ref, small_sems.at[1])
    weight_copy.start()
    copies = [pltpu.make_async_copy(projected_ref.at[1 + c], buffer_ref.at[c], sems.at[c]) for c in (0, 1)]
    later = [
        pltpu.make_async_copy(residue_hbm, residue_ref, sems.at[2]),
        pltpu.make_async_copy(projected_ref.at[0], query_ref, sems.at[3]),
        pltpu.make_async_copy(residual_hbm, residual_ref, sems.at[4]),
    ]
    for copy in copies:
        copy.start()
    shift_ref[...] = shift_matrix(rows)
    rate_copy.wait()
    mode_rate = per_channel(rate_ref[...])
    mode_rate_ref[...] = mode_rate
    eye = own_mode(BF16)
    token = index_of((2 * LANES, rows), 1)
    left = jnp.where(token < 2, -1e30, (token - (rows - 1)).astype(F32)).astype(BF16)

    def exponents(tile):
        high, low = split(mode_rate[:, lanes_of(tile)])
        diagonal = jnp.concatenate([spread(high, eye), spread(low, eye)], axis=1)
        return (jnp.dot(diagonal, left, preferred_element_type=F32),)

    def endings(tile, exponent):
        ending_ref[tile // 2, lanes_of(tile % 2), :] = jnp.exp(exponent).astype(BF16)

    pipelined(width // LANES, exponents, endings)
    weight_copy.wait()
    weights = short_ref[...].astype(F32)
    weight_ref[...] = weights
    mask = group_mask(F32)
    for copy in copies:
        copy.wait()
    for copy in later:
        copy.start()

    def fetch(wide):
        return [earlier_tokens(shift_ref[...], buffer_ref[c, :, lanes_of(wide, WIDE)]) for c in (0, 1)]

    def multiply(wide, *earlier):
        here = lanes_of(wide, WIDE)
        parts = []
        for c in (0, 1):
            head_ref[c, :, here] = buffer_ref[c, 0:16, here].astype(F32)[:8]
            parts.append(wide_conv(buffer_ref[c, :, here], earlier[c], taps_of(weights, c + 1, here)))
        product = (parts[0] * parts[1]).astype(BF16)
        product_ref[:, here] = product
        return (jnp.dot(ending_ref[wide], product, preferred_element_type=F32),)

    def leave(wide, every):
        for half in range(WIDE // LANES):
            own = every[lanes_of(half), lanes_of(half)].reshape(GROUPS, MODES, LANES)
            state_ref[:, lanes_of((WIDE // LANES) * wide + half)] = jnp.sum(own * mask, axis=0)

    pipelined(wides, fetch, multiply, leave)
    for copy in later:
        copy.wait()


def halo(before_ref, place_ref):
    return jnp.where(place_ref[0] > 0, before_ref[...].astype(F32), 0.0)


def head_kernel(rows, place_ref, before_ref, head_ref, weight_ref, state_ref, mode_rate_ref, full_ref, first_ref):
    before = halo(before_ref, place_ref)
    everything = slice(0, head_ref.shape[2])
    parts = [short_conv(head_ref[c], before[c + 1], taps_of(weight_ref, c + 1, everything)) for c in (0, 1)]
    first = (parts[0] * parts[1]).astype(BF16).astype(F32)
    first_ref[...] = first
    rate = mode_rate_ref[...]
    early = jnp.exp(-float(rows - 1) * rate) * first[0:1] + jnp.exp(-float(rows - 2) * rate) * first[1:2]
    full_ref[...] = (state_ref[...] + early).astype(BF16)


def prepare_kernel(
    place_ref,
    query_ref,
    residue_ref,
    before_ref,
    weight_ref,
    mode_rate_ref,
    inner_ref,
    entering_ref,
    carry_ref,
    gate_ref,
    shift_ref,
):
    rows, width = gate_ref.shape
    shift_ref[...] = shift_matrix(rows)
    residue = per_channel(residue_ref[...])
    wide = GROUPS * CHUNK
    step = index_of((CHUNK, LANES), 0).astype(F32)
    causal = (index_of((CHUNK, wide), 1) & (CHUNK - 1)) <= index_of((CHUNK, wide), 0)
    eye = own_mode(BF16)
    flat_eye = jnp.where((index_of((MODES, LANES), 1) & (MODES - 1)) == index_of((MODES, LANES), 0), 1.0, 0.0)
    flat_eye = flat_eye.astype(BF16)
    shape = (2 * LANES, wide)
    source = (index_of(shape, 1) & (CHUNK - 1)).astype(F32)
    own = (index_of(shape, 0) & (LANES - 1)) // MODES == index_of(shape, 1) // CHUNK
    own_chunk = jnp.where(own[:LANES], 1.0, 0.0).astype(BF16)
    risen = source[:, :LANES].astype(BF16)
    left = jnp.where(own, source - (CHUNK - 1), 0.0).astype(BF16)

    def exponents(tile):
        rate = mode_rate_ref[:, lanes_of(tile)]
        high, low = split(rate)
        diagonal = jnp.concatenate([spread(high, eye), spread(low, eye)], axis=1)
        each = jnp.concatenate([high * flat_eye, low * flat_eye], axis=1)
        return (
            jnp.dot(diagonal, risen, preferred_element_type=F32),
            jnp.dot(each, left, preferred_element_type=F32),
        )

    def products(tile, rise, end):
        here = lanes_of(tile)
        rise_high, rise_low = [
            jnp.concatenate([part] * (wide // LANES), axis=1) * own_chunk for part in split(jnp.exp(rise))
        ]
        rate_row = mode_row(mode_rate_ref[:, here])
        falling = mode_row(residue[:, here]) * jnp.exp(-rate_row * step)
        fall_high, fall_low = split(falling)
        half = tile % (WIDE // LANES)
        for chunk in range(rows // CHUNK):
            entering = (falling * jnp.exp(-float(CHUNK * chunk + 1) * rate_row)).astype(BF16)
            carry_ref[tile // (WIDE // LANES), chunk * CHUNK : (chunk + 1) * CHUNK, lanes_of(half)] = entering
            if chunk == 0:
                entering_ref[tile] = entering
        return (
            jnp.dot(jnp.concatenate([fall_high, fall_low], axis=0), rise_high, preferred_element_type=F32),
            jnp.dot(fall_high, rise_low, preferred_element_type=F32),
            jnp.exp(end),
        )

    def finish(tile, taps, rest, ending):
        taps = jnp.where(causal, taps[:CHUNK] + taps[CHUNK:] + rest, 0.0)
        inner_ref[tile] = jnp.concatenate([taps.astype(BF16), ending.astype(BF16)], axis=0)

    pipelined(width // LANES, exponents, products, finish)
    before = halo(before_ref, place_ref)

    def fetch(part):
        return (earlier_tokens(shift_ref[...], query_ref[:, lanes_of(part, WIDE)]),)

    def convolve(part, earlier):
        here = lanes_of(part, WIDE)
        weights = taps_of(weight_ref, 0, here)
        gate_ref[:, here] = wide_conv(query_ref[:, here], earlier, weights)
        head = query_ref[0:16, here].astype(F32)[:8]
        gate_ref[0:8, here] = short_conv(head, before[0, :, here], weights)

    pipelined(width // WIDE, fetch, convolve)


def local_kernel(
    gate_ref,
    residual_ref,
    product_ref,
    first_ref,
    mode_rate_ref,
    inner_ref,
    entering_ref,
    skip_ref,
    base_ref,
):
    rows, width = product_ref.shape
    mask = group_mask(BF16)
    top = index_of((8, LANES), 0) < 2
    chunks = range(rows // CHUNK)

    def inside(tile):
        here = lanes_of(tile)
        pieces = []
        for chunk in chunks:
            piece = product_ref[chunk * CHUNK : (chunk + 1) * CHUNK, here]
            if chunk == 0:
                wide = piece.astype(F32)
                head = jnp.where(top, first_ref[:, here], wide[:8])
                piece = jnp.concatenate([head, wide[8:]], axis=0).astype(BF16)
            pieces.append(piece)
        found = []
        for pair in chunks[::2]:
            sources = jnp.concatenate([spread(pieces[pair + k], mask) for k in (0, 1)], axis=1)
            found.append(jnp.dot(inner_ref[tile], sources, preferred_element_type=F32))
        return found, pieces[0]

    def across(tile, inner, first):
        decay = jnp.exp(-float(CHUNK) * mode_rate_ref[:, lanes_of(tile)])
        state = jnp.zeros((MODES, LANES), F32)
        states = []
        for chunk in chunks:
            states.append(spread(state.astype(BF16), mask))
            state = decay * state + inner[chunk // 2][CHUNK:, lanes_of(chunk % 2)]
        outer = []
        for pair in chunks[::2]:
            two = jnp.concatenate(states[pair : pair + 2], axis=1)
            outer.append(jnp.dot(entering_ref[tile], two, preferred_element_type=F32))
        return [part[:CHUNK] for part in inner], outer, first

    def finish(tile, inner, outer, first):
        here = lanes_of(tile)
        skip = skip_ref[:, here]
        for chunk in chunks:
            span = slice(chunk * CHUNK, (chunk + 1) * CHUNK)
            piece = first if chunk == 0 else product_ref[span, here]
            conv = (inner[chunk // 2] + outer[chunk // 2])[:, lanes_of(chunk % 2)]
            whole = conv + skip * piece.astype(F32)
            base_ref[span, here] = residual_ref[span, here].astype(F32) + gate_ref[span, here] * whole

    pipelined(width // LANES, inside, across, finish)


def join_kernel(tokens, radix, stride, place_ref, own_ref, mode_rate_ref, entry_ref, *refs):
    others, (found_ref, group_ref) = refs[: radix - 1], refs[radix - 1 :]
    rate = mode_rate_ref[...]
    run = lax.rem(place_ref[0] // stride, radix)
    step = float(tokens * stride)

    def decayed(value, runs):
        return jnp.exp(-step * runs.astype(F32) * rate) * value

    found = jnp.zeros_like(rate)
    total = decayed(own_ref[...].astype(F32), radix - 1 - run)
    for k, ref in enumerate(others, 1):
        other = ref[...].astype(F32)
        source = partner(run, k, radix)
        found = found + jnp.where(source < run, decayed(other, jnp.maximum(run - 1 - source, 0)), 0.0)
        total = total + decayed(other, radix - 1 - source)
    within = lax.rem(place_ref[0], stride).astype(F32) * float(tokens)
    found_ref[...] = entry_ref[...] + jnp.exp(-within * rate) * found
    group_ref[...] = total.astype(BF16)


def carry_kernel(stride, radix, place_ref, base_ref, gate_ref, carry_ref, mode_rate_ref, inner_entry_ref, *refs):
    entry_refs, (summed_ref, squares_ref) = refs[:-2], refs[-2:]
    rows, width = base_ref.shape
    run = place_ref[0] // stride
    within = lax.rem(place_ref[0], stride).astype(F32) * float(rows)
    mask = group_mask(BF16)
    totals = [jnp.zeros((rows, LANES), F32)]
    nothing = jnp.zeros((LANES, LANES), BF16)

    def enter(tile):
        here = lanes_of(tile, WIDE)
        rate = mode_rate_ref[:, here]
        step = float(rows * stride)
        outer = jnp.zeros_like(rate)
        for k, ref in enumerate(entry_refs[::-1], 1):
            source = partner(run, k, radix)
            lag = jnp.maximum(run - 1 - source, 0).astype(F32) * step
            outer = outer + jnp.where(source < run, jnp.exp(-lag * rate) * ref[:, here].astype(F32), 0.0)
        entry = (inner_entry_ref[:, here] + jnp.exp(-within * rate) * outer).astype(BF16)
        left, right = spread(entry[:, :LANES], mask), spread(entry[:, LANES:], mask)
        both = jnp.concatenate(
            [jnp.concatenate([left, nothing], axis=1), jnp.concatenate([nothing, right], axis=1)], axis=0
        )
        return (jnp.dot(carry_ref[tile], both, preferred_element_type=F32),)

    def add(tile, carry):
        here = lanes_of(tile, WIDE)
        summed = base_ref[:, here] + gate_ref[:, here] * carry
        summed_ref[:, here] = summed
        square = summed * summed
        totals[0] = totals[0] + (square[:, :LANES] + square[:, LANES:])

    pipelined(width // WIDE, enter, add)
    total = totals[0]
    squares = lax.dot_general(
        jnp.ones((8, 2 * LANES), BF16),
        jnp.concatenate(split(total), axis=1),
        (((1,), (1,)), ((), ())),
        preferred_element_type=F32,
    )
    squares_ref[...] = squares[0:1]


def write_kernel(summed_ref, out_hbm, rounded_ref, sems):
    width = summed_ref.shape[1]
    copies = []
    for tile in range(width // WIDE):
        here = lanes_of(tile, WIDE)
        rounded_ref[:, here] = summed_ref[:, here].astype(BF16)
        span = pl.ds(tile * WIDE, WIDE)
        copies.append(pltpu.make_async_copy(rounded_ref.at[:, span], out_hbm.at[:, span], sems.at[tile]))
        copies[-1].start()
    for copy in copies:
        copy.wait()


def norm_kernel(full_width, summed_ref, gain_ref, *refs):
    squares_refs, (out_hbm, rounded_ref, sems) = refs[:-3], refs[-3:]
    rows, width = summed_ref.shape
    squares = squares_refs[0][...]
    for ref in squares_refs[1:]:
        squares = squares + ref[...]
    scale_row = lax.rsqrt(squares / full_width + 1e-05)
    scale = jnp.concatenate([as_column(scale_row[:, lanes_of(k)]) for k in range(rows // LANES)], axis=0)
    copies = []
    for tile in range(width // WIDE):
        for half in range(WIDE // LANES):
            here = lanes_of(tile * (WIDE // LANES) + half)
            rounded_ref[:, here] = (summed_ref[:, here] * scale * gain_ref[:, here]).astype(BF16)
        span = pl.ds(tile * WIDE, WIDE)
        copies.append(pltpu.make_async_copy(rounded_ref.at[:, span], out_hbm.at[:, span], sems.at[tile]))
        copies[-1].start()
    for copy in copies:
        copy.wait()


def params():
    return pltpu.CompilerParams(vmem_limit_bytes=VMEM_LIMIT)


def cost(microseconds):
    return pl.CostEstimate(flops=0, bytes_accessed=int(microseconds * 3.0e6), transcendentals=0)


def radices(count):
    found = []
    for radix in (2, 4, 4, 4, 3, 2, 5, 7):
        if count % radix == 0:
            found.append(radix)
            count //= radix
    return found + ([count] if count > 1 else [])


def partner(run, k, radix):
    if radix & (radix - 1) == 0:
        return run ^ k
    return (run - k + radix) % radix


def routes(count, stride, radix):
    found = []
    for k in range(1, radix):
        route = []
        for i in range(count):
            run = i // stride % radix
            route.append((i + (partner(run, k, radix) - run) * stride, i))
        found.append(route)
    return found


def ring(count, shift):
    return [(i, (i + shift) % count) for i in range(count)]


def per_device(projected, short_weight, rates, residues, skip, residual, gain):
    rows, width = projected.shape[1:]
    taps = short_weight.shape[0]
    peers = lax.axis_size("ctx")
    full_width = width * lax.axis_size("fsdp")
    place = lax.axis_index("ctx").astype(jnp.int32).reshape(1)
    hbm_spec = pl.BlockSpec(memory_space=pltpu.HBM)
    vmem_spec = pl.BlockSpec(memory_space=pltpu.VMEM)
    smem_spec = pl.BlockSpec(memory_space=pltpu.SMEM)
    tiles = width // LANES
    wides = width // WIDE

    def kept(array):
        return pltpu.with_memory_space_constraint(array, pltpu.HBM)

    def f32(*shape):
        return jax.ShapeDtypeStruct(shape, F32)

    def bf16(*shape):
        return jax.ShapeDtypeStruct(shape, BF16)

    before = lax.ppermute(projected[:, rows - (taps - 1) :, :], "ctx", ring(peers, 1))

    product, state, mode_rate, head, weights, query, residue, residual_here = pl.pallas_call(
        state_kernel,
        in_specs=[hbm_spec] * 5,
        out_shape=[
            bf16(rows, width),
            f32(MODES, width),
            f32(MODES, width),
            f32(2, 8, width),
            f32(*short_weight.shape),
            bf16(rows, width),
            f32(MODES, residues.shape[0]),
            bf16(rows, width),
        ],
        scratch_shapes=[
            pltpu.VMEM((2, rows, width), BF16),
            pltpu.VMEM((wides, WIDE, rows), BF16),
            pltpu.VMEM((2 * rows, rows), BF16),
            pltpu.VMEM(short_weight.shape, BF16),
            pltpu.VMEM((MODES, rates.shape[0]), F32),
            pltpu.SemaphoreType.DMA((5,)),
            pltpu.SemaphoreType.DMA((2,)),
        ],
        compiler_params=params(),
        cost_estimate=cost(3),
        name="block_state",
    )(kept(projected), kept(short_weight), kept(rates.T), kept(residues.T), kept(residual))

    full_state, first = pl.pallas_call(
        lambda *refs: head_kernel(rows, *refs),
        in_specs=[smem_spec] + [vmem_spec] * 5,
        out_shape=[bf16(MODES, width), f32(8, width)],
        compiler_params=params(),
        cost_estimate=cost(0.2),
        name="head_tokens",
    )(place, before, head, weights, state, mode_rate)

    inner, entering, carry_table, gate = pl.pallas_call(
        prepare_kernel,
        in_specs=[smem_spec] + [vmem_spec] * 5,
        out_shape=[
            bf16(tiles, CHUNK + MODES, GROUPS * CHUNK),
            bf16(tiles, CHUNK, LANES),
            bf16(wides, rows, WIDE),
            f32(rows, width),
        ],
        scratch_shapes=[pltpu.VMEM((2 * rows, rows), BF16)],
        compiler_params=params(),
        cost_estimate=cost(2),
        name="prepare",
    )(place, query, residue, before, weights, mode_rate)

    group, entry, stride = full_state, jnp.zeros((MODES, width), F32), 1
    levels = radices(peers)
    for level, radix in enumerate(levels):
        size = stride * radix
        if level == len(levels) - 1:
            break
        others = [lax.ppermute(group, "ctx", route) for route in routes(peers, stride, radix)]
        if level == 0:
            others[0], inner = lax.optimization_barrier((others[0], inner))
        entry, group = pl.pallas_call(
            lambda *refs, radix=radix, stride=stride: join_kernel(rows, radix, stride, *refs),
            in_specs=[smem_spec] + [vmem_spec] * (2 + radix),
            out_shape=[f32(MODES, width), bf16(MODES, width)],
            compiler_params=params(),
            cost_estimate=cost(0.2),
            name="join",
        )(place, group, mode_rate, entry, *others)
        stride = size
    received = [lax.ppermute(group, "ctx", route) for route in routes(peers, stride, levels[-1])[::-1]]

    base = pl.pallas_call(
        local_kernel,
        out_shape=f32(rows, width),
        compiler_params=params(),
        cost_estimate=cost(5),
        name="local_conv",
    )(gate, residual_here, product, first, mode_rate, inner, entering, skip[None])

    count = lax.axis_size("fsdp")
    summed, squares = pl.pallas_call(
        lambda *refs: carry_kernel(stride, levels[-1], *refs),
        in_specs=[smem_spec] + [vmem_spec] * (5 + len(received)),
        out_shape=[f32(rows, width), f32(1, rows)],
        compiler_params=params(),
        cost_estimate=cost(1),
        name="add_carry",
    )(place, base, gate, carry_table, mode_rate, entry, *received)

    parts = [lax.ppermute(squares, "fsdp", route) for route in routes(count, 1, count)[::-1]]

    def write(kernel, operands, name):
        return pl.pallas_call(
            kernel,
            out_specs=hbm_spec,
            out_shape=bf16(rows, width),
            scratch_shapes=[pltpu.VMEM((rows, width), BF16), pltpu.SemaphoreType.DMA((wides,))],
            compiler_params=params(),
            cost_estimate=cost(1),
            name=name,
        )(*operands)

    new_residual = write(write_kernel, (summed,), "new_residual")
    normed = write(
        lambda *refs: norm_kernel(full_width, *refs), (summed, gain[None], squares, *parts), "normed"
    )
    return (new_residual, normed)


def solution(mesh):
    return jax.shard_map(
        per_device,
        mesh=mesh,
        in_specs=(
            P(None, "ctx", "fsdp"),
            P(None, None, "fsdp"),
            P("fsdp", None),
            P("fsdp", None),
            P("fsdp"),
            P("ctx", "fsdp"),
            P("fsdp"),
        ),
        out_specs=(P("ctx", "fsdp"), P("ctx", "fsdp")),
        check_vma=False,
    )
```

```python
import jax
import jax.numpy as jnp
from jax import lax
from jax.experimental import pallas as pl
from jax.experimental.pallas import tpu as pltpu
from jax.sharding import PartitionSpec as P

CHANNELS_PER_GRP = 16
MODES = 16
CHUNK = 32
LANES = 128
WIDE = 256
GROUPS = LANES // CHANNELS_PER_GRP
VMEM_LIMIT = 16 * 1024 * 1024
F32 = jnp.float32
BF16 = jnp.bfloat16


def index_of(shape, dim):
    return lax.broadcasted_iota(jnp.int32, shape, dim)


def pipelined(count, *stages):
    held = {}
    for step in range(count + len(stages) - 1):
        for k, stage in enumerate(stages):
            item = step - k
            if 0 <= item < count:
                held[item] = stage(item, *held.get(item, ()))


def lanes_of(tile, width=LANES):
    return slice(tile * width, (tile + 1) * width)


def per_channel(table):
    groups = table.shape[1]
    width = groups * CHANNELS_PER_GRP
    high = table.astype(BF16)
    rest = table - high.astype(F32)
    middle = rest.astype(BF16)
    low = (rest - middle.astype(F32)).astype(BF16)
    terms = jnp.concatenate([high, middle, low], axis=0)
    parts = []
    for tile in range(width // WIDE):
        shape = (groups, WIDE)
        own = index_of(shape, 0) == index_of(shape, 1) // CHANNELS_PER_GRP + tile * (WIDE // CHANNELS_PER_GRP)
        three = jnp.dot(terms, jnp.where(own, 1.0, 0.0).astype(BF16), preferred_element_type=F32)
        parts.append(three[:MODES] + three[MODES : 2 * MODES] + three[2 * MODES :])
    return jnp.concatenate(parts, axis=1)


def mode_row(channel_table):
    own = index_of(channel_table.shape, 0) == (index_of(channel_table.shape, 1) & (MODES - 1))
    return jnp.sum(jnp.where(own, channel_table, 0.0), axis=0, keepdims=True)


def as_column(row):
    return jnp.transpose(jnp.broadcast_to(row, (LANES, LANES)))


def own_mode(dtype):
    shape = (GROUPS, MODES, LANES)
    own = index_of(shape, 0) * MODES + index_of(shape, 1) == index_of(shape, 2)
    return jnp.where(own, 1.0, 0.0).astype(dtype)


def split(x):
    high = x.astype(BF16)
    return high, (x - high.astype(F32)).astype(BF16)


def group_mask(dtype):
    shape = (GROUPS, MODES, LANES)
    own = index_of(shape, 0) == index_of(shape, 2) // CHANNELS_PER_GRP
    return jnp.where(own, 1.0, 0.0).astype(dtype)


def spread(rows, mask):
    size = rows.shape[0]
    copies = rows.reshape(1, size // MODES, MODES, LANES) * mask.reshape(GROUPS, 1, MODES, LANES)
    return copies.reshape(GROUPS * size, LANES)


def shifted(block, before):
    one = pltpu.roll(block, 1, 0)
    two = pltpu.roll(block, 2, 0)
    first = index_of((8, block.shape[1]), 0)
    near, far = (0.0, 0.0) if before is None else (before[1:2], before[0:1])
    head_one = jnp.where(first == 0, near, one[:8])
    head_two = jnp.where(first == 0, far, jnp.where(first == 1, near, two[:8]))
    if block.shape[0] == 8:
        return head_one, head_two
    return jnp.concatenate([head_one, one[8:]], axis=0), jnp.concatenate([head_two, two[8:]], axis=0)


def short_conv(block, before, weights):
    one, two = shifted(block, before)
    return weights[0] * block + weights[1] * one + weights[2] * two


def shift_matrix(rows):
    own = index_of((rows, rows), 1) == index_of((rows, rows), 0) - 2
    return jnp.where(own, 1.0, 0.0).astype(BF16)


def two_later(shift, block):
    return jnp.dot(shift, block, preferred_element_type=F32)


def wide_conv(block, two, weights):
    wide = block.astype(F32)
    one = pltpu.roll(wide, 1, 0)
    head = jnp.where(index_of((8, wide.shape[1]), 0) == 0, 0.0, one[:8])
    one = jnp.concatenate([head, one[8:]], axis=0)
    return weights[0] * wide + weights[1] * one + weights[2] * two


def taps_of(weights, feature, lanes):
    return [weights[tap, feature : feature + 1, lanes] for tap in range(weights.shape[0])]


def state_kernel(
    projected_ref,
    weight_hbm,
    rate_hbm,
    residue_hbm,
    residual_hbm,
    product_ref,
    state_ref,
    mode_rate_ref,
    head_ref,
    weight_ref,
    query_ref,
    residue_ref,
    residual_ref,
    buffer_ref,
    ending_ref,
    shift_ref,
    short_ref,
    rate_ref,
    sems,
    small_sems,
):
    rows, width = product_ref.shape
    wides = width // WIDE
    rate_copy = pltpu.make_async_copy(rate_hbm, rate_ref, small_sems.at[0])
    rate_copy.start()
    weight_copy = pltpu.make_async_copy(weight_hbm, short_ref, small_sems.at[1])
    weight_copy.start()
    part = width // 2
    copies = [
        pltpu.make_async_copy(
            projected_ref.at[1 + c, :, pl.ds(side * part, part)],
            buffer_ref.at[c, :, pl.ds(side * part, part)],
            sems.at[2 * side + c],
        )
        for side in (0, 1)
        for c in (0, 1)
    ]
    later = [
        pltpu.make_async_copy(residue_hbm, residue_ref, sems.at[4]),
        pltpu.make_async_copy(projected_ref.at[0], query_ref, sems.at[5]),
        pltpu.make_async_copy(residual_hbm, residual_ref, sems.at[6]),
    ]
    for copy in copies:
        copy.start()
    shift_ref[...] = shift_matrix(rows)
    rate_copy.wait()
    mode_rate = per_channel(rate_ref[...])
    mode_rate_ref[...] = mode_rate
    eye = own_mode(BF16)
    side = rows // 2
    left = (index_of((2 * LANES, side), 1) - (side - 1)).astype(F32).astype(BF16)

    def exponents(tile):
        high, low = split(mode_rate[:, lanes_of(tile)])
        diagonal = jnp.concatenate([spread(high, eye), spread(low, eye)], axis=1)
        return (jnp.dot(diagonal, left, preferred_element_type=F32),)

    def endings(tile, exponent):
        ending_ref[tile // 2, lanes_of(tile % 2), :] = jnp.exp(exponent).astype(BF16)

    pipelined(width // LANES, exponents, endings)
    weight_copy.wait()
    weights = short_ref[...].astype(F32)
    weight_ref[...] = weights
    mask = group_mask(F32)
    middle = jnp.exp(-float(side) * mode_rate)

    def fetch(wide):
        if wide % (wides // 2) == 0:
            first = 2 * (wide // (wides // 2))
            for copy in copies[first : first + 2]:
                copy.wait()
            if first > 0:
                for copy in later:
                    copy.start()
        return [two_later(shift_ref[...], buffer_ref[c, :, lanes_of(wide, WIDE)]) for c in (0, 1)]

    def multiply(wide, *later_two):
        here = lanes_of(wide, WIDE)
        parts = []
        for c in (0, 1):
            head_ref[c, :, here] = buffer_ref[c, 0:16, here].astype(F32)[:8]
            parts.append(wide_conv(buffer_ref[c, :, here], later_two[c], taps_of(weights, c + 1, here)))
        product = (parts[0] * parts[1]).astype(BF16)
        product_ref[:, here] = product
        head_ref[2, :, here] = product[:16].astype(F32)[:8]
        sides = jnp.concatenate([product[:side], product[side:]], axis=1)
        return (jnp.dot(ending_ref[wide], sides, preferred_element_type=F32),)

    def leave(wide, every):
        for half in range(WIDE // LANES):
            there = lanes_of((WIDE // LANES) * wide + half)
            early, late = [
                jnp.sum(every[lanes_of(half), lanes_of(k)].reshape(GROUPS, MODES, LANES) * mask, axis=0)
                for k in (half, WIDE // LANES + half)
            ]
            state_ref[:, there] = middle[:, there] * early + late

    pipelined(wides, fetch, multiply, leave)
    for copy in later:
        copy.wait()


def halo(before_ref, place_ref):
    return jnp.where(place_ref[0] > 0, before_ref[...].astype(F32), 0.0)


def head_kernel(rows, place_ref, before_ref, head_ref, weight_ref, state_ref, mode_rate_ref, full_ref, first_ref):
    before = halo(before_ref, place_ref)
    everything = slice(0, head_ref.shape[2])
    parts = [short_conv(head_ref[c], before[c + 1], taps_of(weight_ref, c + 1, everything)) for c in (0, 1)]
    first = (parts[0] * parts[1]).astype(BF16).astype(F32)
    first_ref[...] = first
    rate = mode_rate_ref[...]
    missing = first - head_ref[2]
    early = jnp.exp(-float(rows - 1) * rate) * missing[0:1] + jnp.exp(-float(rows - 2) * rate) * missing[1:2]
    full_ref[...] = (state_ref[...] + early).astype(BF16)


def prepare_kernel(
    place_ref,
    query_ref,
    residue_ref,
    before_ref,
    weight_ref,
    mode_rate_ref,
    inner_ref,
    entering_ref,
    carry_ref,
    gate_ref,
    shift_ref,
):
    rows, width = gate_ref.shape
    shift_ref[...] = shift_matrix(rows)
    residue = per_channel(residue_ref[...])
    wide = GROUPS * CHUNK
    step = index_of((CHUNK, LANES), 0).astype(F32)
    causal = (index_of((CHUNK, wide), 1) & (CHUNK - 1)) <= index_of((CHUNK, wide), 0)
    eye = own_mode(BF16)
    flat_eye = jnp.where((index_of((MODES, LANES), 1) & (MODES - 1)) == index_of((MODES, LANES), 0), 1.0, 0.0)
    flat_eye = flat_eye.astype(BF16)
    shape = (2 * LANES, wide)
    source = (index_of(shape, 1) & (CHUNK - 1)).astype(F32)
    own = (index_of(shape, 0) & (LANES - 1)) // MODES == index_of(shape, 1) // CHUNK
    own_chunk = jnp.where(own[:LANES], 1.0, 0.0).astype(BF16)
    risen = source[:, :LANES].astype(BF16)
    left = jnp.where(own, source - (CHUNK - 1), 0.0).astype(BF16)

    def exponents(tile):
        rate = mode_rate_ref[:, lanes_of(tile)]
        high, low = split(rate)
        diagonal = jnp.concatenate([spread(high, eye), spread(low, eye)], axis=1)
        each = jnp.concatenate([high * flat_eye, low * flat_eye], axis=1)
        return (
            jnp.dot(diagonal, risen, preferred_element_type=F32),
            jnp.dot(each, left, preferred_element_type=F32),
        )

    def products(tile, rise, end):
        here = lanes_of(tile)
        rise_high, rise_low = [
            jnp.concatenate([part] * (wide // LANES), axis=1) * own_chunk for part in split(jnp.exp(rise))
        ]
        rate_row = mode_row(mode_rate_ref[:, here])
        falling = mode_row(residue[:, here]) * jnp.exp(-rate_row * step)
        fall_high, fall_low = split(falling)
        half = tile % (WIDE // LANES)
        for chunk in range(rows // CHUNK):
            entering = (falling * jnp.exp(-float(CHUNK * chunk + 1) * rate_row)).astype(BF16)
            carry_ref[tile // (WIDE // LANES), chunk * CHUNK : (chunk + 1) * CHUNK, lanes_of(half)] = entering
            if chunk == 0:
                entering_ref[tile] = entering
        return (
            jnp.dot(jnp.concatenate([fall_high, fall_low], axis=0), rise_high, preferred_element_type=F32),
            jnp.dot(fall_high, rise_low, preferred_element_type=F32),
            jnp.exp(end),
        )

    def finish(tile, taps, rest, ending):
        taps = jnp.where(causal, taps[:CHUNK] + taps[CHUNK:] + rest, 0.0)
        inner_ref[tile] = jnp.concatenate([taps.astype(BF16), ending.astype(BF16)], axis=0)

    pipelined(width // LANES, exponents, products, finish)
    before = halo(before_ref, place_ref)

    def fetch(part):
        return (two_later(shift_ref[...], query_ref[:, lanes_of(part, WIDE)]),)

    def convolve(part, earlier):
        here = lanes_of(part, WIDE)
        weights = taps_of(weight_ref, 0, here)
        gate_ref[:, here] = wide_conv(query_ref[:, here], earlier, weights)
        head = query_ref[0:16, here].astype(F32)[:8]
        gate_ref[0:8, here] = short_conv(head, before[0, :, here], weights)

    pipelined(width // WIDE, fetch, convolve)


def local_kernel(
    gate_ref,
    residual_ref,
    product_ref,
    first_ref,
    mode_rate_ref,
    inner_ref,
    entering_ref,
    skip_ref,
    base_ref,
):
    rows, width = product_ref.shape
    mask = group_mask(BF16)
    top = index_of((8, LANES), 0) < 2
    chunks = range(rows // CHUNK)

    def inside(tile):
        here = lanes_of(tile)
        pieces = []
        for chunk in chunks:
            piece = product_ref[chunk * CHUNK : (chunk + 1) * CHUNK, here]
            if chunk == 0:
                wide = piece.astype(F32)
                head = jnp.where(top, first_ref[:, here], wide[:8])
                piece = jnp.concatenate([head, wide[8:]], axis=0).astype(BF16)
            pieces.append(piece)
        found = []
        for pair in chunks[::2]:
            sources = jnp.concatenate([spread(pieces[pair + k], mask) for k in (0, 1)], axis=1)
            found.append(jnp.dot(inner_ref[tile], sources, preferred_element_type=F32))
        return found, pieces[0]

    def across(tile, inner, first):
        decay = jnp.exp(-float(CHUNK) * mode_rate_ref[:, lanes_of(tile)])
        state = jnp.zeros((MODES, LANES), F32)
        states = []
        for chunk in chunks:
            states.append(spread(state.astype(BF16), mask))
            state = decay * state + inner[chunk // 2][CHUNK:, lanes_of(chunk % 2)]
        outer = []
        for pair in chunks[::2]:
            two = jnp.concatenate(states[pair : pair + 2], axis=1)
            outer.append(jnp.dot(entering_ref[tile], two, preferred_element_type=F32))
        return [part[:CHUNK] for part in inner], outer, first

    def finish(tile, inner, outer, first):
        here = lanes_of(tile)
        skip = skip_ref[:, here]
        for chunk in chunks:
            span = slice(chunk * CHUNK, (chunk + 1) * CHUNK)
            piece = first if chunk == 0 else product_ref[span, here]
            conv = (inner[chunk // 2] + outer[chunk // 2])[:, lanes_of(chunk % 2)]
            whole = conv + skip * piece.astype(F32)
            base_ref[span, here] = residual_ref[span, here].astype(F32) + gate_ref[span, here] * whole

    pipelined(width // LANES, inside, across, finish)


def join_kernel(tokens, radix, stride, place_ref, own_ref, mode_rate_ref, entry_ref, *refs):
    others, (found_ref, group_ref) = refs[: radix - 1], refs[radix - 1 :]
    rate = mode_rate_ref[...]
    run = lax.rem(place_ref[0] // stride, radix)
    step = float(tokens * stride)

    def decayed(value, runs):
        return jnp.exp(-step * runs.astype(F32) * rate) * value

    found = jnp.zeros_like(rate)
    total = decayed(own_ref[...].astype(F32), radix - 1 - run)
    for k, ref in enumerate(others, 1):
        other = ref[...].astype(F32)
        source = partner(run, k, radix)
        found = found + jnp.where(source < run, decayed(other, jnp.maximum(run - 1 - source, 0)), 0.0)
        total = total + decayed(other, radix - 1 - source)
    within = lax.rem(place_ref[0], stride).astype(F32) * float(tokens)
    found_ref[...] = entry_ref[...] + jnp.exp(-within * rate) * found
    group_ref[...] = total.astype(BF16)


def carry_kernel(stride, radix, place_ref, base_ref, gate_ref, carry_ref, mode_rate_ref, inner_entry_ref, *refs):
    entry_refs, (summed_ref, squares_ref) = refs[:-2], refs[-2:]
    rows, width = base_ref.shape
    run = place_ref[0] // stride
    within = lax.rem(place_ref[0], stride).astype(F32) * float(rows)
    mask = group_mask(BF16)
    totals = [jnp.zeros((rows, LANES), F32)]
    nothing = jnp.zeros((LANES, LANES), BF16)

    def enter(tile):
        here = lanes_of(tile, WIDE)
        rate = mode_rate_ref[:, here]
        step = float(rows * stride)
        outer = jnp.zeros_like(rate)
        for k, ref in enumerate(entry_refs[::-1], 1):
            source = partner(run, k, radix)
            lag = jnp.maximum(run - 1 - source, 0).astype(F32) * step
            outer = outer + jnp.where(source < run, jnp.exp(-lag * rate) * ref[:, here].astype(F32), 0.0)
        entry = (inner_entry_ref[:, here] + jnp.exp(-within * rate) * outer).astype(BF16)
        left, right = spread(entry[:, :LANES], mask), spread(entry[:, LANES:], mask)
        both = jnp.concatenate(
            [jnp.concatenate([left, nothing], axis=1), jnp.concatenate([nothing, right], axis=1)], axis=0
        )
        return (jnp.dot(carry_ref[tile], both, preferred_element_type=F32),)

    def add(tile, carry):
        here = lanes_of(tile, WIDE)
        summed = base_ref[:, here] + gate_ref[:, here] * carry
        summed_ref[:, here] = summed
        square = summed * summed
        totals[0] = totals[0] + (square[:, :LANES] + square[:, LANES:])

    pipelined(width // WIDE, enter, add)
    total = totals[0]
    squares = lax.dot_general(
        jnp.ones((8, 2 * LANES), BF16),
        jnp.concatenate(split(total), axis=1),
        (((1,), (1,)), ((), ())),
        preferred_element_type=F32,
    )
    squares_ref[...] = squares[0:1]


def write_kernel(summed_ref, out_hbm, rounded_ref, sems):
    width = summed_ref.shape[1]
    copies = []
    for tile in range(width // WIDE):
        here = lanes_of(tile, WIDE)
        rounded_ref[:, here] = summed_ref[:, here].astype(BF16)
        span = pl.ds(tile * WIDE, WIDE)
        copies.append(pltpu.make_async_copy(rounded_ref.at[:, span], out_hbm.at[:, span], sems.at[tile]))
        copies[-1].start()
    for copy in copies:
        copy.wait()


def norm_kernel(full_width, summed_ref, gain_ref, *refs):
    squares_refs, (out_hbm, rounded_ref, sems) = refs[:-3], refs[-3:]
    rows, width = summed_ref.shape
    squares = squares_refs[0][...]
    for ref in squares_refs[1:]:
        squares = squares + ref[...]
    scale_row = lax.rsqrt(squares / full_width + 1e-05)
    scale = jnp.concatenate([as_column(scale_row[:, lanes_of(k)]) for k in range(rows // LANES)], axis=0)
    copies = []
    block = rows // 8
    for start in range(0, rows, block):
        span = slice(start, start + block)
        for tile in range(width // LANES):
            here = lanes_of(tile)
            rounded_ref[span, here] = (summed_ref[span, here] * scale[span] * gain_ref[:, here]).astype(BF16)
        there = pl.ds(start, block)
        copies.append(pltpu.make_async_copy(rounded_ref.at[there, :], out_hbm.at[there, :], sems.at[start // block]))
        copies[-1].start()
    for copy in copies:
        copy.wait()


def params():
    return pltpu.CompilerParams(vmem_limit_bytes=VMEM_LIMIT)


def cost(microseconds):
    return pl.CostEstimate(flops=0, bytes_accessed=int(microseconds * 3.0e6), transcendentals=0)


def radices(count):
    found = []
    for radix in (2, 4, 4, 4, 3, 2, 5, 7):
        if count % radix == 0:
            found.append(radix)
            count //= radix
    return found + ([count] if count > 1 else [])


def partner(run, k, radix):
    if radix & (radix - 1) == 0:
        return run ^ k
    return (run - k + radix) % radix


def routes(count, stride, radix):
    found = []
    for k in range(1, radix):
        route = []
        for i in range(count):
            run = i // stride % radix
            route.append((i + (partner(run, k, radix) - run) * stride, i))
        found.append(route)
    return found


def ring(count, shift):
    return [(i, (i + shift) % count) for i in range(count)]


def per_device(projected, short_weight, rates, residues, skip, residual, gain):
    rows, width = projected.shape[1:]
    taps = short_weight.shape[0]
    peers = lax.axis_size("ctx")
    full_width = width * lax.axis_size("fsdp")
    place = lax.axis_index("ctx").astype(jnp.int32).reshape(1)
    hbm_spec = pl.BlockSpec(memory_space=pltpu.HBM)
    vmem_spec = pl.BlockSpec(memory_space=pltpu.VMEM)
    smem_spec = pl.BlockSpec(memory_space=pltpu.SMEM)
    tiles = width // LANES
    wides = width // WIDE

    def kept(array):
        return pltpu.with_memory_space_constraint(array, pltpu.HBM)

    def f32(*shape):
        return jax.ShapeDtypeStruct(shape, F32)

    def bf16(*shape):
        return jax.ShapeDtypeStruct(shape, BF16)

    before = lax.ppermute(projected[:, rows - (taps - 1) :, :], "ctx", ring(peers, 1))

    product, state, mode_rate, head, weights, query, residue, residual_here = pl.pallas_call(
        state_kernel,
        in_specs=[hbm_spec] * 5,
        out_shape=[
            bf16(rows, width),
            f32(MODES, width),
            f32(MODES, width),
            f32(3, 8, width),
            f32(*short_weight.shape),
            bf16(rows, width),
            f32(MODES, residues.shape[0]),
            bf16(rows, width),
        ],
        scratch_shapes=[
            pltpu.VMEM((2, rows, width), BF16),
            pltpu.VMEM((wides, WIDE, rows // 2), BF16),
            pltpu.VMEM((rows, rows), BF16),
            pltpu.VMEM(short_weight.shape, BF16),
            pltpu.VMEM((MODES, rates.shape[0]), F32),
            pltpu.SemaphoreType.DMA((7,)),
            pltpu.SemaphoreType.DMA((2,)),
        ],
        compiler_params=params(),
        cost_estimate=cost(3),
        name="block_state",
    )(kept(projected), kept(short_weight), kept(rates.T), kept(residues.T), kept(residual))

    full_state, first = pl.pallas_call(
        lambda *refs: head_kernel(rows, *refs),
        in_specs=[smem_spec] + [vmem_spec] * 5,
        out_shape=[bf16(MODES, width), f32(8, width)],
        compiler_params=params(),
        cost_estimate=cost(0.2),
        name="head_tokens",
    )(place, before, head, weights, state, mode_rate)

    inner, entering, carry_table, gate = pl.pallas_call(
        prepare_kernel,
        in_specs=[smem_spec] + [vmem_spec] * 5,
        out_shape=[
            bf16(tiles, CHUNK + MODES, GROUPS * CHUNK),
            bf16(tiles, CHUNK, LANES),
            bf16(wides, rows, WIDE),
            f32(rows, width),
        ],
        scratch_shapes=[pltpu.VMEM((rows, rows), BF16)],
        compiler_params=params(),
        cost_estimate=cost(2),
        name="prepare",
    )(place, query, residue, before, weights, mode_rate)

    group, entry, stride = full_state, jnp.zeros((MODES, width), F32), 1
    levels = radices(peers)
    for level, radix in enumerate(levels):
        size = stride * radix
        if level == len(levels) - 1:
            break
        others = [lax.ppermute(group, "ctx", route) for route in routes(peers, stride, radix)]
        if level == 0:
            others[0], inner = lax.optimization_barrier((others[0], inner))
        entry, group = pl.pallas_call(
            lambda *refs, radix=radix, stride=stride: join_kernel(rows, radix, stride, *refs),
            in_specs=[smem_spec] + [vmem_spec] * (2 + radix),
            out_shape=[f32(MODES, width), bf16(MODES, width)],
            compiler_params=params(),
            cost_estimate=cost(0.2),
            name="join",
        )(place, group, mode_rate, entry, *others)
        stride = size
    received = [lax.ppermute(group, "ctx", route) for route in routes(peers, stride, levels[-1])[::-1]]

    base = pl.pallas_call(
        local_kernel,
        out_shape=f32(rows, width),
        compiler_params=params(),
        cost_estimate=cost(5),
        name="local_conv",
    )(gate, residual_here, product, first, mode_rate, inner, entering, skip[None])

    count = lax.axis_size("fsdp")
    summed, squares = pl.pallas_call(
        lambda *refs: carry_kernel(stride, levels[-1], *refs),
        in_specs=[smem_spec] + [vmem_spec] * (5 + len(received)),
        out_shape=[f32(rows, width), f32(1, rows)],
        compiler_params=params(),
        cost_estimate=cost(1),
        name="add_carry",
    )(place, base, gate, carry_table, mode_rate, entry, *received)

    parts = [lax.ppermute(squares, "fsdp", route) for route in routes(count, 1, count)[::-1]]

    def write(kernel, operands, name):
        return pl.pallas_call(
            kernel,
            out_specs=hbm_spec,
            out_shape=bf16(rows, width),
            scratch_shapes=[pltpu.VMEM((rows, width), BF16), pltpu.SemaphoreType.DMA((max(8, wides),))],
            compiler_params=params(),
            cost_estimate=cost(1),
            name=name,
        )(*operands)

    new_residual = write(write_kernel, (summed,), "new_residual")
    normed = write(
        lambda *refs: norm_kernel(full_width, *refs), (summed, gain[None], squares, *parts), "normed"
    )
    return (new_residual, normed)


def solution(mesh):
    return jax.shard_map(
        per_device,
        mesh=mesh,
        in_specs=(
            P(None, "ctx", "fsdp"),
            P(None, None, "fsdp"),
            P("fsdp", None),
            P("fsdp", None),
            P("fsdp"),
            P("ctx", "fsdp"),
            P("fsdp"),
        ),
        out_specs=(P("ctx", "fsdp"), P("ctx", "fsdp")),
        check_vma=False,
    )
```

```python
import jax
import jax.numpy as jnp
from jax import lax
from jax.experimental import pallas as pl
from jax.experimental.pallas import tpu as pltpu
from jax.sharding import PartitionSpec as P

CHANNELS_PER_GRP = 16
MODES = 16
CHUNK = 32
LANES = 128
WIDE = 256
GROUPS = LANES // CHANNELS_PER_GRP
VMEM_LIMIT = 16 * 1024 * 1024
F32 = jnp.float32
BF16 = jnp.bfloat16


def index_of(shape, dim):
    return lax.broadcasted_iota(jnp.int32, shape, dim)


def pipelined(count, *stages):
    held = {}
    for step in range(count + len(stages) - 1):
        for k, stage in enumerate(stages):
            item = step - k
            if 0 <= item < count:
                held[item] = stage(item, *held.get(item, ()))


def lanes_of(tile, width=LANES):
    return slice(tile * width, (tile + 1) * width)


def per_channel(table):
    groups = table.shape[1]
    width = groups * CHANNELS_PER_GRP
    high = table.astype(BF16)
    rest = table - high.astype(F32)
    middle = rest.astype(BF16)
    low = (rest - middle.astype(F32)).astype(BF16)
    terms = jnp.concatenate([high, middle, low], axis=0)
    parts = []
    for tile in range(width // WIDE):
        shape = (groups, WIDE)
        own = index_of(shape, 0) == index_of(shape, 1) // CHANNELS_PER_GRP + tile * (WIDE // CHANNELS_PER_GRP)
        three = jnp.dot(terms, jnp.where(own, 1.0, 0.0).astype(BF16), preferred_element_type=F32)
        parts.append(three[:MODES] + three[MODES : 2 * MODES] + three[2 * MODES :])
    return jnp.concatenate(parts, axis=1)


def mode_row(channel_table):
    own = index_of(channel_table.shape, 0) == (index_of(channel_table.shape, 1) & (MODES - 1))
    return jnp.sum(jnp.where(own, channel_table, 0.0), axis=0, keepdims=True)


def as_column(row):
    return jnp.transpose(jnp.broadcast_to(row, (LANES, LANES)))


def own_mode(dtype):
    shape = (GROUPS, MODES, LANES)
    own = index_of(shape, 0) * MODES + index_of(shape, 1) == index_of(shape, 2)
    return jnp.where(own, 1.0, 0.0).astype(dtype)


def split(x):
    high = x.astype(BF16)
    return high, (x - high.astype(F32)).astype(BF16)


def group_mask(dtype):
    shape = (GROUPS, MODES, LANES)
    own = index_of(shape, 0) == index_of(shape, 2) // CHANNELS_PER_GRP
    return jnp.where(own, 1.0, 0.0).astype(dtype)


def spread(rows, mask):
    size = rows.shape[0]
    copies = rows.reshape(1, size // MODES, MODES, LANES) * mask.reshape(GROUPS, 1, MODES, LANES)
    return copies.reshape(GROUPS * size, LANES)


def shifted(block, before):
    one = pltpu.roll(block, 1, 0)
    two = pltpu.roll(block, 2, 0)
    first = index_of((8, block.shape[1]), 0)
    near, far = (0.0, 0.0) if before is None else (before[1:2], before[0:1])
    head_one = jnp.where(first == 0, near, one[:8])
    head_two = jnp.where(first == 0, far, jnp.where(first == 1, near, two[:8]))
    if block.shape[0] == 8:
        return head_one, head_two
    return jnp.concatenate([head_one, one[8:]], axis=0), jnp.concatenate([head_two, two[8:]], axis=0)


def short_conv(block, before, weights):
    one, two = shifted(block, before)
    return weights[0] * block + weights[1] * one + weights[2] * two


def shift_matrix(rows):
    own = index_of((rows, rows), 1) == index_of((rows, rows), 0) - 2
    return jnp.where(own, 1.0, 0.0).astype(BF16)


def two_later(shift, block):
    return jnp.dot(shift, block, preferred_element_type=F32)


def wide_conv(block, two, weights):
    wide = block.astype(F32)
    one = pltpu.roll(wide, 1, 0)
    head = jnp.where(index_of((8, wide.shape[1]), 0) == 0, 0.0, one[:8])
    one = jnp.concatenate([head, one[8:]], axis=0)
    return weights[0] * wide + weights[1] * one + weights[2] * two


def taps_of(weights, feature, lanes):
    return [weights[tap, feature : feature + 1, lanes] for tap in range(weights.shape[0])]


def state_kernel(
    projected_ref,
    weight_hbm,
    rate_hbm,
    residue_hbm,
    residual_hbm,
    product_ref,
    state_ref,
    mode_rate_ref,
    head_ref,
    weight_ref,
    query_ref,
    residue_ref,
    residual_ref,
    buffer_ref,
    ending_ref,
    shift_ref,
    short_ref,
    rate_ref,
    sems,
    small_sems,
):
    rows, width = product_ref.shape
    wides = width // WIDE
    rate_copy = pltpu.make_async_copy(rate_hbm, rate_ref, small_sems.at[0])
    rate_copy.start()
    weight_copy = pltpu.make_async_copy(weight_hbm, short_ref, small_sems.at[1])
    weight_copy.start()
    part = width // 2
    copies = [
        pltpu.make_async_copy(
            projected_ref.at[1 + c, :, pl.ds(side * part, part)],
            buffer_ref.at[c, :, pl.ds(side * part, part)],
            sems.at[2 * side + c],
        )
        for side in (0, 1)
        for c in (0, 1)
    ]
    later = [
        pltpu.make_async_copy(residue_hbm, residue_ref, sems.at[4]),
        pltpu.make_async_copy(projected_ref.at[0], query_ref, sems.at[5]),
        pltpu.make_async_copy(residual_hbm, residual_ref, sems.at[6]),
    ]
    for copy in copies:
        copy.start()
    shift_ref[...] = shift_matrix(rows)
    rate_copy.wait()
    mode_rate = per_channel(rate_ref[...])
    mode_rate_ref[...] = mode_rate
    eye = own_mode(BF16)
    side = rows // 2
    left = (index_of((2 * LANES, side), 1) - (side - 1)).astype(F32).astype(BF16)

    def exponents(tile):
        high, low = split(mode_rate[:, lanes_of(tile)])
        diagonal = jnp.concatenate([spread(high, eye), spread(low, eye)], axis=1)
        return (jnp.dot(diagonal, left, preferred_element_type=F32),)

    def endings(tile, exponent):
        ending_ref[tile // 2, lanes_of(tile % 2), :] = jnp.exp(exponent).astype(BF16)

    pipelined(width // LANES, exponents, endings)
    weight_copy.wait()
    weights = short_ref[...].astype(F32)
    weight_ref[...] = weights
    mask = group_mask(F32)
    middle = jnp.exp(-float(side) * mode_rate)

    def fetch(wide):
        if wide % (wides // 2) == 0:
            first = 2 * (wide // (wides // 2))
            for copy in copies[first : first + 2]:
                copy.wait()
            if first == 0:
                for copy in later:
                    copy.start()
        return [two_later(shift_ref[...], buffer_ref[c, :, lanes_of(wide, WIDE)]) for c in (0, 1)]

    def multiply(wide, *later_two):
        here = lanes_of(wide, WIDE)
        parts = []
        for c in (0, 1):
            head_ref[c, :, here] = buffer_ref[c, 0:16, here].astype(F32)[:8]
            parts.append(wide_conv(buffer_ref[c, :, here], later_two[c], taps_of(weights, c + 1, here)))
        product = (parts[0] * parts[1]).astype(BF16)
        product_ref[:, here] = product
        head_ref[2, :, here] = product[:16].astype(F32)[:8]
        sides = jnp.concatenate([product[:side], product[side:]], axis=1)
        return (jnp.dot(ending_ref[wide], sides, preferred_element_type=F32),)

    def leave(wide, every):
        for half in range(WIDE // LANES):
            there = lanes_of((WIDE // LANES) * wide + half)
            early, late = [
                jnp.sum(every[lanes_of(half), lanes_of(k)].reshape(GROUPS, MODES, LANES) * mask, axis=0)
                for k in (half, WIDE // LANES + half)
            ]
            state_ref[:, there] = middle[:, there] * early + late

    pipelined(wides, fetch, multiply, leave)
    for copy in later:
        copy.wait()


def halo(before_ref, place_ref):
    return jnp.where(place_ref[0] > 0, before_ref[...].astype(F32), 0.0)


def head_kernel(rows, place_ref, before_ref, head_ref, weight_ref, state_ref, mode_rate_ref, full_ref, first_ref):
    before = halo(before_ref, place_ref)
    everything = slice(0, head_ref.shape[2])
    parts = [short_conv(head_ref[c], before[c + 1], taps_of(weight_ref, c + 1, everything)) for c in (0, 1)]
    first = (parts[0] * parts[1]).astype(BF16).astype(F32)
    first_ref[...] = first
    rate = mode_rate_ref[...]
    missing = first - head_ref[2]
    early = jnp.exp(-float(rows - 1) * rate) * missing[0:1] + jnp.exp(-float(rows - 2) * rate) * missing[1:2]
    full_ref[...] = (state_ref[...] + early).astype(BF16)


def prepare_kernel(
    place_ref,
    query_ref,
    residue_ref,
    before_ref,
    weight_ref,
    mode_rate_ref,
    inner_ref,
    entering_ref,
    carry_ref,
    gate_ref,
    shift_ref,
):
    rows, width = gate_ref.shape
    shift_ref[...] = shift_matrix(rows)
    residue = per_channel(residue_ref[...])
    wide = GROUPS * CHUNK
    step = index_of((CHUNK, LANES), 0).astype(F32)
    causal = (index_of((CHUNK, wide), 1) & (CHUNK - 1)) <= index_of((CHUNK, wide), 0)
    eye = own_mode(BF16)
    flat_eye = jnp.where((index_of((MODES, LANES), 1) & (MODES - 1)) == index_of((MODES, LANES), 0), 1.0, 0.0)
    flat_eye = flat_eye.astype(BF16)
    shape = (2 * LANES, wide)
    source = (index_of(shape, 1) & (CHUNK - 1)).astype(F32)
    own = (index_of(shape, 0) & (LANES - 1)) // MODES == index_of(shape, 1) // CHUNK
    own_chunk = jnp.where(own[:LANES], 1.0, 0.0).astype(BF16)
    risen = source[:, :LANES].astype(BF16)
    left = jnp.where(own, source - (CHUNK - 1), 0.0).astype(BF16)

    def exponents(tile):
        rate = mode_rate_ref[:, lanes_of(tile)]
        high, low = split(rate)
        diagonal = jnp.concatenate([spread(high, eye), spread(low, eye)], axis=1)
        each = jnp.concatenate([high * flat_eye, low * flat_eye], axis=1)
        return (
            jnp.dot(diagonal, risen, preferred_element_type=F32),
            jnp.dot(each, left, preferred_element_type=F32),
        )

    def products(tile, rise, end):
        here = lanes_of(tile)
        rise_high, rise_low = [
            jnp.concatenate([part] * (wide // LANES), axis=1) * own_chunk for part in split(jnp.exp(rise))
        ]
        rate_row = mode_row(mode_rate_ref[:, here])
        falling = mode_row(residue[:, here]) * jnp.exp(-rate_row * step)
        fall_high, fall_low = split(falling)
        half = tile % (WIDE // LANES)
        for chunk in range(rows // CHUNK):
            entering = (falling * jnp.exp(-float(CHUNK * chunk + 1) * rate_row)).astype(BF16)
            carry_ref[tile // (WIDE // LANES), chunk * CHUNK : (chunk + 1) * CHUNK, lanes_of(half)] = entering
            if chunk == 0:
                entering_ref[tile] = entering
        return (
            jnp.dot(jnp.concatenate([fall_high, fall_low], axis=0), rise_high, preferred_element_type=F32),
            jnp.dot(fall_high, rise_low, preferred_element_type=F32),
            jnp.exp(end),
        )

    def finish(tile, taps, rest, ending):
        taps = jnp.where(causal, taps[:CHUNK] + taps[CHUNK:] + rest, 0.0)
        inner_ref[tile] = jnp.concatenate([taps.astype(BF16), ending.astype(BF16)], axis=0)

    pipelined(width // LANES, exponents, products, finish)
    before = halo(before_ref, place_ref)

    def fetch(part):
        return (two_later(shift_ref[...], query_ref[:, lanes_of(part, WIDE)]),)

    def convolve(part, earlier):
        here = lanes_of(part, WIDE)
        weights = taps_of(weight_ref, 0, here)
        gate_ref[:, here] = wide_conv(query_ref[:, here], earlier, weights)
        head = query_ref[0:16, here].astype(F32)[:8]
        gate_ref[0:8, here] = short_conv(head, before[0, :, here], weights)

    pipelined(width // WIDE, fetch, convolve)


def local_kernel(
    gate_ref,
    residual_ref,
    product_ref,
    first_ref,
    mode_rate_ref,
    inner_ref,
    entering_ref,
    skip_ref,
    base_ref,
):
    rows, width = product_ref.shape
    mask = group_mask(BF16)
    top = index_of((8, LANES), 0) < 2
    chunks = range(rows // CHUNK)

    def inside(tile):
        here = lanes_of(tile)
        pieces = []
        for chunk in chunks:
            piece = product_ref[chunk * CHUNK : (chunk + 1) * CHUNK, here]
            if chunk == 0:
                wide = piece.astype(F32)
                head = jnp.where(top, first_ref[:, here], wide[:8])
                piece = jnp.concatenate([head, wide[8:]], axis=0).astype(BF16)
            pieces.append(piece)
        found = []
        for pair in chunks[::2]:
            sources = jnp.concatenate([spread(pieces[pair + k], mask) for k in (0, 1)], axis=1)
            found.append(jnp.dot(inner_ref[tile], sources, preferred_element_type=F32))
        return found, pieces[0]

    def across(tile, inner, first):
        decay = jnp.exp(-float(CHUNK) * mode_rate_ref[:, lanes_of(tile)])
        state = jnp.zeros((MODES, LANES), F32)
        states = []
        for chunk in chunks:
            states.append(spread(state.astype(BF16), mask))
            state = decay * state + inner[chunk // 2][CHUNK:, lanes_of(chunk % 2)]
        outer = []
        for pair in chunks[::2]:
            two = jnp.concatenate(states[pair : pair + 2], axis=1)
            outer.append(jnp.dot(entering_ref[tile], two, preferred_element_type=F32))
        return [part[:CHUNK] for part in inner], outer, first

    def finish(tile, inner, outer, first):
        here = lanes_of(tile)
        skip = skip_ref[:, here]
        for chunk in chunks:
            span = slice(chunk * CHUNK, (chunk + 1) * CHUNK)
            piece = first if chunk == 0 else product_ref[span, here]
            conv = (inner[chunk // 2] + outer[chunk // 2])[:, lanes_of(chunk % 2)]
            whole = conv + skip * piece.astype(F32)
            base_ref[span, here] = residual_ref[span, here].astype(F32) + gate_ref[span, here] * whole

    pipelined(width // LANES, inside, across, finish)


def join_kernel(tokens, radix, stride, place_ref, own_ref, mode_rate_ref, entry_ref, *refs):
    others, (found_ref, group_ref) = refs[: radix - 1], refs[radix - 1 :]
    rate = mode_rate_ref[...]
    run = lax.rem(place_ref[0] // stride, radix)
    step = float(tokens * stride)

    def decayed(value, runs):
        return jnp.exp(-step * runs.astype(F32) * rate) * value

    found = jnp.zeros_like(rate)
    total = decayed(own_ref[...].astype(F32), radix - 1 - run)
    for k, ref in enumerate(others, 1):
        other = ref[...].astype(F32)
        source = partner(run, k, radix)
        found = found + jnp.where(source < run, decayed(other, jnp.maximum(run - 1 - source, 0)), 0.0)
        total = total + decayed(other, radix - 1 - source)
    within = lax.rem(place_ref[0], stride).astype(F32) * float(tokens)
    found_ref[...] = entry_ref[...] + jnp.exp(-within * rate) * found
    group_ref[...] = total.astype(BF16)


def carry_kernel(stride, radix, place_ref, base_ref, gate_ref, carry_ref, mode_rate_ref, inner_entry_ref, *refs):
    entry_refs, (summed_ref, squares_ref) = refs[:-2], refs[-2:]
    rows, width = base_ref.shape
    run = place_ref[0] // stride
    within = lax.rem(place_ref[0], stride).astype(F32) * float(rows)
    mask = group_mask(BF16)
    totals = [jnp.zeros((rows, LANES), F32)]
    nothing = jnp.zeros((LANES, LANES), BF16)

    def enter(tile):
        here = lanes_of(tile, WIDE)
        rate = mode_rate_ref[:, here]
        step = float(rows * stride)
        outer = jnp.zeros_like(rate)
        for k, ref in enumerate(entry_refs[::-1], 1):
            source = partner(run, k, radix)
            lag = jnp.maximum(run - 1 - source, 0).astype(F32) * step
            outer = outer + jnp.where(source < run, jnp.exp(-lag * rate) * ref[:, here].astype(F32), 0.0)
        entry = (inner_entry_ref[:, here] + jnp.exp(-within * rate) * outer).astype(BF16)
        left, right = spread(entry[:, :LANES], mask), spread(entry[:, LANES:], mask)
        both = jnp.concatenate(
            [jnp.concatenate([left, nothing], axis=1), jnp.concatenate([nothing, right], axis=1)], axis=0
        )
        return (jnp.dot(carry_ref[tile], both, preferred_element_type=F32),)

    def add(tile, carry):
        here = lanes_of(tile, WIDE)
        summed = base_ref[:, here] + gate_ref[:, here] * carry
        summed_ref[:, here] = summed
        square = summed * summed
        totals[0] = totals[0] + (square[:, :LANES] + square[:, LANES:])

    pipelined(width // WIDE, enter, add)
    total = totals[0]
    squares = lax.dot_general(
        jnp.ones((8, 2 * LANES), BF16),
        jnp.concatenate(split(total), axis=1),
        (((1,), (1,)), ((), ())),
        preferred_element_type=F32,
    )
    squares_ref[...] = squares[0:1]


def write_kernel(summed_ref, out_hbm, rounded_ref, sems):
    width = summed_ref.shape[1]
    copies = []
    for tile in range(width // WIDE):
        here = lanes_of(tile, WIDE)
        rounded_ref[:, here] = summed_ref[:, here].astype(BF16)
        span = pl.ds(tile * WIDE, WIDE)
        copies.append(pltpu.make_async_copy(rounded_ref.at[:, span], out_hbm.at[:, span], sems.at[tile]))
        copies[-1].start()
    for copy in copies:
        copy.wait()


def norm_kernel(full_width, summed_ref, gain_ref, *refs):
    squares_refs, (out_hbm, rounded_ref, sems) = refs[:-3], refs[-3:]
    rows, width = summed_ref.shape
    squares = squares_refs[0][...]
    for ref in squares_refs[1:]:
        squares = squares + ref[...]
    scale_row = lax.rsqrt(squares / full_width + 1e-05)
    scale = jnp.concatenate([as_column(scale_row[:, lanes_of(k)]) for k in range(rows // LANES)], axis=0)
    copies = []
    block = rows // 8
    for start in range(0, rows, block):
        span = slice(start, start + block)
        for tile in range(width // LANES):
            here = lanes_of(tile)
            rounded_ref[span, here] = (summed_ref[span, here] * scale[span] * gain_ref[:, here]).astype(BF16)
        there = pl.ds(start, block)
        copies.append(pltpu.make_async_copy(rounded_ref.at[there, :], out_hbm.at[there, :], sems.at[start // block]))
        copies[-1].start()
    for copy in copies:
        copy.wait()


def params():
    return pltpu.CompilerParams(vmem_limit_bytes=VMEM_LIMIT)


def cost(microseconds):
    return pl.CostEstimate(flops=0, bytes_accessed=int(microseconds * 3.0e6), transcendentals=0)


def radices(count):
    found = []
    for radix in (2, 4, 4, 4, 3, 2, 5, 7):
        if count % radix == 0:
            found.append(radix)
            count //= radix
    return found + ([count] if count > 1 else [])


def partner(run, k, radix):
    if radix & (radix - 1) == 0:
        return run ^ k
    return (run - k + radix) % radix


def routes(count, stride, radix):
    found = []
    for k in range(1, radix):
        route = []
        for i in range(count):
            run = i // stride % radix
            route.append((i + (partner(run, k, radix) - run) * stride, i))
        found.append(route)
    return found


def ring(count, shift):
    return [(i, (i + shift) % count) for i in range(count)]


def per_device(projected, short_weight, rates, residues, skip, residual, gain):
    rows, width = projected.shape[1:]
    taps = short_weight.shape[0]
    peers = lax.axis_size("ctx")
    full_width = width * lax.axis_size("fsdp")
    place = lax.axis_index("ctx").astype(jnp.int32).reshape(1)
    hbm_spec = pl.BlockSpec(memory_space=pltpu.HBM)
    vmem_spec = pl.BlockSpec(memory_space=pltpu.VMEM)
    smem_spec = pl.BlockSpec(memory_space=pltpu.SMEM)
    tiles = width // LANES
    wides = width // WIDE

    def kept(array):
        return pltpu.with_memory_space_constraint(array, pltpu.HBM)

    def f32(*shape):
        return jax.ShapeDtypeStruct(shape, F32)

    def bf16(*shape):
        return jax.ShapeDtypeStruct(shape, BF16)

    before = lax.ppermute(projected[:, rows - (taps - 1) :, :], "ctx", ring(peers, 1))

    product, state, mode_rate, head, weights, query, residue, residual_here = pl.pallas_call(
        state_kernel,
        in_specs=[hbm_spec] * 5,
        out_shape=[
            bf16(rows, width),
            f32(MODES, width),
            f32(MODES, width),
            f32(3, 8, width),
            f32(*short_weight.shape),
            bf16(rows, width),
            f32(MODES, residues.shape[0]),
            bf16(rows, width),
        ],
        scratch_shapes=[
            pltpu.VMEM((2, rows, width), BF16),
            pltpu.VMEM((wides, WIDE, rows // 2), BF16),
            pltpu.VMEM((rows, rows), BF16),
            pltpu.VMEM(short_weight.shape, BF16),
            pltpu.VMEM((MODES, rates.shape[0]), F32),
            pltpu.SemaphoreType.DMA((7,)),
            pltpu.SemaphoreType.DMA((2,)),
        ],
        compiler_params=params(),
        cost_estimate=cost(3),
        name="block_state",
    )(kept(projected), kept(short_weight), kept(rates.T), kept(residues.T), kept(residual))

    full_state, first = pl.pallas_call(
        lambda *refs: head_kernel(rows, *refs),
        in_specs=[smem_spec] + [vmem_spec] * 5,
        out_shape=[bf16(MODES, width), f32(8, width)],
        compiler_params=params(),
        cost_estimate=cost(0.2),
        name="head_tokens",
    )(place, before, head, weights, state, mode_rate)

    inner, entering, carry_table, gate = pl.pallas_call(
        prepare_kernel,
        in_specs=[smem_spec] + [vmem_spec] * 5,
        out_shape=[
            bf16(tiles, CHUNK + MODES, GROUPS * CHUNK),
            bf16(tiles, CHUNK, LANES),
            bf16(wides, rows, WIDE),
            f32(rows, width),
        ],
        scratch_shapes=[pltpu.VMEM((rows, rows), BF16)],
        compiler_params=params(),
        cost_estimate=cost(2),
        name="prepare",
    )(place, query, residue, before, weights, mode_rate)

    group, entry, stride = full_state, jnp.zeros((MODES, width), F32), 1
    levels = radices(peers)
    for level, radix in enumerate(levels):
        size = stride * radix
        if level == len(levels) - 1:
            break
        others = [lax.ppermute(group, "ctx", route) for route in routes(peers, stride, radix)]
        if level == 0:
            others[0], inner = lax.optimization_barrier((others[0], inner))
        entry, group = pl.pallas_call(
            lambda *refs, radix=radix, stride=stride: join_kernel(rows, radix, stride, *refs),
            in_specs=[smem_spec] + [vmem_spec] * (2 + radix),
            out_shape=[f32(MODES, width), bf16(MODES, width)],
            compiler_params=params(),
            cost_estimate=cost(0.2),
            name="join",
        )(place, group, mode_rate, entry, *others)
        stride = size
    received = [lax.ppermute(group, "ctx", route) for route in routes(peers, stride, levels[-1])[::-1]]

    base = pl.pallas_call(
        local_kernel,
        out_shape=f32(rows, width),
        compiler_params=params(),
        cost_estimate=cost(5),
        name="local_conv",
    )(gate, residual_here, product, first, mode_rate, inner, entering, skip[None])

    count = lax.axis_size("fsdp")
    summed, squares = pl.pallas_call(
        lambda *refs: carry_kernel(stride, levels[-1], *refs),
        in_specs=[smem_spec] + [vmem_spec] * (5 + len(received)),
        out_shape=[f32(rows, width), f32(1, rows)],
        compiler_params=params(),
        cost_estimate=cost(1),
        name="add_carry",
    )(place, base, gate, carry_table, mode_rate, entry, *received)

    parts = [lax.ppermute(squares, "fsdp", route) for route in routes(count, 1, count)[::-1]]

    def write(kernel, operands, name):
        return pl.pallas_call(
            kernel,
            out_specs=hbm_spec,
            out_shape=bf16(rows, width),
            scratch_shapes=[pltpu.VMEM((rows, width), BF16), pltpu.SemaphoreType.DMA((max(8, wides),))],
            compiler_params=params(),
            cost_estimate=cost(1),
            name=name,
        )(*operands)

    new_residual = write(write_kernel, (summed,), "new_residual")
    normed = write(
        lambda *refs: norm_kernel(full_width, *refs), (summed, gain[None], squares, *parts), "normed"
    )
    return (new_residual, normed)


def solution(mesh):
    return jax.shard_map(
        per_device,
        mesh=mesh,
        in_specs=(
            P(None, "ctx", "fsdp"),
            P(None, None, "fsdp"),
            P("fsdp", None),
            P("fsdp", None),
            P("fsdp"),
            P("ctx", "fsdp"),
            P("fsdp"),
        ),
        out_specs=(P("ctx", "fsdp"), P("ctx", "fsdp")),
        check_vma=False,
    )
```

```python
import jax
import jax.numpy as jnp
from jax import lax
from jax.experimental import pallas as pl
from jax.experimental.pallas import tpu as pltpu
from jax.sharding import PartitionSpec as P

CHANNELS_PER_GRP = 16
MODES = 16
CHUNK = 32
LANES = 128
WIDE = 256
GROUPS = LANES // CHANNELS_PER_GRP
VMEM_LIMIT = 16 * 1024 * 1024
F32 = jnp.float32
BF16 = jnp.bfloat16


def index_of(shape, dim):
    return lax.broadcasted_iota(jnp.int32, shape, dim)


def pipelined(count, *stages):
    held = {}
    for step in range(count + len(stages) - 1):
        for k, stage in enumerate(stages):
            item = step - k
            if 0 <= item < count:
                held[item] = stage(item, *held.get(item, ()))


def lanes_of(tile, width=LANES):
    return slice(tile * width, (tile + 1) * width)


def per_channel(table):
    groups = table.shape[1]
    width = groups * CHANNELS_PER_GRP
    high = table.astype(BF16)
    rest = table - high.astype(F32)
    middle = rest.astype(BF16)
    low = (rest - middle.astype(F32)).astype(BF16)
    terms = jnp.concatenate([high, middle, low], axis=0)
    parts = []
    for tile in range(width // WIDE):
        shape = (groups, WIDE)
        own = index_of(shape, 0) == index_of(shape, 1) // CHANNELS_PER_GRP + tile * (WIDE // CHANNELS_PER_GRP)
        three = jnp.dot(terms, jnp.where(own, 1.0, 0.0).astype(BF16), preferred_element_type=F32)
        parts.append(three[:MODES] + three[MODES : 2 * MODES] + three[2 * MODES :])
    return jnp.concatenate(parts, axis=1)


def mode_row(channel_table):
    own = index_of(channel_table.shape, 0) == (index_of(channel_table.shape, 1) & (MODES - 1))
    return jnp.sum(jnp.where(own, channel_table, 0.0), axis=0, keepdims=True)


def as_column(row):
    return jnp.transpose(jnp.broadcast_to(row, (LANES, LANES)))


def own_mode(dtype):
    shape = (GROUPS, MODES, LANES)
    own = index_of(shape, 0) * MODES + index_of(shape, 1) == index_of(shape, 2)
    return jnp.where(own, 1.0, 0.0).astype(dtype)


def split(x):
    high = x.astype(BF16)
    return high, (x - high.astype(F32)).astype(BF16)


def group_mask(dtype):
    shape = (GROUPS, MODES, LANES)
    own = index_of(shape, 0) == index_of(shape, 2) // CHANNELS_PER_GRP
    return jnp.where(own, 1.0, 0.0).astype(dtype)


def spread(rows, mask):
    size = rows.shape[0]
    copies = rows.reshape(1, size // MODES, MODES, LANES) * mask.reshape(GROUPS, 1, MODES, LANES)
    return copies.reshape(GROUPS * size, LANES)


def shifted(block, before):
    one = pltpu.roll(block, 1, 0)
    two = pltpu.roll(block, 2, 0)
    first = index_of((8, block.shape[1]), 0)
    near, far = (0.0, 0.0) if before is None else (before[1:2], before[0:1])
    head_one = jnp.where(first == 0, near, one[:8])
    head_two = jnp.where(first == 0, far, jnp.where(first == 1, near, two[:8]))
    if block.shape[0] == 8:
        return head_one, head_two
    return jnp.concatenate([head_one, one[8:]], axis=0), jnp.concatenate([head_two, two[8:]], axis=0)


def short_conv(block, before, weights):
    one, two = shifted(block, before)
    return weights[0] * block + weights[1] * one + weights[2] * two


def shift_matrix(rows):
    shape = (2 * rows, rows)
    target = index_of(shape, 0)
    source = index_of(shape, 1)
    taken = jnp.where(target < rows, target - 1, target - (rows + 2))
    return jnp.where(source == taken, 1.0, 0.0).astype(BF16)


def earlier_tokens(shift, block):
    return jnp.dot(shift, block, preferred_element_type=F32)


def wide_conv(block, earlier, weights):
    rows = block.shape[0]
    return weights[0] * block.astype(F32) + weights[1] * earlier[:rows] + weights[2] * earlier[rows:]


def taps_of(weights, feature, lanes):
    return [weights[tap, feature : feature + 1, lanes] for tap in range(weights.shape[0])]


def state_kernel(
    projected_ref,
    weight_hbm,
    rate_hbm,
    residue_hbm,
    residual_hbm,
    product_ref,
    swapped_ref,
    mode_rate_ref,
    tail_ref,
    weight_ref,
    query_ref,
    residue_ref,
    residual_ref,
    buffer_ref,
    ending_ref,
    shift_ref,
    short_ref,
    rate_ref,
    sems,
    small_sems,
):
    rows, width = product_ref.shape
    wides = width // WIDE
    rate_copy = pltpu.make_async_copy(rate_hbm, rate_ref, small_sems.at[0])
    rate_copy.start()
    weight_copy = pltpu.make_async_copy(weight_hbm, short_ref, small_sems.at[1])
    weight_copy.start()
    copies = [pltpu.make_async_copy(projected_ref.at[1 + c], buffer_ref.at[c], sems.at[c]) for c in (0, 1)]
    later = [
        pltpu.make_async_copy(residue_hbm, residue_ref, sems.at[2]),
        pltpu.make_async_copy(projected_ref.at[0], query_ref, sems.at[3]),
        pltpu.make_async_copy(residual_hbm, residual_ref, sems.at[4]),
    ]
    for copy in copies:
        copy.start()
    shift_ref[...] = shift_matrix(rows)
    rate_copy.wait()
    mode_rate = per_channel(rate_ref[...])
    mode_rate_ref[...] = mode_rate
    eye = own_mode(BF16)
    token = index_of((2 * LANES, rows), 1)
    left = jnp.where(token < 2, -1e30, (token - (rows - 1)).astype(F32)).astype(BF16)

    def exponents(tile):
        high, low = split(mode_rate[:, lanes_of(tile)])
        diagonal = jnp.concatenate([spread(high, eye), spread(low, eye)], axis=1)
        return (jnp.dot(diagonal, left, preferred_element_type=F32),)

    def endings(tile, exponent):
        ending_ref[tile // 2, lanes_of(tile % 2), :] = jnp.exp(exponent).astype(BF16)

    pipelined(width // LANES, exponents, endings)
    weight_copy.wait()
    weights = short_ref[...].astype(F32)
    weight_ref[...] = weights
    mask = group_mask(F32)
    for copy in copies:
        copy.wait()
    for copy in later:
        copy.start()

    def fetch(wide):
        return [earlier_tokens(shift_ref[...], buffer_ref[c, :, lanes_of(wide, WIDE)]) for c in (0, 1)]

    def multiply(wide, *earlier):
        here = lanes_of(wide, WIDE)
        parts = []
        for c in (0, 1):
            parts.append(wide_conv(buffer_ref[c, :, here], earlier[c], taps_of(weights, c + 1, here)))
        product = (parts[0] * parts[1]).astype(BF16)
        product_ref[:, here] = product
        return (jnp.dot(ending_ref[wide], product, preferred_element_type=F32),)

    def leave(wide, every):
        for half in range(WIDE // LANES):
            own = every[lanes_of(half), lanes_of(half)].reshape(GROUPS, MODES, LANES)
            there = lanes_of((WIDE // LANES) * wide + half)
            swapped_ref[:MODES, there] = jnp.sum(own * mask, axis=0).astype(BF16)

    pipelined(wides, fetch, multiply, leave)
    heads = [buffer_ref[c, 0:16, :].astype(F32)[:8] for c in (0, 1)]
    swapped_ref[MODES:, :] = jnp.concatenate(heads, axis=0).astype(BF16)
    for copy in later:
        copy.wait()
    for c, ref in enumerate((query_ref, buffer_ref.at[0], buffer_ref.at[1])):
        tail_ref[c] = ref[rows - 16 : rows, :].astype(F32)[14:].astype(BF16)


def pair_kernel(
    tokens,
    place_ref,
    got_ref,
    before_ref,
    skipped_ref,
    own_ref,
    tail_ref,
    query_ref,
    weight_ref,
    mode_rate_ref,
    entry_ref,
    group_ref,
    first_ref,
    gate_ref,
):
    odd = lax.rem(place_ref[0], 2) == 1
    before = jnp.where(place_ref[0] > 0, before_ref[...].astype(F32), 0.0)
    skipped = jnp.where(place_ref[0] > 1, skipped_ref[...].astype(F32), 0.0)
    own, got = own_ref[...].astype(F32), got_ref[...].astype(F32)
    everything = slice(0, own.shape[1])
    rate = mode_rate_ref[...]
    blocks = (
        (jnp.where(odd, got, own), jnp.where(odd, skipped, before)),
        (jnp.where(odd, own, got), jnp.where(odd, before, tail_ref[...].astype(F32))),
    )
    states, firsts = [], []
    for block, halo in blocks:
        heads = (block[MODES : MODES + 8], block[MODES + 8 :])
        parts = [short_conv(heads[c], halo[c + 1], taps_of(weight_ref, c + 1, everything)) for c in (0, 1)]
        first = (parts[0] * parts[1]).astype(BF16).astype(F32)
        early = jnp.exp(-float(tokens - 1) * rate) * first[0:1] + jnp.exp(-float(tokens - 2) * rate) * first[1:2]
        states.append(block[:MODES] + early)
        firsts.append(first)
    entry_ref[...] = jnp.where(odd, states[0], 0.0)
    group_ref[...] = (jnp.exp(-float(tokens) * rate) * states[0] + states[1]).astype(BF16)
    first_ref[...] = jnp.where(odd, firsts[1], firsts[0])
    query = query_ref[0:16, :].astype(F32)[:8]
    gate_ref[...] = short_conv(query, before[0], taps_of(weight_ref, 0, everything))


def prepare_kernel(
    query_ref,
    residue_ref,
    weight_ref,
    mode_rate_ref,
    inner_ref,
    entering_ref,
    carry_ref,
    gate_ref,
    shift_ref,
):
    rows, width = gate_ref.shape
    shift_ref[...] = shift_matrix(rows)
    residue = per_channel(residue_ref[...])
    wide = GROUPS * CHUNK
    step = index_of((CHUNK, LANES), 0).astype(F32)
    causal = (index_of((CHUNK, wide), 1) & (CHUNK - 1)) <= index_of((CHUNK, wide), 0)
    eye = own_mode(BF16)
    flat_eye = jnp.where((index_of((MODES, LANES), 1) & (MODES - 1)) == index_of((MODES, LANES), 0), 1.0, 0.0)
    flat_eye = flat_eye.astype(BF16)
    shape = (2 * LANES, wide)
    source = (index_of(shape, 1) & (CHUNK - 1)).astype(F32)
    own = (index_of(shape, 0) & (LANES - 1)) // MODES == index_of(shape, 1) // CHUNK
    own_chunk = jnp.where(own[:LANES], 1.0, 0.0).astype(BF16)
    risen = source[:, :LANES].astype(BF16)
    left = jnp.where(own, source - (CHUNK - 1), 0.0).astype(BF16)

    def exponents(tile):
        rate = mode_rate_ref[:, lanes_of(tile)]
        high, low = split(rate)
        diagonal = jnp.concatenate([spread(high, eye), spread(low, eye)], axis=1)
        each = jnp.concatenate([high * flat_eye, low * flat_eye], axis=1)
        return (
            jnp.dot(diagonal, risen, preferred_element_type=F32),
            jnp.dot(each, left, preferred_element_type=F32),
        )

    def products(tile, rise, end):
        here = lanes_of(tile)
        rise_high, rise_low = [
            jnp.concatenate([part] * (wide // LANES), axis=1) * own_chunk for part in split(jnp.exp(rise))
        ]
        rate_row = mode_row(mode_rate_ref[:, here])
        falling = mode_row(residue[:, here]) * jnp.exp(-rate_row * step)
        fall_high, fall_low = split(falling)
        half = tile % (WIDE // LANES)
        for chunk in range(rows // CHUNK):
            entering = (falling * jnp.exp(-float(CHUNK * chunk + 1) * rate_row)).astype(BF16)
            carry_ref[tile // (WIDE // LANES), chunk * CHUNK : (chunk + 1) * CHUNK, lanes_of(half)] = entering
            if chunk == 0:
                entering_ref[tile] = entering
        return (
            jnp.dot(jnp.concatenate([fall_high, fall_low], axis=0), rise_high, preferred_element_type=F32),
            jnp.dot(fall_high, rise_low, preferred_element_type=F32),
            jnp.exp(end),
        )

    def finish(tile, taps, rest, ending):
        taps = jnp.where(causal, taps[:CHUNK] + taps[CHUNK:] + rest, 0.0)
        inner_ref[tile] = jnp.concatenate([taps.astype(BF16), ending.astype(BF16)], axis=0)

    pipelined(width // LANES, exponents, products, finish)

    def fetch(part):
        return (earlier_tokens(shift_ref[...], query_ref[:, lanes_of(part, WIDE)]),)

    def convolve(part, earlier):
        here = lanes_of(part, WIDE)
        weights = taps_of(weight_ref, 0, here)
        gate_ref[:, here] = wide_conv(query_ref[:, here], earlier, weights)

    pipelined(width // WIDE, fetch, convolve)


def with_head(block, head):
    return jnp.concatenate([head, block[head.shape[0] :]], axis=0)


def local_kernel(
    gate_ref,
    gate_head_ref,
    residual_ref,
    product_ref,
    first_ref,
    mode_rate_ref,
    inner_ref,
    entering_ref,
    skip_ref,
    base_ref,
):
    rows, width = product_ref.shape
    mask = group_mask(BF16)
    top = index_of((8, LANES), 0) < 2
    chunks = range(rows // CHUNK)

    def inside(tile):
        here = lanes_of(tile)
        pieces = []
        for chunk in chunks:
            piece = product_ref[chunk * CHUNK : (chunk + 1) * CHUNK, here]
            if chunk == 0:
                wide = piece.astype(F32)
                head = jnp.where(top, first_ref[:, here], wide[:8])
                piece = jnp.concatenate([head, wide[8:]], axis=0).astype(BF16)
            pieces.append(piece)
        found = []
        for pair in chunks[::2]:
            sources = jnp.concatenate([spread(pieces[pair + k], mask) for k in (0, 1)], axis=1)
            found.append(jnp.dot(inner_ref[tile], sources, preferred_element_type=F32))
        return found, pieces[0]

    def across(tile, inner, first):
        decay = jnp.exp(-float(CHUNK) * mode_rate_ref[:, lanes_of(tile)])
        state = jnp.zeros((MODES, LANES), F32)
        states = []
        for chunk in chunks:
            states.append(spread(state.astype(BF16), mask))
            state = decay * state + inner[chunk // 2][CHUNK:, lanes_of(chunk % 2)]
        outer = []
        for pair in chunks[::2]:
            two = jnp.concatenate(states[pair : pair + 2], axis=1)
            outer.append(jnp.dot(entering_ref[tile], two, preferred_element_type=F32))
        return [part[:CHUNK] for part in inner], outer, first

    def finish(tile, inner, outer, first):
        here = lanes_of(tile)
        skip = skip_ref[:, here]
        for chunk in chunks:
            span = slice(chunk * CHUNK, (chunk + 1) * CHUNK)
            piece = first if chunk == 0 else product_ref[span, here]
            conv = (inner[chunk // 2] + outer[chunk // 2])[:, lanes_of(chunk % 2)]
            whole = conv + skip * piece.astype(F32)
            gate = gate_ref[span, here]
            if chunk == 0:
                gate = with_head(gate, gate_head_ref[:, here])
            base_ref[span, here] = residual_ref[span, here].astype(F32) + gate * whole

    pipelined(width // LANES, inside, across, finish)


def join_kernel(tokens, radix, stride, place_ref, own_ref, mode_rate_ref, entry_ref, *refs):
    others, (found_ref, group_ref) = refs[: radix - 1], refs[radix - 1 :]
    rate = mode_rate_ref[...]
    run = lax.rem(place_ref[0] // stride, radix)
    step = float(tokens * stride)

    def decayed(value, runs):
        return jnp.exp(-step * runs.astype(F32) * rate) * value

    found = jnp.zeros_like(rate)
    total = decayed(own_ref[...].astype(F32), radix - 1 - run)
    for k, ref in enumerate(others, 1):
        other = ref[...].astype(F32)
        source = partner(run, k, radix)
        found = found + jnp.where(source < run, decayed(other, jnp.maximum(run - 1 - source, 0)), 0.0)
        total = total + decayed(other, radix - 1 - source)
    within = lax.rem(place_ref[0], stride).astype(F32) * float(tokens)
    found_ref[...] = entry_ref[...] + jnp.exp(-within * rate) * found
    group_ref[...] = total.astype(BF16)


def carry_kernel(
    stride, radix, place_ref, base_ref, gate_ref, gate_head_ref, carry_ref, mode_rate_ref, inner_entry_ref, *refs
):
    entry_refs, (summed_ref, squares_ref) = refs[:-2], refs[-2:]
    rows, width = base_ref.shape
    run = place_ref[0] // stride
    within = lax.rem(place_ref[0], stride).astype(F32) * float(rows)
    mask = group_mask(BF16)
    totals = [jnp.zeros((rows, LANES), F32)]
    nothing = jnp.zeros((LANES, LANES), BF16)

    def enter(tile):
        here = lanes_of(tile, WIDE)
        rate = mode_rate_ref[:, here]
        step = float(rows * stride)
        outer = jnp.zeros_like(rate)
        for k, ref in enumerate(entry_refs[::-1], 1):
            source = partner(run, k, radix)
            lag = jnp.maximum(run - 1 - source, 0).astype(F32) * step
            outer = outer + jnp.where(source < run, jnp.exp(-lag * rate) * ref[:, here].astype(F32), 0.0)
        entry = (inner_entry_ref[:, here] + jnp.exp(-within * rate) * outer).astype(BF16)
        left, right = spread(entry[:, :LANES], mask), spread(entry[:, LANES:], mask)
        both = jnp.concatenate(
            [jnp.concatenate([left, nothing], axis=1), jnp.concatenate([nothing, right], axis=1)], axis=0
        )
        return (jnp.dot(carry_ref[tile], both, preferred_element_type=F32),)

    def add(tile, carry):
        here = lanes_of(tile, WIDE)
        summed = base_ref[:, here] + with_head(gate_ref[:, here], gate_head_ref[:, here]) * carry
        summed_ref[:, here] = summed
        square = summed * summed
        totals[0] = totals[0] + (square[:, :LANES] + square[:, LANES:])

    pipelined(width // WIDE, enter, add)
    total = totals[0]
    squares = lax.dot_general(
        jnp.ones((8, 2 * LANES), BF16),
        jnp.concatenate(split(total), axis=1),
        (((1,), (1,)), ((), ())),
        preferred_element_type=F32,
    )
    squares_ref[...] = squares[0:1]


def write_kernel(summed_ref, out_hbm, rounded_ref, sems):
    width = summed_ref.shape[1]
    copies = []
    for tile in range(width // WIDE):
        here = lanes_of(tile, WIDE)
        rounded_ref[:, here] = summed_ref[:, here].astype(BF16)
        span = pl.ds(tile * WIDE, WIDE)
        copies.append(pltpu.make_async_copy(rounded_ref.at[:, span], out_hbm.at[:, span], sems.at[tile]))
        copies[-1].start()
    for copy in copies:
        copy.wait()


def norm_kernel(full_width, summed_ref, gain_ref, *refs):
    squares_refs, (out_hbm, rounded_ref, sems) = refs[:-3], refs[-3:]
    rows, width = summed_ref.shape
    squares = squares_refs[0][...]
    for ref in squares_refs[1:]:
        squares = squares + ref[...]
    scale_row = lax.rsqrt(squares / full_width + 1e-05)
    scale = jnp.concatenate([as_column(scale_row[:, lanes_of(k)]) for k in range(rows // LANES)], axis=0)
    copies = []
    block = rows // 8
    for start in range(0, rows, block):
        span = slice(start, start + block)
        for tile in range(width // LANES):
            here = lanes_of(tile)
            rounded_ref[span, here] = (summed_ref[span, here] * scale[span] * gain_ref[:, here]).astype(BF16)
        there = pl.ds(start, block)
        copies.append(pltpu.make_async_copy(rounded_ref.at[there, :], out_hbm.at[there, :], sems.at[start // block]))
        copies[-1].start()
    for copy in copies:
        copy.wait()


def params():
    return pltpu.CompilerParams(vmem_limit_bytes=VMEM_LIMIT)


def cost(microseconds):
    return pl.CostEstimate(flops=0, bytes_accessed=int(microseconds * 3.0e6), transcendentals=0)


def radices(count):
    found = []
    for radix in (2, 4, 4, 4, 3, 2, 5, 7):
        if count % radix == 0:
            found.append(radix)
            count //= radix
    return found + ([count] if count > 1 else [])


def partner(run, k, radix):
    if radix & (radix - 1) == 0:
        return run ^ k
    return (run - k + radix) % radix


def routes(count, stride, radix):
    found = []
    for k in range(1, radix):
        route = []
        for i in range(count):
            run = i // stride % radix
            route.append((i + (partner(run, k, radix) - run) * stride, i))
        found.append(route)
    return found


def ring(count, shift):
    return [(i, (i + shift) % count) for i in range(count)]


def per_device(projected, short_weight, rates, residues, skip, residual, gain):
    rows, width = projected.shape[1:]
    taps = short_weight.shape[0]
    peers = lax.axis_size("ctx")
    full_width = width * lax.axis_size("fsdp")
    place = lax.axis_index("ctx").astype(jnp.int32).reshape(1)
    hbm_spec = pl.BlockSpec(memory_space=pltpu.HBM)
    vmem_spec = pl.BlockSpec(memory_space=pltpu.VMEM)
    smem_spec = pl.BlockSpec(memory_space=pltpu.SMEM)
    tiles = width // LANES
    wides = width // WIDE

    def kept(array):
        return pltpu.with_memory_space_constraint(array, pltpu.HBM)

    def f32(*shape):
        return jax.ShapeDtypeStruct(shape, F32)

    def bf16(*shape):
        return jax.ShapeDtypeStruct(shape, BF16)

    product, swapped, mode_rate, tail, weights, query, residue, residual_here = pl.pallas_call(
        state_kernel,
        in_specs=[hbm_spec] * 5,
        out_shape=[
            bf16(rows, width),
            bf16(2 * MODES, width),
            f32(MODES, width),
            bf16(3, taps - 1, width),
            f32(*short_weight.shape),
            bf16(rows, width),
            f32(MODES, residues.shape[0]),
            bf16(rows, width),
        ],
        scratch_shapes=[
            pltpu.VMEM((2, rows, width), BF16),
            pltpu.VMEM((wides, WIDE, rows), BF16),
            pltpu.VMEM((2 * rows, rows), BF16),
            pltpu.VMEM(short_weight.shape, BF16),
            pltpu.VMEM((MODES, rates.shape[0]), F32),
            pltpu.SemaphoreType.DMA((5,)),
            pltpu.SemaphoreType.DMA((2,)),
        ],
        compiler_params=params(),
        cost_estimate=cost(3),
        name="block_state",
    )(kept(projected), kept(short_weight), kept(rates.T), kept(residues.T), kept(residual))

    levels = radices(peers)
    got = lax.ppermute(swapped, "ctx", routes(peers, 1, levels[0])[0])
    before = lax.ppermute(tail, "ctx", ring(peers, 1))
    skipped = lax.ppermute(tail, "ctx", ring(peers, 2))

    inner, entering, carry_table, gate = pl.pallas_call(
        prepare_kernel,
        in_specs=[vmem_spec] * 4,
        out_shape=[
            bf16(tiles, CHUNK + MODES, GROUPS * CHUNK),
            bf16(tiles, CHUNK, LANES),
            bf16(wides, rows, WIDE),
            f32(rows, width),
        ],
        scratch_shapes=[pltpu.VMEM((2 * rows, rows), BF16)],
        compiler_params=params(),
        cost_estimate=cost(2),
        name="prepare",
    )(query, residue, weights, mode_rate)

    got, inner = lax.optimization_barrier((got, inner))
    entry, group, first, gate_head = pl.pallas_call(
        lambda *refs: pair_kernel(rows, *refs),
        in_specs=[smem_spec] + [vmem_spec] * 8,
        out_shape=[f32(MODES, width), bf16(MODES, width), f32(8, width), f32(8, width)],
        compiler_params=params(),
        cost_estimate=cost(0.2),
        name="pair",
    )(place, got, before, skipped, swapped, tail, query, weights, mode_rate)

    stride = levels[0]
    for radix in levels[1:-1]:
        others = [lax.ppermute(group, "ctx", route) for route in routes(peers, stride, radix)]
        entry, group = pl.pallas_call(
            lambda *refs, radix=radix, stride=stride: join_kernel(rows, radix, stride, *refs),
            in_specs=[smem_spec] + [vmem_spec] * (2 + radix),
            out_shape=[f32(MODES, width), bf16(MODES, width)],
            compiler_params=params(),
            cost_estimate=cost(0.2),
            name="join",
        )(place, group, mode_rate, entry, *others)
        stride *= radix
    received = [lax.ppermute(group, "ctx", route) for route in routes(peers, stride, levels[-1])[::-1]]

    base = pl.pallas_call(
        local_kernel,
        out_shape=f32(rows, width),
        compiler_params=params(),
        cost_estimate=cost(5),
        name="local_conv",
    )(gate, gate_head, residual_here, product, first, mode_rate, inner, entering, skip[None])

    count = lax.axis_size("fsdp")
    summed, squares = pl.pallas_call(
        lambda *refs: carry_kernel(stride, levels[-1], *refs),
        in_specs=[smem_spec] + [vmem_spec] * (6 + len(received)),
        out_shape=[f32(rows, width), f32(1, rows)],
        compiler_params=params(),
        cost_estimate=cost(1),
        name="add_carry",
    )(place, base, gate, gate_head, carry_table, mode_rate, entry, *received)

    parts = [lax.ppermute(squares, "fsdp", route) for route in routes(count, 1, count)[::-1]]

    def write(kernel, operands, name):
        return pl.pallas_call(
            kernel,
            out_specs=hbm_spec,
            out_shape=bf16(rows, width),
            scratch_shapes=[pltpu.VMEM((rows, width), BF16), pltpu.SemaphoreType.DMA((max(8, wides),))],
            compiler_params=params(),
            cost_estimate=cost(1),
            name=name,
        )(*operands)

    new_residual = write(write_kernel, (summed,), "new_residual")
    normed = write(
        lambda *refs: norm_kernel(full_width, *refs), (summed, gain[None], squares, *parts), "normed"
    )
    return (new_residual, normed)


def solution(mesh):
    return jax.shard_map(
        per_device,
        mesh=mesh,
        in_specs=(
            P(None, "ctx", "fsdp"),
            P(None, None, "fsdp"),
            P("fsdp", None),
            P("fsdp", None),
            P("fsdp"),
            P("ctx", "fsdp"),
            P("fsdp"),
        ),
        out_specs=(P("ctx", "fsdp"), P("ctx", "fsdp")),
        check_vma=False,
    )
```

```python
import jax
import jax.numpy as jnp
from jax import lax
from jax.experimental import pallas as pl
from jax.experimental.pallas import tpu as pltpu
from jax.sharding import PartitionSpec as P

CHANNELS_PER_GRP = 16
MODES = 16
CHUNK = 32
LANES = 128
WIDE = 256
GROUPS = LANES // CHANNELS_PER_GRP
VMEM_LIMIT = 16 * 1024 * 1024
F32 = jnp.float32
BF16 = jnp.bfloat16


def index_of(shape, dim):
    return lax.broadcasted_iota(jnp.int32, shape, dim)


def pipelined(count, *stages):
    held = {}
    for step in range(count + len(stages) - 1):
        for k, stage in enumerate(stages):
            item = step - k
            if 0 <= item < count:
                held[item] = stage(item, *held.get(item, ()))


def lanes_of(tile, width=LANES):
    return slice(tile * width, (tile + 1) * width)


def per_channel(table):
    groups = table.shape[1]
    width = groups * CHANNELS_PER_GRP
    high = table.astype(BF16)
    rest = table - high.astype(F32)
    middle = rest.astype(BF16)
    low = (rest - middle.astype(F32)).astype(BF16)
    terms = jnp.concatenate([high, middle, low], axis=0)
    parts = []
    for tile in range(width // WIDE):
        shape = (groups, WIDE)
        own = index_of(shape, 0) == index_of(shape, 1) // CHANNELS_PER_GRP + tile * (WIDE // CHANNELS_PER_GRP)
        three = jnp.dot(terms, jnp.where(own, 1.0, 0.0).astype(BF16), preferred_element_type=F32)
        parts.append(three[:MODES] + three[MODES : 2 * MODES] + three[2 * MODES :])
    return jnp.concatenate(parts, axis=1)


def mode_row(channel_table):
    own = index_of(channel_table.shape, 0) == (index_of(channel_table.shape, 1) & (MODES - 1))
    return jnp.sum(jnp.where(own, channel_table, 0.0), axis=0, keepdims=True)


def as_column(row):
    return jnp.transpose(jnp.broadcast_to(row, (LANES, LANES)))


def own_mode(dtype):
    shape = (GROUPS, MODES, LANES)
    own = index_of(shape, 0) * MODES + index_of(shape, 1) == index_of(shape, 2)
    return jnp.where(own, 1.0, 0.0).astype(dtype)


def split(x):
    high = x.astype(BF16)
    return high, (x - high.astype(F32)).astype(BF16)


def group_mask(dtype):
    shape = (GROUPS, MODES, LANES)
    own = index_of(shape, 0) == index_of(shape, 2) // CHANNELS_PER_GRP
    return jnp.where(own, 1.0, 0.0).astype(dtype)


def spread(rows, mask):
    size = rows.shape[0]
    copies = rows.reshape(1, size // MODES, MODES, LANES) * mask.reshape(GROUPS, 1, MODES, LANES)
    return copies.reshape(GROUPS * size, LANES)


def shifted(block, before):
    one = pltpu.roll(block, 1, 0)
    two = pltpu.roll(block, 2, 0)
    first = index_of((8, block.shape[1]), 0)
    near, far = (0.0, 0.0) if before is None else (before[1:2], before[0:1])
    head_one = jnp.where(first == 0, near, one[:8])
    head_two = jnp.where(first == 0, far, jnp.where(first == 1, near, two[:8]))
    if block.shape[0] == 8:
        return head_one, head_two
    return jnp.concatenate([head_one, one[8:]], axis=0), jnp.concatenate([head_two, two[8:]], axis=0)


def short_conv(block, before, weights):
    one, two = shifted(block, before)
    return weights[0] * block + weights[1] * one + weights[2] * two


def shift_matrix(rows):
    shape = (2 * rows, rows)
    target = index_of(shape, 0)
    source = index_of(shape, 1)
    taken = jnp.where(target < rows, target - 1, target - (rows + 2))
    return jnp.where(source == taken, 1.0, 0.0).astype(BF16)


def earlier_tokens(shift, block):
    return jnp.dot(shift, block, preferred_element_type=F32)


def wide_conv(block, earlier, weights):
    rows = block.shape[0]
    return weights[0] * block.astype(F32) + weights[1] * earlier[:rows] + weights[2] * earlier[rows:]


def taps_of(weights, feature, lanes):
    return [weights[tap, feature : feature + 1, lanes] for tap in range(weights.shape[0])]


def state_kernel(
    projected_ref,
    weight_hbm,
    rate_hbm,
    residue_hbm,
    residual_hbm,
    product_ref,
    state_ref,
    mode_rate_ref,
    head_ref,
    weight_ref,
    query_ref,
    residue_ref,
    residual_ref,
    buffer_ref,
    shift_ref,
    short_ref,
    rate_ref,
    sems,
    small_sems,
):
    rows, width = product_ref.shape
    wides = width // WIDE
    rate_copy = pltpu.make_async_copy(rate_hbm, rate_ref, small_sems.at[0])
    rate_copy.start()
    weight_copy = pltpu.make_async_copy(weight_hbm, short_ref, small_sems.at[1])
    weight_copy.start()
    part = width // 2
    copies = [
        pltpu.make_async_copy(
            projected_ref.at[1 + c, :, pl.ds(side * part, part)],
            buffer_ref.at[c, :, pl.ds(side * part, part)],
            sems.at[2 * side + c],
        )
        for side in (0, 1)
        for c in (0, 1)
    ]
    later = [
        pltpu.make_async_copy(residue_hbm, residue_ref, sems.at[4]),
        pltpu.make_async_copy(projected_ref.at[0], query_ref, sems.at[5]),
        pltpu.make_async_copy(residual_hbm, residual_ref, sems.at[6]),
    ]
    for copy in copies:
        copy.start()
    shift_ref[...] = shift_matrix(rows)
    rate_copy.wait()
    mode_rate = per_channel(rate_ref[...])
    mode_rate_ref[...] = mode_rate
    eye = own_mode(BF16)
    token = index_of((2 * LANES, rows), 1)
    left = jnp.where(token < 2, -1e30, (token - (rows - 1)).astype(F32)).astype(BF16)
    weight_copy.wait()
    weights = short_ref[...].astype(F32)
    weight_ref[...] = weights
    mask = group_mask(F32)

    def fetch(wide):
        if wide % (wides // 2) == 0:
            first = 2 * (wide // (wides // 2))
            for copy in copies[first : first + 2]:
                copy.wait()
            if first == 0:
                for copy in later:
                    copy.start()
        exponents = []
        for half in range(WIDE // LANES):
            high, low = split(mode_rate[:, lanes_of((WIDE // LANES) * wide + half)])
            diagonal = jnp.concatenate([spread(high, eye), spread(low, eye)], axis=1)
            exponents.append(jnp.dot(diagonal, left, preferred_element_type=F32))
        earlier = [earlier_tokens(shift_ref[...], buffer_ref[c, :, lanes_of(wide, WIDE)]) for c in (0, 1)]
        return exponents + earlier

    def multiply(wide, *found):
        here = lanes_of(wide, WIDE)
        ending = jnp.concatenate([jnp.exp(exponent).astype(BF16) for exponent in found[:-2]], axis=0)
        parts = []
        for c in (0, 1):
            head_ref[c, :, here] = buffer_ref[c, 0:16, here].astype(F32)[:8]
            parts.append(wide_conv(buffer_ref[c, :, here], found[c - 2], taps_of(weights, c + 1, here)))
        product = (parts[0] * parts[1]).astype(BF16)
        product_ref[:, here] = product
        return (jnp.dot(ending, product, preferred_element_type=F32),)

    def leave(wide, every):
        for half in range(WIDE // LANES):
            own = every[lanes_of(half), lanes_of(half)].reshape(GROUPS, MODES, LANES)
            state_ref[:, lanes_of((WIDE // LANES) * wide + half)] = jnp.sum(own * mask, axis=0)

    pipelined(wides, fetch, multiply, leave)
    for copy in later:
        copy.wait()


def halo(before_ref, place_ref):
    return jnp.where(place_ref[0] > 0, before_ref[...].astype(F32), 0.0)


def head_kernel(rows, place_ref, before_ref, head_ref, weight_ref, state_ref, mode_rate_ref, full_ref, first_ref):
    before = halo(before_ref, place_ref)
    everything = slice(0, head_ref.shape[2])
    parts = [short_conv(head_ref[c], before[c + 1], taps_of(weight_ref, c + 1, everything)) for c in (0, 1)]
    first = (parts[0] * parts[1]).astype(BF16).astype(F32)
    first_ref[...] = first
    rate = mode_rate_ref[...]
    early = jnp.exp(-float(rows - 1) * rate) * first[0:1] + jnp.exp(-float(rows - 2) * rate) * first[1:2]
    full_ref[...] = (state_ref[...] + early).astype(BF16)


def prepare_kernel(
    place_ref,
    query_ref,
    residue_ref,
    before_ref,
    weight_ref,
    mode_rate_ref,
    inner_ref,
    entering_ref,
    carry_ref,
    gate_ref,
    shift_ref,
):
    rows, width = gate_ref.shape
    shift_ref[...] = shift_matrix(rows)
    residue = per_channel(residue_ref[...])
    wide = GROUPS * CHUNK
    step = index_of((CHUNK, LANES), 0).astype(F32)
    causal = (index_of((CHUNK, wide), 1) & (CHUNK - 1)) <= index_of((CHUNK, wide), 0)
    eye = own_mode(BF16)
    flat_eye = jnp.where((index_of((MODES, LANES), 1) & (MODES - 1)) == index_of((MODES, LANES), 0), 1.0, 0.0)
    flat_eye = flat_eye.astype(BF16)
    shape = (2 * LANES, wide)
    source = (index_of(shape, 1) & (CHUNK - 1)).astype(F32)
    own = (index_of(shape, 0) & (LANES - 1)) // MODES == index_of(shape, 1) // CHUNK
    own_chunk = jnp.where(own[:LANES], 1.0, 0.0).astype(BF16)
    risen = source[:, :LANES].astype(BF16)
    left = jnp.where(own, source - (CHUNK - 1), 0.0).astype(BF16)

    def exponents(tile):
        rate = mode_rate_ref[:, lanes_of(tile)]
        high, low = split(rate)
        diagonal = jnp.concatenate([spread(high, eye), spread(low, eye)], axis=1)
        each = jnp.concatenate([high * flat_eye, low * flat_eye], axis=1)
        return (
            jnp.dot(diagonal, risen, preferred_element_type=F32),
            jnp.dot(each, left, preferred_element_type=F32),
        )

    def products(tile, rise, end):
        here = lanes_of(tile)
        rise_high, rise_low = [
            jnp.concatenate([part] * (wide // LANES), axis=1) * own_chunk for part in split(jnp.exp(rise))
        ]
        rate_row = mode_row(mode_rate_ref[:, here])
        falling = mode_row(residue[:, here]) * jnp.exp(-rate_row * step)
        fall_high, fall_low = split(falling)
        half = tile % (WIDE // LANES)
        for chunk in range(rows // CHUNK):
            entering = (falling * jnp.exp(-float(CHUNK * chunk + 1) * rate_row)).astype(BF16)
            carry_ref[tile // (WIDE // LANES), chunk * CHUNK : (chunk + 1) * CHUNK, lanes_of(half)] = entering
            if chunk == 0:
                entering_ref[tile] = entering
        return (
            jnp.dot(jnp.concatenate([fall_high, fall_low], axis=0), rise_high, preferred_element_type=F32),
            jnp.dot(fall_high, rise_low, preferred_element_type=F32),
            jnp.exp(end),
        )

    def finish(tile, taps, rest, ending):
        taps = jnp.where(causal, taps[:CHUNK] + taps[CHUNK:] + rest, 0.0)
        inner_ref[tile] = jnp.concatenate([taps.astype(BF16), ending.astype(BF16)], axis=0)

    pipelined(width // LANES, exponents, products, finish)
    before = halo(before_ref, place_ref)

    def fetch(part):
        return (earlier_tokens(shift_ref[...], query_ref[:, lanes_of(part, WIDE)]),)

    def convolve(part, earlier):
        here = lanes_of(part, WIDE)
        weights = taps_of(weight_ref, 0, here)
        gate_ref[:, here] = wide_conv(query_ref[:, here], earlier, weights)
        head = query_ref[0:16, here].astype(F32)[:8]
        gate_ref[0:8, here] = short_conv(head, before[0, :, here], weights)

    pipelined(width // WIDE, fetch, convolve)


def local_kernel(
    gate_ref,
    residual_ref,
    product_ref,
    first_ref,
    mode_rate_ref,
    inner_ref,
    entering_ref,
    skip_ref,
    base_ref,
):
    rows, width = product_ref.shape
    mask = group_mask(BF16)
    top = index_of((8, LANES), 0) < 2
    chunks = range(rows // CHUNK)

    def inside(tile):
        here = lanes_of(tile)
        pieces = []
        for chunk in chunks:
            piece = product_ref[chunk * CHUNK : (chunk + 1) * CHUNK, here]
            if chunk == 0:
                wide = piece.astype(F32)
                head = jnp.where(top, first_ref[:, here], wide[:8])
                piece = jnp.concatenate([head, wide[8:]], axis=0).astype(BF16)
            pieces.append(piece)
        found = []
        for pair in chunks[::2]:
            sources = jnp.concatenate([spread(pieces[pair + k], mask) for k in (0, 1)], axis=1)
            found.append(jnp.dot(inner_ref[tile], sources, preferred_element_type=F32))
        return found, pieces[0]

    def across(tile, inner, first):
        decay = jnp.exp(-float(CHUNK) * mode_rate_ref[:, lanes_of(tile)])
        state = jnp.zeros((MODES, LANES), F32)
        states = []
        for chunk in chunks:
            states.append(spread(state.astype(BF16), mask))
            state = decay * state + inner[chunk // 2][CHUNK:, lanes_of(chunk % 2)]
        outer = []
        for pair in chunks[::2]:
            two = jnp.concatenate(states[pair : pair + 2], axis=1)
            outer.append(jnp.dot(entering_ref[tile], two, preferred_element_type=F32))
        return [part[:CHUNK] for part in inner], outer, first

    def finish(tile, inner, outer, first):
        here = lanes_of(tile)
        skip = skip_ref[:, here]
        for chunk in chunks:
            span = slice(chunk * CHUNK, (chunk + 1) * CHUNK)
            piece = first if chunk == 0 else product_ref[span, here]
            conv = (inner[chunk // 2] + outer[chunk // 2])[:, lanes_of(chunk % 2)]
            whole = conv + skip * piece.astype(F32)
            base_ref[span, here] = residual_ref[span, here].astype(F32) + gate_ref[span, here] * whole

    pipelined(width // LANES, inside, across, finish)


def join_kernel(tokens, radix, stride, place_ref, own_ref, mode_rate_ref, entry_ref, *refs):
    others, (found_ref, group_ref) = refs[: radix - 1], refs[radix - 1 :]
    rate = mode_rate_ref[...]
    run = lax.rem(place_ref[0] // stride, radix)
    step = float(tokens * stride)

    def decayed(value, runs):
        return jnp.exp(-step * runs.astype(F32) * rate) * value

    found = jnp.zeros_like(rate)
    total = decayed(own_ref[...].astype(F32), radix - 1 - run)
    for k, ref in enumerate(others, 1):
        other = ref[...].astype(F32)
        source = partner(run, k, radix)
        found = found + jnp.where(source < run, decayed(other, jnp.maximum(run - 1 - source, 0)), 0.0)
        total = total + decayed(other, radix - 1 - source)
    within = lax.rem(place_ref[0], stride).astype(F32) * float(tokens)
    found_ref[...] = entry_ref[...] + jnp.exp(-within * rate) * found
    group_ref[...] = total.astype(BF16)


def carry_kernel(stride, radix, place_ref, base_ref, gate_ref, carry_ref, mode_rate_ref, inner_entry_ref, *refs):
    entry_refs, (summed_ref, squares_ref) = refs[:-2], refs[-2:]
    rows, width = base_ref.shape
    run = place_ref[0] // stride
    within = lax.rem(place_ref[0], stride).astype(F32) * float(rows)
    mask = group_mask(BF16)
    totals = [jnp.zeros((rows, LANES), F32)]
    nothing = jnp.zeros((LANES, LANES), BF16)

    def enter(tile):
        here = lanes_of(tile, WIDE)
        rate = mode_rate_ref[:, here]
        step = float(rows * stride)
        outer = jnp.zeros_like(rate)
        for k, ref in enumerate(entry_refs[::-1], 1):
            source = partner(run, k, radix)
            lag = jnp.maximum(run - 1 - source, 0).astype(F32) * step
            outer = outer + jnp.where(source < run, jnp.exp(-lag * rate) * ref[:, here].astype(F32), 0.0)
        entry = (inner_entry_ref[:, here] + jnp.exp(-within * rate) * outer).astype(BF16)
        left, right = spread(entry[:, :LANES], mask), spread(entry[:, LANES:], mask)
        both = jnp.concatenate(
            [jnp.concatenate([left, nothing], axis=1), jnp.concatenate([nothing, right], axis=1)], axis=0
        )
        return (jnp.dot(carry_ref[tile], both, preferred_element_type=F32),)

    def add(tile, carry):
        here = lanes_of(tile, WIDE)
        summed = base_ref[:, here] + gate_ref[:, here] * carry
        summed_ref[:, here] = summed
        square = summed * summed
        totals[0] = totals[0] + (square[:, :LANES] + square[:, LANES:])

    pipelined(width // WIDE, enter, add)
    total = totals[0]
    squares = lax.dot_general(
        jnp.ones((8, 2 * LANES), BF16),
        jnp.concatenate(split(total), axis=1),
        (((1,), (1,)), ((), ())),
        preferred_element_type=F32,
    )
    squares_ref[...] = squares[0:1]


def write_kernel(summed_ref, out_hbm, rounded_ref, sems):
    width = summed_ref.shape[1]
    copies = []
    for tile in range(width // WIDE):
        here = lanes_of(tile, WIDE)
        rounded_ref[:, here] = summed_ref[:, here].astype(BF16)
        span = pl.ds(tile * WIDE, WIDE)
        copies.append(pltpu.make_async_copy(rounded_ref.at[:, span], out_hbm.at[:, span], sems.at[tile]))
        copies[-1].start()
    for copy in copies:
        copy.wait()


def norm_kernel(full_width, summed_ref, gain_ref, *refs):
    squares_refs, (out_hbm, rounded_ref, sems) = refs[:-3], refs[-3:]
    rows, width = summed_ref.shape
    squares = squares_refs[0][...]
    for ref in squares_refs[1:]:
        squares = squares + ref[...]
    scale_row = lax.rsqrt(squares / full_width + 1e-05)
    scale = jnp.concatenate([as_column(scale_row[:, lanes_of(k)]) for k in range(rows // LANES)], axis=0)
    copies = []
    block = rows // 8
    for start in range(0, rows, block):
        span = slice(start, start + block)
        for tile in range(width // LANES):
            here = lanes_of(tile)
            rounded_ref[span, here] = (summed_ref[span, here] * scale[span] * gain_ref[:, here]).astype(BF16)
        there = pl.ds(start, block)
        copies.append(pltpu.make_async_copy(rounded_ref.at[there, :], out_hbm.at[there, :], sems.at[start // block]))
        copies[-1].start()
    for copy in copies:
        copy.wait()


def params():
    return pltpu.CompilerParams(vmem_limit_bytes=VMEM_LIMIT)


def cost(microseconds):
    return pl.CostEstimate(flops=0, bytes_accessed=int(microseconds * 3.0e6), transcendentals=0)


def radices(count):
    found = []
    for radix in (2, 4, 4, 4, 3, 2, 5, 7):
        if count % radix == 0:
            found.append(radix)
            count //= radix
    return found + ([count] if count > 1 else [])


def partner(run, k, radix):
    if radix & (radix - 1) == 0:
        return run ^ k
    return (run - k + radix) % radix


def routes(count, stride, radix):
    found = []
    for k in range(1, radix):
        route = []
        for i in range(count):
            run = i // stride % radix
            route.append((i + (partner(run, k, radix) - run) * stride, i))
        found.append(route)
    return found


def ring(count, shift):
    return [(i, (i + shift) % count) for i in range(count)]


def per_device(projected, short_weight, rates, residues, skip, residual, gain):
    rows, width = projected.shape[1:]
    taps = short_weight.shape[0]
    peers = lax.axis_size("ctx")
    full_width = width * lax.axis_size("fsdp")
    place = lax.axis_index("ctx").astype(jnp.int32).reshape(1)
    hbm_spec = pl.BlockSpec(memory_space=pltpu.HBM)
    vmem_spec = pl.BlockSpec(memory_space=pltpu.VMEM)
    smem_spec = pl.BlockSpec(memory_space=pltpu.SMEM)
    tiles = width // LANES
    wides = width // WIDE

    def kept(array):
        return pltpu.with_memory_space_constraint(array, pltpu.HBM)

    def f32(*shape):
        return jax.ShapeDtypeStruct(shape, F32)

    def bf16(*shape):
        return jax.ShapeDtypeStruct(shape, BF16)

    before = lax.ppermute(projected[:, rows - (taps - 1) :, :], "ctx", ring(peers, 1))

    product, state, mode_rate, head, weights, query, residue, residual_here = pl.pallas_call(
        state_kernel,
        in_specs=[hbm_spec] * 5,
        out_shape=[
            bf16(rows, width),
            f32(MODES, width),
            f32(MODES, width),
            f32(2, 8, width),
            f32(*short_weight.shape),
            bf16(rows, width),
            f32(MODES, residues.shape[0]),
            bf16(rows, width),
        ],
        scratch_shapes=[
            pltpu.VMEM((2, rows, width), BF16),
            pltpu.VMEM((2 * rows, rows), BF16),
            pltpu.VMEM(short_weight.shape, BF16),
            pltpu.VMEM((MODES, rates.shape[0]), F32),
            pltpu.SemaphoreType.DMA((7,)),
            pltpu.SemaphoreType.DMA((2,)),
        ],
        compiler_params=params(),
        cost_estimate=cost(3),
        name="block_state",
    )(kept(projected), kept(short_weight), kept(rates.T), kept(residues.T), kept(residual))

    full_state, first = pl.pallas_call(
        lambda *refs: head_kernel(rows, *refs),
        in_specs=[smem_spec] + [vmem_spec] * 5,
        out_shape=[bf16(MODES, width), f32(8, width)],
        compiler_params=params(),
        cost_estimate=cost(0.2),
        name="head_tokens",
    )(place, before, head, weights, state, mode_rate)

    inner, entering, carry_table, gate = pl.pallas_call(
        prepare_kernel,
        in_specs=[smem_spec] + [vmem_spec] * 5,
        out_shape=[
            bf16(tiles, CHUNK + MODES, GROUPS * CHUNK),
            bf16(tiles, CHUNK, LANES),
            bf16(wides, rows, WIDE),
            f32(rows, width),
        ],
        scratch_shapes=[pltpu.VMEM((2 * rows, rows), BF16)],
        compiler_params=params(),
        cost_estimate=cost(2),
        name="prepare",
    )(place, query, residue, before, weights, mode_rate)

    group, entry, stride = full_state, jnp.zeros((MODES, width), F32), 1
    levels = radices(peers)
    for level, radix in enumerate(levels):
        size = stride * radix
        if level == len(levels) - 1:
            break
        others = [lax.ppermute(group, "ctx", route) for route in routes(peers, stride, radix)]
        if level == 0:
            others[0], inner = lax.optimization_barrier((others[0], inner))
        entry, group = pl.pallas_call(
            lambda *refs, radix=radix, stride=stride: join_kernel(rows, radix, stride, *refs),
            in_specs=[smem_spec] + [vmem_spec] * (2 + radix),
            out_shape=[f32(MODES, width), bf16(MODES, width)],
            compiler_params=params(),
            cost_estimate=cost(0.2),
            name="join",
        )(place, group, mode_rate, entry, *others)
        stride = size
    received = [lax.ppermute(group, "ctx", route) for route in routes(peers, stride, levels[-1])[::-1]]

    base = pl.pallas_call(
        local_kernel,
        out_shape=f32(rows, width),
        compiler_params=params(),
        cost_estimate=cost(5),
        name="local_conv",
    )(gate, residual_here, product, first, mode_rate, inner, entering, skip[None])

    count = lax.axis_size("fsdp")
    summed, squares = pl.pallas_call(
        lambda *refs: carry_kernel(stride, levels[-1], *refs),
        in_specs=[smem_spec] + [vmem_spec] * (5 + len(received)),
        out_shape=[f32(rows, width), f32(1, rows)],
        compiler_params=params(),
        cost_estimate=cost(1),
        name="add_carry",
    )(place, base, gate, carry_table, mode_rate, entry, *received)

    parts = [lax.ppermute(squares, "fsdp", route) for route in routes(count, 1, count)[::-1]]

    def write(kernel, operands, name):
        return pl.pallas_call(
            kernel,
            out_specs=hbm_spec,
            out_shape=bf16(rows, width),
            scratch_shapes=[pltpu.VMEM((rows, width), BF16), pltpu.SemaphoreType.DMA((max(8, wides),))],
            compiler_params=params(),
            cost_estimate=cost(1),
            name=name,
        )(*operands)

    new_residual = write(write_kernel, (summed,), "new_residual")
    normed = write(
        lambda *refs: norm_kernel(full_width, *refs), (summed, gain[None], squares, *parts), "normed"
    )
    return (new_residual, normed)


def solution(mesh):
    return jax.shard_map(
        per_device,
        mesh=mesh,
        in_specs=(
            P(None, "ctx", "fsdp"),
            P(None, None, "fsdp"),
            P("fsdp", None),
            P("fsdp", None),
            P("fsdp"),
            P("ctx", "fsdp"),
            P("fsdp"),
        ),
        out_specs=(P("ctx", "fsdp"), P("ctx", "fsdp")),
        check_vma=False,
    )
```

```python
import jax
import jax.numpy as jnp
from jax import lax
from jax.experimental import pallas as pl
from jax.experimental.pallas import tpu as pltpu
from jax.sharding import PartitionSpec as P

CHANNELS_PER_GRP = 16
MODES = 16
CHUNK = 32
LANES = 128
WIDE = 256
GROUPS = LANES // CHANNELS_PER_GRP
VMEM_LIMIT = 16 * 1024 * 1024
F32 = jnp.float32
BF16 = jnp.bfloat16


def index_of(shape, dim):
    return lax.broadcasted_iota(jnp.int32, shape, dim)


def pipelined(count, *stages):
    held = {}
    for step in range(count + len(stages) - 1):
        for k, stage in enumerate(stages):
            item = step - k
            if 0 <= item < count:
                held[item] = stage(item, *held.get(item, ()))


def lanes_of(tile, width=LANES):
    return slice(tile * width, (tile + 1) * width)


def per_channel(table):
    groups = table.shape[1]
    width = groups * CHANNELS_PER_GRP
    high = table.astype(BF16)
    rest = table - high.astype(F32)
    middle = rest.astype(BF16)
    low = (rest - middle.astype(F32)).astype(BF16)
    terms = jnp.concatenate([high, middle, low], axis=0)
    parts = []
    for tile in range(width // WIDE):
        shape = (groups, WIDE)
        own = index_of(shape, 0) == index_of(shape, 1) // CHANNELS_PER_GRP + tile * (WIDE // CHANNELS_PER_GRP)
        three = jnp.dot(terms, jnp.where(own, 1.0, 0.0).astype(BF16), preferred_element_type=F32)
        parts.append(three[:MODES] + three[MODES : 2 * MODES] + three[2 * MODES :])
    return jnp.concatenate(parts, axis=1)


def mode_row(channel_table):
    own = index_of(channel_table.shape, 0) == (index_of(channel_table.shape, 1) & (MODES - 1))
    return jnp.sum(jnp.where(own, channel_table, 0.0), axis=0, keepdims=True)


def as_column(row):
    return jnp.transpose(jnp.broadcast_to(row, (LANES, LANES)))


def own_mode(dtype):
    shape = (GROUPS, MODES, LANES)
    own = index_of(shape, 0) * MODES + index_of(shape, 1) == index_of(shape, 2)
    return jnp.where(own, 1.0, 0.0).astype(dtype)


def split(x):
    high = x.astype(BF16)
    return high, (x - high.astype(F32)).astype(BF16)


def group_mask(dtype):
    shape = (GROUPS, MODES, LANES)
    own = index_of(shape, 0) == index_of(shape, 2) // CHANNELS_PER_GRP
    return jnp.where(own, 1.0, 0.0).astype(dtype)


def spread(rows, mask):
    size = rows.shape[0]
    copies = rows.reshape(1, size // MODES, MODES, LANES) * mask.reshape(GROUPS, 1, MODES, LANES)
    return copies.reshape(GROUPS * size, LANES)


def shifted(block, before):
    one = pltpu.roll(block, 1, 0)
    two = pltpu.roll(block, 2, 0)
    first = index_of((8, block.shape[1]), 0)
    near, far = (0.0, 0.0) if before is None else (before[1:2], before[0:1])
    head_one = jnp.where(first == 0, near, one[:8])
    head_two = jnp.where(first == 0, far, jnp.where(first == 1, near, two[:8]))
    if block.shape[0] == 8:
        return head_one, head_two
    return jnp.concatenate([head_one, one[8:]], axis=0), jnp.concatenate([head_two, two[8:]], axis=0)


def short_conv(block, before, weights):
    one, two = shifted(block, before)
    return weights[0] * block + weights[1] * one + weights[2] * two


def shift_matrix(rows):
    shape = (2 * rows, rows)
    target = index_of(shape, 0)
    source = index_of(shape, 1)
    taken = jnp.where(target < rows, target - 1, target - (rows + 2))
    return jnp.where(source == taken, 1.0, 0.0).astype(BF16)


def earlier_tokens(shift, block):
    return jnp.dot(shift, block, preferred_element_type=F32)


def wide_conv(block, earlier, weights):
    rows = block.shape[0]
    return weights[0] * block.astype(F32) + weights[1] * earlier[:rows] + weights[2] * earlier[rows:]


def taps_of(weights, feature, lanes):
    return [weights[tap, feature : feature + 1, lanes] for tap in range(weights.shape[0])]


def state_kernel(
    projected_ref,
    weight_hbm,
    rate_hbm,
    residue_hbm,
    product_ref,
    state_ref,
    mode_rate_ref,
    head_ref,
    weight_ref,
    residue_ref,
    buffer_ref,
    shift_ref,
    short_ref,
    rate_ref,
    sems,
    small_sems,
):
    rows, width = product_ref.shape
    wides = width // WIDE
    rate_copy = pltpu.make_async_copy(rate_hbm, rate_ref, small_sems.at[0])
    rate_copy.start()
    weight_copy = pltpu.make_async_copy(weight_hbm, short_ref, small_sems.at[1])
    weight_copy.start()
    part = width // 2
    copies = [
        pltpu.make_async_copy(
            projected_ref.at[1 + c, :, pl.ds(side * part, part)],
            buffer_ref.at[c, :, pl.ds(side * part, part)],
            sems.at[2 * side + c],
        )
        for side in (0, 1)
        for c in (0, 1)
    ]
    residue_copy = pltpu.make_async_copy(residue_hbm, residue_ref, sems.at[4])
    for copy in copies:
        copy.start()
    residue_copy.start()
    shift_ref[...] = shift_matrix(rows)
    rate_copy.wait()
    mode_rate = per_channel(rate_ref[...])
    mode_rate_ref[...] = mode_rate
    eye = own_mode(BF16)
    token = index_of((2 * LANES, rows), 1)
    left = jnp.where(token < 2, -1e30, (token - (rows - 1)).astype(F32)).astype(BF16)
    weight_copy.wait()
    weights = short_ref[...].astype(F32)
    weight_ref[...] = weights
    mask = group_mask(F32)

    def fetch(wide):
        if wide % (wides // 2) == 0:
            first = 2 * (wide // (wides // 2))
            for copy in copies[first : first + 2]:
                copy.wait()
        exponents = []
        for half in range(WIDE // LANES):
            high, low = split(mode_rate[:, lanes_of((WIDE // LANES) * wide + half)])
            diagonal = jnp.concatenate([spread(high, eye), spread(low, eye)], axis=1)
            exponents.append(jnp.dot(diagonal, left, preferred_element_type=F32))
        earlier = [earlier_tokens(shift_ref[...], buffer_ref[c, :, lanes_of(wide, WIDE)]) for c in (0, 1)]
        return exponents + earlier

    def multiply(wide, *found):
        here = lanes_of(wide, WIDE)
        ending = jnp.concatenate([jnp.exp(exponent).astype(BF16) for exponent in found[:-2]], axis=0)
        parts = []
        for c in (0, 1):
            head_ref[c, :, here] = buffer_ref[c, 0:16, here].astype(F32)[:8]
            parts.append(wide_conv(buffer_ref[c, :, here], found[c - 2], taps_of(weights, c + 1, here)))
        product = (parts[0] * parts[1]).astype(BF16)
        product_ref[:, here] = product
        return (jnp.dot(ending, product, preferred_element_type=F32),)

    def leave(wide, every):
        for half in range(WIDE // LANES):
            own = every[lanes_of(half), lanes_of(half)].reshape(GROUPS, MODES, LANES)
            state_ref[:, lanes_of((WIDE // LANES) * wide + half)] = jnp.sum(own * mask, axis=0)

    pipelined(wides, fetch, multiply, leave)
    residue_copy.wait()


def halo(before_ref, place_ref):
    return jnp.where(place_ref[0] > 0, before_ref[...].astype(F32), 0.0)


def head_kernel(rows, place_ref, before_ref, head_ref, weight_ref, state_ref, mode_rate_ref, full_ref, first_ref):
    before = halo(before_ref, place_ref)
    everything = slice(0, head_ref.shape[2])
    parts = [short_conv(head_ref[c], before[c + 1], taps_of(weight_ref, c + 1, everything)) for c in (0, 1)]
    first = (parts[0] * parts[1]).astype(BF16).astype(F32)
    first_ref[...] = first
    rate = mode_rate_ref[...]
    early = jnp.exp(-float(rows - 1) * rate) * first[0:1] + jnp.exp(-float(rows - 2) * rate) * first[1:2]
    full_ref[...] = (state_ref[...] + early).astype(BF16)


def prepare_kernel(
    place_ref,
    projected_ref,
    residual_hbm,
    residue_ref,
    before_ref,
    weight_ref,
    mode_rate_ref,
    inner_ref,
    entering_ref,
    carry_ref,
    gate_ref,
    residual_ref,
    query_ref,
    shift_ref,
    sems,
):
    rows, width = gate_ref.shape
    query_copy = pltpu.make_async_copy(projected_ref.at[0], query_ref, sems.at[0])
    query_copy.start()
    residual_copy = pltpu.make_async_copy(residual_hbm, residual_ref, sems.at[1])
    residual_copy.start()
    shift_ref[...] = shift_matrix(rows)
    residue = per_channel(residue_ref[...])
    wide = GROUPS * CHUNK
    step = index_of((CHUNK, LANES), 0).astype(F32)
    causal = (index_of((CHUNK, wide), 1) & (CHUNK - 1)) <= index_of((CHUNK, wide), 0)
    eye = own_mode(BF16)
    flat_eye = jnp.where((index_of((MODES, LANES), 1) & (MODES - 1)) == index_of((MODES, LANES), 0), 1.0, 0.0)
    flat_eye = flat_eye.astype(BF16)
    shape = (2 * LANES, wide)
    source = (index_of(shape, 1) & (CHUNK - 1)).astype(F32)
    own = (index_of(shape, 0) & (LANES - 1)) // MODES == index_of(shape, 1) // CHUNK
    own_chunk = jnp.where(own[:LANES], 1.0, 0.0).astype(BF16)
    risen = source[:, :LANES].astype(BF16)
    left = jnp.where(own, source - (CHUNK - 1), 0.0).astype(BF16)

    def exponents(tile):
        rate = mode_rate_ref[:, lanes_of(tile)]
        high, low = split(rate)
        diagonal = jnp.concatenate([spread(high, eye), spread(low, eye)], axis=1)
        each = jnp.concatenate([high * flat_eye, low * flat_eye], axis=1)
        return (
            jnp.dot(diagonal, risen, preferred_element_type=F32),
            jnp.dot(each, left, preferred_element_type=F32),
        )

    def products(tile, rise, end):
        here = lanes_of(tile)
        rise_high, rise_low = [
            jnp.concatenate([part] * (wide // LANES), axis=1) * own_chunk for part in split(jnp.exp(rise))
        ]
        rate_row = mode_row(mode_rate_ref[:, here])
        falling = mode_row(residue[:, here]) * jnp.exp(-rate_row * step)
        fall_high, fall_low = split(falling)
        half = tile % (WIDE // LANES)
        for chunk in range(rows // CHUNK):
            entering = (falling * jnp.exp(-float(CHUNK * chunk + 1) * rate_row)).astype(BF16)
            carry_ref[tile // (WIDE // LANES), chunk * CHUNK : (chunk + 1) * CHUNK, lanes_of(half)] = entering
            if chunk == 0:
                entering_ref[tile] = entering
        return (
            jnp.dot(jnp.concatenate([fall_high, fall_low], axis=0), rise_high, preferred_element_type=F32),
            jnp.dot(fall_high, rise_low, preferred_element_type=F32),
            jnp.exp(end),
        )

    def finish(tile, taps, rest, ending):
        taps = jnp.where(causal, taps[:CHUNK] + taps[CHUNK:] + rest, 0.0)
        inner_ref[tile] = jnp.concatenate([taps.astype(BF16), ending.astype(BF16)], axis=0)

    pipelined(width // LANES, exponents, products, finish)
    before = halo(before_ref, place_ref)
    query_copy.wait()

    def fetch(part):
        return (earlier_tokens(shift_ref[...], query_ref[:, lanes_of(part, WIDE)]),)

    def convolve(part, earlier):
        here = lanes_of(part, WIDE)
        weights = taps_of(weight_ref, 0, here)
        gate_ref[:, here] = wide_conv(query_ref[:, here], earlier, weights)
        head = query_ref[0:16, here].astype(F32)[:8]
        gate_ref[0:8, here] = short_conv(head, before[0, :, here], weights)

    pipelined(width // WIDE, fetch, convolve)
    residual_copy.wait()


def local_kernel(
    gate_ref,
    residual_ref,
    product_ref,
    first_ref,
    mode_rate_ref,
    inner_ref,
    entering_ref,
    skip_ref,
    base_ref,
):
    rows, width = product_ref.shape
    mask = group_mask(BF16)
    top = index_of((8, LANES), 0) < 2
    chunks = range(rows // CHUNK)

    def inside(tile):
        here = lanes_of(tile)
        pieces = []
        for chunk in chunks:
            piece = product_ref[chunk * CHUNK : (chunk + 1) * CHUNK, here]
            if chunk == 0:
                wide = piece.astype(F32)
                head = jnp.where(top, first_ref[:, here], wide[:8])
                piece = jnp.concatenate([head, wide[8:]], axis=0).astype(BF16)
            pieces.append(piece)
        found = []
        for pair in chunks[::2]:
            sources = jnp.concatenate([spread(pieces[pair + k], mask) for k in (0, 1)], axis=1)
            found.append(jnp.dot(inner_ref[tile], sources, preferred_element_type=F32))
        return found, pieces[0]

    def across(tile, inner, first):
        decay = jnp.exp(-float(CHUNK) * mode_rate_ref[:, lanes_of(tile)])
        state = jnp.zeros((MODES, LANES), F32)
        states = []
        for chunk in chunks:
            states.append(spread(state.astype(BF16), mask))
            state = decay * state + inner[chunk // 2][CHUNK:, lanes_of(chunk % 2)]
        outer = []
        for pair in chunks[::2]:
            two = jnp.concatenate(states[pair : pair + 2], axis=1)
            outer.append(jnp.dot(entering_ref[tile], two, preferred_element_type=F32))
        return [part[:CHUNK] for part in inner], outer, first

    def finish(tile, inner, outer, first):
        here = lanes_of(tile)
        skip = skip_ref[:, here]
        for chunk in chunks:
            span = slice(chunk * CHUNK, (chunk + 1) * CHUNK)
            piece = first if chunk == 0 else product_ref[span, here]
            conv = (inner[chunk // 2] + outer[chunk // 2])[:, lanes_of(chunk % 2)]
            whole = conv + skip * piece.astype(F32)
            base_ref[span, here] = residual_ref[span, here].astype(F32) + gate_ref[span, here] * whole

    pipelined(width // LANES, inside, across, finish)


def join_kernel(tokens, radix, stride, place_ref, own_ref, mode_rate_ref, entry_ref, *refs):
    others, (found_ref, group_ref) = refs[: radix - 1], refs[radix - 1 :]
    rate = mode_rate_ref[...]
    run = lax.rem(place_ref[0] // stride, radix)
    step = float(tokens * stride)

    def decayed(value, runs):
        return jnp.exp(-step * runs.astype(F32) * rate) * value

    found = jnp.zeros_like(rate)
    total = decayed(own_ref[...].astype(F32), radix - 1 - run)
    for k, ref in enumerate(others, 1):
        other = ref[...].astype(F32)
        source = partner(run, k, radix)
        found = found + jnp.where(source < run, decayed(other, jnp.maximum(run - 1 - source, 0)), 0.0)
        total = total + decayed(other, radix - 1 - source)
    within = lax.rem(place_ref[0], stride).astype(F32) * float(tokens)
    found_ref[...] = entry_ref[...] + jnp.exp(-within * rate) * found
    group_ref[...] = total.astype(BF16)


def carry_kernel(stride, radix, place_ref, base_ref, gate_ref, carry_ref, mode_rate_ref, inner_entry_ref, *refs):
    entry_refs, (summed_ref, squares_ref) = refs[:-2], refs[-2:]
    rows, width = base_ref.shape
    run = place_ref[0] // stride
    within = lax.rem(place_ref[0], stride).astype(F32) * float(rows)
    mask = group_mask(BF16)
    totals = [jnp.zeros((rows, LANES), F32)]
    nothing = jnp.zeros((LANES, LANES), BF16)

    def enter(tile):
        here = lanes_of(tile, WIDE)
        rate = mode_rate_ref[:, here]
        step = float(rows * stride)
        outer = jnp.zeros_like(rate)
        for k, ref in enumerate(entry_refs[::-1], 1):
            source = partner(run, k, radix)
            lag = jnp.maximum(run - 1 - source, 0).astype(F32) * step
            outer = outer + jnp.where(source < run, jnp.exp(-lag * rate) * ref[:, here].astype(F32), 0.0)
        entry = (inner_entry_ref[:, here] + jnp.exp(-within * rate) * outer).astype(BF16)
        left, right = spread(entry[:, :LANES], mask), spread(entry[:, LANES:], mask)
        both = jnp.concatenate(
            [jnp.concatenate([left, nothing], axis=1), jnp.concatenate([nothing, right], axis=1)], axis=0
        )
        return (jnp.dot(carry_ref[tile], both, preferred_element_type=F32),)

    def add(tile, carry):
        here = lanes_of(tile, WIDE)
        summed = base_ref[:, here] + gate_ref[:, here] * carry
        summed_ref[:, here] = summed
        square = summed * summed
        totals[0] = totals[0] + (square[:, :LANES] + square[:, LANES:])

    pipelined(width // WIDE, enter, add)
    total = totals[0]
    squares = lax.dot_general(
        jnp.ones((8, 2 * LANES), BF16),
        jnp.concatenate(split(total), axis=1),
        (((1,), (1,)), ((), ())),
        preferred_element_type=F32,
    )
    squares_ref[...] = squares[0:1]


def write_kernel(summed_ref, out_hbm, rounded_ref, sems):
    width = summed_ref.shape[1]
    copies = []
    for tile in range(width // WIDE):
        here = lanes_of(tile, WIDE)
        rounded_ref[:, here] = summed_ref[:, here].astype(BF16)
        span = pl.ds(tile * WIDE, WIDE)
        copies.append(pltpu.make_async_copy(rounded_ref.at[:, span], out_hbm.at[:, span], sems.at[tile]))
        copies[-1].start()
    for copy in copies:
        copy.wait()


def norm_kernel(full_width, summed_ref, gain_ref, *refs):
    squares_refs, (out_hbm, rounded_ref, sems) = refs[:-3], refs[-3:]
    rows, width = summed_ref.shape
    squares = squares_refs[0][...]
    for ref in squares_refs[1:]:
        squares = squares + ref[...]
    scale_row = lax.rsqrt(squares / full_width + 1e-05)
    scale = jnp.concatenate([as_column(scale_row[:, lanes_of(k)]) for k in range(rows // LANES)], axis=0)
    copies = []
    block = rows // 8
    for start in range(0, rows, block):
        span = slice(start, start + block)
        for tile in range(width // LANES):
            here = lanes_of(tile)
            rounded_ref[span, here] = (summed_ref[span, here] * scale[span] * gain_ref[:, here]).astype(BF16)
        there = pl.ds(start, block)
        copies.append(pltpu.make_async_copy(rounded_ref.at[there, :], out_hbm.at[there, :], sems.at[start // block]))
        copies[-1].start()
    for copy in copies:
        copy.wait()


def params():
    return pltpu.CompilerParams(vmem_limit_bytes=VMEM_LIMIT)


def cost(microseconds):
    return pl.CostEstimate(flops=0, bytes_accessed=int(microseconds * 3.0e6), transcendentals=0)


def radices(count):
    found = []
    for radix in (2, 4, 4, 4, 3, 2, 5, 7):
        if count % radix == 0:
            found.append(radix)
            count //= radix
    return found + ([count] if count > 1 else [])


def partner(run, k, radix):
    if radix & (radix - 1) == 0:
        return run ^ k
    return (run - k + radix) % radix


def routes(count, stride, radix):
    found = []
    for k in range(1, radix):
        route = []
        for i in range(count):
            run = i // stride % radix
            route.append((i + (partner(run, k, radix) - run) * stride, i))
        found.append(route)
    return found


def ring(count, shift):
    return [(i, (i + shift) % count) for i in range(count)]


def per_device(projected, short_weight, rates, residues, skip, residual, gain):
    rows, width = projected.shape[1:]
    taps = short_weight.shape[0]
    peers = lax.axis_size("ctx")
    full_width = width * lax.axis_size("fsdp")
    place = lax.axis_index("ctx").astype(jnp.int32).reshape(1)
    hbm_spec = pl.BlockSpec(memory_space=pltpu.HBM)
    vmem_spec = pl.BlockSpec(memory_space=pltpu.VMEM)
    smem_spec = pl.BlockSpec(memory_space=pltpu.SMEM)
    tiles = width // LANES
    wides = width // WIDE

    def kept(array):
        return pltpu.with_memory_space_constraint(array, pltpu.HBM)

    def f32(*shape):
        return jax.ShapeDtypeStruct(shape, F32)

    def bf16(*shape):
        return jax.ShapeDtypeStruct(shape, BF16)

    before = lax.ppermute(projected[:, rows - (taps - 1) :, :], "ctx", ring(peers, 1))

    product, state, mode_rate, head, weights, residue = pl.pallas_call(
        state_kernel,
        in_specs=[hbm_spec] * 4,
        out_shape=[
            bf16(rows, width),
            f32(MODES, width),
            f32(MODES, width),
            f32(2, 8, width),
            f32(*short_weight.shape),
            f32(MODES, residues.shape[0]),
        ],
        scratch_shapes=[
            pltpu.VMEM((2, rows, width), BF16),
            pltpu.VMEM((2 * rows, rows), BF16),
            pltpu.VMEM(short_weight.shape, BF16),
            pltpu.VMEM((MODES, rates.shape[0]), F32),
            pltpu.SemaphoreType.DMA((5,)),
            pltpu.SemaphoreType.DMA((2,)),
        ],
        compiler_params=params(),
        cost_estimate=cost(3),
        name="block_state",
    )(kept(projected), kept(short_weight), kept(rates.T), kept(residues.T))

    full_state, first = pl.pallas_call(
        lambda *refs: head_kernel(rows, *refs),
        in_specs=[smem_spec] + [vmem_spec] * 5,
        out_shape=[bf16(MODES, width), f32(8, width)],
        compiler_params=params(),
        cost_estimate=cost(0.2),
        name="head_tokens",
    )(place, before, head, weights, state, mode_rate)

    inner, entering, carry_table, gate, residual_here = pl.pallas_call(
        prepare_kernel,
        in_specs=[smem_spec] + [hbm_spec] * 2 + [vmem_spec] * 4,
        out_shape=[
            bf16(tiles, CHUNK + MODES, GROUPS * CHUNK),
            bf16(tiles, CHUNK, LANES),
            bf16(wides, rows, WIDE),
            f32(rows, width),
            bf16(rows, width),
        ],
        scratch_shapes=[
            pltpu.VMEM((rows, width), BF16),
            pltpu.VMEM((2 * rows, rows), BF16),
            pltpu.SemaphoreType.DMA((2,)),
        ],
        compiler_params=params(),
        cost_estimate=cost(2),
        name="prepare",
    )(place, kept(projected), kept(residual), residue, before, weights, mode_rate)

    group, entry, stride = full_state, jnp.zeros((MODES, width), F32), 1
    levels = radices(peers)
    for level, radix in enumerate(levels):
        size = stride * radix
        if level == len(levels) - 1:
            break
        others = [lax.ppermute(group, "ctx", route) for route in routes(peers, stride, radix)]
        if level == 0:
            others[0], inner = lax.optimization_barrier((others[0], inner))
        entry, group = pl.pallas_call(
            lambda *refs, radix=radix, stride=stride: join_kernel(rows, radix, stride, *refs),
            in_specs=[smem_spec] + [vmem_spec] * (2 + radix),
            out_shape=[f32(MODES, width), bf16(MODES, width)],
            compiler_params=params(),
            cost_estimate=cost(0.2),
            name="join",
        )(place, group, mode_rate, entry, *others)
        stride = size
    received = [lax.ppermute(group, "ctx", route) for route in routes(peers, stride, levels[-1])[::-1]]

    base = pl.pallas_call(
        local_kernel,
        out_shape=f32(rows, width),
        compiler_params=params(),
        cost_estimate=cost(5),
        name="local_conv",
    )(gate, residual_here, product, first, mode_rate, inner, entering, skip[None])

    count = lax.axis_size("fsdp")
    summed, squares = pl.pallas_call(
        lambda *refs: carry_kernel(stride, levels[-1], *refs),
        in_specs=[smem_spec] + [vmem_spec] * (5 + len(received)),
        out_shape=[f32(rows, width), f32(1, rows)],
        compiler_params=params(),
        cost_estimate=cost(1),
        name="add_carry",
    )(place, base, gate, carry_table, mode_rate, entry, *received)

    parts = [lax.ppermute(squares, "fsdp", route) for route in routes(count, 1, count)[::-1]]

    def write(kernel, operands, name):
        return pl.pallas_call(
            kernel,
            out_specs=hbm_spec,
            out_shape=bf16(rows, width),
            scratch_shapes=[pltpu.VMEM((rows, width), BF16), pltpu.SemaphoreType.DMA((max(8, wides),))],
            compiler_params=params(),
            cost_estimate=cost(1),
            name=name,
        )(*operands)

    new_residual = write(write_kernel, (summed,), "new_residual")
    normed = write(
        lambda *refs: norm_kernel(full_width, *refs), (summed, gain[None], squares, *parts), "normed"
    )
    return (new_residual, normed)


def solution(mesh):
    return jax.shard_map(
        per_device,
        mesh=mesh,
        in_specs=(
            P(None, "ctx", "fsdp"),
            P(None, None, "fsdp"),
            P("fsdp", None),
            P("fsdp", None),
            P("fsdp"),
            P("ctx", "fsdp"),
            P("fsdp"),
        ),
        out_specs=(P("ctx", "fsdp"), P("ctx", "fsdp")),
        check_vma=False,
    )
```

```python
import jax
import jax.numpy as jnp
from jax import lax
from jax.experimental import pallas as pl
from jax.experimental.pallas import tpu as pltpu
from jax.sharding import PartitionSpec as P

CHANNELS_PER_GRP = 16
MODES = 16
CHUNK = 32
LANES = 128
WIDE = 256
GROUPS = LANES // CHANNELS_PER_GRP
VMEM_LIMIT = 16 * 1024 * 1024
F32 = jnp.float32
BF16 = jnp.bfloat16


def index_of(shape, dim):
    return lax.broadcasted_iota(jnp.int32, shape, dim)


def pipelined(count, *stages):
    held = {}
    for step in range(count + len(stages) - 1):
        for k, stage in enumerate(stages):
            item = step - k
            if 0 <= item < count:
                held[item] = stage(item, *held.get(item, ()))


def lanes_of(tile, width=LANES):
    return slice(tile * width, (tile + 1) * width)


def per_channel(table):
    groups = table.shape[1]
    width = groups * CHANNELS_PER_GRP
    high = table.astype(BF16)
    rest = table - high.astype(F32)
    middle = rest.astype(BF16)
    low = (rest - middle.astype(F32)).astype(BF16)
    terms = jnp.concatenate([high, middle, low], axis=0)
    parts = []
    for tile in range(width // WIDE):
        shape = (groups, WIDE)
        own = index_of(shape, 0) == index_of(shape, 1) // CHANNELS_PER_GRP + tile * (WIDE // CHANNELS_PER_GRP)
        three = jnp.dot(terms, jnp.where(own, 1.0, 0.0).astype(BF16), preferred_element_type=F32)
        parts.append(three[:MODES] + three[MODES : 2 * MODES] + three[2 * MODES :])
    return jnp.concatenate(parts, axis=1)


def mode_row(channel_table):
    own = index_of(channel_table.shape, 0) == (index_of(channel_table.shape, 1) & (MODES - 1))
    return jnp.sum(jnp.where(own, channel_table, 0.0), axis=0, keepdims=True)


def as_column(row):
    return jnp.transpose(jnp.broadcast_to(row, (LANES, LANES)))


def own_mode(dtype):
    shape = (GROUPS, MODES, LANES)
    own = index_of(shape, 0) * MODES + index_of(shape, 1) == index_of(shape, 2)
    return jnp.where(own, 1.0, 0.0).astype(dtype)


def split(x):
    high = x.astype(BF16)
    return high, (x - high.astype(F32)).astype(BF16)


def group_mask(dtype):
    shape = (GROUPS, MODES, LANES)
    own = index_of(shape, 0) == index_of(shape, 2) // CHANNELS_PER_GRP
    return jnp.where(own, 1.0, 0.0).astype(dtype)


def spread(rows, mask):
    size = rows.shape[0]
    copies = rows.reshape(1, size // MODES, MODES, LANES) * mask.reshape(GROUPS, 1, MODES, LANES)
    return copies.reshape(GROUPS * size, LANES)


def shifted(block, before):
    one = pltpu.roll(block, 1, 0)
    two = pltpu.roll(block, 2, 0)
    first = index_of((8, block.shape[1]), 0)
    near, far = (0.0, 0.0) if before is None else (before[1:2], before[0:1])
    head_one = jnp.where(first == 0, near, one[:8])
    head_two = jnp.where(first == 0, far, jnp.where(first == 1, near, two[:8]))
    if block.shape[0] == 8:
        return head_one, head_two
    return jnp.concatenate([head_one, one[8:]], axis=0), jnp.concatenate([head_two, two[8:]], axis=0)


def short_conv(block, before, weights):
    one, two = shifted(block, before)
    return weights[0] * block + weights[1] * one + weights[2] * two


def shift_matrix(rows):
    shape = (2 * rows, rows)
    target = index_of(shape, 0)
    source = index_of(shape, 1)
    taken = jnp.where(target < rows, target - 1, target - (rows + 2))
    return jnp.where(source == taken, 1.0, 0.0).astype(BF16)


def earlier_tokens(shift, block):
    return jnp.dot(shift, block, preferred_element_type=F32)


def wide_conv(block, earlier, weights):
    rows = block.shape[0]
    return weights[0] * block.astype(F32) + weights[1] * earlier[:rows] + weights[2] * earlier[rows:]


def taps_of(weights, feature, lanes):
    return [weights[tap, feature : feature + 1, lanes] for tap in range(weights.shape[0])]


def fetch_kernel(
    place_ref,
    projected_ref,
    weight_hbm,
    rate_hbm,
    residue_hbm,
    block_ref,
    tail_ref,
    weight_ref,
    mode_rate_ref,
    ending_ref,
    shift_ref,
    residue_ref,
    place_out_ref,
    last_ref,
    short_ref,
    rate_ref,
    sems,
):
    rows, width = block_ref.shape[1:]
    place_out_ref[0] = place_ref[0]
    copies = [
        pltpu.make_async_copy(rate_hbm, rate_ref, sems.at[0]),
        pltpu.make_async_copy(projected_ref.at[:, pl.ds(rows - 16, 16), :], last_ref, sems.at[1]),
        pltpu.make_async_copy(weight_hbm, short_ref, sems.at[2]),
        pltpu.make_async_copy(projected_ref.at[1], block_ref.at[0], sems.at[3]),
        pltpu.make_async_copy(projected_ref.at[2], block_ref.at[1], sems.at[4]),
        pltpu.make_async_copy(residue_hbm, residue_ref, sems.at[5]),
    ]
    for copy in copies:
        copy.start()
    shift_ref[...] = shift_matrix(rows)
    copies[0].wait()
    mode_rate = per_channel(rate_ref[...])
    mode_rate_ref[...] = mode_rate
    eye = own_mode(BF16)
    token = index_of((2 * LANES, rows), 1)
    left = jnp.where(token < 2, -1e30, (token - (rows - 1)).astype(F32)).astype(BF16)

    def exponents(tile):
        high, low = split(mode_rate[:, lanes_of(tile)])
        diagonal = jnp.concatenate([spread(high, eye), spread(low, eye)], axis=1)
        return (jnp.dot(diagonal, left, preferred_element_type=F32),)

    def endings(tile, exponent):
        ending_ref[tile // 2, lanes_of(tile % 2), :] = jnp.exp(exponent).astype(BF16)

    pipelined(width // LANES, exponents, endings)
    copies[1].wait()
    for c in range(3):
        tail_ref[c] = last_ref[c].astype(F32)[14:].astype(BF16)
    copies[2].wait()
    weight_ref[...] = short_ref[...].astype(F32)
    for copy in copies[3:]:
        copy.wait()


def state_kernel(
    block_ref,
    weight_ref,
    ending_ref,
    shift_ref,
    projected_ref,
    residual_hbm,
    product_ref,
    state_ref,
    query_ref,
    residual_ref,
    sems,
):
    rows, width = product_ref.shape
    copies = [
        pltpu.make_async_copy(projected_ref.at[0], query_ref, sems.at[0]),
        pltpu.make_async_copy(residual_hbm, residual_ref, sems.at[1]),
    ]
    for copy in copies:
        copy.start()
    mask = group_mask(F32)

    def fetch(wide):
        return [earlier_tokens(shift_ref[...], block_ref[c, :, lanes_of(wide, WIDE)]) for c in (0, 1)]

    def multiply(wide, *earlier):
        here = lanes_of(wide, WIDE)
        parts = [wide_conv(block_ref[c, :, here], earlier[c], taps_of(weight_ref, c + 1, here)) for c in (0, 1)]
        product = (parts[0] * parts[1]).astype(BF16)
        product_ref[:, here] = product
        return (jnp.dot(ending_ref[wide], product, preferred_element_type=F32),)

    def leave(wide, every):
        for half in range(WIDE // LANES):
            own = every[lanes_of(half), lanes_of(half)].reshape(GROUPS, MODES, LANES)
            state_ref[:, lanes_of((WIDE // LANES) * wide + half)] = jnp.sum(own * mask, axis=0)

    pipelined(width // WIDE, fetch, multiply, leave)
    for copy in copies:
        copy.wait()


def halo(before_ref, place_ref):
    return jnp.where(place_ref[0] > 0, before_ref[...].astype(F32), 0.0)


def head_kernel(place_ref, before_ref, block_ref, weight_ref, state_ref, mode_rate_ref, full_ref, first_ref):
    before = halo(before_ref, place_ref)
    rows, width = block_ref.shape[1:]
    everything = slice(0, width)
    heads = [block_ref[c, 0:16, :].astype(F32)[:8] for c in (0, 1)]
    parts = [short_conv(heads[c], before[c + 1], taps_of(weight_ref, c + 1, everything)) for c in (0, 1)]
    first = (parts[0] * parts[1]).astype(BF16).astype(F32)
    first_ref[...] = first
    rate = mode_rate_ref[...]
    early = jnp.exp(-float(rows - 1) * rate) * first[0:1] + jnp.exp(-float(rows - 2) * rate) * first[1:2]
    full_ref[...] = (state_ref[...] + early).astype(BF16)


def prepare_kernel(
    place_ref,
    query_ref,
    residue_ref,
    before_ref,
    weight_ref,
    mode_rate_ref,
    shift_ref,
    inner_ref,
    entering_ref,
    carry_ref,
    gate_ref,
):
    rows, width = gate_ref.shape
    residue = per_channel(residue_ref[...])
    wide = GROUPS * CHUNK
    step = index_of((CHUNK, LANES), 0).astype(F32)
    causal = (index_of((CHUNK, wide), 1) & (CHUNK - 1)) <= index_of((CHUNK, wide), 0)
    eye = own_mode(BF16)
    flat_eye = jnp.where((index_of((MODES, LANES), 1) & (MODES - 1)) == index_of((MODES, LANES), 0), 1.0, 0.0)
    flat_eye = flat_eye.astype(BF16)
    shape = (2 * LANES, wide)
    source = (index_of(shape, 1) & (CHUNK - 1)).astype(F32)
    own = (index_of(shape, 0) & (LANES - 1)) // MODES == index_of(shape, 1) // CHUNK
    own_chunk = jnp.where(own[:LANES], 1.0, 0.0).astype(BF16)
    risen = source[:, :LANES].astype(BF16)
    left = jnp.where(own, source - (CHUNK - 1), 0.0).astype(BF16)

    def exponents(tile):
        rate = mode_rate_ref[:, lanes_of(tile)]
        high, low = split(rate)
        diagonal = jnp.concatenate([spread(high, eye), spread(low, eye)], axis=1)
        each = jnp.concatenate([high * flat_eye, low * flat_eye], axis=1)
        return (
            jnp.dot(diagonal, risen, preferred_element_type=F32),
            jnp.dot(each, left, preferred_element_type=F32),
        )

    def products(tile, rise, end):
        here = lanes_of(tile)
        rise_high, rise_low = [
            jnp.concatenate([part] * (wide // LANES), axis=1) * own_chunk for part in split(jnp.exp(rise))
        ]
        rate_row = mode_row(mode_rate_ref[:, here])
        falling = mode_row(residue[:, here]) * jnp.exp(-rate_row * step)
        fall_high, fall_low = split(falling)
        half = tile % (WIDE // LANES)
        for chunk in range(rows // CHUNK):
            entering = (falling * jnp.exp(-float(CHUNK * chunk + 1) * rate_row)).astype(BF16)
            carry_ref[tile // (WIDE // LANES), chunk * CHUNK : (chunk + 1) * CHUNK, lanes_of(half)] = entering
            if chunk == 0:
                entering_ref[tile] = entering
        return (
            jnp.dot(jnp.concatenate([fall_high, fall_low], axis=0), rise_high, preferred_element_type=F32),
            jnp.dot(fall_high, rise_low, preferred_element_type=F32),
            jnp.exp(end),
        )

    def finish(tile, taps, rest, ending):
        taps = jnp.where(causal, taps[:CHUNK] + taps[CHUNK:] + rest, 0.0)
        inner_ref[tile] = jnp.concatenate([taps.astype(BF16), ending.astype(BF16)], axis=0)

    pipelined(width // LANES, exponents, products, finish)
    before = halo(before_ref, place_ref)

    def fetch(part):
        return (earlier_tokens(shift_ref[...], query_ref[:, lanes_of(part, WIDE)]),)

    def convolve(part, earlier):
        here = lanes_of(part, WIDE)
        weights = taps_of(weight_ref, 0, here)
        gate_ref[:, here] = wide_conv(query_ref[:, here], earlier, weights)
        head = query_ref[0:16, here].astype(F32)[:8]
        gate_ref[0:8, here] = short_conv(head, before[0, :, here], weights)

    pipelined(width // WIDE, fetch, convolve)


def local_kernel(
    gate_ref,
    residual_ref,
    product_ref,
    first_ref,
    mode_rate_ref,
    inner_ref,
    entering_ref,
    skip_ref,
    base_ref,
):
    rows, width = product_ref.shape
    mask = group_mask(BF16)
    top = index_of((8, LANES), 0) < 2
    chunks = range(rows // CHUNK)

    def inside(tile):
        here = lanes_of(tile)
        pieces = []
        for chunk in chunks:
            piece = product_ref[chunk * CHUNK : (chunk + 1) * CHUNK, here]
            if chunk == 0:
                wide = piece.astype(F32)
                head = jnp.where(top, first_ref[:, here], wide[:8])
                piece = jnp.concatenate([head, wide[8:]], axis=0).astype(BF16)
            pieces.append(piece)
        found = []
        for pair in chunks[::2]:
            sources = jnp.concatenate([spread(pieces[pair + k], mask) for k in (0, 1)], axis=1)
            found.append(jnp.dot(inner_ref[tile], sources, preferred_element_type=F32))
        return found, pieces[0]

    def across(tile, inner, first):
        decay = jnp.exp(-float(CHUNK) * mode_rate_ref[:, lanes_of(tile)])
        state = jnp.zeros((MODES, LANES), F32)
        states = []
        for chunk in chunks:
            states.append(spread(state.astype(BF16), mask))
            state = decay * state + inner[chunk // 2][CHUNK:, lanes_of(chunk % 2)]
        outer = []
        for pair in chunks[::2]:
            two = jnp.concatenate(states[pair : pair + 2], axis=1)
            outer.append(jnp.dot(entering_ref[tile], two, preferred_element_type=F32))
        return [part[:CHUNK] for part in inner], outer, first

    def finish(tile, inner, outer, first):
        here = lanes_of(tile)
        skip = skip_ref[:, here]
        for chunk in chunks:
            span = slice(chunk * CHUNK, (chunk + 1) * CHUNK)
            piece = first if chunk == 0 else product_ref[span, here]
            conv = (inner[chunk // 2] + outer[chunk // 2])[:, lanes_of(chunk % 2)]
            whole = conv + skip * piece.astype(F32)
            base_ref[span, here] = residual_ref[span, here].astype(F32) + gate_ref[span, here] * whole

    pipelined(width // LANES, inside, across, finish)


def join_kernel(tokens, radix, stride, place_ref, own_ref, mode_rate_ref, entry_ref, *refs):
    others, (found_ref, group_ref) = refs[: radix - 1], refs[radix - 1 :]
    rate = mode_rate_ref[...]
    run = lax.rem(place_ref[0] // stride, radix)
    step = float(tokens * stride)

    def decayed(value, runs):
        return jnp.exp(-step * runs.astype(F32) * rate) * value

    found = jnp.zeros_like(rate)
    total = decayed(own_ref[...].astype(F32), radix - 1 - run)
    for k, ref in enumerate(others, 1):
        other = ref[...].astype(F32)
        source = partner(run, k, radix)
        found = found + jnp.where(source < run, decayed(other, jnp.maximum(run - 1 - source, 0)), 0.0)
        total = total + decayed(other, radix - 1 - source)
    within = lax.rem(place_ref[0], stride).astype(F32) * float(tokens)
    found_ref[...] = entry_ref[...] + jnp.exp(-within * rate) * found
    group_ref[...] = total.astype(BF16)


def carry_kernel(stride, radix, place_ref, base_ref, gate_ref, carry_ref, mode_rate_ref, inner_entry_ref, *refs):
    entry_refs, (summed_ref, squares_ref) = refs[:-2], refs[-2:]
    rows, width = base_ref.shape
    run = place_ref[0] // stride
    within = lax.rem(place_ref[0], stride).astype(F32) * float(rows)
    mask = group_mask(BF16)
    totals = [jnp.zeros((rows, LANES), F32)]
    nothing = jnp.zeros((LANES, LANES), BF16)

    def enter(tile):
        here = lanes_of(tile, WIDE)
        rate = mode_rate_ref[:, here]
        step = float(rows * stride)
        outer = jnp.zeros_like(rate)
        for k, ref in enumerate(entry_refs, 1):
            source = partner(run, k, radix)
            lag = jnp.maximum(run - 1 - source, 0).astype(F32) * step
            outer = outer + jnp.where(source < run, jnp.exp(-lag * rate) * ref[:, here].astype(F32), 0.0)
        entry = (inner_entry_ref[:, here] + jnp.exp(-within * rate) * outer).astype(BF16)
        left, right = spread(entry[:, :LANES], mask), spread(entry[:, LANES:], mask)
        both = jnp.concatenate(
            [jnp.concatenate([left, nothing], axis=1), jnp.concatenate([nothing, right], axis=1)], axis=0
        )
        return (jnp.dot(carry_ref[tile], both, preferred_element_type=F32),)

    def add(tile, carry):
        here = lanes_of(tile, WIDE)
        summed = base_ref[:, here] + gate_ref[:, here] * carry
        summed_ref[:, here] = summed
        square = summed * summed
        totals[0] = totals[0] + (square[:, :LANES] + square[:, LANES:])

    pipelined(width // WIDE, enter, add)
    total = totals[0]
    squares = lax.dot_general(
        jnp.ones((8, 2 * LANES), BF16),
        jnp.concatenate(split(total), axis=1),
        (((1,), (1,)), ((), ())),
        preferred_element_type=F32,
    )
    squares_ref[...] = squares[0:1]


def write_kernel(summed_ref, out_hbm, rounded_ref, sems):
    width = summed_ref.shape[1]
    copies = []
    for tile in range(width // WIDE):
        here = lanes_of(tile, WIDE)
        rounded_ref[:, here] = summed_ref[:, here].astype(BF16)
        span = pl.ds(tile * WIDE, WIDE)
        copies.append(pltpu.make_async_copy(rounded_ref.at[:, span], out_hbm.at[:, span], sems.at[tile]))
        copies[-1].start()
    for copy in copies:
        copy.wait()


def norm_kernel(full_width, summed_ref, gain_ref, *refs):
    squares_refs, (out_hbm, rounded_ref, sems) = refs[:-3], refs[-3:]
    rows, width = summed_ref.shape
    squares = squares_refs[0][...]
    for ref in squares_refs[1:]:
        squares = squares + ref[...]
    scale_row = lax.rsqrt(squares / full_width + 1e-05)
    scale = jnp.concatenate([as_column(scale_row[:, lanes_of(k)]) for k in range(rows // LANES)], axis=0)
    copies = []
    block = rows // 8
    for start in range(0, rows, block):
        span = slice(start, start + block)
        for tile in range(width // LANES):
            here = lanes_of(tile)
            rounded_ref[span, here] = (summed_ref[span, here] * scale[span] * gain_ref[:, here]).astype(BF16)
        there = pl.ds(start, block)
        copies.append(pltpu.make_async_copy(rounded_ref.at[there, :], out_hbm.at[there, :], sems.at[start // block]))
        copies[-1].start()
    for copy in copies:
        copy.wait()


def params():
    return pltpu.CompilerParams(vmem_limit_bytes=VMEM_LIMIT)


def cost(microseconds):
    return pl.CostEstimate(flops=0, bytes_accessed=int(microseconds * 3.0e6), transcendentals=0)


def radices(count):
    found = []
    for radix in (2, 4, 4, 4, 3, 2, 5, 7):
        if count % radix == 0:
            found.append(radix)
            count //= radix
    return found + ([count] if count > 1 else [])


def partner(run, k, radix):
    if radix & (radix - 1) == 0:
        return run ^ k
    return (run - k + radix) % radix


def routes(count, stride, radix):
    found = []
    for k in range(1, radix):
        route = []
        for i in range(count):
            run = i // stride % radix
            route.append((i + (partner(run, k, radix) - run) * stride, i))
        found.append(route)
    return found


def ring(count, shift):
    return [(i, (i + shift) % count) for i in range(count)]


def per_device(projected, short_weight, rates, residues, skip, residual, gain):
    rows, width = projected.shape[1:]
    taps = short_weight.shape[0]
    peers = lax.axis_size("ctx")
    full_width = width * lax.axis_size("fsdp")
    place = lax.axis_index("ctx").astype(jnp.int32).reshape(1)
    hbm_spec = pl.BlockSpec(memory_space=pltpu.HBM)
    vmem_spec = pl.BlockSpec(memory_space=pltpu.VMEM)
    smem_spec = pl.BlockSpec(memory_space=pltpu.SMEM)
    tiles = width // LANES
    wides = width // WIDE

    def kept(array):
        return pltpu.with_memory_space_constraint(array, pltpu.HBM)

    def f32(*shape):
        return jax.ShapeDtypeStruct(shape, F32)

    def bf16(*shape):
        return jax.ShapeDtypeStruct(shape, BF16)

    block, tail, weights, mode_rate, ending, shift, residue, place = pl.pallas_call(
        fetch_kernel,
        in_specs=[smem_spec] + [hbm_spec] * 4,
        out_specs=[vmem_spec] * 7 + [smem_spec],
        out_shape=[
            bf16(2, rows, width),
            bf16(3, taps - 1, width),
            f32(*short_weight.shape),
            f32(MODES, width),
            bf16(wides, WIDE, rows),
            bf16(2 * rows, rows),
            f32(MODES, residues.shape[0]),
            jax.ShapeDtypeStruct((1,), jnp.int32),
        ],
        scratch_shapes=[
            pltpu.VMEM((3, 16, width), BF16),
            pltpu.VMEM(short_weight.shape, BF16),
            pltpu.VMEM((MODES, rates.shape[0]), F32),
            pltpu.SemaphoreType.DMA((6,)),
        ],
        compiler_params=params(),
        cost_estimate=cost(2),
        name="fetch",
    )(place, kept(projected), kept(short_weight), kept(rates.T), kept(residues.T))

    before = lax.ppermute(tail, "ctx", ring(peers, 1))

    product, state, query, residual_here = pl.pallas_call(
        state_kernel,
        in_specs=[vmem_spec] * 4 + [hbm_spec] * 2,
        out_shape=[bf16(rows, width), f32(MODES, width), bf16(rows, width), bf16(rows, width)],
        scratch_shapes=[pltpu.SemaphoreType.DMA((2,))],
        compiler_params=params(),
        cost_estimate=cost(2),
        name="block_state",
    )(block, weights, ending, shift, kept(projected), kept(residual))

    full_state, first = pl.pallas_call(
        head_kernel,
        in_specs=[smem_spec] + [vmem_spec] * 5,
        out_shape=[bf16(MODES, width), f32(8, width)],
        compiler_params=params(),
        cost_estimate=cost(0.2),
        name="head_tokens",
    )(place, before, block, weights, state, mode_rate)

    inner, entering, carry_table, gate = pl.pallas_call(
        prepare_kernel,
        in_specs=[smem_spec] + [vmem_spec] * 6,
        out_shape=[
            bf16(tiles, CHUNK + MODES, GROUPS * CHUNK),
            bf16(tiles, CHUNK, LANES),
            bf16(wides, rows, WIDE),
            f32(rows, width),
        ],
        compiler_params=params(),
        cost_estimate=cost(2),
        name="prepare",
    )(place, query, residue, before, weights, mode_rate, shift)

    group, entry, stride = full_state, jnp.zeros((MODES, width), F32), 1
    levels = radices(peers)
    for level, radix in enumerate(levels):
        size = stride * radix
        if level == len(levels) - 1:
            break
        others = [lax.ppermute(group, "ctx", route) for route in routes(peers, stride, radix)]
        if level == 0:
            others[0], inner = lax.optimization_barrier((others[0], inner))
        entry, group = pl.pallas_call(
            lambda *refs, radix=radix, stride=stride: join_kernel(rows, radix, stride, *refs),
            in_specs=[smem_spec] + [vmem_spec] * (2 + radix),
            out_shape=[f32(MODES, width), bf16(MODES, width)],
            compiler_params=params(),
            cost_estimate=cost(0.2),
            name="join",
        )(place, group, mode_rate, entry, *others)
        stride = size
    received = [lax.ppermute(group, "ctx", route) for route in routes(peers, stride, levels[-1])]

    base = pl.pallas_call(
        local_kernel,
        out_shape=f32(rows, width),
        compiler_params=params(),
        cost_estimate=cost(5),
        name="local_conv",
    )(gate, residual_here, product, first, mode_rate, inner, entering, skip[None])

    count = lax.axis_size("fsdp")
    summed, squares = pl.pallas_call(
        lambda *refs: carry_kernel(stride, levels[-1], *refs),
        in_specs=[smem_spec] + [vmem_spec] * (5 + len(received)),
        out_shape=[f32(rows, width), f32(1, rows)],
        compiler_params=params(),
        cost_estimate=cost(1),
        name="add_carry",
    )(place, base, gate, carry_table, mode_rate, entry, *received)

    parts = [lax.ppermute(squares, "fsdp", route) for route in routes(count, 1, count)]

    def write(kernel, operands, name):
        return pl.pallas_call(
            kernel,
            out_specs=hbm_spec,
            out_shape=bf16(rows, width),
            scratch_shapes=[pltpu.VMEM((rows, width), BF16), pltpu.SemaphoreType.DMA((max(8, wides),))],
            compiler_params=params(),
            cost_estimate=cost(1),
            name=name,
        )(*operands)

    new_residual = write(write_kernel, (summed,), "new_residual")
    normed = write(
        lambda *refs: norm_kernel(full_width, *refs), (summed, gain[None], squares, *parts), "normed"
    )
    return (new_residual, normed)


def solution(mesh):
    return jax.shard_map(
        per_device,
        mesh=mesh,
        in_specs=(
            P(None, "ctx", "fsdp"),
            P(None, None, "fsdp"),
            P("fsdp", None),
            P("fsdp", None),
            P("fsdp"),
            P("ctx", "fsdp"),
            P("fsdp"),
        ),
        out_specs=(P("ctx", "fsdp"), P("ctx", "fsdp")),
        check_vma=False,
    )
```

```python
import jax
import jax.numpy as jnp
from jax import lax
from jax.experimental import pallas as pl
from jax.experimental.pallas import tpu as pltpu
from jax.sharding import PartitionSpec as P

CHANNELS_PER_GRP = 16
MODES = 16
CHUNK = 32
LANES = 128
WIDE = 256
GROUPS = LANES // CHANNELS_PER_GRP
VMEM_LIMIT = 16 * 1024 * 1024
F32 = jnp.float32
BF16 = jnp.bfloat16


def index_of(shape, dim):
    return lax.broadcasted_iota(jnp.int32, shape, dim)


def pipelined(count, *stages):
    held = {}
    for step in range(count + len(stages) - 1):
        for k, stage in enumerate(stages):
            item = step - k
            if 0 <= item < count:
                held[item] = stage(item, *held.get(item, ()))


def lanes_of(tile, width=LANES):
    return slice(tile * width, (tile + 1) * width)


def selectors(groups):
    shape = (groups, WIDE)
    found = []
    for tile in range(groups * CHANNELS_PER_GRP // WIDE):
        own = index_of(shape, 0) == index_of(shape, 1) // CHANNELS_PER_GRP + tile * (WIDE // CHANNELS_PER_GRP)
        found.append(jnp.where(own, 1.0, 0.0).astype(BF16))
    return found


def per_channel(table, chosen):
    high = table.astype(BF16)
    rest = table - high.astype(F32)
    middle = rest.astype(BF16)
    low = (rest - middle.astype(F32)).astype(BF16)
    terms = jnp.concatenate([high, middle, low], axis=0)
    parts = []
    for selector in chosen:
        three = jnp.dot(terms, selector, preferred_element_type=F32)
        parts.append(three[:MODES] + three[MODES : 2 * MODES] + three[2 * MODES :])
    return jnp.concatenate(parts, axis=1)


def mode_row(channel_table):
    own = index_of(channel_table.shape, 0) == (index_of(channel_table.shape, 1) & (MODES - 1))
    return jnp.sum(jnp.where(own, channel_table, 0.0), axis=0, keepdims=True)


def as_column(row):
    return jnp.transpose(jnp.broadcast_to(row, (LANES, LANES)))


def own_mode(dtype):
    shape = (GROUPS, MODES, LANES)
    own = index_of(shape, 0) * MODES + index_of(shape, 1) == index_of(shape, 2)
    return jnp.where(own, 1.0, 0.0).astype(dtype)


def split(x):
    high = x.astype(BF16)
    return high, (x - high.astype(F32)).astype(BF16)


def group_mask(dtype):
    shape = (GROUPS, MODES, LANES)
    own = index_of(shape, 0) == index_of(shape, 2) // CHANNELS_PER_GRP
    return jnp.where(own, 1.0, 0.0).astype(dtype)


def spread(rows, mask):
    size = rows.shape[0]
    copies = rows.reshape(1, size // MODES, MODES, LANES) * mask.reshape(GROUPS, 1, MODES, LANES)
    return copies.reshape(GROUPS * size, LANES)


def shifted(block, before):
    one = pltpu.roll(block, 1, 0)
    two = pltpu.roll(block, 2, 0)
    first = index_of((8, block.shape[1]), 0)
    near, far = (0.0, 0.0) if before is None else (before[1:2], before[0:1])
    head_one = jnp.where(first == 0, near, one[:8])
    head_two = jnp.where(first == 0, far, jnp.where(first == 1, near, two[:8]))
    if block.shape[0] == 8:
        return head_one, head_two
    return jnp.concatenate([head_one, one[8:]], axis=0), jnp.concatenate([head_two, two[8:]], axis=0)


def short_conv(block, before, weights):
    one, two = shifted(block, before)
    return weights[0] * block + weights[1] * one + weights[2] * two


def shift_matrix(rows):
    shape = (2 * rows, rows)
    target = index_of(shape, 0)
    source = index_of(shape, 1)
    taken = jnp.where(target < rows, target - 1, target - (rows + 2))
    return jnp.where(source == taken, 1.0, 0.0).astype(BF16)


def earlier_tokens(shift, block):
    return jnp.dot(shift, block, preferred_element_type=F32)


def wide_conv(block, earlier, weights):
    rows = block.shape[0]
    return weights[0] * block.astype(F32) + weights[1] * earlier[:rows] + weights[2] * earlier[rows:]


def taps_of(weights, feature, lanes):
    return [weights[tap, feature : feature + 1, lanes] for tap in range(weights.shape[0])]


def state_kernel(
    projected_ref,
    weight_hbm,
    rate_hbm,
    residue_hbm,
    residual_hbm,
    product_ref,
    state_ref,
    mode_rate_ref,
    head_ref,
    weight_ref,
    query_ref,
    residue_ref,
    residual_ref,
    buffer_ref,
    ending_ref,
    shift_ref,
    short_ref,
    rate_ref,
    sems,
    small_sems,
):
    rows, width = product_ref.shape
    wides = width // WIDE
    rate_copy = pltpu.make_async_copy(rate_hbm, rate_ref, small_sems.at[0])
    rate_copy.start()
    weight_copy = pltpu.make_async_copy(weight_hbm, short_ref, small_sems.at[1])
    weight_copy.start()
    copies = [pltpu.make_async_copy(projected_ref.at[1 + c], buffer_ref.at[c], sems.at[c]) for c in (0, 1)]
    later = [
        pltpu.make_async_copy(residue_hbm, residue_ref, sems.at[2]),
        pltpu.make_async_copy(projected_ref.at[0], query_ref, sems.at[3]),
        pltpu.make_async_copy(residual_hbm, residual_ref, sems.at[4]),
    ]
    for copy in copies:
        copy.start()
    shift_ref[...] = shift_matrix(rows)
    chosen = selectors(rate_ref.shape[1])
    eye = own_mode(BF16)
    mask = group_mask(F32)
    token = index_of((2 * LANES, rows), 1)
    left = jnp.where(token < 2, -1e30, (token - (rows - 1)).astype(F32)).astype(BF16)
    rate_copy.wait()
    mode_rate = per_channel(rate_ref[...], chosen)
    mode_rate_ref[...] = mode_rate

    def exponents(tile):
        high, low = split(mode_rate[:, lanes_of(tile)])
        diagonal = jnp.concatenate([spread(high, eye), spread(low, eye)], axis=1)
        return (jnp.dot(diagonal, left, preferred_element_type=F32),)

    def endings(tile, exponent):
        ending_ref[tile // 2, lanes_of(tile % 2), :] = jnp.exp(exponent).astype(BF16)

    pipelined(width // LANES, exponents, endings)
    weight_copy.wait()
    weights = short_ref[...].astype(F32)
    weight_ref[...] = weights
    for copy in copies:
        copy.wait()
    for copy in later:
        copy.start()

    def fetch(wide):
        return [earlier_tokens(shift_ref[...], buffer_ref[c, :, lanes_of(wide, WIDE)]) for c in (0, 1)]

    def multiply(wide, *earlier):
        here = lanes_of(wide, WIDE)
        parts = []
        for c in (0, 1):
            head_ref[c, :, here] = buffer_ref[c, 0:16, here].astype(F32)[:8]
            parts.append(wide_conv(buffer_ref[c, :, here], earlier[c], taps_of(weights, c + 1, here)))
        product = (parts[0] * parts[1]).astype(BF16)
        product_ref[:, here] = product
        return (jnp.dot(ending_ref[wide], product, preferred_element_type=F32),)

    def leave(wide, every):
        for half in range(WIDE // LANES):
            own = every[lanes_of(half), lanes_of(half)].reshape(GROUPS, MODES, LANES)
            state_ref[:, lanes_of((WIDE // LANES) * wide + half)] = jnp.sum(own * mask, axis=0)

    pipelined(wides, fetch, multiply, leave)
    for copy in later:
        copy.wait()


def halo(before_ref, place_ref):
    return jnp.where(place_ref[0] > 0, before_ref[...].astype(F32), 0.0)


def head_kernel(rows, place_ref, before_ref, head_ref, weight_ref, state_ref, mode_rate_ref, full_ref, first_ref):
    before = halo(before_ref, place_ref)
    everything = slice(0, head_ref.shape[2])
    parts = [short_conv(head_ref[c], before[c + 1], taps_of(weight_ref, c + 1, everything)) for c in (0, 1)]
    first = (parts[0] * parts[1]).astype(BF16).astype(F32)
    first_ref[...] = first
    rate = mode_rate_ref[...]
    early = jnp.exp(-float(rows - 1) * rate) * first[0:1] + jnp.exp(-float(rows - 2) * rate) * first[1:2]
    full_ref[...] = (state_ref[...] + early).astype(BF16)


def prepare_kernel(
    place_ref,
    query_ref,
    residue_ref,
    before_ref,
    weight_ref,
    mode_rate_ref,
    inner_ref,
    entering_ref,
    carry_ref,
    gate_ref,
    shift_ref,
):
    rows, width = gate_ref.shape
    shift_ref[...] = shift_matrix(rows)
    residue = per_channel(residue_ref[...], selectors(residue_ref.shape[1]))
    wide = GROUPS * CHUNK
    step = index_of((CHUNK, LANES), 0).astype(F32)
    causal = (index_of((CHUNK, wide), 1) & (CHUNK - 1)) <= index_of((CHUNK, wide), 0)
    eye = own_mode(BF16)
    flat_eye = jnp.where((index_of((MODES, LANES), 1) & (MODES - 1)) == index_of((MODES, LANES), 0), 1.0, 0.0)
    flat_eye = flat_eye.astype(BF16)
    shape = (2 * LANES, wide)
    source = (index_of(shape, 1) & (CHUNK - 1)).astype(F32)
    own = (index_of(shape, 0) & (LANES - 1)) // MODES == index_of(shape, 1) // CHUNK
    own_chunk = jnp.where(own[:LANES], 1.0, 0.0).astype(BF16)
    risen = source[:, :LANES].astype(BF16)
    left = jnp.where(own, source - (CHUNK - 1), 0.0).astype(BF16)

    def exponents(tile):
        rate = mode_rate_ref[:, lanes_of(tile)]
        high, low = split(rate)
        diagonal = jnp.concatenate([spread(high, eye), spread(low, eye)], axis=1)
        each = jnp.concatenate([high * flat_eye, low * flat_eye], axis=1)
        return (
            jnp.dot(diagonal, risen, preferred_element_type=F32),
            jnp.dot(each, left, preferred_element_type=F32),
        )

    def products(tile, rise, end):
        here = lanes_of(tile)
        rise_high, rise_low = [
            jnp.concatenate([part] * (wide // LANES), axis=1) * own_chunk for part in split(jnp.exp(rise))
        ]
        rate_row = mode_row(mode_rate_ref[:, here])
        falling = mode_row(residue[:, here]) * jnp.exp(-rate_row * step)
        fall_high, fall_low = split(falling)
        half = tile % (WIDE // LANES)
        for chunk in range(rows // CHUNK):
            entering = (falling * jnp.exp(-float(CHUNK * chunk + 1) * rate_row)).astype(BF16)
            carry_ref[tile // (WIDE // LANES), chunk * CHUNK : (chunk + 1) * CHUNK, lanes_of(half)] = entering
            if chunk == 0:
                entering_ref[tile] = entering
        return (
            jnp.dot(jnp.concatenate([fall_high, fall_low], axis=0), rise_high, preferred_element_type=F32),
            jnp.dot(fall_high, rise_low, preferred_element_type=F32),
            jnp.exp(end),
        )

    def finish(tile, taps, rest, ending):
        taps = jnp.where(causal, taps[:CHUNK] + taps[CHUNK:] + rest, 0.0)
        inner_ref[tile] = jnp.concatenate([taps.astype(BF16), ending.astype(BF16)], axis=0)

    pipelined(width // LANES, exponents, products, finish)
    before = halo(before_ref, place_ref)

    def fetch(part):
        return (earlier_tokens(shift_ref[...], query_ref[:, lanes_of(part, WIDE)]),)

    def convolve(part, earlier):
        here = lanes_of(part, WIDE)
        weights = taps_of(weight_ref, 0, here)
        gate_ref[:, here] = wide_conv(query_ref[:, here], earlier, weights)
        head = query_ref[0:16, here].astype(F32)[:8]
        gate_ref[0:8, here] = short_conv(head, before[0, :, here], weights)

    pipelined(width // WIDE, fetch, convolve)


def local_kernel(
    gate_ref,
    residual_ref,
    product_ref,
    first_ref,
    mode_rate_ref,
    inner_ref,
    entering_ref,
    skip_ref,
    base_ref,
):
    rows, width = product_ref.shape
    mask = group_mask(BF16)
    top = index_of((8, LANES), 0) < 2
    chunks = range(rows // CHUNK)

    def inside(tile):
        here = lanes_of(tile)
        pieces = []
        for chunk in chunks:
            piece = product_ref[chunk * CHUNK : (chunk + 1) * CHUNK, here]
            if chunk == 0:
                wide = piece.astype(F32)
                head = jnp.where(top, first_ref[:, here], wide[:8])
                piece = jnp.concatenate([head, wide[8:]], axis=0).astype(BF16)
            pieces.append(piece)
        found = []
        for pair in chunks[::2]:
            sources = jnp.concatenate([spread(pieces[pair + k], mask) for k in (0, 1)], axis=1)
            found.append(jnp.dot(inner_ref[tile], sources, preferred_element_type=F32))
        return found, pieces[0]

    def across(tile, inner, first):
        decay = jnp.exp(-float(CHUNK) * mode_rate_ref[:, lanes_of(tile)])
        state = jnp.zeros((MODES, LANES), F32)
        states = []
        for chunk in chunks:
            states.append(spread(state.astype(BF16), mask))
            state = decay * state + inner[chunk // 2][CHUNK:, lanes_of(chunk % 2)]
        outer = []
        for pair in chunks[::2]:
            two = jnp.concatenate(states[pair : pair + 2], axis=1)
            outer.append(jnp.dot(entering_ref[tile], two, preferred_element_type=F32))
        return [part[:CHUNK] for part in inner], outer, first

    def finish(tile, inner, outer, first):
        here = lanes_of(tile)
        skip = skip_ref[:, here]
        for chunk in chunks:
            span = slice(chunk * CHUNK, (chunk + 1) * CHUNK)
            piece = first if chunk == 0 else product_ref[span, here]
            conv = (inner[chunk // 2] + outer[chunk // 2])[:, lanes_of(chunk % 2)]
            whole = conv + skip * piece.astype(F32)
            base_ref[span, here] = residual_ref[span, here].astype(F32) + gate_ref[span, here] * whole

    pipelined(width // LANES, inside, across, finish)


def join_kernel(tokens, radix, stride, place_ref, own_ref, mode_rate_ref, entry_ref, *refs):
    others, (found_ref, group_ref) = refs[: radix - 1], refs[radix - 1 :]
    rate = mode_rate_ref[...]
    run = lax.rem(place_ref[0] // stride, radix)
    step = float(tokens * stride)

    def decayed(value, runs):
        return jnp.exp(-step * runs.astype(F32) * rate) * value

    found = jnp.zeros_like(rate)
    total = decayed(own_ref[...].astype(F32), radix - 1 - run)
    for k, ref in enumerate(others, 1):
        other = ref[...].astype(F32)
        source = partner(run, k, radix)
        found = found + jnp.where(source < run, decayed(other, jnp.maximum(run - 1 - source, 0)), 0.0)
        total = total + decayed(other, radix - 1 - source)
    within = lax.rem(place_ref[0], stride).astype(F32) * float(tokens)
    found_ref[...] = entry_ref[...] + jnp.exp(-within * rate) * found
    group_ref[...] = total.astype(BF16)


def carry_kernel(stride, radix, place_ref, base_ref, gate_ref, carry_ref, mode_rate_ref, inner_entry_ref, *refs):
    entry_refs, (summed_ref, squares_ref) = refs[:-2], refs[-2:]
    rows, width = base_ref.shape
    run = place_ref[0] // stride
    within = lax.rem(place_ref[0], stride).astype(F32) * float(rows)
    mask = group_mask(BF16)
    totals = [jnp.zeros((rows, LANES), F32)]
    nothing = jnp.zeros((LANES, LANES), BF16)

    def enter(tile):
        here = lanes_of(tile, WIDE)
        rate = mode_rate_ref[:, here]
        step = float(rows * stride)
        outer = jnp.zeros_like(rate)
        for k, ref in enumerate(entry_refs[::-1], 1):
            source = partner(run, k, radix)
            lag = jnp.maximum(run - 1 - source, 0).astype(F32) * step
            outer = outer + jnp.where(source < run, jnp.exp(-lag * rate) * ref[:, here].astype(F32), 0.0)
        entry = (inner_entry_ref[:, here] + jnp.exp(-within * rate) * outer).astype(BF16)
        left, right = spread(entry[:, :LANES], mask), spread(entry[:, LANES:], mask)
        both = jnp.concatenate(
            [jnp.concatenate([left, nothing], axis=1), jnp.concatenate([nothing, right], axis=1)], axis=0
        )
        return (jnp.dot(carry_ref[tile], both, preferred_element_type=F32),)

    def add(tile, carry):
        here = lanes_of(tile, WIDE)
        summed = base_ref[:, here] + gate_ref[:, here] * carry
        summed_ref[:, here] = summed
        square = summed * summed
        totals[0] = totals[0] + (square[:, :LANES] + square[:, LANES:])

    pipelined(width // WIDE, enter, add)
    total = totals[0]
    squares = lax.dot_general(
        jnp.ones((8, 2 * LANES), BF16),
        jnp.concatenate(split(total), axis=1),
        (((1,), (1,)), ((), ())),
        preferred_element_type=F32,
    )
    squares_ref[...] = squares[0:1]


def write_kernel(summed_ref, out_hbm, rounded_ref, sems):
    width = summed_ref.shape[1]
    copies = []
    for tile in range(width // WIDE):
        here = lanes_of(tile, WIDE)
        rounded_ref[:, here] = summed_ref[:, here].astype(BF16)
        span = pl.ds(tile * WIDE, WIDE)
        copies.append(pltpu.make_async_copy(rounded_ref.at[:, span], out_hbm.at[:, span], sems.at[tile]))
        copies[-1].start()
    for copy in copies:
        copy.wait()


def norm_kernel(full_width, summed_ref, gain_ref, *refs):
    squares_refs, (out_hbm, rounded_ref, sems) = refs[:-3], refs[-3:]
    rows, width = summed_ref.shape
    squares = squares_refs[0][...]
    for ref in squares_refs[1:]:
        squares = squares + ref[...]
    scale_row = lax.rsqrt(squares / full_width + 1e-05)
    scale = jnp.concatenate([as_column(scale_row[:, lanes_of(k)]) for k in range(rows // LANES)], axis=0)
    copies = []
    block = rows // 8
    for start in range(0, rows, block):
        span = slice(start, start + block)
        for tile in range(width // LANES):
            here = lanes_of(tile)
            rounded_ref[span, here] = (summed_ref[span, here] * scale[span] * gain_ref[:, here]).astype(BF16)
        there = pl.ds(start, block)
        copies.append(pltpu.make_async_copy(rounded_ref.at[there, :], out_hbm.at[there, :], sems.at[start // block]))
        copies[-1].start()
    for copy in copies:
        copy.wait()


def params():
    return pltpu.CompilerParams(vmem_limit_bytes=VMEM_LIMIT)


def cost(microseconds):
    return pl.CostEstimate(flops=0, bytes_accessed=int(microseconds * 3.0e6), transcendentals=0)


def radices(count):
    found = []
    for radix in (2, 4, 4, 4, 3, 2, 5, 7):
        if count % radix == 0:
            found.append(radix)
            count //= radix
    return found + ([count] if count > 1 else [])


def partner(run, k, radix):
    if radix & (radix - 1) == 0:
        return run ^ k
    return (run - k + radix) % radix


def routes(count, stride, radix):
    found = []
    for k in range(1, radix):
        route = []
        for i in range(count):
            run = i // stride % radix
            route.append((i + (partner(run, k, radix) - run) * stride, i))
        found.append(route)
    return found


def ring(count, shift):
    return [(i, (i + shift) % count) for i in range(count)]


def per_device(projected, short_weight, rates, residues, skip, residual, gain):
    rows, width = projected.shape[1:]
    taps = short_weight.shape[0]
    peers = lax.axis_size("ctx")
    full_width = width * lax.axis_size("fsdp")
    place = lax.axis_index("ctx").astype(jnp.int32).reshape(1)
    hbm_spec = pl.BlockSpec(memory_space=pltpu.HBM)
    vmem_spec = pl.BlockSpec(memory_space=pltpu.VMEM)
    smem_spec = pl.BlockSpec(memory_space=pltpu.SMEM)
    tiles = width // LANES
    wides = width // WIDE

    def kept(array):
        return pltpu.with_memory_space_constraint(array, pltpu.HBM)

    def f32(*shape):
        return jax.ShapeDtypeStruct(shape, F32)

    def bf16(*shape):
        return jax.ShapeDtypeStruct(shape, BF16)

    before = lax.ppermute(projected[:, rows - (taps - 1) :, :], "ctx", ring(peers, 1))

    product, state, mode_rate, head, weights, query, residue, residual_here = pl.pallas_call(
        state_kernel,
        in_specs=[hbm_spec] * 5,
        out_shape=[
            bf16(rows, width),
            f32(MODES, width),
            f32(MODES, width),
            f32(2, 8, width),
            f32(*short_weight.shape),
            bf16(rows, width),
            f32(MODES, residues.shape[0]),
            bf16(rows, width),
        ],
        scratch_shapes=[
            pltpu.VMEM((2, rows, width), BF16),
            pltpu.VMEM((wides, WIDE, rows), BF16),
            pltpu.VMEM((2 * rows, rows), BF16),
            pltpu.VMEM(short_weight.shape, BF16),
            pltpu.VMEM((MODES, rates.shape[0]), F32),
            pltpu.SemaphoreType.DMA((5,)),
            pltpu.SemaphoreType.DMA((2,)),
        ],
        compiler_params=params(),
        cost_estimate=cost(3),
        name="block_state",
    )(kept(projected), kept(short_weight), kept(rates.T), kept(residues.T), kept(residual))

    full_state, first = pl.pallas_call(
        lambda *refs: head_kernel(rows, *refs),
        in_specs=[smem_spec] + [vmem_spec] * 5,
        out_shape=[bf16(MODES, width), f32(8, width)],
        compiler_params=params(),
        cost_estimate=cost(0.2),
        name="head_tokens",
    )(place, before, head, weights, state, mode_rate)

    inner, entering, carry_table, gate = pl.pallas_call(
        prepare_kernel,
        in_specs=[smem_spec] + [vmem_spec] * 5,
        out_shape=[
            bf16(tiles, CHUNK + MODES, GROUPS * CHUNK),
            bf16(tiles, CHUNK, LANES),
            bf16(wides, rows, WIDE),
            f32(rows, width),
        ],
        scratch_shapes=[pltpu.VMEM((2 * rows, rows), BF16)],
        compiler_params=params(),
        cost_estimate=cost(2),
        name="prepare",
    )(place, query, residue, before, weights, mode_rate)

    group, entry, stride = full_state, jnp.zeros((MODES, width), F32), 1
    levels = radices(peers)
    for level, radix in enumerate(levels):
        size = stride * radix
        if level == len(levels) - 1:
            break
        others = [lax.ppermute(group, "ctx", route) for route in routes(peers, stride, radix)]
        if level == 0:
            others[0], inner = lax.optimization_barrier((others[0], inner))
        entry, group = pl.pallas_call(
            lambda *refs, radix=radix, stride=stride: join_kernel(rows, radix, stride, *refs),
            in_specs=[smem_spec] + [vmem_spec] * (2 + radix),
            out_shape=[f32(MODES, width), bf16(MODES, width)],
            compiler_params=params(),
            cost_estimate=cost(0.2),
            name="join",
        )(place, group, mode_rate, entry, *others)
        stride = size
    received = [lax.ppermute(group, "ctx", route) for route in routes(peers, stride, levels[-1])[::-1]]

    base = pl.pallas_call(
        local_kernel,
        out_shape=f32(rows, width),
        compiler_params=params(),
        cost_estimate=cost(5),
        name="local_conv",
    )(gate, residual_here, product, first, mode_rate, inner, entering, skip[None])

    count = lax.axis_size("fsdp")
    summed, squares = pl.pallas_call(
        lambda *refs: carry_kernel(stride, levels[-1], *refs),
        in_specs=[smem_spec] + [vmem_spec] * (5 + len(received)),
        out_shape=[f32(rows, width), f32(1, rows)],
        compiler_params=params(),
        cost_estimate=cost(1),
        name="add_carry",
    )(place, base, gate, carry_table, mode_rate, entry, *received)

    parts = [lax.ppermute(squares, "fsdp", route) for route in routes(count, 1, count)[::-1]]

    def write(kernel, operands, name):
        return pl.pallas_call(
            kernel,
            out_specs=hbm_spec,
            out_shape=bf16(rows, width),
            scratch_shapes=[pltpu.VMEM((rows, width), BF16), pltpu.SemaphoreType.DMA((max(8, wides),))],
            compiler_params=params(),
            cost_estimate=cost(1),
            name=name,
        )(*operands)

    new_residual = write(write_kernel, (summed,), "new_residual")
    normed = write(
        lambda *refs: norm_kernel(full_width, *refs), (summed, gain[None], squares, *parts), "normed"
    )
    return (new_residual, normed)


def solution(mesh):
    return jax.shard_map(
        per_device,
        mesh=mesh,
        in_specs=(
            P(None, "ctx", "fsdp"),
            P(None, None, "fsdp"),
            P("fsdp", None),
            P("fsdp", None),
            P("fsdp"),
            P("ctx", "fsdp"),
            P("fsdp"),
        ),
        out_specs=(P("ctx", "fsdp"), P("ctx", "fsdp")),
        check_vma=False,
    )
```

```python
import jax
import jax.numpy as jnp
from jax import lax
from jax.experimental import pallas as pl
from jax.experimental.pallas import tpu as pltpu
from jax.sharding import PartitionSpec as P

CHANNELS_PER_GRP = 16
MODES = 16
CHUNK = 32
LANES = 128
WIDE = 256
GROUPS = LANES // CHANNELS_PER_GRP
VMEM_LIMIT = 16 * 1024 * 1024
F32 = jnp.float32
BF16 = jnp.bfloat16


def index_of(shape, dim):
    return lax.broadcasted_iota(jnp.int32, shape, dim)


def pipelined(count, *stages):
    held = {}
    for step in range(count + len(stages) - 1):
        for k, stage in enumerate(stages):
            item = step - k
            if 0 <= item < count:
                held[item] = stage(item, *held.get(item, ()))


def lanes_of(tile, width=LANES):
    return slice(tile * width, (tile + 1) * width)


def selectors(groups):
    shape = (groups, WIDE)
    found = []
    for tile in range(groups * CHANNELS_PER_GRP // WIDE):
        own = index_of(shape, 0) == index_of(shape, 1) // CHANNELS_PER_GRP + tile * (WIDE // CHANNELS_PER_GRP)
        found.append(jnp.where(own, 1.0, 0.0).astype(BF16))
    return found


def per_channel(table, chosen):
    high = table.astype(BF16)
    rest = table - high.astype(F32)
    middle = rest.astype(BF16)
    low = (rest - middle.astype(F32)).astype(BF16)
    terms = jnp.concatenate([high, middle, low], axis=0)
    parts = []
    for selector in chosen:
        three = jnp.dot(terms, selector, preferred_element_type=F32)
        parts.append(three[:MODES] + three[MODES : 2 * MODES] + three[2 * MODES :])
    return jnp.concatenate(parts, axis=1)


def mode_row(channel_table):
    own = index_of(channel_table.shape, 0) == (index_of(channel_table.shape, 1) & (MODES - 1))
    return jnp.sum(jnp.where(own, channel_table, 0.0), axis=0, keepdims=True)


def as_column(row):
    return jnp.transpose(jnp.broadcast_to(row, (LANES, LANES)))


def own_mode(dtype):
    shape = (GROUPS, MODES, LANES)
    own = index_of(shape, 0) * MODES + index_of(shape, 1) == index_of(shape, 2)
    return jnp.where(own, 1.0, 0.0).astype(dtype)


def split(x):
    high = x.astype(BF16)
    return high, (x - high.astype(F32)).astype(BF16)


def group_mask(dtype):
    shape = (GROUPS, MODES, LANES)
    own = index_of(shape, 0) == index_of(shape, 2) // CHANNELS_PER_GRP
    return jnp.where(own, 1.0, 0.0).astype(dtype)


def spread(rows, mask):
    size = rows.shape[0]
    copies = rows.reshape(1, size // MODES, MODES, LANES) * mask.reshape(GROUPS, 1, MODES, LANES)
    return copies.reshape(GROUPS * size, LANES)


def shifted(block, before):
    one = pltpu.roll(block, 1, 0)
    two = pltpu.roll(block, 2, 0)
    first = index_of((8, block.shape[1]), 0)
    near, far = (0.0, 0.0) if before is None else (before[1:2], before[0:1])
    head_one = jnp.where(first == 0, near, one[:8])
    head_two = jnp.where(first == 0, far, jnp.where(first == 1, near, two[:8]))
    if block.shape[0] == 8:
        return head_one, head_two
    return jnp.concatenate([head_one, one[8:]], axis=0), jnp.concatenate([head_two, two[8:]], axis=0)


def short_conv(block, before, weights):
    one, two = shifted(block, before)
    return weights[0] * block + weights[1] * one + weights[2] * two


def shift_matrix(rows):
    shape = (2 * rows, rows)
    target = index_of(shape, 0)
    source = index_of(shape, 1)
    taken = jnp.where(target < rows, target - 1, target - (rows + 2))
    return jnp.where(source == taken, 1.0, 0.0).astype(BF16)


def earlier_tokens(shift, block):
    return jnp.dot(shift, block, preferred_element_type=F32)


def wide_conv(block, earlier, weights):
    rows = block.shape[0]
    return weights[0] * block.astype(F32) + weights[1] * earlier[:rows] + weights[2] * earlier[rows:]


def taps_of(weights, feature, lanes):
    return [weights[tap, feature : feature + 1, lanes] for tap in range(weights.shape[0])]


def state_kernel(
    projected_ref,
    weight_hbm,
    rate_hbm,
    residue_hbm,
    residual_hbm,
    product_ref,
    state_ref,
    mode_rate_ref,
    head_ref,
    weight_ref,
    query_ref,
    residue_ref,
    residual_ref,
    buffer_ref,
    ending_ref,
    shift_ref,
    short_ref,
    rate_ref,
    sems,
    small_sems,
):
    rows, width = product_ref.shape
    wides = width // WIDE
    rate_copy = pltpu.make_async_copy(rate_hbm, rate_ref, small_sems.at[0])
    rate_copy.start()
    weight_copy = pltpu.make_async_copy(weight_hbm, short_ref, small_sems.at[1])
    weight_copy.start()
    copies = [pltpu.make_async_copy(projected_ref.at[1 + c], buffer_ref.at[c], sems.at[c]) for c in (0, 1)]
    later = [
        pltpu.make_async_copy(residue_hbm, residue_ref, sems.at[2]),
        pltpu.make_async_copy(projected_ref.at[0], query_ref, sems.at[3]),
        pltpu.make_async_copy(residual_hbm, residual_ref, sems.at[4]),
    ]
    for copy in copies:
        copy.start()
    shift_ref[...] = shift_matrix(rows)
    chosen = selectors(rate_ref.shape[1])
    eye = own_mode(BF16)
    mask = group_mask(F32)
    token = index_of((2 * LANES, rows), 1)
    left = jnp.where(token < 2, -1e30, (token - (rows - 1)).astype(F32)).astype(BF16)
    rate_copy.wait()
    mode_rate = per_channel(rate_ref[...], chosen)
    mode_rate_ref[...] = mode_rate

    def exponents(tile):
        high, low = split(mode_rate[:, lanes_of(tile)])
        diagonal = jnp.concatenate([spread(high, eye), spread(low, eye)], axis=1)
        return (jnp.dot(diagonal, left, preferred_element_type=F32),)

    def endings(tile, exponent):
        ending_ref[tile // 2, lanes_of(tile % 2), :] = jnp.exp(exponent).astype(BF16)

    pipelined(width // LANES, exponents, endings)
    weight_copy.wait()
    weights = short_ref[...].astype(F32)
    weight_ref[...] = weights
    for copy in copies:
        copy.wait()
    for copy in later:
        copy.start()

    def fetch(wide):
        return [earlier_tokens(shift_ref[...], buffer_ref[c, :, lanes_of(wide, WIDE)]) for c in (0, 1)]

    def multiply(wide, *earlier):
        here = lanes_of(wide, WIDE)
        parts = []
        for c in (0, 1):
            head_ref[c, :, here] = buffer_ref[c, 0:16, here].astype(F32)[:8]
            parts.append(wide_conv(buffer_ref[c, :, here], earlier[c], taps_of(weights, c + 1, here)))
        product = (parts[0] * parts[1]).astype(BF16)
        product_ref[:, here] = product
        return (jnp.dot(ending_ref[wide], product, preferred_element_type=F32),)

    def leave(wide, every):
        for half in range(WIDE // LANES):
            own = every[lanes_of(half), lanes_of(half)].reshape(GROUPS, MODES, LANES)
            state_ref[:, lanes_of((WIDE // LANES) * wide + half)] = jnp.sum(own * mask, axis=0)

    pipelined(wides, fetch, multiply, leave)
    for copy in later:
        copy.wait()


def halo(before_ref, place_ref):
    return jnp.where(place_ref[0] > 0, before_ref[...].astype(F32), 0.0)


def head_kernel(rows, place_ref, before_ref, head_ref, weight_ref, state_ref, mode_rate_ref, full_ref, first_ref):
    before = halo(before_ref, place_ref)
    everything = slice(0, head_ref.shape[2])
    parts = [short_conv(head_ref[c], before[c + 1], taps_of(weight_ref, c + 1, everything)) for c in (0, 1)]
    first = (parts[0] * parts[1]).astype(BF16).astype(F32)
    first_ref[...] = first
    rate = mode_rate_ref[...]
    early = jnp.exp(-float(rows - 1) * rate) * first[0:1] + jnp.exp(-float(rows - 2) * rate) * first[1:2]
    full_ref[...] = (state_ref[...] + early).astype(BF16)


def prepare_kernel(
    place_ref,
    query_ref,
    residue_ref,
    before_ref,
    weight_ref,
    mode_rate_ref,
    inner_ref,
    entering_ref,
    carry_ref,
    gate_ref,
    shift_ref,
):
    rows, width = gate_ref.shape
    shift_ref[...] = shift_matrix(rows)
    residue = per_channel(residue_ref[...], selectors(residue_ref.shape[1]))
    wide = GROUPS * CHUNK
    step = index_of((CHUNK, LANES), 0).astype(F32)
    causal = (index_of((CHUNK, wide), 1) & (CHUNK - 1)) <= index_of((CHUNK, wide), 0)
    eye = own_mode(BF16)
    flat_eye = jnp.where((index_of((MODES, LANES), 1) & (MODES - 1)) == index_of((MODES, LANES), 0), 1.0, 0.0)
    flat_eye = flat_eye.astype(BF16)
    shape = (2 * LANES, wide)
    source = (index_of(shape, 1) & (CHUNK - 1)).astype(F32)
    own = (index_of(shape, 0) & (LANES - 1)) // MODES == index_of(shape, 1) // CHUNK
    own_chunk = jnp.where(own[:LANES], 1.0, 0.0).astype(BF16)
    risen = source[:, :LANES].astype(BF16)
    left = jnp.where(own, source - (CHUNK - 1), 0.0).astype(BF16)

    def exponents(tile):
        rate = mode_rate_ref[:, lanes_of(tile)]
        high, low = split(rate)
        diagonal = jnp.concatenate([spread(high, eye), spread(low, eye)], axis=1)
        each = jnp.concatenate([high * flat_eye, low * flat_eye], axis=1)
        return (
            jnp.dot(diagonal, risen, preferred_element_type=F32),
            jnp.dot(each, left, preferred_element_type=F32),
        )

    def products(tile, rise, end):
        here = lanes_of(tile)
        rise_high, rise_low = [
            jnp.concatenate([part] * (wide // LANES), axis=1) * own_chunk for part in split(jnp.exp(rise))
        ]
        rate_row = mode_row(mode_rate_ref[:, here])
        falling = mode_row(residue[:, here]) * jnp.exp(-rate_row * step)
        fall_high, fall_low = split(falling)
        half = tile % (WIDE // LANES)
        for chunk in range(rows // CHUNK):
            entering = (falling * jnp.exp(-float(CHUNK * chunk + 1) * rate_row)).astype(BF16)
            carry_ref[tile // (WIDE // LANES), chunk * CHUNK : (chunk + 1) * CHUNK, lanes_of(half)] = entering
            if chunk == 0:
                entering_ref[tile] = entering
        return (
            jnp.dot(jnp.concatenate([fall_high, fall_low], axis=0), rise_high, preferred_element_type=F32),
            jnp.dot(fall_high, rise_low, preferred_element_type=F32),
            jnp.exp(end),
        )

    def finish(tile, taps, rest, ending):
        taps = jnp.where(causal, taps[:CHUNK] + taps[CHUNK:] + rest, 0.0)
        inner_ref[tile] = jnp.concatenate([taps.astype(BF16), ending.astype(BF16)], axis=0)

    pipelined(width // LANES, exponents, products, finish)
    before = halo(before_ref, place_ref)

    def fetch(part):
        return (earlier_tokens(shift_ref[...], query_ref[:, lanes_of(part, WIDE)]),)

    def convolve(part, earlier):
        here = lanes_of(part, WIDE)
        weights = taps_of(weight_ref, 0, here)
        gate_ref[:, here] = wide_conv(query_ref[:, here], earlier, weights)
        head = query_ref[0:16, here].astype(F32)[:8]
        gate_ref[0:8, here] = short_conv(head, before[0, :, here], weights)

    pipelined(width // WIDE, fetch, convolve)


def local_kernel(
    gate_ref,
    residual_ref,
    product_ref,
    first_ref,
    mode_rate_ref,
    inner_ref,
    entering_ref,
    skip_ref,
    base_ref,
):
    rows, width = product_ref.shape
    mask = group_mask(BF16)
    top = index_of((8, LANES), 0) < 2
    chunks = range(rows // CHUNK)

    def inside(tile):
        here = lanes_of(tile)
        pieces = []
        for chunk in chunks:
            piece = product_ref[chunk * CHUNK : (chunk + 1) * CHUNK, here]
            if chunk == 0:
                wide = piece.astype(F32)
                head = jnp.where(top, first_ref[:, here], wide[:8])
                piece = jnp.concatenate([head, wide[8:]], axis=0).astype(BF16)
            pieces.append(piece)
        found = []
        for pair in chunks[::2]:
            sources = jnp.concatenate([spread(pieces[pair + k], mask) for k in (0, 1)], axis=1)
            found.append(jnp.dot(inner_ref[tile], sources, preferred_element_type=F32))
        return found, pieces[0]

    def across(tile, inner, first):
        decay = jnp.exp(-float(CHUNK) * mode_rate_ref[:, lanes_of(tile)])
        state = jnp.zeros((MODES, LANES), F32)
        states = []
        for chunk in chunks:
            states.append(spread(state.astype(BF16), mask))
            state = decay * state + inner[chunk // 2][CHUNK:, lanes_of(chunk % 2)]
        outer = []
        for pair in chunks[::2]:
            two = jnp.concatenate(states[pair : pair + 2], axis=1)
            outer.append(jnp.dot(entering_ref[tile], two, preferred_element_type=F32))
        return [part[:CHUNK] for part in inner], outer, first

    def finish(tile, inner, outer, first):
        here = lanes_of(tile)
        skip = skip_ref[:, here]
        for chunk in chunks:
            span = slice(chunk * CHUNK, (chunk + 1) * CHUNK)
            piece = first if chunk == 0 else product_ref[span, here]
            conv = (inner[chunk // 2] + outer[chunk // 2])[:, lanes_of(chunk % 2)]
            whole = conv + skip * piece.astype(F32)
            base_ref[span, here] = residual_ref[span, here].astype(F32) + gate_ref[span, here] * whole

    pipelined(width // LANES, inside, across, finish)


def join_kernel(tokens, radix, stride, place_ref, own_ref, mode_rate_ref, entry_ref, *refs):
    others, (found_ref, group_ref) = refs[: radix - 1], refs[radix - 1 :]
    rate = mode_rate_ref[...]
    run = lax.rem(place_ref[0] // stride, radix)
    step = float(tokens * stride)

    def decayed(value, runs):
        return jnp.exp(-step * runs.astype(F32) * rate) * value

    found = jnp.zeros_like(rate)
    total = decayed(own_ref[...].astype(F32), radix - 1 - run)
    for k, ref in enumerate(others[::-1], 1):
        other = ref[...].astype(F32)
        source = partner(run, k, radix)
        found = found + jnp.where(source < run, decayed(other, jnp.maximum(run - 1 - source, 0)), 0.0)
        total = total + decayed(other, radix - 1 - source)
    within = lax.rem(place_ref[0], stride).astype(F32) * float(tokens)
    found_ref[...] = entry_ref[...] + jnp.exp(-within * rate) * found
    group_ref[...] = total.astype(BF16)


def carry_kernel(stride, radix, place_ref, base_ref, gate_ref, carry_ref, mode_rate_ref, inner_entry_ref, *refs):
    entry_refs, (summed_ref, squares_ref) = refs[:-2], refs[-2:]
    rows, width = base_ref.shape
    run = place_ref[0] // stride
    within = lax.rem(place_ref[0], stride).astype(F32) * float(rows)
    mask = group_mask(BF16)
    totals = [jnp.zeros((rows, LANES), F32)]
    nothing = jnp.zeros((LANES, LANES), BF16)

    def enter(tile):
        here = lanes_of(tile, WIDE)
        rate = mode_rate_ref[:, here]
        step = float(rows * stride)
        outer = jnp.zeros_like(rate)
        for k, ref in enumerate(entry_refs[::-1], 1):
            source = partner(run, k, radix)
            lag = jnp.maximum(run - 1 - source, 0).astype(F32) * step
            outer = outer + jnp.where(source < run, jnp.exp(-lag * rate) * ref[:, here].astype(F32), 0.0)
        entry = (inner_entry_ref[:, here] + jnp.exp(-within * rate) * outer).astype(BF16)
        left, right = spread(entry[:, :LANES], mask), spread(entry[:, LANES:], mask)
        both = jnp.concatenate(
            [jnp.concatenate([left, nothing], axis=1), jnp.concatenate([nothing, right], axis=1)], axis=0
        )
        return (jnp.dot(carry_ref[tile], both, preferred_element_type=F32),)

    def add(tile, carry):
        here = lanes_of(tile, WIDE)
        summed = base_ref[:, here] + gate_ref[:, here] * carry
        summed_ref[:, here] = summed
        square = summed * summed
        totals[0] = totals[0] + (square[:, :LANES] + square[:, LANES:])

    pipelined(width // WIDE, enter, add)
    total = totals[0]
    squares = lax.dot_general(
        jnp.ones((8, 2 * LANES), BF16),
        jnp.concatenate(split(total), axis=1),
        (((1,), (1,)), ((), ())),
        preferred_element_type=F32,
    )
    squares_ref[...] = squares[0:1]


def write_kernel(summed_ref, out_hbm, rounded_ref, sems):
    width = summed_ref.shape[1]
    copies = []
    for tile in range(width // WIDE):
        here = lanes_of(tile, WIDE)
        rounded_ref[:, here] = summed_ref[:, here].astype(BF16)
        span = pl.ds(tile * WIDE, WIDE)
        copies.append(pltpu.make_async_copy(rounded_ref.at[:, span], out_hbm.at[:, span], sems.at[tile]))
        copies[-1].start()
    for copy in copies:
        copy.wait()


def norm_kernel(full_width, summed_ref, gain_ref, *refs):
    squares_refs, (out_hbm, rounded_ref, sems) = refs[:-3], refs[-3:]
    rows, width = summed_ref.shape
    squares = squares_refs[0][...]
    for ref in squares_refs[1:]:
        squares = squares + ref[...]
    scale_row = lax.rsqrt(squares / full_width + 1e-05)
    scale = jnp.concatenate([as_column(scale_row[:, lanes_of(k)]) for k in range(rows // LANES)], axis=0)
    copies = []
    block = rows // 8
    for start in range(0, rows, block):
        span = slice(start, start + block)
        for tile in range(width // LANES):
            here = lanes_of(tile)
            rounded_ref[span, here] = (summed_ref[span, here] * scale[span] * gain_ref[:, here]).astype(BF16)
        there = pl.ds(start, block)
        copies.append(pltpu.make_async_copy(rounded_ref.at[there, :], out_hbm.at[there, :], sems.at[start // block]))
        copies[-1].start()
    for copy in copies:
        copy.wait()


def params():
    return pltpu.CompilerParams(vmem_limit_bytes=VMEM_LIMIT)


def cost(microseconds):
    return pl.CostEstimate(flops=0, bytes_accessed=int(microseconds * 3.0e6), transcendentals=0)


def radices(count):
    found = []
    for radix in (4, 4, 4, 3, 3, 2, 5, 7):
        if count % radix == 0:
            found.append(radix)
            count //= radix
    return found + ([count] if count > 1 else [])


def partner(run, k, radix):
    if radix & (radix - 1) == 0:
        return run ^ k
    return (run - k + radix) % radix


def routes(count, stride, radix):
    found = []
    for k in range(1, radix):
        route = []
        for i in range(count):
            run = i // stride % radix
            route.append((i + (partner(run, k, radix) - run) * stride, i))
        found.append(route)
    return found


def ring(count, shift):
    return [(i, (i + shift) % count) for i in range(count)]


def per_device(projected, short_weight, rates, residues, skip, residual, gain):
    rows, width = projected.shape[1:]
    taps = short_weight.shape[0]
    peers = lax.axis_size("ctx")
    full_width = width * lax.axis_size("fsdp")
    place = lax.axis_index("ctx").astype(jnp.int32).reshape(1)
    hbm_spec = pl.BlockSpec(memory_space=pltpu.HBM)
    vmem_spec = pl.BlockSpec(memory_space=pltpu.VMEM)
    smem_spec = pl.BlockSpec(memory_space=pltpu.SMEM)
    tiles = width // LANES
    wides = width // WIDE

    def kept(array):
        return pltpu.with_memory_space_constraint(array, pltpu.HBM)

    def f32(*shape):
        return jax.ShapeDtypeStruct(shape, F32)

    def bf16(*shape):
        return jax.ShapeDtypeStruct(shape, BF16)

    before = lax.ppermute(projected[:, rows - (taps - 1) :, :], "ctx", ring(peers, 1))

    product, state, mode_rate, head, weights, query, residue, residual_here = pl.pallas_call(
        state_kernel,
        in_specs=[hbm_spec] * 5,
        out_shape=[
            bf16(rows, width),
            f32(MODES, width),
            f32(MODES, width),
            f32(2, 8, width),
            f32(*short_weight.shape),
            bf16(rows, width),
            f32(MODES, residues.shape[0]),
            bf16(rows, width),
        ],
        scratch_shapes=[
            pltpu.VMEM((2, rows, width), BF16),
            pltpu.VMEM((wides, WIDE, rows), BF16),
            pltpu.VMEM((2 * rows, rows), BF16),
            pltpu.VMEM(short_weight.shape, BF16),
            pltpu.VMEM((MODES, rates.shape[0]), F32),
            pltpu.SemaphoreType.DMA((5,)),
            pltpu.SemaphoreType.DMA((2,)),
        ],
        compiler_params=params(),
        cost_estimate=cost(3),
        name="block_state",
    )(kept(projected), kept(short_weight), kept(rates.T), kept(residues.T), kept(residual))

    full_state, first = pl.pallas_call(
        lambda *refs: head_kernel(rows, *refs),
        in_specs=[smem_spec] + [vmem_spec] * 5,
        out_shape=[bf16(MODES, width), f32(8, width)],
        compiler_params=params(),
        cost_estimate=cost(0.2),
        name="head_tokens",
    )(place, before, head, weights, state, mode_rate)

    inner, entering, carry_table, gate = pl.pallas_call(
        prepare_kernel,
        in_specs=[smem_spec] + [vmem_spec] * 5,
        out_shape=[
            bf16(tiles, CHUNK + MODES, GROUPS * CHUNK),
            bf16(tiles, CHUNK, LANES),
            bf16(wides, rows, WIDE),
            f32(rows, width),
        ],
        scratch_shapes=[pltpu.VMEM((2 * rows, rows), BF16)],
        compiler_params=params(),
        cost_estimate=cost(2),
        name="prepare",
    )(place, query, residue, before, weights, mode_rate)

    group, entry, stride = full_state, jnp.zeros((MODES, width), F32), 1
    levels = radices(peers)
    for level, radix in enumerate(levels):
        size = stride * radix
        if level == len(levels) - 1:
            break
        others = [lax.ppermute(group, "ctx", route) for route in routes(peers, stride, radix)[::-1]]
        if level == 0:
            others[0], inner = lax.optimization_barrier((others[0], inner))
        entry, group = pl.pallas_call(
            lambda *refs, radix=radix, stride=stride: join_kernel(rows, radix, stride, *refs),
            in_specs=[smem_spec] + [vmem_spec] * (2 + radix),
            out_shape=[f32(MODES, width), bf16(MODES, width)],
            compiler_params=params(),
            cost_estimate=cost(0.2),
            name="join",
        )(place, group, mode_rate, entry, *others)
        stride = size
    received = [lax.ppermute(group, "ctx", route) for route in routes(peers, stride, levels[-1])[::-1]]

    base = pl.pallas_call(
        local_kernel,
        out_shape=f32(rows, width),
        compiler_params=params(),
        cost_estimate=cost(5),
        name="local_conv",
    )(gate, residual_here, product, first, mode_rate, inner, entering, skip[None])

    count = lax.axis_size("fsdp")
    summed, squares = pl.pallas_call(
        lambda *refs: carry_kernel(stride, levels[-1], *refs),
        in_specs=[smem_spec] + [vmem_spec] * (5 + len(received)),
        out_shape=[f32(rows, width), f32(1, rows)],
        compiler_params=params(),
        cost_estimate=cost(1),
        name="add_carry",
    )(place, base, gate, carry_table, mode_rate, entry, *received)

    parts = [lax.ppermute(squares, "fsdp", route) for route in routes(count, 1, count)[::-1]]

    def write(kernel, operands, name):
        return pl.pallas_call(
            kernel,
            out_specs=hbm_spec,
            out_shape=bf16(rows, width),
            scratch_shapes=[pltpu.VMEM((rows, width), BF16), pltpu.SemaphoreType.DMA((max(8, wides),))],
            compiler_params=params(),
            cost_estimate=cost(1),
            name=name,
        )(*operands)

    new_residual = write(write_kernel, (summed,), "new_residual")
    normed = write(
        lambda *refs: norm_kernel(full_width, *refs), (summed, gain[None], squares, *parts), "normed"
    )
    return (new_residual, normed)


def solution(mesh):
    return jax.shard_map(
        per_device,
        mesh=mesh,
        in_specs=(
            P(None, "ctx", "fsdp"),
            P(None, None, "fsdp"),
            P("fsdp", None),
            P("fsdp", None),
            P("fsdp"),
            P("ctx", "fsdp"),
            P("fsdp"),
        ),
        out_specs=(P("ctx", "fsdp"), P("ctx", "fsdp")),
        check_vma=False,
    )
```

```python
import jax
import jax.numpy as jnp
from jax import lax
from jax.experimental import pallas as pl
from jax.experimental.pallas import tpu as pltpu
from jax.sharding import PartitionSpec as P

CHANNELS_PER_GRP = 16
MODES = 16
CHUNK = 32
LANES = 128
WIDE = 256
GROUPS = LANES // CHANNELS_PER_GRP
VMEM_LIMIT = 16 * 1024 * 1024
F32 = jnp.float32
BF16 = jnp.bfloat16


def index_of(shape, dim):
    return lax.broadcasted_iota(jnp.int32, shape, dim)


def pipelined(count, *stages):
    held = {}
    for step in range(count + len(stages) - 1):
        for k, stage in enumerate(stages):
            item = step - k
            if 0 <= item < count:
                held[item] = stage(item, *held.get(item, ()))


def lanes_of(tile, width=LANES):
    return slice(tile * width, (tile + 1) * width)


def selectors(groups):
    shape = (groups, WIDE)
    found = []
    for tile in range(groups * CHANNELS_PER_GRP // WIDE):
        own = index_of(shape, 0) == index_of(shape, 1) // CHANNELS_PER_GRP + tile * (WIDE // CHANNELS_PER_GRP)
        found.append(jnp.where(own, 1.0, 0.0).astype(BF16))
    return found


def per_channel(table, chosen):
    high = table.astype(BF16)
    rest = table - high.astype(F32)
    middle = rest.astype(BF16)
    low = (rest - middle.astype(F32)).astype(BF16)
    terms = jnp.concatenate([high, middle, low], axis=0)
    parts = []
    for selector in chosen:
        three = jnp.dot(terms, selector, preferred_element_type=F32)
        parts.append(three[:MODES] + three[MODES : 2 * MODES] + three[2 * MODES :])
    return jnp.concatenate(parts, axis=1)


def mode_row(channel_table):
    own = index_of(channel_table.shape, 0) == (index_of(channel_table.shape, 1) & (MODES - 1))
    return jnp.sum(jnp.where(own, channel_table, 0.0), axis=0, keepdims=True)


def as_column(row):
    return jnp.transpose(jnp.broadcast_to(row, (LANES, LANES)))


def own_mode(dtype):
    shape = (GROUPS, MODES, LANES)
    own = index_of(shape, 0) * MODES + index_of(shape, 1) == index_of(shape, 2)
    return jnp.where(own, 1.0, 0.0).astype(dtype)


def split(x):
    high = x.astype(BF16)
    return high, (x - high.astype(F32)).astype(BF16)


def group_mask(dtype):
    shape = (GROUPS, MODES, LANES)
    own = index_of(shape, 0) == index_of(shape, 2) // CHANNELS_PER_GRP
    return jnp.where(own, 1.0, 0.0).astype(dtype)


def spread(rows, mask):
    size = rows.shape[0]
    copies = rows.reshape(1, size // MODES, MODES, LANES) * mask.reshape(GROUPS, 1, MODES, LANES)
    return copies.reshape(GROUPS * size, LANES)


def shifted(block, before):
    one = pltpu.roll(block, 1, 0)
    two = pltpu.roll(block, 2, 0)
    first = index_of((8, block.shape[1]), 0)
    near, far = (0.0, 0.0) if before is None else (before[1:2], before[0:1])
    head_one = jnp.where(first == 0, near, one[:8])
    head_two = jnp.where(first == 0, far, jnp.where(first == 1, near, two[:8]))
    if block.shape[0] == 8:
        return head_one, head_two
    return jnp.concatenate([head_one, one[8:]], axis=0), jnp.concatenate([head_two, two[8:]], axis=0)


def short_conv(block, before, weights):
    one, two = shifted(block, before)
    return weights[0] * block + weights[1] * one + weights[2] * two


def shift_matrix(rows):
    shape = (2 * rows, rows)
    target = index_of(shape, 0)
    source = index_of(shape, 1)
    taken = jnp.where(target < rows, target - 1, target - (rows + 2))
    return jnp.where(source == taken, 1.0, 0.0).astype(BF16)


def earlier_tokens(shift, block):
    return jnp.dot(shift, block, preferred_element_type=F32)


def wide_conv(block, earlier, weights):
    rows = block.shape[0]
    wide = block.astype(F32)
    if earlier.shape[0] == rows:
        one = pltpu.roll(wide, 1, 0)
        head = jnp.where(index_of((8, wide.shape[1]), 0) == 0, 0.0, one[:8])
        one = jnp.concatenate([head, one[8:]], axis=0)
    else:
        one = earlier[:rows]
    return weights[0] * wide + weights[1] * one + weights[2] * earlier[-rows:]


def taps_of(weights, feature, lanes):
    return [weights[tap, feature : feature + 1, lanes] for tap in range(weights.shape[0])]


def state_kernel(
    projected_ref,
    weight_hbm,
    rate_hbm,
    residue_hbm,
    residual_hbm,
    product_ref,
    state_ref,
    mode_rate_ref,
    head_ref,
    weight_ref,
    query_ref,
    residue_ref,
    residual_ref,
    buffer_ref,
    ending_ref,
    shift_ref,
    short_ref,
    rate_ref,
    sems,
    small_sems,
):
    rows, width = product_ref.shape
    wides = width // WIDE
    rate_copy = pltpu.make_async_copy(rate_hbm, rate_ref, small_sems.at[0])
    rate_copy.start()
    weight_copy = pltpu.make_async_copy(weight_hbm, short_ref, small_sems.at[1])
    weight_copy.start()
    copies = [pltpu.make_async_copy(projected_ref.at[1 + c], buffer_ref.at[c], sems.at[c]) for c in (0, 1)]
    later = [
        pltpu.make_async_copy(residue_hbm, residue_ref, sems.at[2]),
        pltpu.make_async_copy(projected_ref.at[0], query_ref, sems.at[3]),
        pltpu.make_async_copy(residual_hbm, residual_ref, sems.at[4]),
    ]
    for copy in copies:
        copy.start()
    shift_ref[...] = shift_matrix(rows)
    chosen = selectors(rate_ref.shape[1])
    eye = own_mode(BF16)
    mask = group_mask(F32)
    token = index_of((2 * LANES, rows), 1)
    left = jnp.where(token < 2, -1e30, (token - (rows - 1)).astype(F32)).astype(BF16)
    rate_copy.wait()
    mode_rate = per_channel(rate_ref[...], chosen)
    mode_rate_ref[...] = mode_rate

    def exponents(tile):
        high, low = split(mode_rate[:, lanes_of(tile)])
        diagonal = jnp.concatenate([spread(high, eye), spread(low, eye)], axis=1)
        return (jnp.dot(diagonal, left, preferred_element_type=F32),)

    def endings(tile, exponent):
        ending_ref[tile // 2, lanes_of(tile % 2), :] = jnp.exp(exponent).astype(BF16)

    pipelined(width // LANES, exponents, endings)
    weight_copy.wait()
    weights = short_ref[...].astype(F32)
    weight_ref[...] = weights
    for copy in copies:
        copy.wait()
    for copy in later:
        copy.start()

    def fetch(wide):
        here = lanes_of(wide, WIDE)
        return (
            earlier_tokens(shift_ref[...], buffer_ref[0, :, here]),
            earlier_tokens(shift_ref[rows:, :], buffer_ref[1, :, here]),
        )

    def multiply(wide, *earlier):
        here = lanes_of(wide, WIDE)
        parts = []
        for c in (0, 1):
            head_ref[c, :, here] = buffer_ref[c, 0:16, here].astype(F32)[:8]
            parts.append(wide_conv(buffer_ref[c, :, here], earlier[c], taps_of(weights, c + 1, here)))
        product = (parts[0] * parts[1]).astype(BF16)
        product_ref[:, here] = product
        return (jnp.dot(ending_ref[wide], product, preferred_element_type=F32),)

    def leave(wide, every):
        for half in range(WIDE // LANES):
            own = every[lanes_of(half), lanes_of(half)].reshape(GROUPS, MODES, LANES)
            state_ref[:, lanes_of((WIDE // LANES) * wide + half)] = jnp.sum(own * mask, axis=0)

    pipelined(wides, fetch, multiply, leave)
    for copy in later:
        copy.wait()


def halo(before_ref, place_ref):
    return jnp.where(place_ref[0] > 0, before_ref[...].astype(F32), 0.0)


def head_kernel(rows, place_ref, before_ref, head_ref, weight_ref, state_ref, mode_rate_ref, full_ref, first_ref):
    before = halo(before_ref, place_ref)
    everything = slice(0, head_ref.shape[2])
    parts = [short_conv(head_ref[c], before[c + 1], taps_of(weight_ref, c + 1, everything)) for c in (0, 1)]
    first = (parts[0] * parts[1]).astype(BF16).astype(F32)
    first_ref[...] = first
    rate = mode_rate_ref[...]
    early = jnp.exp(-float(rows - 1) * rate) * first[0:1] + jnp.exp(-float(rows - 2) * rate) * first[1:2]
    full_ref[...] = (state_ref[...] + early).astype(BF16)


def prepare_kernel(
    place_ref,
    query_ref,
    residue_ref,
    before_ref,
    weight_ref,
    mode_rate_ref,
    inner_ref,
    entering_ref,
    carry_ref,
    gate_ref,
    shift_ref,
):
    rows, width = gate_ref.shape
    shift_ref[...] = shift_matrix(rows)
    residue = per_channel(residue_ref[...], selectors(residue_ref.shape[1]))
    wide = GROUPS * CHUNK
    step = index_of((CHUNK, LANES), 0).astype(F32)
    causal = (index_of((CHUNK, wide), 1) & (CHUNK - 1)) <= index_of((CHUNK, wide), 0)
    eye = own_mode(BF16)
    flat_eye = jnp.where((index_of((MODES, LANES), 1) & (MODES - 1)) == index_of((MODES, LANES), 0), 1.0, 0.0)
    flat_eye = flat_eye.astype(BF16)
    shape = (2 * LANES, wide)
    source = (index_of(shape, 1) & (CHUNK - 1)).astype(F32)
    own = (index_of(shape, 0) & (LANES - 1)) // MODES == index_of(shape, 1) // CHUNK
    own_chunk = jnp.where(own[:LANES], 1.0, 0.0).astype(BF16)
    risen = source[:, :LANES].astype(BF16)
    left = jnp.where(own, source - (CHUNK - 1), 0.0).astype(BF16)

    def exponents(tile):
        rate = mode_rate_ref[:, lanes_of(tile)]
        high, low = split(rate)
        diagonal = jnp.concatenate([spread(high, eye), spread(low, eye)], axis=1)
        each = jnp.concatenate([high * flat_eye, low * flat_eye], axis=1)
        return (
            jnp.dot(diagonal, risen, preferred_element_type=F32),
            jnp.dot(each, left, preferred_element_type=F32),
        )

    def products(tile, rise, end):
        here = lanes_of(tile)
        rise_high, rise_low = [
            jnp.concatenate([part] * (wide // LANES), axis=1) * own_chunk for part in split(jnp.exp(rise))
        ]
        rate_row = mode_row(mode_rate_ref[:, here])
        falling = mode_row(residue[:, here]) * jnp.exp(-rate_row * step)
        fall_high, fall_low = split(falling)
        half = tile % (WIDE // LANES)
        for chunk in range(rows // CHUNK):
            entering = (falling * jnp.exp(-float(CHUNK * chunk + 1) * rate_row)).astype(BF16)
            carry_ref[tile // (WIDE // LANES), chunk * CHUNK : (chunk + 1) * CHUNK, lanes_of(half)] = entering
            if chunk == 0:
                entering_ref[tile] = entering
        return (
            jnp.dot(jnp.concatenate([fall_high, fall_low], axis=0), rise_high, preferred_element_type=F32),
            jnp.dot(fall_high, rise_low, preferred_element_type=F32),
            jnp.exp(end),
        )

    def finish(tile, taps, rest, ending):
        taps = jnp.where(causal, taps[:CHUNK] + taps[CHUNK:] + rest, 0.0)
        inner_ref[tile] = jnp.concatenate([taps.astype(BF16), ending.astype(BF16)], axis=0)

    pipelined(width // LANES, exponents, products, finish)
    before = halo(before_ref, place_ref)

    def fetch(part):
        return (earlier_tokens(shift_ref[...], query_ref[:, lanes_of(part, WIDE)]),)

    def convolve(part, earlier):
        here = lanes_of(part, WIDE)
        weights = taps_of(weight_ref, 0, here)
        gate_ref[:, here] = wide_conv(query_ref[:, here], earlier, weights)
        head = query_ref[0:16, here].astype(F32)[:8]
        gate_ref[0:8, here] = short_conv(head, before[0, :, here], weights)

    pipelined(width // WIDE, fetch, convolve)


def local_kernel(
    gate_ref,
    residual_ref,
    product_ref,
    first_ref,
    mode_rate_ref,
    inner_ref,
    entering_ref,
    skip_ref,
    base_ref,
):
    rows, width = product_ref.shape
    mask = group_mask(BF16)
    top = index_of((8, LANES), 0) < 2
    chunks = range(rows // CHUNK)

    def inside(tile):
        here = lanes_of(tile)
        pieces = []
        for chunk in chunks:
            piece = product_ref[chunk * CHUNK : (chunk + 1) * CHUNK, here]
            if chunk == 0:
                wide = piece.astype(F32)
                head = jnp.where(top, first_ref[:, here], wide[:8])
                piece = jnp.concatenate([head, wide[8:]], axis=0).astype(BF16)
            pieces.append(piece)
        found = []
        for pair in chunks[::2]:
            sources = jnp.concatenate([spread(pieces[pair + k], mask) for k in (0, 1)], axis=1)
            found.append(jnp.dot(inner_ref[tile], sources, preferred_element_type=F32))
        return found, pieces[0]

    def across(tile, inner, first):
        decay = jnp.exp(-float(CHUNK) * mode_rate_ref[:, lanes_of(tile)])
        state = jnp.zeros((MODES, LANES), F32)
        states = []
        for chunk in chunks:
            states.append(spread(state.astype(BF16), mask))
            state = decay * state + inner[chunk // 2][CHUNK:, lanes_of(chunk % 2)]
        outer = []
        for pair in chunks[::2]:
            two = jnp.concatenate(states[pair : pair + 2], axis=1)
            outer.append(jnp.dot(entering_ref[tile], two, preferred_element_type=F32))
        return [part[:CHUNK] for part in inner], outer, first

    def finish(tile, inner, outer, first):
        here = lanes_of(tile)
        skip = skip_ref[:, here]
        for chunk in chunks:
            span = slice(chunk * CHUNK, (chunk + 1) * CHUNK)
            piece = first if chunk == 0 else product_ref[span, here]
            conv = (inner[chunk // 2] + outer[chunk // 2])[:, lanes_of(chunk % 2)]
            whole = conv + skip * piece.astype(F32)
            base_ref[span, here] = residual_ref[span, here].astype(F32) + gate_ref[span, here] * whole

    pipelined(width // LANES, inside, across, finish)


def join_kernel(tokens, radix, stride, place_ref, own_ref, mode_rate_ref, entry_ref, *refs):
    others, (found_ref, group_ref) = refs[: radix - 1], refs[radix - 1 :]
    rate = mode_rate_ref[...]
    run = lax.rem(place_ref[0] // stride, radix)
    decay = jnp.exp(-float(tokens * stride) * rate)
    own = own_ref[...].astype(F32)
    values = [ref[...].astype(F32) for ref in others[::-1]]
    found = jnp.zeros_like(rate)
    total = jnp.zeros_like(rate)
    for position in range(radix):
        found = jnp.where(run == position, total, found)
        state = own
        for k, other in enumerate(values, 1):
            state = jnp.where(partner(run, k, radix) == position, other, state)
        total = decay * total + state
    if stride > 1:
        within = lax.rem(place_ref[0], stride).astype(F32) * float(tokens)
        found = jnp.exp(-within * rate) * found
    found_ref[...] = entry_ref[...] + found
    group_ref[...] = total.astype(BF16)


def carry_kernel(stride, radix, place_ref, base_ref, gate_ref, carry_ref, mode_rate_ref, inner_entry_ref, *refs):
    entry_refs, (summed_ref, squares_ref) = refs[:-2], refs[-2:]
    rows, width = base_ref.shape
    run = place_ref[0] // stride
    within = lax.rem(place_ref[0], stride).astype(F32) * float(rows)
    mask = group_mask(BF16)
    totals = [jnp.zeros((rows, LANES), F32)]
    nothing = jnp.zeros((LANES, LANES), BF16)

    def enter(tile):
        here = lanes_of(tile, WIDE)
        rate = mode_rate_ref[:, here]
        step = float(rows * stride)
        outer = jnp.zeros_like(rate)
        for k, ref in enumerate(entry_refs[::-1], 1):
            source = partner(run, k, radix)
            lag = jnp.maximum(run - 1 - source, 0).astype(F32) * step
            outer = outer + jnp.where(source < run, jnp.exp(-lag * rate) * ref[:, here].astype(F32), 0.0)
        entry = (inner_entry_ref[:, here] + jnp.exp(-within * rate) * outer).astype(BF16)
        left, right = spread(entry[:, :LANES], mask), spread(entry[:, LANES:], mask)
        both = jnp.concatenate(
            [jnp.concatenate([left, nothing], axis=1), jnp.concatenate([nothing, right], axis=1)], axis=0
        )
        return (jnp.dot(carry_ref[tile], both, preferred_element_type=F32),)

    def add(tile, carry):
        here = lanes_of(tile, WIDE)
        summed = base_ref[:, here] + gate_ref[:, here] * carry
        summed_ref[:, here] = summed
        square = summed * summed
        totals[0] = totals[0] + (square[:, :LANES] + square[:, LANES:])

    pipelined(width // WIDE, enter, add)
    total = totals[0]
    squares = lax.dot_general(
        jnp.ones((8, 2 * LANES), BF16),
        jnp.concatenate(split(total), axis=1),
        (((1,), (1,)), ((), ())),
        preferred_element_type=F32,
    )
    squares_ref[...] = squares[0:1]


def write_kernel(summed_ref, out_hbm, rounded_ref, sems):
    width = summed_ref.shape[1]
    copies = []
    for tile in range(width // WIDE):
        here = lanes_of(tile, WIDE)
        rounded_ref[:, here] = summed_ref[:, here].astype(BF16)
        span = pl.ds(tile * WIDE, WIDE)
        copies.append(pltpu.make_async_copy(rounded_ref.at[:, span], out_hbm.at[:, span], sems.at[tile]))
        copies[-1].start()
    for copy in copies:
        copy.wait()


def norm_kernel(full_width, summed_ref, gain_ref, *refs):
    squares_refs, (out_hbm, rounded_ref, sems) = refs[:-3], refs[-3:]
    rows, width = summed_ref.shape
    squares = squares_refs[0][...]
    for ref in squares_refs[1:]:
        squares = squares + ref[...]
    scale_row = lax.rsqrt(squares / full_width + 1e-05)
    scale = jnp.concatenate([as_column(scale_row[:, lanes_of(k)]) for k in range(rows // LANES)], axis=0)
    copies = []
    block = rows // 8
    for start in range(0, rows, block):
        span = slice(start, start + block)
        for tile in range(width // LANES):
            here = lanes_of(tile)
            rounded_ref[span, here] = (summed_ref[span, here] * scale[span] * gain_ref[:, here]).astype(BF16)
        there = pl.ds(start, block)
        copies.append(pltpu.make_async_copy(rounded_ref.at[there, :], out_hbm.at[there, :], sems.at[start // block]))
        copies[-1].start()
    for copy in copies:
        copy.wait()


def params():
    return pltpu.CompilerParams(vmem_limit_bytes=VMEM_LIMIT)


def cost(microseconds):
    return pl.CostEstimate(flops=0, bytes_accessed=int(microseconds * 3.0e6), transcendentals=0)


def radices(count):
    found = []
    for radix in (4, 4, 4, 3, 3, 2, 5, 7):
        if count % radix == 0:
            found.append(radix)
            count //= radix
    return found + ([count] if count > 1 else [])


def partner(run, k, radix):
    if radix & (radix - 1) == 0:
        return run ^ k
    return (run - k + radix) % radix


def routes(count, stride, radix):
    found = []
    for k in range(1, radix):
        route = []
        for i in range(count):
            run = i // stride % radix
            route.append((i + (partner(run, k, radix) - run) * stride, i))
        found.append(route)
    return found


def ring(count, shift):
    return [(i, (i + shift) % count) for i in range(count)]


def per_device(projected, short_weight, rates, residues, skip, residual, gain):
    rows, width = projected.shape[1:]
    taps = short_weight.shape[0]
    peers = lax.axis_size("ctx")
    full_width = width * lax.axis_size("fsdp")
    place = lax.axis_index("ctx").astype(jnp.int32).reshape(1)
    hbm_spec = pl.BlockSpec(memory_space=pltpu.HBM)
    vmem_spec = pl.BlockSpec(memory_space=pltpu.VMEM)
    smem_spec = pl.BlockSpec(memory_space=pltpu.SMEM)
    tiles = width // LANES
    wides = width // WIDE

    def kept(array):
        return pltpu.with_memory_space_constraint(array, pltpu.HBM)

    def f32(*shape):
        return jax.ShapeDtypeStruct(shape, F32)

    def bf16(*shape):
        return jax.ShapeDtypeStruct(shape, BF16)

    before = lax.ppermute(projected[:, rows - (taps - 1) :, :], "ctx", ring(peers, 1))

    product, state, mode_rate, head, weights, query, residue, residual_here = pl.pallas_call(
        state_kernel,
        in_specs=[hbm_spec] * 5,
        out_shape=[
            bf16(rows, width),
            f32(MODES, width),
            f32(MODES, width),
            f32(2, 8, width),
            f32(*short_weight.shape),
            bf16(rows, width),
            f32(MODES, residues.shape[0]),
            bf16(rows, width),
        ],
        scratch_shapes=[
            pltpu.VMEM((2, rows, width), BF16),
            pltpu.VMEM((wides, WIDE, rows), BF16),
            pltpu.VMEM((2 * rows, rows), BF16),
            pltpu.VMEM(short_weight.shape, BF16),
            pltpu.VMEM((MODES, rates.shape[0]), F32),
            pltpu.SemaphoreType.DMA((5,)),
            pltpu.SemaphoreType.DMA((2,)),
        ],
        compiler_params=params(),
        cost_estimate=cost(3),
        name="block_state",
    )(kept(projected), kept(short_weight), kept(rates.T), kept(residues.T), kept(residual))

    full_state, first = pl.pallas_call(
        lambda *refs: head_kernel(rows, *refs),
        in_specs=[smem_spec] + [vmem_spec] * 5,
        out_shape=[bf16(MODES, width), f32(8, width)],
        compiler_params=params(),
        cost_estimate=cost(0.2),
        name="head_tokens",
    )(place, before, head, weights, state, mode_rate)

    inner, entering, carry_table, gate = pl.pallas_call(
        prepare_kernel,
        in_specs=[smem_spec] + [vmem_spec] * 5,
        out_shape=[
            bf16(tiles, CHUNK + MODES, GROUPS * CHUNK),
            bf16(tiles, CHUNK, LANES),
            bf16(wides, rows, WIDE),
            f32(rows, width),
        ],
        scratch_shapes=[pltpu.VMEM((2 * rows, rows), BF16)],
        compiler_params=params(),
        cost_estimate=cost(2),
        name="prepare",
    )(place, query, residue, before, weights, mode_rate)

    group, entry, stride = full_state, jnp.zeros((MODES, width), F32), 1
    levels = radices(peers)
    for level, radix in enumerate(levels):
        size = stride * radix
        if level == len(levels) - 1:
            break
        others = [lax.ppermute(group, "ctx", route) for route in routes(peers, stride, radix)[::-1]]
        if level == 0:
            others[0], inner = lax.optimization_barrier((others[0], inner))
        entry, group = pl.pallas_call(
            lambda *refs, radix=radix, stride=stride: join_kernel(rows, radix, stride, *refs),
            in_specs=[smem_spec] + [vmem_spec] * (2 + radix),
            out_shape=[f32(MODES, width), bf16(MODES, width)],
            compiler_params=params(),
            cost_estimate=cost(0.2),
            name="join",
        )(place, group, mode_rate, entry, *others)
        stride = size
    received = [lax.ppermute(group, "ctx", route) for route in routes(peers, stride, levels[-1])[::-1]]

    base = pl.pallas_call(
        local_kernel,
        out_shape=f32(rows, width),
        compiler_params=params(),
        cost_estimate=cost(5),
        name="local_conv",
    )(gate, residual_here, product, first, mode_rate, inner, entering, skip[None])

    count = lax.axis_size("fsdp")
    summed, squares = pl.pallas_call(
        lambda *refs: carry_kernel(stride, levels[-1], *refs),
        in_specs=[smem_spec] + [vmem_spec] * (5 + len(received)),
        out_shape=[f32(rows, width), f32(1, rows)],
        compiler_params=params(),
        cost_estimate=cost(1),
        name="add_carry",
    )(place, base, gate, carry_table, mode_rate, entry, *received)

    parts = [lax.ppermute(squares, "fsdp", route) for route in routes(count, 1, count)[::-1]]

    def write(kernel, operands, name):
        return pl.pallas_call(
            kernel,
            out_specs=hbm_spec,
            out_shape=bf16(rows, width),
            scratch_shapes=[pltpu.VMEM((rows, width), BF16), pltpu.SemaphoreType.DMA((max(8, wides),))],
            compiler_params=params(),
            cost_estimate=cost(1),
            name=name,
        )(*operands)

    new_residual = write(write_kernel, (summed,), "new_residual")
    normed = write(
        lambda *refs: norm_kernel(full_width, *refs), (summed, gain[None], squares, *parts), "normed"
    )
    return (new_residual, normed)


def solution(mesh):
    return jax.shard_map(
        per_device,
        mesh=mesh,
        in_specs=(
            P(None, "ctx", "fsdp"),
            P(None, None, "fsdp"),
            P("fsdp", None),
            P("fsdp", None),
            P("fsdp"),
            P("ctx", "fsdp"),
            P("fsdp"),
        ),
        out_specs=(P("ctx", "fsdp"), P("ctx", "fsdp")),
        check_vma=False,
    )
```

```python
import jax
import jax.numpy as jnp
from jax import lax
from jax.experimental import pallas as pl
from jax.experimental.pallas import tpu as pltpu
from jax.sharding import PartitionSpec as P

CHANNELS_PER_GRP = 16
MODES = 16
CHUNK = 32
LANES = 128
WIDE = 256
GROUPS = LANES // CHANNELS_PER_GRP
VMEM_LIMIT = 16 * 1024 * 1024
F32 = jnp.float32
BF16 = jnp.bfloat16


def index_of(shape, dim):
    return lax.broadcasted_iota(jnp.int32, shape, dim)


def pipelined(count, *stages):
    held = {}
    for step in range(count + len(stages) - 1):
        for k, stage in enumerate(stages):
            item = step - k
            if 0 <= item < count:
                held[item] = stage(item, *held.get(item, ()))


def lanes_of(tile, width=LANES):
    return slice(tile * width, (tile + 1) * width)


def selectors(groups):
    shape = (groups, WIDE)
    found = []
    for tile in range(groups * CHANNELS_PER_GRP // WIDE):
        own = index_of(shape, 0) == index_of(shape, 1) // CHANNELS_PER_GRP + tile * (WIDE // CHANNELS_PER_GRP)
        found.append(jnp.where(own, 1.0, 0.0).astype(BF16))
    return found


def per_channel(table, chosen):
    high = table.astype(BF16)
    rest = table - high.astype(F32)
    middle = rest.astype(BF16)
    low = (rest - middle.astype(F32)).astype(BF16)
    terms = jnp.concatenate([high, middle, low], axis=0)
    parts = []
    for selector in chosen:
        three = jnp.dot(terms, selector, preferred_element_type=F32)
        parts.append(three[:MODES] + three[MODES : 2 * MODES] + three[2 * MODES :])
    return jnp.concatenate(parts, axis=1)


def mode_row(channel_table):
    own = index_of(channel_table.shape, 0) == (index_of(channel_table.shape, 1) & (MODES - 1))
    return jnp.sum(jnp.where(own, channel_table, 0.0), axis=0, keepdims=True)


def as_column(row):
    return jnp.transpose(jnp.broadcast_to(row, (LANES, LANES)))


def own_mode(dtype):
    shape = (GROUPS, MODES, LANES)
    own = index_of(shape, 0) * MODES + index_of(shape, 1) == index_of(shape, 2)
    return jnp.where(own, 1.0, 0.0).astype(dtype)


def split(x):
    high = x.astype(BF16)
    return high, (x - high.astype(F32)).astype(BF16)


def group_mask(dtype):
    shape = (GROUPS, MODES, LANES)
    own = index_of(shape, 0) == index_of(shape, 2) // CHANNELS_PER_GRP
    return jnp.where(own, 1.0, 0.0).astype(dtype)


def spread(rows, mask):
    size = rows.shape[0]
    copies = rows.reshape(1, size // MODES, MODES, LANES) * mask.reshape(GROUPS, 1, MODES, LANES)
    return copies.reshape(GROUPS * size, LANES)


def shifted(block, before):
    one = pltpu.roll(block, 1, 0)
    two = pltpu.roll(block, 2, 0)
    first = index_of((8, block.shape[1]), 0)
    near, far = (0.0, 0.0) if before is None else (before[1:2], before[0:1])
    head_one = jnp.where(first == 0, near, one[:8])
    head_two = jnp.where(first == 0, far, jnp.where(first == 1, near, two[:8]))
    if block.shape[0] == 8:
        return head_one, head_two
    return jnp.concatenate([head_one, one[8:]], axis=0), jnp.concatenate([head_two, two[8:]], axis=0)


def short_conv(block, before, weights):
    one, two = shifted(block, before)
    return weights[0] * block + weights[1] * one + weights[2] * two


def shift_matrix(rows):
    shape = (2 * rows, rows)
    target = index_of(shape, 0)
    source = index_of(shape, 1)
    taken = jnp.where(target < rows, target - 1, target - (rows + 2))
    return jnp.where(source == taken, 1.0, 0.0).astype(BF16)


def earlier_tokens(shift, block):
    return jnp.dot(shift, block, preferred_element_type=F32)


def wide_conv(block, earlier, weights):
    rows = block.shape[0]
    wide = block.astype(F32)
    if earlier.shape[0] == rows:
        one = pltpu.roll(wide, 1, 0)
        head = jnp.where(index_of((8, wide.shape[1]), 0) == 0, 0.0, one[:8])
        one = jnp.concatenate([head, one[8:]], axis=0)
    else:
        one = earlier[:rows]
    return weights[0] * wide + weights[1] * one + weights[2] * earlier[-rows:]


def taps_of(weights, feature, lanes):
    return [weights[tap, feature : feature + 1, lanes] for tap in range(weights.shape[0])]


def state_kernel(
    projected_ref,
    weight_hbm,
    rate_hbm,
    residue_hbm,
    product_ref,
    state_ref,
    mode_rate_ref,
    head_ref,
    weight_ref,
    residue_ref,
    buffer_ref,
    ending_ref,
    shift_ref,
    short_ref,
    rate_ref,
    sems,
    small_sems,
):
    rows, width = product_ref.shape
    wides = width // WIDE
    rate_copy = pltpu.make_async_copy(rate_hbm, rate_ref, small_sems.at[0])
    rate_copy.start()
    weight_copy = pltpu.make_async_copy(weight_hbm, short_ref, small_sems.at[1])
    weight_copy.start()
    part = width // 2
    copies = [
        pltpu.make_async_copy(
            projected_ref.at[1 + c, :, pl.ds(side * part, part)],
            buffer_ref.at[c, :, pl.ds(side * part, part)],
            sems.at[2 * side + c],
        )
        for side in (0, 1)
        for c in (0, 1)
    ]
    residue_copy = pltpu.make_async_copy(residue_hbm, residue_ref, sems.at[4])
    for copy in copies:
        copy.start()
    residue_copy.start()
    shift_ref[...] = shift_matrix(rows)
    chosen = selectors(rate_ref.shape[1])
    eye = own_mode(BF16)
    mask = group_mask(F32)
    token = index_of((2 * LANES, rows), 1)
    left = jnp.where(token < 2, -1e30, (token - (rows - 1)).astype(F32)).astype(BF16)
    rate_copy.wait()
    mode_rate = per_channel(rate_ref[...], chosen)
    mode_rate_ref[...] = mode_rate

    def exponents(tile):
        high, low = split(mode_rate[:, lanes_of(tile)])
        diagonal = jnp.concatenate([spread(high, eye), spread(low, eye)], axis=1)
        return (jnp.dot(diagonal, left, preferred_element_type=F32),)

    def endings(tile, exponent):
        ending_ref[tile // 2, lanes_of(tile % 2), :] = jnp.exp(exponent).astype(BF16)

    pipelined(width // LANES, exponents, endings)
    weight_copy.wait()
    weights = short_ref[...].astype(F32)
    weight_ref[...] = weights

    def fetch(wide):
        if wide % (wides // 2) == 0:
            first = 2 * (wide // (wides // 2))
            for copy in copies[first : first + 2]:
                copy.wait()
        here = lanes_of(wide, WIDE)
        return (
            earlier_tokens(shift_ref[...], buffer_ref[0, :, here]),
            earlier_tokens(shift_ref[rows:, :], buffer_ref[1, :, here]),
        )

    def multiply(wide, *earlier):
        here = lanes_of(wide, WIDE)
        parts = []
        for c in (0, 1):
            head_ref[c, :, here] = buffer_ref[c, 0:16, here].astype(F32)[:8]
            parts.append(wide_conv(buffer_ref[c, :, here], earlier[c], taps_of(weights, c + 1, here)))
        product = (parts[0] * parts[1]).astype(BF16)
        product_ref[:, here] = product
        return (jnp.dot(ending_ref[wide], product, preferred_element_type=F32),)

    def leave(wide, every):
        for half in range(WIDE // LANES):
            own = every[lanes_of(half), lanes_of(half)].reshape(GROUPS, MODES, LANES)
            state_ref[:, lanes_of((WIDE // LANES) * wide + half)] = jnp.sum(own * mask, axis=0)

    pipelined(wides, fetch, multiply, leave)
    residue_copy.wait()


def halo(before_ref, place_ref):
    return jnp.where(place_ref[0] > 0, before_ref[...].astype(F32), 0.0)


def head_kernel(rows, place_ref, before_ref, head_ref, weight_ref, state_ref, mode_rate_ref, full_ref, first_ref):
    before = halo(before_ref, place_ref)
    everything = slice(0, head_ref.shape[2])
    parts = [short_conv(head_ref[c], before[c + 1], taps_of(weight_ref, c + 1, everything)) for c in (0, 1)]
    first = (parts[0] * parts[1]).astype(BF16).astype(F32)
    first_ref[...] = first
    rate = mode_rate_ref[...]
    early = jnp.exp(-float(rows - 1) * rate) * first[0:1] + jnp.exp(-float(rows - 2) * rate) * first[1:2]
    full_ref[...] = (state_ref[...] + early).astype(BF16)


def prepare_kernel(
    place_ref,
    projected_ref,
    residual_hbm,
    residue_ref,
    before_ref,
    weight_ref,
    mode_rate_ref,
    inner_ref,
    entering_ref,
    carry_ref,
    gate_ref,
    residual_ref,
    query_ref,
    shift_ref,
    sems,
):
    rows, width = gate_ref.shape
    query_copy = pltpu.make_async_copy(projected_ref.at[0], query_ref, sems.at[0])
    query_copy.start()
    residual_copy = pltpu.make_async_copy(residual_hbm, residual_ref, sems.at[1])
    residual_copy.start()
    shift_ref[...] = shift_matrix(rows)
    residue = per_channel(residue_ref[...], selectors(residue_ref.shape[1]))
    wide = GROUPS * CHUNK
    step = index_of((CHUNK, LANES), 0).astype(F32)
    causal = (index_of((CHUNK, wide), 1) & (CHUNK - 1)) <= index_of((CHUNK, wide), 0)
    eye = own_mode(BF16)
    flat_eye = jnp.where((index_of((MODES, LANES), 1) & (MODES - 1)) == index_of((MODES, LANES), 0), 1.0, 0.0)
    flat_eye = flat_eye.astype(BF16)
    shape = (2 * LANES, wide)
    source = (index_of(shape, 1) & (CHUNK - 1)).astype(F32)
    own = (index_of(shape, 0) & (LANES - 1)) // MODES == index_of(shape, 1) // CHUNK
    own_chunk = jnp.where(own[:LANES], 1.0, 0.0).astype(BF16)
    risen = source[:, :LANES].astype(BF16)
    left = jnp.where(own, source - (CHUNK - 1), 0.0).astype(BF16)

    def exponents(tile):
        rate = mode_rate_ref[:, lanes_of(tile)]
        high, low = split(rate)
        diagonal = jnp.concatenate([spread(high, eye), spread(low, eye)], axis=1)
        each = jnp.concatenate([high * flat_eye, low * flat_eye], axis=1)
        return (
            jnp.dot(diagonal, risen, preferred_element_type=F32),
            jnp.dot(each, left, preferred_element_type=F32),
        )

    def products(tile, rise, end):
        here = lanes_of(tile)
        rise_high, rise_low = [
            jnp.concatenate([part] * (wide // LANES), axis=1) * own_chunk for part in split(jnp.exp(rise))
        ]
        rate_row = mode_row(mode_rate_ref[:, here])
        falling = mode_row(residue[:, here]) * jnp.exp(-rate_row * step)
        fall_high, fall_low = split(falling)
        half = tile % (WIDE // LANES)
        for chunk in range(rows // CHUNK):
            entering = (falling * jnp.exp(-float(CHUNK * chunk + 1) * rate_row)).astype(BF16)
            carry_ref[tile // (WIDE // LANES), chunk * CHUNK : (chunk + 1) * CHUNK, lanes_of(half)] = entering
            if chunk == 0:
                entering_ref[tile] = entering
        return (
            jnp.dot(jnp.concatenate([fall_high, fall_low], axis=0), rise_high, preferred_element_type=F32),
            jnp.dot(fall_high, rise_low, preferred_element_type=F32),
            jnp.exp(end),
        )

    def finish(tile, taps, rest, ending):
        taps = jnp.where(causal, taps[:CHUNK] + taps[CHUNK:] + rest, 0.0)
        inner_ref[tile] = jnp.concatenate([taps.astype(BF16), ending.astype(BF16)], axis=0)

    pipelined(width // LANES, exponents, products, finish)
    before = halo(before_ref, place_ref)
    query_copy.wait()

    def fetch(part):
        return (earlier_tokens(shift_ref[...], query_ref[:, lanes_of(part, WIDE)]),)

    def convolve(part, earlier):
        here = lanes_of(part, WIDE)
        weights = taps_of(weight_ref, 0, here)
        gate_ref[:, here] = wide_conv(query_ref[:, here], earlier, weights)
        head = query_ref[0:16, here].astype(F32)[:8]
        gate_ref[0:8, here] = short_conv(head, before[0, :, here], weights)

    pipelined(width // WIDE, fetch, convolve)
    residual_copy.wait()


def local_kernel(
    gate_ref,
    residual_ref,
    product_ref,
    first_ref,
    mode_rate_ref,
    inner_ref,
    entering_ref,
    skip_ref,
    base_ref,
):
    rows, width = product_ref.shape
    mask = group_mask(BF16)
    top = index_of((8, LANES), 0) < 2
    chunks = range(rows // CHUNK)

    def inside(tile):
        here = lanes_of(tile)
        pieces = []
        for chunk in chunks:
            piece = product_ref[chunk * CHUNK : (chunk + 1) * CHUNK, here]
            if chunk == 0:
                wide = piece.astype(F32)
                head = jnp.where(top, first_ref[:, here], wide[:8])
                piece = jnp.concatenate([head, wide[8:]], axis=0).astype(BF16)
            pieces.append(piece)
        found = []
        for pair in chunks[::2]:
            sources = jnp.concatenate([spread(pieces[pair + k], mask) for k in (0, 1)], axis=1)
            found.append(jnp.dot(inner_ref[tile], sources, preferred_element_type=F32))
        return found, pieces[0]

    def across(tile, inner, first):
        decay = jnp.exp(-float(CHUNK) * mode_rate_ref[:, lanes_of(tile)])
        state = jnp.zeros((MODES, LANES), F32)
        states = []
        for chunk in chunks:
            states.append(spread(state.astype(BF16), mask))
            state = decay * state + inner[chunk // 2][CHUNK:, lanes_of(chunk % 2)]
        outer = []
        for pair in chunks[::2]:
            two = jnp.concatenate(states[pair : pair + 2], axis=1)
            outer.append(jnp.dot(entering_ref[tile], two, preferred_element_type=F32))
        return [part[:CHUNK] for part in inner], outer, first

    def finish(tile, inner, outer, first):
        here = lanes_of(tile)
        skip = skip_ref[:, here]
        for chunk in chunks:
            span = slice(chunk * CHUNK, (chunk + 1) * CHUNK)
            piece = first if chunk == 0 else product_ref[span, here]
            conv = (inner[chunk // 2] + outer[chunk // 2])[:, lanes_of(chunk % 2)]
            whole = conv + skip * piece.astype(F32)
            base_ref[span, here] = residual_ref[span, here].astype(F32) + gate_ref[span, here] * whole

    pipelined(width // LANES, inside, across, finish)


def join_kernel(tokens, radix, stride, place_ref, own_ref, mode_rate_ref, entry_ref, *refs):
    others, (found_ref, group_ref) = refs[: radix - 1], refs[radix - 1 :]
    rate = mode_rate_ref[...]
    run = lax.rem(place_ref[0] // stride, radix)
    decay = jnp.exp(-float(tokens * stride) * rate)
    own = own_ref[...].astype(F32)
    values = [ref[...].astype(F32) for ref in others[::-1]]
    found = jnp.zeros_like(rate)
    total = jnp.zeros_like(rate)
    for position in range(radix):
        found = jnp.where(run == position, total, found)
        state = own
        for k, other in enumerate(values, 1):
            state = jnp.where(partner(run, k, radix) == position, other, state)
        total = decay * total + state
    if stride > 1:
        within = lax.rem(place_ref[0], stride).astype(F32) * float(tokens)
        found = jnp.exp(-within * rate) * found
    found_ref[...] = entry_ref[...] + found
    group_ref[...] = total.astype(BF16)


def carry_kernel(stride, radix, place_ref, base_ref, gate_ref, carry_ref, mode_rate_ref, inner_entry_ref, *refs):
    entry_refs, (summed_ref, squares_ref) = refs[:-2], refs[-2:]
    rows, width = base_ref.shape
    run = place_ref[0] // stride
    within = lax.rem(place_ref[0], stride).astype(F32) * float(rows)
    mask = group_mask(BF16)
    totals = [jnp.zeros((rows, LANES), F32)]
    nothing = jnp.zeros((LANES, LANES), BF16)

    def enter(tile):
        here = lanes_of(tile, WIDE)
        rate = mode_rate_ref[:, here]
        step = float(rows * stride)
        outer = jnp.zeros_like(rate)
        for k, ref in enumerate(entry_refs[::-1], 1):
            source = partner(run, k, radix)
            lag = jnp.maximum(run - 1 - source, 0).astype(F32) * step
            outer = outer + jnp.where(source < run, jnp.exp(-lag * rate) * ref[:, here].astype(F32), 0.0)
        entry = (inner_entry_ref[:, here] + jnp.exp(-within * rate) * outer).astype(BF16)
        left, right = spread(entry[:, :LANES], mask), spread(entry[:, LANES:], mask)
        both = jnp.concatenate(
            [jnp.concatenate([left, nothing], axis=1), jnp.concatenate([nothing, right], axis=1)], axis=0
        )
        return (jnp.dot(carry_ref[tile], both, preferred_element_type=F32),)

    def add(tile, carry):
        here = lanes_of(tile, WIDE)
        summed = base_ref[:, here] + gate_ref[:, here] * carry
        summed_ref[:, here] = summed
        square = summed * summed
        totals[0] = totals[0] + (square[:, :LANES] + square[:, LANES:])

    pipelined(width // WIDE, enter, add)
    total = totals[0]
    squares = lax.dot_general(
        jnp.ones((8, 2 * LANES), BF16),
        jnp.concatenate(split(total), axis=1),
        (((1,), (1,)), ((), ())),
        preferred_element_type=F32,
    )
    squares_ref[...] = squares[0:1]


def write_kernel(summed_ref, out_hbm, rounded_ref, sems):
    width = summed_ref.shape[1]
    copies = []
    for tile in range(width // WIDE):
        here = lanes_of(tile, WIDE)
        rounded_ref[:, here] = summed_ref[:, here].astype(BF16)
        span = pl.ds(tile * WIDE, WIDE)
        copies.append(pltpu.make_async_copy(rounded_ref.at[:, span], out_hbm.at[:, span], sems.at[tile]))
        copies[-1].start()
    for copy in copies:
        copy.wait()


def norm_kernel(full_width, summed_ref, gain_ref, *refs):
    squares_refs, (out_hbm, rounded_ref, sems) = refs[:-3], refs[-3:]
    rows, width = summed_ref.shape
    squares = squares_refs[0][...]
    for ref in squares_refs[1:]:
        squares = squares + ref[...]
    scale_row = lax.rsqrt(squares / full_width + 1e-05)
    scale = jnp.concatenate([as_column(scale_row[:, lanes_of(k)]) for k in range(rows // LANES)], axis=0)
    copies = []
    block = rows // 8
    for start in range(0, rows, block):
        span = slice(start, start + block)
        for tile in range(width // LANES):
            here = lanes_of(tile)
            rounded_ref[span, here] = (summed_ref[span, here] * scale[span] * gain_ref[:, here]).astype(BF16)
        there = pl.ds(start, block)
        copies.append(pltpu.make_async_copy(rounded_ref.at[there, :], out_hbm.at[there, :], sems.at[start // block]))
        copies[-1].start()
    for copy in copies:
        copy.wait()


def params():
    return pltpu.CompilerParams(vmem_limit_bytes=VMEM_LIMIT)


def cost(microseconds):
    return pl.CostEstimate(flops=0, bytes_accessed=int(microseconds * 3.0e6), transcendentals=0)


def radices(count):
    found = []
    for radix in (4, 4, 4, 3, 3, 2, 5, 7):
        if count % radix == 0:
            found.append(radix)
            count //= radix
    return found + ([count] if count > 1 else [])


def partner(run, k, radix):
    if radix & (radix - 1) == 0:
        return run ^ k
    return (run - k + radix) % radix


def routes(count, stride, radix):
    found = []
    for k in range(1, radix):
        route = []
        for i in range(count):
            run = i // stride % radix
            route.append((i + (partner(run, k, radix) - run) * stride, i))
        found.append(route)
    return found


def ring(count, shift):
    return [(i, (i + shift) % count) for i in range(count)]


def per_device(projected, short_weight, rates, residues, skip, residual, gain):
    rows, width = projected.shape[1:]
    taps = short_weight.shape[0]
    peers = lax.axis_size("ctx")
    full_width = width * lax.axis_size("fsdp")
    place = lax.axis_index("ctx").astype(jnp.int32).reshape(1)
    hbm_spec = pl.BlockSpec(memory_space=pltpu.HBM)
    vmem_spec = pl.BlockSpec(memory_space=pltpu.VMEM)
    smem_spec = pl.BlockSpec(memory_space=pltpu.SMEM)
    tiles = width // LANES
    wides = width // WIDE

    def kept(array):
        return pltpu.with_memory_space_constraint(array, pltpu.HBM)

    def f32(*shape):
        return jax.ShapeDtypeStruct(shape, F32)

    def bf16(*shape):
        return jax.ShapeDtypeStruct(shape, BF16)

    before = lax.ppermute(projected[:, rows - (taps - 1) :, :], "ctx", ring(peers, 1))

    product, state, mode_rate, head, weights, residue = pl.pallas_call(
        state_kernel,
        in_specs=[hbm_spec] * 4,
        out_shape=[
            bf16(rows, width),
            f32(MODES, width),
            f32(MODES, width),
            f32(2, 8, width),
            f32(*short_weight.shape),
            f32(MODES, residues.shape[0]),
        ],
        scratch_shapes=[
            pltpu.VMEM((2, rows, width), BF16),
            pltpu.VMEM((wides, WIDE, rows), BF16),
            pltpu.VMEM((2 * rows, rows), BF16),
            pltpu.VMEM(short_weight.shape, BF16),
            pltpu.VMEM((MODES, rates.shape[0]), F32),
            pltpu.SemaphoreType.DMA((5,)),
            pltpu.SemaphoreType.DMA((2,)),
        ],
        compiler_params=params(),
        cost_estimate=cost(3),
        name="block_state",
    )(kept(projected), kept(short_weight), kept(rates.T), kept(residues.T))

    full_state, first = pl.pallas_call(
        lambda *refs: head_kernel(rows, *refs),
        in_specs=[smem_spec] + [vmem_spec] * 5,
        out_shape=[bf16(MODES, width), f32(8, width)],
        compiler_params=params(),
        cost_estimate=cost(0.2),
        name="head_tokens",
    )(place, before, head, weights, state, mode_rate)

    inner, entering, carry_table, gate, residual_here = pl.pallas_call(
        prepare_kernel,
        in_specs=[smem_spec] + [hbm_spec] * 2 + [vmem_spec] * 4,
        out_shape=[
            bf16(tiles, CHUNK + MODES, GROUPS * CHUNK),
            bf16(tiles, CHUNK, LANES),
            bf16(wides, rows, WIDE),
            f32(rows, width),
            bf16(rows, width),
        ],
        scratch_shapes=[
            pltpu.VMEM((rows, width), BF16),
            pltpu.VMEM((2 * rows, rows), BF16),
            pltpu.SemaphoreType.DMA((2,)),
        ],
        compiler_params=params(),
        cost_estimate=cost(2),
        name="prepare",
    )(place, kept(projected), kept(residual), residue, before, weights, mode_rate)

    group, entry, stride = full_state, jnp.zeros((MODES, width), F32), 1
    levels = radices(peers)
    for level, radix in enumerate(levels):
        size = stride * radix
        if level == len(levels) - 1:
            break
        others = [lax.ppermute(group, "ctx", route) for route in routes(peers, stride, radix)[::-1]]
        if level == 0:
            others[0], inner = lax.optimization_barrier((others[0], inner))
        entry, group = pl.pallas_call(
            lambda *refs, radix=radix, stride=stride: join_kernel(rows, radix, stride, *refs),
            in_specs=[smem_spec] + [vmem_spec] * (2 + radix),
            out_shape=[f32(MODES, width), bf16(MODES, width)],
            compiler_params=params(),
            cost_estimate=cost(0.2),
            name="join",
        )(place, group, mode_rate, entry, *others)
        stride = size
    received = [lax.ppermute(group, "ctx", route) for route in routes(peers, stride, levels[-1])[::-1]]

    base = pl.pallas_call(
        local_kernel,
        out_shape=f32(rows, width),
        compiler_params=params(),
        cost_estimate=cost(5),
        name="local_conv",
    )(gate, residual_here, product, first, mode_rate, inner, entering, skip[None])

    count = lax.axis_size("fsdp")
    summed, squares = pl.pallas_call(
        lambda *refs: carry_kernel(stride, levels[-1], *refs),
        in_specs=[smem_spec] + [vmem_spec] * (5 + len(received)),
        out_shape=[f32(rows, width), f32(1, rows)],
        compiler_params=params(),
        cost_estimate=cost(1),
        name="add_carry",
    )(place, base, gate, carry_table, mode_rate, entry, *received)

    parts = [lax.ppermute(squares, "fsdp", route) for route in routes(count, 1, count)[::-1]]

    def write(kernel, operands, name):
        return pl.pallas_call(
            kernel,
            out_specs=hbm_spec,
            out_shape=bf16(rows, width),
            scratch_shapes=[pltpu.VMEM((rows, width), BF16), pltpu.SemaphoreType.DMA((max(8, wides),))],
            compiler_params=params(),
            cost_estimate=cost(1),
            name=name,
        )(*operands)

    new_residual = write(write_kernel, (summed,), "new_residual")
    normed = write(
        lambda *refs: norm_kernel(full_width, *refs), (summed, gain[None], squares, *parts), "normed"
    )
    return (new_residual, normed)


def solution(mesh):
    return jax.shard_map(
        per_device,
        mesh=mesh,
        in_specs=(
            P(None, "ctx", "fsdp"),
            P(None, None, "fsdp"),
            P("fsdp", None),
            P("fsdp", None),
            P("fsdp"),
            P("ctx", "fsdp"),
            P("fsdp"),
        ),
        out_specs=(P("ctx", "fsdp"), P("ctx", "fsdp")),
        check_vma=False,
    )
```

```python
import jax
import jax.numpy as jnp
from jax import lax
from jax.experimental import pallas as pl
from jax.experimental.pallas import tpu as pltpu
from jax.sharding import PartitionSpec as P

CHANNELS_PER_GRP = 16
MODES = 16
CHUNK = 32
LANES = 128
WIDE = 256
GROUPS = LANES // CHANNELS_PER_GRP
VMEM_LIMIT = 16 * 1024 * 1024
F32 = jnp.float32
BF16 = jnp.bfloat16


def index_of(shape, dim):
    return lax.broadcasted_iota(jnp.int32, shape, dim)


def pipelined(count, *stages):
    held = {}
    for step in range(count + len(stages) - 1):
        for k, stage in enumerate(stages):
            item = step - k
            if 0 <= item < count:
                held[item] = stage(item, *held.get(item, ()))


def lanes_of(tile, width=LANES):
    return slice(tile * width, (tile + 1) * width)


def selectors(groups):
    shape = (groups, WIDE)
    found = []
    for tile in range(groups * CHANNELS_PER_GRP // WIDE):
        own = index_of(shape, 0) == index_of(shape, 1) // CHANNELS_PER_GRP + tile * (WIDE // CHANNELS_PER_GRP)
        found.append(jnp.where(own, 1.0, 0.0).astype(BF16))
    return found


def per_channel(table, chosen):
    high = table.astype(BF16)
    rest = table - high.astype(F32)
    middle = rest.astype(BF16)
    low = (rest - middle.astype(F32)).astype(BF16)
    terms = jnp.concatenate([high, middle, low], axis=0)
    parts = []
    for selector in chosen:
        three = jnp.dot(terms, selector, preferred_element_type=F32)
        parts.append(three[:MODES] + three[MODES : 2 * MODES] + three[2 * MODES :])
    return jnp.concatenate(parts, axis=1)


def mode_row(channel_table):
    own = index_of(channel_table.shape, 0) == (index_of(channel_table.shape, 1) & (MODES - 1))
    return jnp.sum(jnp.where(own, channel_table, 0.0), axis=0, keepdims=True)


def as_column(row):
    return jnp.transpose(jnp.broadcast_to(row, (LANES, LANES)))


def own_mode(dtype):
    shape = (GROUPS, MODES, LANES)
    own = index_of(shape, 0) * MODES + index_of(shape, 1) == index_of(shape, 2)
    return jnp.where(own, 1.0, 0.0).astype(dtype)


def split(x):
    high = x.astype(BF16)
    return high, (x - high.astype(F32)).astype(BF16)


def group_mask(dtype):
    shape = (GROUPS, MODES, LANES)
    own = index_of(shape, 0) == index_of(shape, 2) // CHANNELS_PER_GRP
    return jnp.where(own, 1.0, 0.0).astype(dtype)


def spread(rows, mask):
    size = rows.shape[0]
    copies = rows.reshape(1, size // MODES, MODES, LANES) * mask.reshape(GROUPS, 1, MODES, LANES)
    return copies.reshape(GROUPS * size, LANES)


def shifted(block, before):
    one = pltpu.roll(block, 1, 0)
    two = pltpu.roll(block, 2, 0)
    first = index_of((8, block.shape[1]), 0)
    near, far = (0.0, 0.0) if before is None else (before[1:2], before[0:1])
    head_one = jnp.where(first == 0, near, one[:8])
    head_two = jnp.where(first == 0, far, jnp.where(first == 1, near, two[:8]))
    if block.shape[0] == 8:
        return head_one, head_two
    return jnp.concatenate([head_one, one[8:]], axis=0), jnp.concatenate([head_two, two[8:]], axis=0)


def short_conv(block, before, weights):
    one, two = shifted(block, before)
    return weights[0] * block + weights[1] * one + weights[2] * two


def shift_matrix(rows):
    shape = (2 * rows, rows)
    target = index_of(shape, 0)
    source = index_of(shape, 1)
    taken = jnp.where(target < rows, target - 1, target - (rows + 2))
    return jnp.where(source == taken, 1.0, 0.0).astype(BF16)


def earlier_tokens(shift, block):
    return jnp.dot(shift, block, preferred_element_type=F32)


def wide_conv(block, earlier, weights):
    rows = block.shape[0]
    wide = block.astype(F32)
    if earlier.shape[0] == rows:
        one = pltpu.roll(wide, 1, 0)
        head = jnp.where(index_of((8, wide.shape[1]), 0) == 0, 0.0, one[:8])
        one = jnp.concatenate([head, one[8:]], axis=0)
    else:
        one = earlier[:rows]
    return weights[0] * wide + weights[1] * one + weights[2] * earlier[-rows:]


def taps_of(weights, feature, lanes):
    return [weights[tap, feature : feature + 1, lanes] for tap in range(weights.shape[0])]


def state_kernel(
    projected_ref,
    weight_hbm,
    rate_hbm,
    residue_hbm,
    product_ref,
    state_ref,
    mode_rate_ref,
    head_ref,
    weight_ref,
    residue_ref,
    buffer_ref,
    ending_ref,
    shift_ref,
    short_ref,
    rate_ref,
    sems,
    small_sems,
):
    rows, width = product_ref.shape
    wides = width // WIDE
    rate_copy = pltpu.make_async_copy(rate_hbm, rate_ref, small_sems.at[0])
    rate_copy.start()
    weight_copy = pltpu.make_async_copy(weight_hbm, short_ref, small_sems.at[1])
    weight_copy.start()
    part = rows // 4
    copies = [
        pltpu.make_async_copy(
            projected_ref.at[1 + c, pl.ds(side * part, part), :],
            buffer_ref.at[c, pl.ds(side * part, part), :],
            sems.at[2 * side + c],
        )
        for side in range(4)
        for c in (0, 1)
    ]
    residue_copy = pltpu.make_async_copy(residue_hbm, residue_ref, sems.at[8])
    for copy in copies:
        copy.start()
    residue_copy.start()
    shift_ref[...] = shift_matrix(rows)
    chosen = selectors(rate_ref.shape[1])
    eye = own_mode(BF16)
    mask = group_mask(F32)
    token = index_of((2 * LANES, rows), 1)
    left = jnp.where(token < 2, -1e30, (token - (rows - 1)).astype(F32)).astype(BF16)
    rate_copy.wait()
    mode_rate = per_channel(rate_ref[...], chosen)
    mode_rate_ref[...] = mode_rate

    def exponents(tile):
        high, low = split(mode_rate[:, lanes_of(tile)])
        diagonal = jnp.concatenate([spread(high, eye), spread(low, eye)], axis=1)
        return (jnp.dot(diagonal, left, preferred_element_type=F32),)

    def endings(tile, exponent):
        ending_ref[tile // 2, lanes_of(tile % 2), :] = jnp.exp(exponent).astype(BF16)

    pipelined(width // LANES, exponents, endings)
    weight_copy.wait()
    weights = short_ref[...].astype(F32)
    weight_ref[...] = weights
    for copy in copies:
        copy.wait()

    def fetch(wide):
        here = lanes_of(wide, WIDE)
        return (
            earlier_tokens(shift_ref[...], buffer_ref[0, :, here]),
            earlier_tokens(shift_ref[rows:, :], buffer_ref[1, :, here]),
        )

    def multiply(wide, *earlier):
        here = lanes_of(wide, WIDE)
        parts = []
        for c in (0, 1):
            head_ref[c, :, here] = buffer_ref[c, 0:16, here].astype(F32)[:8]
            parts.append(wide_conv(buffer_ref[c, :, here], earlier[c], taps_of(weights, c + 1, here)))
        product = (parts[0] * parts[1]).astype(BF16)
        product_ref[:, here] = product
        return (jnp.dot(ending_ref[wide], product, preferred_element_type=F32),)

    def leave(wide, every):
        for half in range(WIDE // LANES):
            own = every[lanes_of(half), lanes_of(half)].reshape(GROUPS, MODES, LANES)
            state_ref[:, lanes_of((WIDE // LANES) * wide + half)] = jnp.sum(own * mask, axis=0)

    pipelined(wides, fetch, multiply, leave)
    residue_copy.wait()


def halo(before_ref, place_ref):
    return jnp.where(place_ref[0] > 0, before_ref[...].astype(F32), 0.0)


def head_kernel(rows, place_ref, before_ref, head_ref, weight_ref, state_ref, mode_rate_ref, full_ref, first_ref):
    before = halo(before_ref, place_ref)
    everything = slice(0, head_ref.shape[2])
    parts = [short_conv(head_ref[c], before[c + 1], taps_of(weight_ref, c + 1, everything)) for c in (0, 1)]
    first = (parts[0] * parts[1]).astype(BF16).astype(F32)
    first_ref[...] = first
    rate = mode_rate_ref[...]
    early = jnp.exp(-float(rows - 1) * rate) * first[0:1] + jnp.exp(-float(rows - 2) * rate) * first[1:2]
    full_ref[...] = (state_ref[...] + early).astype(BF16)


def prepare_kernel(
    place_ref,
    projected_ref,
    residual_hbm,
    residue_ref,
    before_ref,
    weight_ref,
    mode_rate_ref,
    inner_ref,
    entering_ref,
    carry_ref,
    gate_ref,
    residual_ref,
    query_ref,
    shift_ref,
    sems,
):
    rows, width = gate_ref.shape
    query_copy = pltpu.make_async_copy(projected_ref.at[0], query_ref, sems.at[0])
    query_copy.start()
    residual_copy = pltpu.make_async_copy(residual_hbm, residual_ref, sems.at[1])
    residual_copy.start()
    shift_ref[...] = shift_matrix(rows)
    residue = per_channel(residue_ref[...], selectors(residue_ref.shape[1]))
    wide = GROUPS * CHUNK
    step = index_of((CHUNK, LANES), 0).astype(F32)
    causal = (index_of((CHUNK, wide), 1) & (CHUNK - 1)) <= index_of((CHUNK, wide), 0)
    eye = own_mode(BF16)
    flat_eye = jnp.where((index_of((MODES, LANES), 1) & (MODES - 1)) == index_of((MODES, LANES), 0), 1.0, 0.0)
    flat_eye = flat_eye.astype(BF16)
    shape = (2 * LANES, wide)
    source = (index_of(shape, 1) & (CHUNK - 1)).astype(F32)
    own = (index_of(shape, 0) & (LANES - 1)) // MODES == index_of(shape, 1) // CHUNK
    own_chunk = jnp.where(own[:LANES], 1.0, 0.0).astype(BF16)
    risen = source[:, :LANES].astype(BF16)
    left = jnp.where(own, source - (CHUNK - 1), 0.0).astype(BF16)

    def exponents(tile):
        rate = mode_rate_ref[:, lanes_of(tile)]
        high, low = split(rate)
        diagonal = jnp.concatenate([spread(high, eye), spread(low, eye)], axis=1)
        each = jnp.concatenate([high * flat_eye, low * flat_eye], axis=1)
        return (
            jnp.dot(diagonal, risen, preferred_element_type=F32),
            jnp.dot(each, left, preferred_element_type=F32),
        )

    def products(tile, rise, end):
        here = lanes_of(tile)
        rise_high, rise_low = [
            jnp.concatenate([part] * (wide // LANES), axis=1) * own_chunk for part in split(jnp.exp(rise))
        ]
        rate_row = mode_row(mode_rate_ref[:, here])
        falling = mode_row(residue[:, here]) * jnp.exp(-rate_row * step)
        fall_high, fall_low = split(falling)
        half = tile % (WIDE // LANES)
        for chunk in range(rows // CHUNK):
            entering = (falling * jnp.exp(-float(CHUNK * chunk + 1) * rate_row)).astype(BF16)
            carry_ref[tile // (WIDE // LANES), chunk * CHUNK : (chunk + 1) * CHUNK, lanes_of(half)] = entering
            if chunk == 0:
                entering_ref[tile] = entering
        return (
            jnp.dot(jnp.concatenate([fall_high, fall_low], axis=0), rise_high, preferred_element_type=F32),
            jnp.dot(fall_high, rise_low, preferred_element_type=F32),
            jnp.exp(end),
        )

    def finish(tile, taps, rest, ending):
        taps = jnp.where(causal, taps[:CHUNK] + taps[CHUNK:] + rest, 0.0)
        inner_ref[tile] = jnp.concatenate([taps.astype(BF16), ending.astype(BF16)], axis=0)

    pipelined(width // LANES, exponents, products, finish)
    before = halo(before_ref, place_ref)
    query_copy.wait()

    def fetch(part):
        return (earlier_tokens(shift_ref[...], query_ref[:, lanes_of(part, WIDE)]),)

    def convolve(part, earlier):
        here = lanes_of(part, WIDE)
        weights = taps_of(weight_ref, 0, here)
        gate_ref[:, here] = wide_conv(query_ref[:, here], earlier, weights)
        head = query_ref[0:16, here].astype(F32)[:8]
        gate_ref[0:8, here] = short_conv(head, before[0, :, here], weights)

    pipelined(width // WIDE, fetch, convolve)
    residual_copy.wait()


def local_kernel(
    gate_ref,
    residual_ref,
    product_ref,
    first_ref,
    mode_rate_ref,
    inner_ref,
    entering_ref,
    skip_ref,
    base_ref,
):
    rows, width = product_ref.shape
    mask = group_mask(BF16)
    top = index_of((8, LANES), 0) < 2
    chunks = range(rows // CHUNK)

    def inside(tile):
        here = lanes_of(tile)
        pieces = []
        for chunk in chunks:
            piece = product_ref[chunk * CHUNK : (chunk + 1) * CHUNK, here]
            if chunk == 0:
                wide = piece.astype(F32)
                head = jnp.where(top, first_ref[:, here], wide[:8])
                piece = jnp.concatenate([head, wide[8:]], axis=0).astype(BF16)
            pieces.append(piece)
        found = []
        for pair in chunks[::2]:
            sources = jnp.concatenate([spread(pieces[pair + k], mask) for k in (0, 1)], axis=1)
            found.append(jnp.dot(inner_ref[tile], sources, preferred_element_type=F32))
        return found, pieces[0]

    def across(tile, inner, first):
        decay = jnp.exp(-float(CHUNK) * mode_rate_ref[:, lanes_of(tile)])
        state = jnp.zeros((MODES, LANES), F32)
        states = []
        for chunk in chunks:
            states.append(spread(state.astype(BF16), mask))
            state = decay * state + inner[chunk // 2][CHUNK:, lanes_of(chunk % 2)]
        outer = []
        for pair in chunks[::2]:
            two = jnp.concatenate(states[pair : pair + 2], axis=1)
            outer.append(jnp.dot(entering_ref[tile], two, preferred_element_type=F32))
        return [part[:CHUNK] for part in inner], outer, first

    def finish(tile, inner, outer, first):
        here = lanes_of(tile)
        skip = skip_ref[:, here]
        for chunk in chunks:
            span = slice(chunk * CHUNK, (chunk + 1) * CHUNK)
            piece = first if chunk == 0 else product_ref[span, here]
            conv = (inner[chunk // 2] + outer[chunk // 2])[:, lanes_of(chunk % 2)]
            whole = conv + skip * piece.astype(F32)
            base_ref[span, here] = residual_ref[span, here].astype(F32) + gate_ref[span, here] * whole

    pipelined(width // LANES, inside, across, finish)


def join_kernel(tokens, radix, stride, place_ref, own_ref, mode_rate_ref, entry_ref, *refs):
    others, (found_ref, group_ref) = refs[: radix - 1], refs[radix - 1 :]
    rate = mode_rate_ref[...]
    run = lax.rem(place_ref[0] // stride, radix)
    decay = jnp.exp(-float(tokens * stride) * rate)
    own = own_ref[...].astype(F32)
    values = [ref[...].astype(F32) for ref in others[::-1]]
    found = jnp.zeros_like(rate)
    total = jnp.zeros_like(rate)
    for position in range(radix):
        found = jnp.where(run == position, total, found)
        state = own
        for k, other in enumerate(values, 1):
            state = jnp.where(partner(run, k, radix) == position, other, state)
        total = decay * total + state
    if stride > 1:
        within = lax.rem(place_ref[0], stride).astype(F32) * float(tokens)
        found = jnp.exp(-within * rate) * found
    found_ref[...] = entry_ref[...] + found
    group_ref[...] = total.astype(BF16)


def carry_kernel(stride, radix, place_ref, base_ref, gate_ref, carry_ref, mode_rate_ref, inner_entry_ref, *refs):
    entry_refs, (summed_ref, squares_ref) = refs[:-2], refs[-2:]
    rows, width = base_ref.shape
    run = place_ref[0] // stride
    within = lax.rem(place_ref[0], stride).astype(F32) * float(rows)
    mask = group_mask(BF16)
    totals = [jnp.zeros((rows, LANES), F32)]
    nothing = jnp.zeros((LANES, LANES), BF16)

    def enter(tile):
        here = lanes_of(tile, WIDE)
        rate = mode_rate_ref[:, here]
        step = float(rows * stride)
        outer = jnp.zeros_like(rate)
        for k, ref in enumerate(entry_refs[::-1], 1):
            source = partner(run, k, radix)
            lag = jnp.maximum(run - 1 - source, 0).astype(F32) * step
            outer = outer + jnp.where(source < run, jnp.exp(-lag * rate) * ref[:, here].astype(F32), 0.0)
        entry = (inner_entry_ref[:, here] + jnp.exp(-within * rate) * outer).astype(BF16)
        left, right = spread(entry[:, :LANES], mask), spread(entry[:, LANES:], mask)
        both = jnp.concatenate(
            [jnp.concatenate([left, nothing], axis=1), jnp.concatenate([nothing, right], axis=1)], axis=0
        )
        return (jnp.dot(carry_ref[tile], both, preferred_element_type=F32),)

    def add(tile, carry):
        here = lanes_of(tile, WIDE)
        summed = base_ref[:, here] + gate_ref[:, here] * carry
        summed_ref[:, here] = summed
        square = summed * summed
        totals[0] = totals[0] + (square[:, :LANES] + square[:, LANES:])

    pipelined(width // WIDE, enter, add)
    total = totals[0]
    squares = lax.dot_general(
        jnp.ones((8, 2 * LANES), BF16),
        jnp.concatenate(split(total), axis=1),
        (((1,), (1,)), ((), ())),
        preferred_element_type=F32,
    )
    squares_ref[...] = squares[0:1]


def write_kernel(summed_ref, out_hbm, rounded_ref, sems):
    width = summed_ref.shape[1]
    copies = []
    for tile in range(width // WIDE):
        here = lanes_of(tile, WIDE)
        rounded_ref[:, here] = summed_ref[:, here].astype(BF16)
        span = pl.ds(tile * WIDE, WIDE)
        copies.append(pltpu.make_async_copy(rounded_ref.at[:, span], out_hbm.at[:, span], sems.at[tile]))
        copies[-1].start()
    for copy in copies:
        copy.wait()


def norm_kernel(full_width, summed_ref, gain_ref, *refs):
    squares_refs, (out_hbm, rounded_ref, sems) = refs[:-3], refs[-3:]
    rows, width = summed_ref.shape
    squares = squares_refs[0][...]
    for ref in squares_refs[1:]:
        squares = squares + ref[...]
    scale_row = lax.rsqrt(squares / full_width + 1e-05)
    scale = jnp.concatenate([as_column(scale_row[:, lanes_of(k)]) for k in range(rows // LANES)], axis=0)
    copies = []
    block = rows // 8
    for start in range(0, rows, block):
        span = slice(start, start + block)
        for tile in range(width // LANES):
            here = lanes_of(tile)
            rounded_ref[span, here] = (summed_ref[span, here] * scale[span] * gain_ref[:, here]).astype(BF16)
        there = pl.ds(start, block)
        copies.append(pltpu.make_async_copy(rounded_ref.at[there, :], out_hbm.at[there, :], sems.at[start // block]))
        copies[-1].start()
    for copy in copies:
        copy.wait()


def params():
    return pltpu.CompilerParams(vmem_limit_bytes=VMEM_LIMIT)


def cost(microseconds):
    return pl.CostEstimate(flops=0, bytes_accessed=int(microseconds * 3.0e6), transcendentals=0)


def radices(count):
    found = []
    for radix in (4, 4, 4, 3, 3, 2, 5, 7):
        if count % radix == 0:
            found.append(radix)
            count //= radix
    return found + ([count] if count > 1 else [])


def partner(run, k, radix):
    if radix & (radix - 1) == 0:
        return run ^ k
    return (run - k + radix) % radix


def routes(count, stride, radix):
    found = []
    for k in range(1, radix):
        route = []
        for i in range(count):
            run = i // stride % radix
            route.append((i + (partner(run, k, radix) - run) * stride, i))
        found.append(route)
    return found


def ring(count, shift):
    return [(i, (i + shift) % count) for i in range(count)]


def per_device(projected, short_weight, rates, residues, skip, residual, gain):
    rows, width = projected.shape[1:]
    taps = short_weight.shape[0]
    peers = lax.axis_size("ctx")
    full_width = width * lax.axis_size("fsdp")
    place = lax.axis_index("ctx").astype(jnp.int32).reshape(1)
    hbm_spec = pl.BlockSpec(memory_space=pltpu.HBM)
    vmem_spec = pl.BlockSpec(memory_space=pltpu.VMEM)
    smem_spec = pl.BlockSpec(memory_space=pltpu.SMEM)
    tiles = width // LANES
    wides = width // WIDE

    def kept(array):
        return pltpu.with_memory_space_constraint(array, pltpu.HBM)

    def f32(*shape):
        return jax.ShapeDtypeStruct(shape, F32)

    def bf16(*shape):
        return jax.ShapeDtypeStruct(shape, BF16)

    before = lax.ppermute(projected[:, rows - (taps - 1) :, :], "ctx", ring(peers, 1))

    product, state, mode_rate, head, weights, residue = pl.pallas_call(
        state_kernel,
        in_specs=[hbm_spec] * 4,
        out_shape=[
            bf16(rows, width),
            f32(MODES, width),
            f32(MODES, width),
            f32(2, 8, width),
            f32(*short_weight.shape),
            f32(MODES, residues.shape[0]),
        ],
        scratch_shapes=[
            pltpu.VMEM((2, rows, width), BF16),
            pltpu.VMEM((wides, WIDE, rows), BF16),
            pltpu.VMEM((2 * rows, rows), BF16),
            pltpu.VMEM(short_weight.shape, BF16),
            pltpu.VMEM((MODES, rates.shape[0]), F32),
            pltpu.SemaphoreType.DMA((9,)),
            pltpu.SemaphoreType.DMA((2,)),
        ],
        compiler_params=params(),
        cost_estimate=cost(3),
        name="block_state",
    )(kept(projected), kept(short_weight), kept(rates.T), kept(residues.T))

    full_state, first = pl.pallas_call(
        lambda *refs: head_kernel(rows, *refs),
        in_specs=[smem_spec] + [vmem_spec] * 5,
        out_shape=[bf16(MODES, width), f32(8, width)],
        compiler_params=params(),
        cost_estimate=cost(0.2),
        name="head_tokens",
    )(place, before, head, weights, state, mode_rate)

    inner, entering, carry_table, gate, residual_here = pl.pallas_call(
        prepare_kernel,
        in_specs=[smem_spec] + [hbm_spec] * 2 + [vmem_spec] * 4,
        out_shape=[
            bf16(tiles, CHUNK + MODES, GROUPS * CHUNK),
            bf16(tiles, CHUNK, LANES),
            bf16(wides, rows, WIDE),
            f32(rows, width),
            bf16(rows, width),
        ],
        scratch_shapes=[
            pltpu.VMEM((rows, width), BF16),
            pltpu.VMEM((2 * rows, rows), BF16),
            pltpu.SemaphoreType.DMA((2,)),
        ],
        compiler_params=params(),
        cost_estimate=cost(2),
        name="prepare",
    )(place, kept(projected), kept(residual), residue, before, weights, mode_rate)

    group, entry, stride = full_state, jnp.zeros((MODES, width), F32), 1
    levels = radices(peers)
    for level, radix in enumerate(levels):
        size = stride * radix
        if level == len(levels) - 1:
            break
        others = [lax.ppermute(group, "ctx", route) for route in routes(peers, stride, radix)[::-1]]
        if level == 0:
            others[0], inner = lax.optimization_barrier((others[0], inner))
        entry, group = pl.pallas_call(
            lambda *refs, radix=radix, stride=stride: join_kernel(rows, radix, stride, *refs),
            in_specs=[smem_spec] + [vmem_spec] * (2 + radix),
            out_shape=[f32(MODES, width), bf16(MODES, width)],
            compiler_params=params(),
            cost_estimate=cost(0.2),
            name="join",
        )(place, group, mode_rate, entry, *others)
        stride = size
    received = [lax.ppermute(group, "ctx", route) for route in routes(peers, stride, levels[-1])[::-1]]

    base = pl.pallas_call(
        local_kernel,
        out_shape=f32(rows, width),
        compiler_params=params(),
        cost_estimate=cost(5),
        name="local_conv",
    )(gate, residual_here, product, first, mode_rate, inner, entering, skip[None])

    count = lax.axis_size("fsdp")
    summed, squares = pl.pallas_call(
        lambda *refs: carry_kernel(stride, levels[-1], *refs),
        in_specs=[smem_spec] + [vmem_spec] * (5 + len(received)),
        out_shape=[f32(rows, width), f32(1, rows)],
        compiler_params=params(),
        cost_estimate=cost(1),
        name="add_carry",
    )(place, base, gate, carry_table, mode_rate, entry, *received)

    parts = [lax.ppermute(squares, "fsdp", route) for route in routes(count, 1, count)[::-1]]

    def write(kernel, operands, name):
        return pl.pallas_call(
            kernel,
            out_specs=hbm_spec,
            out_shape=bf16(rows, width),
            scratch_shapes=[pltpu.VMEM((rows, width), BF16), pltpu.SemaphoreType.DMA((max(8, wides),))],
            compiler_params=params(),
            cost_estimate=cost(1),
            name=name,
        )(*operands)

    new_residual = write(write_kernel, (summed,), "new_residual")
    normed = write(
        lambda *refs: norm_kernel(full_width, *refs), (summed, gain[None], squares, *parts), "normed"
    )
    return (new_residual, normed)


def solution(mesh):
    return jax.shard_map(
        per_device,
        mesh=mesh,
        in_specs=(
            P(None, "ctx", "fsdp"),
            P(None, None, "fsdp"),
            P("fsdp", None),
            P("fsdp", None),
            P("fsdp"),
            P("ctx", "fsdp"),
            P("fsdp"),
        ),
        out_specs=(P("ctx", "fsdp"), P("ctx", "fsdp")),
        check_vma=False,
    )
```

```python
import jax
import jax.numpy as jnp
from jax import lax
from jax.experimental import pallas as pl
from jax.experimental.pallas import tpu as pltpu
from jax.sharding import PartitionSpec as P

CHANNELS_PER_GRP = 16
MODES = 16
CHUNK = 32
LANES = 128
WIDE = 256
GROUPS = LANES // CHANNELS_PER_GRP
VMEM_LIMIT = 16 * 1024 * 1024
F32 = jnp.float32
BF16 = jnp.bfloat16


def index_of(shape, dim):
    return lax.broadcasted_iota(jnp.int32, shape, dim)


def pipelined(count, *stages):
    held = {}
    for step in range(count + len(stages) - 1):
        for k, stage in enumerate(stages):
            item = step - k
            if 0 <= item < count:
                held[item] = stage(item, *held.get(item, ()))


def lanes_of(tile, width=LANES):
    return slice(tile * width, (tile + 1) * width)


def selectors(groups):
    shape = (groups, WIDE)
    found = []
    for tile in range(groups * CHANNELS_PER_GRP // WIDE):
        own = index_of(shape, 0) == index_of(shape, 1) // CHANNELS_PER_GRP + tile * (WIDE // CHANNELS_PER_GRP)
        found.append(jnp.where(own, 1.0, 0.0).astype(BF16))
    return found


def per_channel(table, chosen):
    high = table.astype(BF16)
    rest = table - high.astype(F32)
    middle = rest.astype(BF16)
    low = (rest - middle.astype(F32)).astype(BF16)
    terms = jnp.concatenate([high, middle, low], axis=0)
    parts = []
    for selector in chosen:
        three = jnp.dot(terms, selector, preferred_element_type=F32)
        parts.append(three[:MODES] + three[MODES : 2 * MODES] + three[2 * MODES :])
    return jnp.concatenate(parts, axis=1)


def mode_row(channel_table):
    own = index_of(channel_table.shape, 0) == (index_of(channel_table.shape, 1) & (MODES - 1))
    return jnp.sum(jnp.where(own, channel_table, 0.0), axis=0, keepdims=True)


def as_column(row):
    return jnp.transpose(jnp.broadcast_to(row, (LANES, LANES)))


def own_mode(dtype):
    shape = (GROUPS, MODES, LANES)
    own = index_of(shape, 0) * MODES + index_of(shape, 1) == index_of(shape, 2)
    return jnp.where(own, 1.0, 0.0).astype(dtype)


def split(x):
    high = x.astype(BF16)
    return high, (x - high.astype(F32)).astype(BF16)


def group_mask(dtype):
    shape = (GROUPS, MODES, LANES)
    own = index_of(shape, 0) == index_of(shape, 2) // CHANNELS_PER_GRP
    return jnp.where(own, 1.0, 0.0).astype(dtype)


def spread(rows, mask):
    size = rows.shape[0]
    copies = rows.reshape(1, size // MODES, MODES, LANES) * mask.reshape(GROUPS, 1, MODES, LANES)
    return copies.reshape(GROUPS * size, LANES)


def shifted(block, before):
    one = pltpu.roll(block, 1, 0)
    two = pltpu.roll(block, 2, 0)
    first = index_of((8, block.shape[1]), 0)
    near, far = (0.0, 0.0) if before is None else (before[1:2], before[0:1])
    head_one = jnp.where(first == 0, near, one[:8])
    head_two = jnp.where(first == 0, far, jnp.where(first == 1, near, two[:8]))
    if block.shape[0] == 8:
        return head_one, head_two
    return jnp.concatenate([head_one, one[8:]], axis=0), jnp.concatenate([head_two, two[8:]], axis=0)


def short_conv(block, before, weights):
    one, two = shifted(block, before)
    return weights[0] * block + weights[1] * one + weights[2] * two


def shift_matrix(rows):
    shape = (2 * rows, rows)
    target = index_of(shape, 0)
    source = index_of(shape, 1)
    taken = jnp.where(target < rows, target - 1, target - (rows + 2))
    return jnp.where(source == taken, 1.0, 0.0).astype(BF16)


def earlier_tokens(shift, block):
    return jnp.dot(shift, block, preferred_element_type=F32)


def wide_conv(block, earlier, weights):
    rows = block.shape[0]
    wide = block.astype(F32)
    if earlier.shape[0] == rows:
        one = pltpu.roll(wide, 1, 0)
        head = jnp.where(index_of((8, wide.shape[1]), 0) == 0, 0.0, one[:8])
        one = jnp.concatenate([head, one[8:]], axis=0)
    else:
        one = earlier[:rows]
    return weights[0] * wide + weights[1] * one + weights[2] * earlier[-rows:]


def taps_of(weights, feature, lanes):
    return [weights[tap, feature : feature + 1, lanes] for tap in range(weights.shape[0])]


def state_kernel(
    projected_ref,
    weight_hbm,
    rate_hbm,
    residue_hbm,
    residual_hbm,
    product_ref,
    state_ref,
    mode_rate_ref,
    head_ref,
    weight_ref,
    query_ref,
    residue_ref,
    residual_ref,
    buffer_ref,
    ending_ref,
    shift_ref,
    short_ref,
    rate_ref,
    sems,
    small_sems,
):
    rows, width = product_ref.shape
    wides = width // WIDE
    rate_copy = pltpu.make_async_copy(rate_hbm, rate_ref, small_sems.at[0])
    rate_copy.start()
    weight_copy = pltpu.make_async_copy(weight_hbm, short_ref, small_sems.at[1])
    weight_copy.start()
    copies = [pltpu.make_async_copy(projected_ref.at[1 + c], buffer_ref.at[c], sems.at[c]) for c in (0, 1)]
    later = [
        pltpu.make_async_copy(residue_hbm, residue_ref, sems.at[2]),
        pltpu.make_async_copy(projected_ref.at[0], query_ref, sems.at[3]),
        pltpu.make_async_copy(residual_hbm, residual_ref, sems.at[4]),
    ]
    for copy in copies:
        copy.start()
    shift_ref[...] = shift_matrix(rows)
    chosen = selectors(rate_ref.shape[1])
    eye = own_mode(BF16)
    mask = group_mask(F32)
    token = index_of((2 * LANES, rows), 1)
    left = jnp.where(token < 2, -1e30, (token - (rows - 1)).astype(F32)).astype(BF16)
    rate_copy.wait()
    mode_rate = per_channel(rate_ref[...], chosen)
    mode_rate_ref[...] = mode_rate

    def exponents(tile):
        high, low = split(mode_rate[:, lanes_of(tile)])
        diagonal = jnp.concatenate([spread(high, eye), spread(low, eye)], axis=1)
        return (jnp.dot(diagonal, left, preferred_element_type=F32),)

    def endings(tile, exponent):
        ending_ref[tile // 2, lanes_of(tile % 2), :] = jnp.exp(exponent).astype(BF16)

    pipelined(width // LANES, exponents, endings)
    weight_copy.wait()
    weights = short_ref[...].astype(F32)
    weight_ref[...] = weights
    for copy in copies:
        copy.wait()
    for copy in later:
        copy.start()

    def fetch(wide):
        here = lanes_of(wide, WIDE)
        return (
            earlier_tokens(shift_ref[...], buffer_ref[0, :, here]),
            earlier_tokens(shift_ref[rows:, :], buffer_ref[1, :, here]),
        )

    def multiply(wide, *earlier):
        here = lanes_of(wide, WIDE)
        parts = []
        for c in (0, 1):
            head_ref[c, :, here] = buffer_ref[c, 0:16, here].astype(F32)[:8]
            parts.append(wide_conv(buffer_ref[c, :, here], earlier[c], taps_of(weights, c + 1, here)))
        product = (parts[0] * parts[1]).astype(BF16)
        product_ref[:, here] = product
        return (jnp.dot(ending_ref[wide], product, preferred_element_type=F32),)

    def leave(wide, every):
        for half in range(WIDE // LANES):
            own = every[lanes_of(half), lanes_of(half)].reshape(GROUPS, MODES, LANES)
            state_ref[:, lanes_of((WIDE // LANES) * wide + half)] = jnp.sum(own * mask, axis=0)

    pipelined(wides, fetch, multiply, leave)
    for copy in later:
        copy.wait()


def halo(before_ref, place_ref):
    return jnp.where(place_ref[0] > 0, before_ref[...].astype(F32), 0.0)


def head_kernel(rows, place_ref, before_ref, head_ref, weight_ref, state_ref, mode_rate_ref, full_ref, first_ref):
    before = halo(before_ref, place_ref)
    everything = slice(0, head_ref.shape[2])
    parts = [short_conv(head_ref[c], before[c + 1], taps_of(weight_ref, c + 1, everything)) for c in (0, 1)]
    first = (parts[0] * parts[1]).astype(BF16).astype(F32)
    first_ref[...] = first
    rate = mode_rate_ref[...]
    early = jnp.exp(-float(rows - 1) * rate) * first[0:1] + jnp.exp(-float(rows - 2) * rate) * first[1:2]
    full_ref[...] = (state_ref[...] + early).astype(BF16)


def prepare_kernel(
    place_ref,
    query_ref,
    residue_ref,
    before_ref,
    weight_ref,
    mode_rate_ref,
    inner_ref,
    entering_ref,
    carry_ref,
    gate_ref,
    shift_ref,
):
    rows, width = gate_ref.shape
    shift_ref[...] = shift_matrix(rows)
    residue = per_channel(residue_ref[...], selectors(residue_ref.shape[1]))
    wide = GROUPS * CHUNK
    step = index_of((CHUNK, LANES), 0).astype(F32)
    causal = (index_of((CHUNK, wide), 1) & (CHUNK - 1)) <= index_of((CHUNK, wide), 0)
    eye = own_mode(BF16)
    flat_eye = jnp.where((index_of((MODES, LANES), 1) & (MODES - 1)) == index_of((MODES, LANES), 0), 1.0, 0.0)
    flat_eye = flat_eye.astype(BF16)
    shape = (2 * LANES, wide)
    source = (index_of(shape, 1) & (CHUNK - 1)).astype(F32)
    own = (index_of(shape, 0) & (LANES - 1)) // MODES == index_of(shape, 1) // CHUNK
    own_chunk = jnp.where(own[:LANES], 1.0, 0.0).astype(BF16)
    risen = source[:, :LANES].astype(BF16)
    left = jnp.where(own, source - (CHUNK - 1), 0.0).astype(BF16)

    def exponents(tile):
        rate = mode_rate_ref[:, lanes_of(tile)]
        high, low = split(rate)
        diagonal = jnp.concatenate([spread(high, eye), spread(low, eye)], axis=1)
        each = jnp.concatenate([high * flat_eye, low * flat_eye], axis=1)
        return (
            jnp.dot(diagonal, risen, preferred_element_type=F32),
            jnp.dot(each, left, preferred_element_type=F32),
        )

    def products(tile, rise, end):
        here = lanes_of(tile)
        rise_high, rise_low = [
            jnp.concatenate([part] * (wide // LANES), axis=1) * own_chunk for part in split(jnp.exp(rise))
        ]
        rate_row = mode_row(mode_rate_ref[:, here])
        falling = mode_row(residue[:, here]) * jnp.exp(-rate_row * step)
        fall_high, fall_low = split(falling)
        half = tile % (WIDE // LANES)
        for chunk in range(rows // CHUNK):
            entering = (falling * jnp.exp(-float(CHUNK * chunk + 1) * rate_row)).astype(BF16)
            carry_ref[tile // (WIDE // LANES), chunk * CHUNK : (chunk + 1) * CHUNK, lanes_of(half)] = entering
            if chunk == 0:
                entering_ref[tile] = entering
        return (
            jnp.dot(jnp.concatenate([fall_high, fall_low], axis=0), rise_high, preferred_element_type=F32),
            jnp.dot(fall_high, rise_low, preferred_element_type=F32),
            jnp.exp(end),
        )

    def finish(tile, taps, rest, ending):
        taps = jnp.where(causal, taps[:CHUNK] + taps[CHUNK:] + rest, 0.0)
        inner_ref[tile] = jnp.concatenate([taps.astype(BF16), ending.astype(BF16)], axis=0)

    pipelined(width // LANES, exponents, products, finish)
    before = halo(before_ref, place_ref)

    def fetch(part):
        return (earlier_tokens(shift_ref[...], query_ref[:, lanes_of(part, WIDE)]),)

    def convolve(part, earlier):
        here = lanes_of(part, WIDE)
        weights = taps_of(weight_ref, 0, here)
        gate_ref[:, here] = wide_conv(query_ref[:, here], earlier, weights)
        head = query_ref[0:16, here].astype(F32)[:8]
        gate_ref[0:8, here] = short_conv(head, before[0, :, here], weights)

    pipelined(width // WIDE, fetch, convolve)


def local_kernel(
    start,
    gate_ref,
    residual_ref,
    product_ref,
    first_ref,
    mode_rate_ref,
    inner_ref,
    entering_ref,
    skip_ref,
    base_ref,
):
    rows, width = base_ref.shape
    mask = group_mask(BF16)
    top = index_of((8, LANES), 0) < 2
    chunks = range(rows // CHUNK)

    def inside(item):
        tile = start + item
        here = lanes_of(tile)
        pieces = []
        for chunk in chunks:
            piece = product_ref[chunk * CHUNK : (chunk + 1) * CHUNK, here]
            if chunk == 0:
                wide = piece.astype(F32)
                head = jnp.where(top, first_ref[:, here], wide[:8])
                piece = jnp.concatenate([head, wide[8:]], axis=0).astype(BF16)
            pieces.append(piece)
        found = []
        for pair in chunks[::2]:
            sources = jnp.concatenate([spread(pieces[pair + k], mask) for k in (0, 1)], axis=1)
            found.append(jnp.dot(inner_ref[tile], sources, preferred_element_type=F32))
        return found, pieces[0]

    def across(item, inner, first):
        tile = start + item
        decay = jnp.exp(-float(CHUNK) * mode_rate_ref[:, lanes_of(tile)])
        state = jnp.zeros((MODES, LANES), F32)
        states = []
        for chunk in chunks:
            states.append(spread(state.astype(BF16), mask))
            state = decay * state + inner[chunk // 2][CHUNK:, lanes_of(chunk % 2)]
        outer = []
        for pair in chunks[::2]:
            two = jnp.concatenate(states[pair : pair + 2], axis=1)
            outer.append(jnp.dot(entering_ref[tile], two, preferred_element_type=F32))
        return [part[:CHUNK] for part in inner], outer, first

    def finish(item, inner, outer, first):
        here = lanes_of(start + item)
        skip = skip_ref[:, here]
        for chunk in chunks:
            span = slice(chunk * CHUNK, (chunk + 1) * CHUNK)
            piece = first if chunk == 0 else product_ref[span, here]
            conv = (inner[chunk // 2] + outer[chunk // 2])[:, lanes_of(chunk % 2)]
            whole = conv + skip * piece.astype(F32)
            base_ref[span, lanes_of(item)] = residual_ref[span, here].astype(F32) + gate_ref[span, here] * whole

    pipelined(width // LANES, inside, across, finish)


def join_kernel(tokens, radix, stride, place_ref, own_ref, mode_rate_ref, entry_ref, *refs):
    others, (found_ref, group_ref) = refs[: radix - 1], refs[radix - 1 :]
    rate = mode_rate_ref[...]
    run = lax.rem(place_ref[0] // stride, radix)
    decay = jnp.exp(-float(tokens * stride) * rate)
    own = own_ref[...].astype(F32)
    values = [ref[...].astype(F32) for ref in others[::-1]]
    found = jnp.zeros_like(rate)
    total = jnp.zeros_like(rate)
    for position in range(radix):
        found = jnp.where(run == position, total, found)
        state = own
        for k, other in enumerate(values, 1):
            state = jnp.where(partner(run, k, radix) == position, other, state)
        total = decay * total + state
    if stride > 1:
        within = lax.rem(place_ref[0], stride).astype(F32) * float(tokens)
        found = jnp.exp(-within * rate) * found
    found_ref[...] = entry_ref[...] + found
    group_ref[...] = total.astype(BF16)


def carry_kernel(
    stride, radix, place_ref, left_ref, right_ref, gate_ref, carry_ref, mode_rate_ref, inner_entry_ref, *refs
):
    entry_refs, (summed_ref, squares_ref) = refs[:-2], refs[-2:]
    rows, width = gate_ref.shape
    split_at = left_ref.shape[1] // WIDE
    run = place_ref[0] // stride
    within = lax.rem(place_ref[0], stride).astype(F32) * float(rows)
    mask = group_mask(BF16)
    totals = [jnp.zeros((rows, LANES), F32)]
    nothing = jnp.zeros((LANES, LANES), BF16)

    def enter(tile):
        here = lanes_of(tile, WIDE)
        rate = mode_rate_ref[:, here]
        step = float(rows * stride)
        outer = jnp.zeros_like(rate)
        for k, ref in enumerate(entry_refs[::-1], 1):
            source = partner(run, k, radix)
            lag = jnp.maximum(run - 1 - source, 0).astype(F32) * step
            outer = outer + jnp.where(source < run, jnp.exp(-lag * rate) * ref[:, here].astype(F32), 0.0)
        entry = (inner_entry_ref[:, here] + jnp.exp(-within * rate) * outer).astype(BF16)
        left, right = spread(entry[:, :LANES], mask), spread(entry[:, LANES:], mask)
        both = jnp.concatenate(
            [jnp.concatenate([left, nothing], axis=1), jnp.concatenate([nothing, right], axis=1)], axis=0
        )
        return (jnp.dot(carry_ref[tile], both, preferred_element_type=F32),)

    def add(tile, carry):
        here = lanes_of(tile, WIDE)
        if tile < split_at:
            base = left_ref[:, here]
        else:
            base = right_ref[:, lanes_of(tile - split_at, WIDE)]
        summed = base + gate_ref[:, here] * carry
        summed_ref[:, here] = summed
        square = summed * summed
        totals[0] = totals[0] + (square[:, :LANES] + square[:, LANES:])

    pipelined(width // WIDE, enter, add)
    total = totals[0]
    squares = lax.dot_general(
        jnp.ones((8, 2 * LANES), BF16),
        jnp.concatenate(split(total), axis=1),
        (((1,), (1,)), ((), ())),
        preferred_element_type=F32,
    )
    squares_ref[...] = squares[0:1]


def write_kernel(summed_ref, out_hbm, rounded_ref, sems):
    width = summed_ref.shape[1]
    copies = []
    for tile in range(width // WIDE):
        here = lanes_of(tile, WIDE)
        rounded_ref[:, here] = summed_ref[:, here].astype(BF16)
        span = pl.ds(tile * WIDE, WIDE)
        copies.append(pltpu.make_async_copy(rounded_ref.at[:, span], out_hbm.at[:, span], sems.at[tile]))
        copies[-1].start()
    for copy in copies:
        copy.wait()


def norm_kernel(full_width, summed_ref, gain_ref, *refs):
    squares_refs, (out_hbm, rounded_ref, sems) = refs[:-3], refs[-3:]
    rows, width = summed_ref.shape
    squares = squares_refs[0][...]
    for ref in squares_refs[1:]:
        squares = squares + ref[...]
    scale_row = lax.rsqrt(squares / full_width + 1e-05)
    scale = jnp.concatenate([as_column(scale_row[:, lanes_of(k)]) for k in range(rows // LANES)], axis=0)
    copies = []
    block = rows // 8
    for start in range(0, rows, block):
        span = slice(start, start + block)
        for tile in range(width // LANES):
            here = lanes_of(tile)
            rounded_ref[span, here] = (summed_ref[span, here] * scale[span] * gain_ref[:, here]).astype(BF16)
        there = pl.ds(start, block)
        copies.append(pltpu.make_async_copy(rounded_ref.at[there, :], out_hbm.at[there, :], sems.at[start // block]))
        copies[-1].start()
    for copy in copies:
        copy.wait()


def params():
    return pltpu.CompilerParams(vmem_limit_bytes=VMEM_LIMIT)


def cost(microseconds):
    return pl.CostEstimate(flops=0, bytes_accessed=int(microseconds * 3.0e6), transcendentals=0)


def radices(count):
    found = []
    for radix in (4, 4, 4, 3, 3, 2, 5, 7):
        if count % radix == 0:
            found.append(radix)
            count //= radix
    return found + ([count] if count > 1 else [])


def partner(run, k, radix):
    if radix & (radix - 1) == 0:
        return run ^ k
    return (run - k + radix) % radix


def routes(count, stride, radix):
    found = []
    for k in range(1, radix):
        route = []
        for i in range(count):
            run = i // stride % radix
            route.append((i + (partner(run, k, radix) - run) * stride, i))
        found.append(route)
    return found


def ring(count, shift):
    return [(i, (i + shift) % count) for i in range(count)]


def per_device(projected, short_weight, rates, residues, skip, residual, gain):
    rows, width = projected.shape[1:]
    taps = short_weight.shape[0]
    peers = lax.axis_size("ctx")
    full_width = width * lax.axis_size("fsdp")
    place = lax.axis_index("ctx").astype(jnp.int32).reshape(1)
    hbm_spec = pl.BlockSpec(memory_space=pltpu.HBM)
    vmem_spec = pl.BlockSpec(memory_space=pltpu.VMEM)
    smem_spec = pl.BlockSpec(memory_space=pltpu.SMEM)
    tiles = width // LANES
    wides = width // WIDE

    def kept(array):
        return pltpu.with_memory_space_constraint(array, pltpu.HBM)

    def f32(*shape):
        return jax.ShapeDtypeStruct(shape, F32)

    def bf16(*shape):
        return jax.ShapeDtypeStruct(shape, BF16)

    before = lax.ppermute(projected[:, rows - (taps - 1) :, :], "ctx", ring(peers, 1))

    product, state, mode_rate, head, weights, query, residue, residual_here = pl.pallas_call(
        state_kernel,
        in_specs=[hbm_spec] * 5,
        out_shape=[
            bf16(rows, width),
            f32(MODES, width),
            f32(MODES, width),
            f32(2, 8, width),
            f32(*short_weight.shape),
            bf16(rows, width),
            f32(MODES, residues.shape[0]),
            bf16(rows, width),
        ],
        scratch_shapes=[
            pltpu.VMEM((2, rows, width), BF16),
            pltpu.VMEM((wides, WIDE, rows), BF16),
            pltpu.VMEM((2 * rows, rows), BF16),
            pltpu.VMEM(short_weight.shape, BF16),
            pltpu.VMEM((MODES, rates.shape[0]), F32),
            pltpu.SemaphoreType.DMA((5,)),
            pltpu.SemaphoreType.DMA((2,)),
        ],
        compiler_params=params(),
        cost_estimate=cost(3),
        name="block_state",
    )(kept(projected), kept(short_weight), kept(rates.T), kept(residues.T), kept(residual))

    full_state, first = pl.pallas_call(
        lambda *refs: head_kernel(rows, *refs),
        in_specs=[smem_spec] + [vmem_spec] * 5,
        out_shape=[bf16(MODES, width), f32(8, width)],
        compiler_params=params(),
        cost_estimate=cost(0.2),
        name="head_tokens",
    )(place, before, head, weights, state, mode_rate)

    inner, entering, carry_table, gate = pl.pallas_call(
        prepare_kernel,
        in_specs=[smem_spec] + [vmem_spec] * 5,
        out_shape=[
            bf16(tiles, CHUNK + MODES, GROUPS * CHUNK),
            bf16(tiles, CHUNK, LANES),
            bf16(wides, rows, WIDE),
            f32(rows, width),
        ],
        scratch_shapes=[pltpu.VMEM((2 * rows, rows), BF16)],
        compiler_params=params(),
        cost_estimate=cost(2),
        name="prepare",
    )(place, query, residue, before, weights, mode_rate)

    def local(start, count):
        return pl.pallas_call(
            lambda *refs: local_kernel(start, *refs),
            out_shape=f32(rows, count * LANES),
            compiler_params=params(),
            cost_estimate=cost(0.15 * count),
            name="local_conv",
        )(gate, residual_here, product, first, mode_rate, inner, entering, skip[None])

    early = max(2, tiles // 8 * 2)
    left = local(0, early)

    group, entry, stride = full_state, jnp.zeros((MODES, width), F32), 1
    levels = radices(peers)
    for level, radix in enumerate(levels):
        size = stride * radix
        if level == len(levels) - 1:
            break
        others = [lax.ppermute(group, "ctx", route) for route in routes(peers, stride, radix)[::-1]]
        if level == 0:
            others[0], left = lax.optimization_barrier((others[0], left))
        entry, group = pl.pallas_call(
            lambda *refs, radix=radix, stride=stride: join_kernel(rows, radix, stride, *refs),
            in_specs=[smem_spec] + [vmem_spec] * (2 + radix),
            out_shape=[f32(MODES, width), bf16(MODES, width)],
            compiler_params=params(),
            cost_estimate=cost(0.2),
            name="join",
        )(place, group, mode_rate, entry, *others)
        stride = size
    received = [lax.ppermute(group, "ctx", route) for route in routes(peers, stride, levels[-1])[::-1]]

    right = local(early, tiles - early)

    count = lax.axis_size("fsdp")
    summed, squares = pl.pallas_call(
        lambda *refs: carry_kernel(stride, levels[-1], *refs),
        in_specs=[smem_spec] + [vmem_spec] * (6 + len(received)),
        out_shape=[f32(rows, width), f32(1, rows)],
        compiler_params=params(),
        cost_estimate=cost(1),
        name="add_carry",
    )(place, left, right, gate, carry_table, mode_rate, entry, *received)

    parts = [lax.ppermute(squares, "fsdp", route) for route in routes(count, 1, count)[::-1]]

    def write(kernel, operands, name):
        return pl.pallas_call(
            kernel,
            out_specs=hbm_spec,
            out_shape=bf16(rows, width),
            scratch_shapes=[pltpu.VMEM((rows, width), BF16), pltpu.SemaphoreType.DMA((max(8, wides),))],
            compiler_params=params(),
            cost_estimate=cost(1),
            name=name,
        )(*operands)

    new_residual = write(write_kernel, (summed,), "new_residual")
    normed = write(
        lambda *refs: norm_kernel(full_width, *refs), (summed, gain[None], squares, *parts), "normed"
    )
    return (new_residual, normed)


def solution(mesh):
    return jax.shard_map(
        per_device,
        mesh=mesh,
        in_specs=(
            P(None, "ctx", "fsdp"),
            P(None, None, "fsdp"),
            P("fsdp", None),
            P("fsdp", None),
            P("fsdp"),
            P("ctx", "fsdp"),
            P("fsdp"),
        ),
        out_specs=(P("ctx", "fsdp"), P("ctx", "fsdp")),
        check_vma=False,
    )
```

```python
import jax
import jax.numpy as jnp
from jax import lax
from jax.experimental import pallas as pl
from jax.experimental.pallas import tpu as pltpu
from jax.sharding import PartitionSpec as P

CHANNELS_PER_GRP = 16
MODES = 16
CHUNK = 32
LANES = 128
WIDE = 256
GROUPS = LANES // CHANNELS_PER_GRP
VMEM_LIMIT = 16 * 1024 * 1024
F32 = jnp.float32
BF16 = jnp.bfloat16


def index_of(shape, dim):
    return lax.broadcasted_iota(jnp.int32, shape, dim)


def pipelined(count, *stages):
    held = {}
    for step in range(count + len(stages) - 1):
        for k, stage in enumerate(stages):
            item = step - k
            if 0 <= item < count:
                held[item] = stage(item, *held.get(item, ()))


def lanes_of(tile, width=LANES):
    return slice(tile * width, (tile + 1) * width)


def selectors(groups):
    shape = (groups, WIDE)
    found = []
    for tile in range(groups * CHANNELS_PER_GRP // WIDE):
        own = index_of(shape, 0) == index_of(shape, 1) // CHANNELS_PER_GRP + tile * (WIDE // CHANNELS_PER_GRP)
        found.append(jnp.where(own, 1.0, 0.0).astype(BF16))
    return found


def per_channel(table, chosen):
    high = table.astype(BF16)
    rest = table - high.astype(F32)
    middle = rest.astype(BF16)
    low = (rest - middle.astype(F32)).astype(BF16)
    terms = jnp.concatenate([high, middle, low], axis=0)
    parts = []
    for selector in chosen:
        three = jnp.dot(terms, selector, preferred_element_type=F32)
        parts.append(three[:MODES] + three[MODES : 2 * MODES] + three[2 * MODES :])
    return jnp.concatenate(parts, axis=1)


def mode_row(channel_table):
    own = index_of(channel_table.shape, 0) == (index_of(channel_table.shape, 1) & (MODES - 1))
    return jnp.sum(jnp.where(own, channel_table, 0.0), axis=0, keepdims=True)


def as_column(row):
    return jnp.transpose(jnp.broadcast_to(row, (LANES, LANES)))


def own_mode(dtype):
    shape = (GROUPS, MODES, LANES)
    own = index_of(shape, 0) * MODES + index_of(shape, 1) == index_of(shape, 2)
    return jnp.where(own, 1.0, 0.0).astype(dtype)


def split(x):
    high = x.astype(BF16)
    return high, (x - high.astype(F32)).astype(BF16)


def group_mask(dtype):
    shape = (GROUPS, MODES, LANES)
    own = index_of(shape, 0) == index_of(shape, 2) // CHANNELS_PER_GRP
    return jnp.where(own, 1.0, 0.0).astype(dtype)


def spread(rows, mask):
    size = rows.shape[0]
    copies = rows.reshape(1, size // MODES, MODES, LANES) * mask.reshape(GROUPS, 1, MODES, LANES)
    return copies.reshape(GROUPS * size, LANES)


def shifted(block, before):
    one = pltpu.roll(block, 1, 0)
    two = pltpu.roll(block, 2, 0)
    first = index_of((8, block.shape[1]), 0)
    near, far = (0.0, 0.0) if before is None else (before[1:2], before[0:1])
    head_one = jnp.where(first == 0, near, one[:8])
    head_two = jnp.where(first == 0, far, jnp.where(first == 1, near, two[:8]))
    if block.shape[0] == 8:
        return head_one, head_two
    return jnp.concatenate([head_one, one[8:]], axis=0), jnp.concatenate([head_two, two[8:]], axis=0)


def short_conv(block, before, weights):
    one, two = shifted(block, before)
    return weights[0] * block + weights[1] * one + weights[2] * two


def shift_matrix(rows):
    shape = (2 * rows, rows)
    target = index_of(shape, 0)
    source = index_of(shape, 1)
    taken = jnp.where(target < rows, target - 1, target - (rows + 2))
    return jnp.where(source == taken, 1.0, 0.0).astype(BF16)


def earlier_tokens(shift, block):
    return jnp.dot(shift, block, preferred_element_type=F32)


def wide_conv(block, earlier, weights):
    rows = block.shape[0]
    wide = block.astype(F32)
    if earlier.shape[0] == rows:
        one = pltpu.roll(wide, 1, 0)
        head = jnp.where(index_of((8, wide.shape[1]), 0) == 0, 0.0, one[:8])
        one = jnp.concatenate([head, one[8:]], axis=0)
    else:
        one = earlier[:rows]
    return weights[0] * wide + weights[1] * one + weights[2] * earlier[-rows:]


def taps_of(weights, feature, lanes):
    return [weights[tap, feature : feature + 1, lanes] for tap in range(weights.shape[0])]


def state_kernel(
    projected_ref,
    weight_hbm,
    rate_hbm,
    residue_hbm,
    product_ref,
    state_ref,
    mode_rate_ref,
    head_ref,
    weight_ref,
    query_ref,
    residue_ref,
    buffer_ref,
    ending_ref,
    shift_ref,
    short_ref,
    rate_ref,
    sems,
    small_sems,
):
    rows, width = product_ref.shape
    wides = width // WIDE
    rate_copy = pltpu.make_async_copy(rate_hbm, rate_ref, small_sems.at[0])
    rate_copy.start()
    weight_copy = pltpu.make_async_copy(weight_hbm, short_ref, small_sems.at[1])
    weight_copy.start()
    copies = [pltpu.make_async_copy(projected_ref.at[1 + c], buffer_ref.at[c], sems.at[c]) for c in (0, 1)]
    later = [
        pltpu.make_async_copy(residue_hbm, residue_ref, sems.at[2]),
        pltpu.make_async_copy(projected_ref.at[0], query_ref, sems.at[3]),
    ]
    for copy in copies:
        copy.start()
    shift_ref[...] = shift_matrix(rows)
    chosen = selectors(rate_ref.shape[1])
    eye = own_mode(BF16)
    mask = group_mask(F32)
    token = index_of((2 * LANES, rows), 1)
    left = jnp.where(token < 2, -1e30, (token - (rows - 1)).astype(F32)).astype(BF16)
    rate_copy.wait()
    mode_rate = per_channel(rate_ref[...], chosen)
    mode_rate_ref[...] = mode_rate

    def exponents(tile):
        high, low = split(mode_rate[:, lanes_of(tile)])
        diagonal = jnp.concatenate([spread(high, eye), spread(low, eye)], axis=1)
        return (jnp.dot(diagonal, left, preferred_element_type=F32),)

    def endings(tile, exponent):
        ending_ref[tile // 2, lanes_of(tile % 2), :] = jnp.exp(exponent).astype(BF16)

    pipelined(width // LANES, exponents, endings)
    weight_copy.wait()
    weights = short_ref[...].astype(F32)
    weight_ref[...] = weights
    for copy in copies:
        copy.wait()
    for copy in later:
        copy.start()

    def fetch(wide):
        here = lanes_of(wide, WIDE)
        return (
            earlier_tokens(shift_ref[...], buffer_ref[0, :, here]),
            earlier_tokens(shift_ref[rows:, :], buffer_ref[1, :, here]),
        )

    def multiply(wide, *earlier):
        here = lanes_of(wide, WIDE)
        parts = []
        for c in (0, 1):
            head_ref[c, :, here] = buffer_ref[c, 0:16, here].astype(F32)[:8]
            parts.append(wide_conv(buffer_ref[c, :, here], earlier[c], taps_of(weights, c + 1, here)))
        product = (parts[0] * parts[1]).astype(BF16)
        product_ref[:, here] = product
        return (jnp.dot(ending_ref[wide], product, preferred_element_type=F32),)

    def leave(wide, every):
        for half in range(WIDE // LANES):
            own = every[lanes_of(half), lanes_of(half)].reshape(GROUPS, MODES, LANES)
            state_ref[:, lanes_of((WIDE // LANES) * wide + half)] = jnp.sum(own * mask, axis=0)

    pipelined(wides, fetch, multiply, leave)
    for copy in later:
        copy.wait()


def halo(before_ref, place_ref):
    return jnp.where(place_ref[0] > 0, before_ref[...].astype(F32), 0.0)


def head_kernel(rows, place_ref, before_ref, head_ref, weight_ref, state_ref, mode_rate_ref, full_ref, first_ref):
    before = halo(before_ref, place_ref)
    everything = slice(0, head_ref.shape[2])
    parts = [short_conv(head_ref[c], before[c + 1], taps_of(weight_ref, c + 1, everything)) for c in (0, 1)]
    first = (parts[0] * parts[1]).astype(BF16).astype(F32)
    first_ref[...] = first
    rate = mode_rate_ref[...]
    early = jnp.exp(-float(rows - 1) * rate) * first[0:1] + jnp.exp(-float(rows - 2) * rate) * first[1:2]
    full_ref[...] = (state_ref[...] + early).astype(BF16)


def prepare_kernel(
    place_ref,
    residual_hbm,
    query_ref,
    residue_ref,
    before_ref,
    weight_ref,
    mode_rate_ref,
    inner_ref,
    entering_ref,
    carry_ref,
    gate_ref,
    residual_ref,
    shift_ref,
    sem,
):
    rows, width = gate_ref.shape
    residual_copy = pltpu.make_async_copy(residual_hbm, residual_ref, sem)
    residual_copy.start()
    shift_ref[...] = shift_matrix(rows)
    residue = per_channel(residue_ref[...], selectors(residue_ref.shape[1]))
    wide = GROUPS * CHUNK
    step = index_of((CHUNK, LANES), 0).astype(F32)
    causal = (index_of((CHUNK, wide), 1) & (CHUNK - 1)) <= index_of((CHUNK, wide), 0)
    eye = own_mode(BF16)
    flat_eye = jnp.where((index_of((MODES, LANES), 1) & (MODES - 1)) == index_of((MODES, LANES), 0), 1.0, 0.0)
    flat_eye = flat_eye.astype(BF16)
    shape = (2 * LANES, wide)
    source = (index_of(shape, 1) & (CHUNK - 1)).astype(F32)
    own = (index_of(shape, 0) & (LANES - 1)) // MODES == index_of(shape, 1) // CHUNK
    own_chunk = jnp.where(own[:LANES], 1.0, 0.0).astype(BF16)
    risen = source[:, :LANES].astype(BF16)
    left = jnp.where(own, source - (CHUNK - 1), 0.0).astype(BF16)

    def exponents(tile):
        rate = mode_rate_ref[:, lanes_of(tile)]
        high, low = split(rate)
        diagonal = jnp.concatenate([spread(high, eye), spread(low, eye)], axis=1)
        each = jnp.concatenate([high * flat_eye, low * flat_eye], axis=1)
        return (
            jnp.dot(diagonal, risen, preferred_element_type=F32),
            jnp.dot(each, left, preferred_element_type=F32),
        )

    def products(tile, rise, end):
        here = lanes_of(tile)
        rise_high, rise_low = [
            jnp.concatenate([part] * (wide // LANES), axis=1) * own_chunk for part in split(jnp.exp(rise))
        ]
        rate_row = mode_row(mode_rate_ref[:, here])
        falling = mode_row(residue[:, here]) * jnp.exp(-rate_row * step)
        fall_high, fall_low = split(falling)
        half = tile % (WIDE // LANES)
        for chunk in range(rows // CHUNK):
            entering = (falling * jnp.exp(-float(CHUNK * chunk + 1) * rate_row)).astype(BF16)
            carry_ref[tile // (WIDE // LANES), chunk * CHUNK : (chunk + 1) * CHUNK, lanes_of(half)] = entering
            if chunk == 0:
                entering_ref[tile] = entering
        return (
            jnp.dot(jnp.concatenate([fall_high, fall_low], axis=0), rise_high, preferred_element_type=F32),
            jnp.dot(fall_high, rise_low, preferred_element_type=F32),
            jnp.exp(end),
        )

    def finish(tile, taps, rest, ending):
        taps = jnp.where(causal, taps[:CHUNK] + taps[CHUNK:] + rest, 0.0)
        inner_ref[tile] = jnp.concatenate([taps.astype(BF16), ending.astype(BF16)], axis=0)

    pipelined(width // LANES, exponents, products, finish)
    before = halo(before_ref, place_ref)

    def fetch(part):
        return (earlier_tokens(shift_ref[...], query_ref[:, lanes_of(part, WIDE)]),)

    def convolve(part, earlier):
        here = lanes_of(part, WIDE)
        weights = taps_of(weight_ref, 0, here)
        gate_ref[:, here] = wide_conv(query_ref[:, here], earlier, weights)
        head = query_ref[0:16, here].astype(F32)[:8]
        gate_ref[0:8, here] = short_conv(head, before[0, :, here], weights)

    pipelined(width // WIDE, fetch, convolve)
    residual_copy.wait()


def local_kernel(
    gate_ref,
    residual_ref,
    product_ref,
    first_ref,
    mode_rate_ref,
    inner_ref,
    entering_ref,
    skip_ref,
    base_ref,
):
    rows, width = product_ref.shape
    mask = group_mask(BF16)
    top = index_of((8, LANES), 0) < 2
    chunks = range(rows // CHUNK)

    def inside(tile):
        here = lanes_of(tile)
        pieces = []
        for chunk in chunks:
            piece = product_ref[chunk * CHUNK : (chunk + 1) * CHUNK, here]
            if chunk == 0:
                wide = piece.astype(F32)
                head = jnp.where(top, first_ref[:, here], wide[:8])
                piece = jnp.concatenate([head, wide[8:]], axis=0).astype(BF16)
            pieces.append(piece)
        found = []
        for pair in chunks[::2]:
            sources = jnp.concatenate([spread(pieces[pair + k], mask) for k in (0, 1)], axis=1)
            found.append(jnp.dot(inner_ref[tile], sources, preferred_element_type=F32))
        return found, pieces[0]

    def across(tile, inner, first):
        decay = jnp.exp(-float(CHUNK) * mode_rate_ref[:, lanes_of(tile)])
        state = jnp.zeros((MODES, LANES), F32)
        states = []
        for chunk in chunks:
            states.append(spread(state.astype(BF16), mask))
            state = decay * state + inner[chunk // 2][CHUNK:, lanes_of(chunk % 2)]
        outer = []
        for pair in chunks[::2]:
            two = jnp.concatenate(states[pair : pair + 2], axis=1)
            outer.append(jnp.dot(entering_ref[tile], two, preferred_element_type=F32))
        return [part[:CHUNK] for part in inner], outer, first

    def finish(tile, inner, outer, first):
        here = lanes_of(tile)
        skip = skip_ref[:, here]
        for chunk in chunks:
            span = slice(chunk * CHUNK, (chunk + 1) * CHUNK)
            piece = first if chunk == 0 else product_ref[span, here]
            conv = (inner[chunk // 2] + outer[chunk // 2])[:, lanes_of(chunk % 2)]
            whole = conv + skip * piece.astype(F32)
            base_ref[span, here] = residual_ref[span, here].astype(F32) + gate_ref[span, here] * whole

    pipelined(width // LANES, inside, across, finish)


def join_kernel(tokens, radix, stride, place_ref, own_ref, mode_rate_ref, entry_ref, *refs):
    others, (found_ref, group_ref) = refs[: radix - 1], refs[radix - 1 :]
    rate = mode_rate_ref[...]
    run = lax.rem(place_ref[0] // stride, radix)
    decay = jnp.exp(-float(tokens * stride) * rate)
    own = own_ref[...].astype(F32)
    values = [ref[...].astype(F32) for ref in others[::-1]]
    found = jnp.zeros_like(rate)
    total = jnp.zeros_like(rate)
    for position in range(radix):
        found = jnp.where(run == position, total, found)
        state = own
        for k, other in enumerate(values, 1):
            state = jnp.where(partner(run, k, radix) == position, other, state)
        total = decay * total + state
    if stride > 1:
        within = lax.rem(place_ref[0], stride).astype(F32) * float(tokens)
        found = jnp.exp(-within * rate) * found
    found_ref[...] = entry_ref[...] + found
    group_ref[...] = total.astype(BF16)


def carry_kernel(stride, radix, place_ref, base_ref, gate_ref, carry_ref, mode_rate_ref, inner_entry_ref, *refs):
    entry_refs, (summed_ref, squares_ref) = refs[:-2], refs[-2:]
    rows, width = base_ref.shape
    run = place_ref[0] // stride
    within = lax.rem(place_ref[0], stride).astype(F32) * float(rows)
    mask = group_mask(BF16)
    totals = [jnp.zeros((rows, LANES), F32)]
    nothing = jnp.zeros((LANES, LANES), BF16)

    def enter(tile):
        here = lanes_of(tile, WIDE)
        rate = mode_rate_ref[:, here]
        step = float(rows * stride)
        outer = jnp.zeros_like(rate)
        for k, ref in enumerate(entry_refs[::-1], 1):
            source = partner(run, k, radix)
            lag = jnp.maximum(run - 1 - source, 0).astype(F32) * step
            outer = outer + jnp.where(source < run, jnp.exp(-lag * rate) * ref[:, here].astype(F32), 0.0)
        entry = (inner_entry_ref[:, here] + jnp.exp(-within * rate) * outer).astype(BF16)
        left, right = spread(entry[:, :LANES], mask), spread(entry[:, LANES:], mask)
        both = jnp.concatenate(
            [jnp.concatenate([left, nothing], axis=1), jnp.concatenate([nothing, right], axis=1)], axis=0
        )
        return (jnp.dot(carry_ref[tile], both, preferred_element_type=F32),)

    def add(tile, carry):
        here = lanes_of(tile, WIDE)
        summed = base_ref[:, here] + gate_ref[:, here] * carry
        summed_ref[:, here] = summed
        square = summed * summed
        totals[0] = totals[0] + (square[:, :LANES] + square[:, LANES:])

    pipelined(width // WIDE, enter, add)
    total = totals[0]
    squares = lax.dot_general(
        jnp.ones((8, 2 * LANES), BF16),
        jnp.concatenate(split(total), axis=1),
        (((1,), (1,)), ((), ())),
        preferred_element_type=F32,
    )
    squares_ref[...] = squares[0:1]


def write_kernel(summed_ref, out_hbm, rounded_ref, sems):
    width = summed_ref.shape[1]
    copies = []
    for tile in range(width // WIDE):
        here = lanes_of(tile, WIDE)
        rounded_ref[:, here] = summed_ref[:, here].astype(BF16)
        span = pl.ds(tile * WIDE, WIDE)
        copies.append(pltpu.make_async_copy(rounded_ref.at[:, span], out_hbm.at[:, span], sems.at[tile]))
        copies[-1].start()
    for copy in copies:
        copy.wait()


def norm_kernel(full_width, summed_ref, gain_ref, *refs):
    squares_refs, (out_hbm, rounded_ref, sems) = refs[:-3], refs[-3:]
    rows, width = summed_ref.shape
    squares = squares_refs[0][...]
    for ref in squares_refs[1:]:
        squares = squares + ref[...]
    scale_row = lax.rsqrt(squares / full_width + 1e-05)
    scale = jnp.concatenate([as_column(scale_row[:, lanes_of(k)]) for k in range(rows // LANES)], axis=0)
    copies = []
    block = rows // 8
    for start in range(0, rows, block):
        span = slice(start, start + block)
        for tile in range(width // LANES):
            here = lanes_of(tile)
            rounded_ref[span, here] = (summed_ref[span, here] * scale[span] * gain_ref[:, here]).astype(BF16)
        there = pl.ds(start, block)
        copies.append(pltpu.make_async_copy(rounded_ref.at[there, :], out_hbm.at[there, :], sems.at[start // block]))
        copies[-1].start()
    for copy in copies:
        copy.wait()


def params():
    return pltpu.CompilerParams(vmem_limit_bytes=VMEM_LIMIT)


def cost(microseconds):
    return pl.CostEstimate(flops=0, bytes_accessed=int(microseconds * 3.0e6), transcendentals=0)


def radices(count):
    found = []
    for radix in (4, 4, 4, 3, 3, 2, 5, 7):
        if count % radix == 0:
            found.append(radix)
            count //= radix
    return found + ([count] if count > 1 else [])


def partner(run, k, radix):
    if radix & (radix - 1) == 0:
        return run ^ k
    return (run - k + radix) % radix


def routes(count, stride, radix):
    found = []
    for k in range(1, radix):
        route = []
        for i in range(count):
            run = i // stride % radix
            route.append((i + (partner(run, k, radix) - run) * stride, i))
        found.append(route)
    return found


def ring(count, shift):
    return [(i, (i + shift) % count) for i in range(count)]


def per_device(projected, short_weight, rates, residues, skip, residual, gain):
    rows, width = projected.shape[1:]
    taps = short_weight.shape[0]
    peers = lax.axis_size("ctx")
    full_width = width * lax.axis_size("fsdp")
    place = lax.axis_index("ctx").astype(jnp.int32).reshape(1)
    hbm_spec = pl.BlockSpec(memory_space=pltpu.HBM)
    vmem_spec = pl.BlockSpec(memory_space=pltpu.VMEM)
    smem_spec = pl.BlockSpec(memory_space=pltpu.SMEM)
    tiles = width // LANES
    wides = width // WIDE

    def kept(array):
        return pltpu.with_memory_space_constraint(array, pltpu.HBM)

    def f32(*shape):
        return jax.ShapeDtypeStruct(shape, F32)

    def bf16(*shape):
        return jax.ShapeDtypeStruct(shape, BF16)

    before = lax.ppermute(projected[:, rows - (taps - 1) :, :], "ctx", ring(peers, 1))

    product, state, mode_rate, head, weights, query, residue = pl.pallas_call(
        state_kernel,
        in_specs=[hbm_spec] * 4,
        out_shape=[
            bf16(rows, width),
            f32(MODES, width),
            f32(MODES, width),
            f32(2, 8, width),
            f32(*short_weight.shape),
            bf16(rows, width),
            f32(MODES, residues.shape[0]),
        ],
        scratch_shapes=[
            pltpu.VMEM((2, rows, width), BF16),
            pltpu.VMEM((wides, WIDE, rows), BF16),
            pltpu.VMEM((2 * rows, rows), BF16),
            pltpu.VMEM(short_weight.shape, BF16),
            pltpu.VMEM((MODES, rates.shape[0]), F32),
            pltpu.SemaphoreType.DMA((4,)),
            pltpu.SemaphoreType.DMA((2,)),
        ],
        compiler_params=params(),
        cost_estimate=cost(3),
        name="block_state",
    )(kept(projected), kept(short_weight), kept(rates.T), kept(residues.T))

    full_state, first = pl.pallas_call(
        lambda *refs: head_kernel(rows, *refs),
        in_specs=[smem_spec] + [vmem_spec] * 5,
        out_shape=[bf16(MODES, width), f32(8, width)],
        compiler_params=params(),
        cost_estimate=cost(0.2),
        name="head_tokens",
    )(place, before, head, weights, state, mode_rate)

    inner, entering, carry_table, gate, residual_here = pl.pallas_call(
        prepare_kernel,
        in_specs=[smem_spec, hbm_spec] + [vmem_spec] * 5,
        out_shape=[
            bf16(tiles, CHUNK + MODES, GROUPS * CHUNK),
            bf16(tiles, CHUNK, LANES),
            bf16(wides, rows, WIDE),
            f32(rows, width),
            bf16(rows, width),
        ],
        scratch_shapes=[pltpu.VMEM((2 * rows, rows), BF16), pltpu.SemaphoreType.DMA],
        compiler_params=params(),
        cost_estimate=cost(2),
        name="prepare",
    )(place, kept(residual), query, residue, before, weights, mode_rate)

    group, entry, stride = full_state, jnp.zeros((MODES, width), F32), 1
    levels = radices(peers)
    for level, radix in enumerate(levels):
        size = stride * radix
        if level == len(levels) - 1:
            break
        others = [lax.ppermute(group, "ctx", route) for route in routes(peers, stride, radix)[::-1]]
        if level == 0:
            others[0], inner = lax.optimization_barrier((others[0], inner))
        entry, group = pl.pallas_call(
            lambda *refs, radix=radix, stride=stride: join_kernel(rows, radix, stride, *refs),
            in_specs=[smem_spec] + [vmem_spec] * (2 + radix),
            out_shape=[f32(MODES, width), bf16(MODES, width)],
            compiler_params=params(),
            cost_estimate=cost(0.2),
            name="join",
        )(place, group, mode_rate, entry, *others)
        stride = size
    received = [lax.ppermute(group, "ctx", route) for route in routes(peers, stride, levels[-1])[::-1]]

    base = pl.pallas_call(
        local_kernel,
        out_shape=f32(rows, width),
        compiler_params=params(),
        cost_estimate=cost(5),
        name="local_conv",
    )(gate, residual_here, product, first, mode_rate, inner, entering, skip[None])

    count = lax.axis_size("fsdp")
    summed, squares = pl.pallas_call(
        lambda *refs: carry_kernel(stride, levels[-1], *refs),
        in_specs=[smem_spec] + [vmem_spec] * (5 + len(received)),
        out_shape=[f32(rows, width), f32(1, rows)],
        compiler_params=params(),
        cost_estimate=cost(1),
        name="add_carry",
    )(place, base, gate, carry_table, mode_rate, entry, *received)

    parts = [lax.ppermute(squares, "fsdp", route) for route in routes(count, 1, count)[::-1]]

    def write(kernel, operands, name):
        return pl.pallas_call(
            kernel,
            out_specs=hbm_spec,
            out_shape=bf16(rows, width),
            scratch_shapes=[pltpu.VMEM((rows, width), BF16), pltpu.SemaphoreType.DMA((max(8, wides),))],
            compiler_params=params(),
            cost_estimate=cost(1),
            name=name,
        )(*operands)

    new_residual = write(write_kernel, (summed,), "new_residual")
    normed = write(
        lambda *refs: norm_kernel(full_width, *refs), (summed, gain[None], squares, *parts), "normed"
    )
    return (new_residual, normed)


def solution(mesh):
    return jax.shard_map(
        per_device,
        mesh=mesh,
        in_specs=(
            P(None, "ctx", "fsdp"),
            P(None, None, "fsdp"),
            P("fsdp", None),
            P("fsdp", None),
            P("fsdp"),
            P("ctx", "fsdp"),
            P("fsdp"),
        ),
        out_specs=(P("ctx", "fsdp"), P("ctx", "fsdp")),
        check_vma=False,
    )
```

```python
import jax
import jax.numpy as jnp
from jax import lax
from jax.experimental import pallas as pl
from jax.experimental.pallas import tpu as pltpu
from jax.sharding import PartitionSpec as P

CHANNELS_PER_GRP = 16
MODES = 16
CHUNK = 32
LANES = 128
WIDE = 256
GROUPS = LANES // CHANNELS_PER_GRP
VMEM_LIMIT = 16 * 1024 * 1024
F32 = jnp.float32
BF16 = jnp.bfloat16


def index_of(shape, dim):
    return lax.broadcasted_iota(jnp.int32, shape, dim)


def pipelined(count, *stages):
    held = {}
    for step in range(count + len(stages) - 1):
        for k, stage in enumerate(stages):
            item = step - k
            if 0 <= item < count:
                held[item] = stage(item, *held.get(item, ()))


def lanes_of(tile, width=LANES):
    return slice(tile * width, (tile + 1) * width)


def selectors(groups):
    shape = (groups, WIDE)
    found = []
    for tile in range(groups * CHANNELS_PER_GRP // WIDE):
        own = index_of(shape, 0) == index_of(shape, 1) // CHANNELS_PER_GRP + tile * (WIDE // CHANNELS_PER_GRP)
        found.append(jnp.where(own, 1.0, 0.0).astype(BF16))
    return found


def per_channel(table, chosen):
    high = table.astype(BF16)
    rest = table - high.astype(F32)
    middle = rest.astype(BF16)
    low = (rest - middle.astype(F32)).astype(BF16)
    terms = jnp.concatenate([high, middle, low], axis=0)
    parts = []
    for selector in chosen:
        three = jnp.dot(terms, selector, preferred_element_type=F32)
        parts.append(three[:MODES] + three[MODES : 2 * MODES] + three[2 * MODES :])
    return jnp.concatenate(parts, axis=1)


def mode_row(channel_table):
    own = index_of(channel_table.shape, 0) == (index_of(channel_table.shape, 1) & (MODES - 1))
    return jnp.sum(jnp.where(own, channel_table, 0.0), axis=0, keepdims=True)


def as_column(row):
    return jnp.transpose(jnp.broadcast_to(row, (LANES, LANES)))


def own_mode(dtype):
    shape = (GROUPS, MODES, LANES)
    own = index_of(shape, 0) * MODES + index_of(shape, 1) == index_of(shape, 2)
    return jnp.where(own, 1.0, 0.0).astype(dtype)


def split(x):
    high = x.astype(BF16)
    return high, (x - high.astype(F32)).astype(BF16)


def group_mask(dtype):
    shape = (GROUPS, MODES, LANES)
    own = index_of(shape, 0) == index_of(shape, 2) // CHANNELS_PER_GRP
    return jnp.where(own, 1.0, 0.0).astype(dtype)


def spread(rows, mask):
    size = rows.shape[0]
    copies = rows.reshape(1, size // MODES, MODES, LANES) * mask.reshape(GROUPS, 1, MODES, LANES)
    return copies.reshape(GROUPS * size, LANES)


def shifted(block, before):
    one = pltpu.roll(block, 1, 0)
    two = pltpu.roll(block, 2, 0)
    first = index_of((8, block.shape[1]), 0)
    near, far = (0.0, 0.0) if before is None else (before[1:2], before[0:1])
    head_one = jnp.where(first == 0, near, one[:8])
    head_two = jnp.where(first == 0, far, jnp.where(first == 1, near, two[:8]))
    if block.shape[0] == 8:
        return head_one, head_two
    return jnp.concatenate([head_one, one[8:]], axis=0), jnp.concatenate([head_two, two[8:]], axis=0)


def short_conv(block, before, weights):
    one, two = shifted(block, before)
    return weights[0] * block + weights[1] * one + weights[2] * two


def shift_matrix(rows):
    shape = (2 * rows, rows)
    target = index_of(shape, 0)
    source = index_of(shape, 1)
    taken = jnp.where(target < rows, target - 1, target - (rows + 2))
    return jnp.where(source == taken, 1.0, 0.0).astype(BF16)


def earlier_tokens(shift, block):
    return jnp.dot(shift, block, preferred_element_type=F32)


def wide_conv(block, earlier, weights):
    rows = block.shape[0]
    wide = block.astype(F32)
    if earlier.shape[0] == rows:
        one = pltpu.roll(wide, 1, 0)
        head = jnp.where(index_of((8, wide.shape[1]), 0) == 0, 0.0, one[:8])
        one = jnp.concatenate([head, one[8:]], axis=0)
    else:
        one = earlier[:rows]
    return weights[0] * wide + weights[1] * one + weights[2] * earlier[-rows:]


def taps_of(weights, feature, lanes):
    return [weights[tap, feature : feature + 1, lanes] for tap in range(weights.shape[0])]


def state_kernel(
    projected_ref,
    weight_hbm,
    rate_hbm,
    residue_hbm,
    product_ref,
    state_ref,
    mode_rate_ref,
    head_ref,
    weight_ref,
    query_ref,
    residue_ref,
    buffer_ref,
    ending_ref,
    shift_ref,
    short_ref,
    rate_ref,
    sems,
    small_sems,
):
    rows, width = product_ref.shape
    wides = width // WIDE
    rate_copy = pltpu.make_async_copy(rate_hbm, rate_ref, small_sems.at[0])
    rate_copy.start()
    weight_copy = pltpu.make_async_copy(weight_hbm, short_ref, small_sems.at[1])
    copies = [pltpu.make_async_copy(projected_ref.at[pl.ds(1, 2)], buffer_ref, sems.at[0])]
    later = [
        pltpu.make_async_copy(residue_hbm, residue_ref, sems.at[2]),
        pltpu.make_async_copy(projected_ref.at[0], query_ref, sems.at[3]),
    ]
    for copy in copies:
        copy.start()
    weight_copy.start()
    shift_ref[...] = shift_matrix(rows)
    chosen = selectors(rate_ref.shape[1])
    eye = own_mode(BF16)
    mask = group_mask(F32)
    token = index_of((2 * LANES, rows), 1)
    left = jnp.where(token < 2, -1e30, (token - (rows - 1)).astype(F32)).astype(BF16)
    rate_copy.wait()
    mode_rate = per_channel(rate_ref[...], chosen)
    mode_rate_ref[...] = mode_rate

    def exponents(tile):
        high, low = split(mode_rate[:, lanes_of(tile)])
        diagonal = jnp.concatenate([spread(high, eye), spread(low, eye)], axis=1)
        return (jnp.dot(diagonal, left, preferred_element_type=F32),)

    def endings(tile, exponent):
        ending_ref[tile // 2, lanes_of(tile % 2), :] = jnp.exp(exponent).astype(BF16)

    pipelined(width // LANES, exponents, endings)
    weight_copy.wait()
    weights = short_ref[...].astype(F32)
    weight_ref[...] = weights
    for copy in copies:
        copy.wait()
    for copy in later:
        copy.start()

    def fetch(wide):
        here = lanes_of(wide, WIDE)
        return (
            earlier_tokens(shift_ref[...], buffer_ref[0, :, here]),
            earlier_tokens(shift_ref[rows:, :], buffer_ref[1, :, here]),
        )

    def multiply(wide, *earlier):
        here = lanes_of(wide, WIDE)
        parts = []
        for c in (0, 1):
            head_ref[c, :, here] = buffer_ref[c, 0:16, here].astype(F32)[:8]
            parts.append(wide_conv(buffer_ref[c, :, here], earlier[c], taps_of(weights, c + 1, here)))
        product = (parts[0] * parts[1]).astype(BF16)
        product_ref[:, here] = product
        return (jnp.dot(ending_ref[wide], product, preferred_element_type=F32),)

    def leave(wide, every):
        for half in range(WIDE // LANES):
            own = every[lanes_of(half), lanes_of(half)].reshape(GROUPS, MODES, LANES)
            state_ref[:, lanes_of((WIDE // LANES) * wide + half)] = jnp.sum(own * mask, axis=0)

    pipelined(wides, fetch, multiply, leave)
    for copy in later:
        copy.wait()


def halo(before_ref, place_ref):
    return jnp.where(place_ref[0] > 0, before_ref[...].astype(F32), 0.0)


def head_kernel(rows, place_ref, before_ref, head_ref, weight_ref, state_ref, mode_rate_ref, full_ref, first_ref):
    before = halo(before_ref, place_ref)
    everything = slice(0, head_ref.shape[2])
    parts = [short_conv(head_ref[c], before[c + 1], taps_of(weight_ref, c + 1, everything)) for c in (0, 1)]
    first = (parts[0] * parts[1]).astype(BF16).astype(F32)
    first_ref[...] = first
    rate = mode_rate_ref[...]
    early = jnp.exp(-float(rows - 1) * rate) * first[0:1] + jnp.exp(-float(rows - 2) * rate) * first[1:2]
    full_ref[...] = (state_ref[...] + early).astype(BF16)


def prepare_kernel(
    place_ref,
    residual_hbm,
    query_ref,
    residue_ref,
    before_ref,
    weight_ref,
    mode_rate_ref,
    inner_ref,
    entering_ref,
    carry_ref,
    gate_ref,
    residual_ref,
    shift_ref,
    sem,
):
    rows, width = gate_ref.shape
    residual_copy = pltpu.make_async_copy(residual_hbm, residual_ref, sem)
    residual_copy.start()
    shift_ref[...] = shift_matrix(rows)
    residue = per_channel(residue_ref[...], selectors(residue_ref.shape[1]))
    wide = GROUPS * CHUNK
    step = index_of((CHUNK, LANES), 0).astype(F32)
    causal = (index_of((CHUNK, wide), 1) & (CHUNK - 1)) <= index_of((CHUNK, wide), 0)
    eye = own_mode(BF16)
    flat_eye = jnp.where((index_of((MODES, LANES), 1) & (MODES - 1)) == index_of((MODES, LANES), 0), 1.0, 0.0)
    flat_eye = flat_eye.astype(BF16)
    shape = (2 * LANES, wide)
    source = (index_of(shape, 1) & (CHUNK - 1)).astype(F32)
    own = (index_of(shape, 0) & (LANES - 1)) // MODES == index_of(shape, 1) // CHUNK
    own_chunk = jnp.where(own[:LANES], 1.0, 0.0).astype(BF16)
    risen = source[:, :LANES].astype(BF16)
    left = jnp.where(own, source - (CHUNK - 1), 0.0).astype(BF16)

    def exponents(tile):
        rate = mode_rate_ref[:, lanes_of(tile)]
        high, low = split(rate)
        diagonal = jnp.concatenate([spread(high, eye), spread(low, eye)], axis=1)
        each = jnp.concatenate([high * flat_eye, low * flat_eye], axis=1)
        return (
            jnp.dot(diagonal, risen, preferred_element_type=F32),
            jnp.dot(each, left, preferred_element_type=F32),
        )

    def products(tile, rise, end):
        here = lanes_of(tile)
        rise_high, rise_low = [
            jnp.concatenate([part] * (wide // LANES), axis=1) * own_chunk for part in split(jnp.exp(rise))
        ]
        rate_row = mode_row(mode_rate_ref[:, here])
        falling = mode_row(residue[:, here]) * jnp.exp(-rate_row * step)
        fall_high, fall_low = split(falling)
        half = tile % (WIDE // LANES)
        for chunk in range(rows // CHUNK):
            entering = (falling * jnp.exp(-float(CHUNK * chunk + 1) * rate_row)).astype(BF16)
            carry_ref[tile // (WIDE // LANES), chunk * CHUNK : (chunk + 1) * CHUNK, lanes_of(half)] = entering
            if chunk == 0:
                entering_ref[tile] = entering
        return (
            jnp.dot(jnp.concatenate([fall_high, fall_low], axis=0), rise_high, preferred_element_type=F32),
            jnp.dot(fall_high, rise_low, preferred_element_type=F32),
            jnp.exp(end),
        )

    def finish(tile, taps, rest, ending):
        taps = jnp.where(causal, taps[:CHUNK] + taps[CHUNK:] + rest, 0.0)
        inner_ref[tile] = jnp.concatenate([taps.astype(BF16), ending.astype(BF16)], axis=0)

    pipelined(width // LANES, exponents, products, finish)
    before = halo(before_ref, place_ref)

    def fetch(part):
        return (earlier_tokens(shift_ref[...], query_ref[:, lanes_of(part, WIDE)]),)

    def convolve(part, earlier):
        here = lanes_of(part, WIDE)
        weights = taps_of(weight_ref, 0, here)
        gate_ref[:, here] = wide_conv(query_ref[:, here], earlier, weights)
        head = query_ref[0:16, here].astype(F32)[:8]
        gate_ref[0:8, here] = short_conv(head, before[0, :, here], weights)

    pipelined(width // WIDE, fetch, convolve)
    residual_copy.wait()


def local_kernel(
    gate_ref,
    residual_ref,
    product_ref,
    first_ref,
    mode_rate_ref,
    inner_ref,
    entering_ref,
    skip_ref,
    base_ref,
):
    rows, width = product_ref.shape
    mask = group_mask(BF16)
    top = index_of((8, LANES), 0) < 2
    chunks = range(rows // CHUNK)

    def inside(tile):
        here = lanes_of(tile)
        pieces = []
        for chunk in chunks:
            piece = product_ref[chunk * CHUNK : (chunk + 1) * CHUNK, here]
            if chunk == 0:
                wide = piece.astype(F32)
                head = jnp.where(top, first_ref[:, here], wide[:8])
                piece = jnp.concatenate([head, wide[8:]], axis=0).astype(BF16)
            pieces.append(piece)
        found = []
        for pair in chunks[::2]:
            sources = jnp.concatenate([spread(pieces[pair + k], mask) for k in (0, 1)], axis=1)
            found.append(jnp.dot(inner_ref[tile], sources, preferred_element_type=F32))
        return found, pieces[0]

    def across(tile, inner, first):
        decay = jnp.exp(-float(CHUNK) * mode_rate_ref[:, lanes_of(tile)])
        state = jnp.zeros((MODES, LANES), F32)
        states = []
        for chunk in chunks:
            states.append(spread(state.astype(BF16), mask))
            state = decay * state + inner[chunk // 2][CHUNK:, lanes_of(chunk % 2)]
        outer = []
        for pair in chunks[::2]:
            two = jnp.concatenate(states[pair : pair + 2], axis=1)
            outer.append(jnp.dot(entering_ref[tile], two, preferred_element_type=F32))
        return [part[:CHUNK] for part in inner], outer, first

    def finish(tile, inner, outer, first):
        here = lanes_of(tile)
        skip = skip_ref[:, here]
        for chunk in chunks:
            span = slice(chunk * CHUNK, (chunk + 1) * CHUNK)
            piece = first if chunk == 0 else product_ref[span, here]
            conv = (inner[chunk // 2] + outer[chunk // 2])[:, lanes_of(chunk % 2)]
            whole = conv + skip * piece.astype(F32)
            base_ref[span, here] = residual_ref[span, here].astype(F32) + gate_ref[span, here] * whole

    pipelined(width // LANES, inside, across, finish)


def join_kernel(tokens, radix, stride, place_ref, own_ref, mode_rate_ref, entry_ref, *refs):
    others, (found_ref, group_ref) = refs[: radix - 1], refs[radix - 1 :]
    rate = mode_rate_ref[...]
    run = lax.rem(place_ref[0] // stride, radix)
    decay = jnp.exp(-float(tokens * stride) * rate)
    own = own_ref[...].astype(F32)
    values = [ref[...].astype(F32) for ref in others[::-1]]
    found = jnp.zeros_like(rate)
    total = jnp.zeros_like(rate)
    for position in range(radix):
        found = jnp.where(run == position, total, found)
        state = own
        for k, other in enumerate(values, 1):
            state = jnp.where(partner(run, k, radix) == position, other, state)
        total = decay * total + state
    if stride > 1:
        within = lax.rem(place_ref[0], stride).astype(F32) * float(tokens)
        found = jnp.exp(-within * rate) * found
    found_ref[...] = entry_ref[...] + found
    group_ref[...] = total.astype(BF16)


def carry_kernel(stride, radix, place_ref, base_ref, gate_ref, carry_ref, mode_rate_ref, inner_entry_ref, *refs):
    entry_refs, (summed_ref, squares_ref) = refs[:-2], refs[-2:]
    rows, width = base_ref.shape
    run = place_ref[0] // stride
    within = lax.rem(place_ref[0], stride).astype(F32) * float(rows)
    mask = group_mask(BF16)
    totals = [jnp.zeros((rows, LANES), F32)]
    nothing = jnp.zeros((LANES, LANES), BF16)

    def enter(tile):
        here = lanes_of(tile, WIDE)
        rate = mode_rate_ref[:, here]
        step = float(rows * stride)
        outer = jnp.zeros_like(rate)
        for k, ref in enumerate(entry_refs[::-1], 1):
            source = partner(run, k, radix)
            lag = jnp.maximum(run - 1 - source, 0).astype(F32) * step
            outer = outer + jnp.where(source < run, jnp.exp(-lag * rate) * ref[:, here].astype(F32), 0.0)
        entry = (inner_entry_ref[:, here] + jnp.exp(-within * rate) * outer).astype(BF16)
        left, right = spread(entry[:, :LANES], mask), spread(entry[:, LANES:], mask)
        both = jnp.concatenate(
            [jnp.concatenate([left, nothing], axis=1), jnp.concatenate([nothing, right], axis=1)], axis=0
        )
        return (jnp.dot(carry_ref[tile], both, preferred_element_type=F32),)

    def add(tile, carry):
        here = lanes_of(tile, WIDE)
        summed = base_ref[:, here] + gate_ref[:, here] * carry
        summed_ref[:, here] = summed
        square = summed * summed
        totals[0] = totals[0] + (square[:, :LANES] + square[:, LANES:])

    pipelined(width // WIDE, enter, add)
    total = totals[0]
    squares = lax.dot_general(
        jnp.ones((8, 2 * LANES), BF16),
        jnp.concatenate(split(total), axis=1),
        (((1,), (1,)), ((), ())),
        preferred_element_type=F32,
    )
    squares_ref[...] = squares[0:1]


def write_kernel(summed_ref, out_hbm, rounded_ref, sems):
    width = summed_ref.shape[1]
    copies = []
    for tile in range(width // WIDE):
        here = lanes_of(tile, WIDE)
        rounded_ref[:, here] = summed_ref[:, here].astype(BF16)
        span = pl.ds(tile * WIDE, WIDE)
        copies.append(pltpu.make_async_copy(rounded_ref.at[:, span], out_hbm.at[:, span], sems.at[tile]))
        copies[-1].start()
    for copy in copies:
        copy.wait()


def norm_kernel(full_width, summed_ref, gain_ref, *refs):
    squares_refs, (out_hbm, rounded_ref, sems) = refs[:-3], refs[-3:]
    rows, width = summed_ref.shape
    squares = squares_refs[0][...]
    for ref in squares_refs[1:]:
        squares = squares + ref[...]
    scale_row = lax.rsqrt(squares / full_width + 1e-05)
    scale = jnp.concatenate([as_column(scale_row[:, lanes_of(k)]) for k in range(rows // LANES)], axis=0)
    copies = []
    block = rows // 8
    for start in range(0, rows, block):
        span = slice(start, start + block)
        for tile in range(width // LANES):
            here = lanes_of(tile)
            rounded_ref[span, here] = (summed_ref[span, here] * scale[span] * gain_ref[:, here]).astype(BF16)
        there = pl.ds(start, block)
        copies.append(pltpu.make_async_copy(rounded_ref.at[there, :], out_hbm.at[there, :], sems.at[start // block]))
        copies[-1].start()
    for copy in copies:
        copy.wait()


def params():
    return pltpu.CompilerParams(vmem_limit_bytes=VMEM_LIMIT)


def cost(microseconds):
    return pl.CostEstimate(flops=0, bytes_accessed=int(microseconds * 3.0e6), transcendentals=0)


def radices(count):
    found = []
    for radix in (4, 4, 4, 3, 3, 2, 5, 7):
        if count % radix == 0:
            found.append(radix)
            count //= radix
    return found + ([count] if count > 1 else [])


def partner(run, k, radix):
    if radix & (radix - 1) == 0:
        return run ^ k
    return (run - k + radix) % radix


def routes(count, stride, radix):
    found = []
    for k in range(1, radix):
        route = []
        for i in range(count):
            run = i // stride % radix
            route.append((i + (partner(run, k, radix) - run) * stride, i))
        found.append(route)
    return found


def ring(count, shift):
    return [(i, (i + shift) % count) for i in range(count)]


def per_device(projected, short_weight, rates, residues, skip, residual, gain):
    rows, width = projected.shape[1:]
    taps = short_weight.shape[0]
    peers = lax.axis_size("ctx")
    full_width = width * lax.axis_size("fsdp")
    place = lax.axis_index("ctx").astype(jnp.int32).reshape(1)
    hbm_spec = pl.BlockSpec(memory_space=pltpu.HBM)
    vmem_spec = pl.BlockSpec(memory_space=pltpu.VMEM)
    smem_spec = pl.BlockSpec(memory_space=pltpu.SMEM)
    tiles = width // LANES
    wides = width // WIDE

    def kept(array):
        return pltpu.with_memory_space_constraint(array, pltpu.HBM)

    def f32(*shape):
        return jax.ShapeDtypeStruct(shape, F32)

    def bf16(*shape):
        return jax.ShapeDtypeStruct(shape, BF16)

    before = lax.ppermute(projected[:, rows - (taps - 1) :, :], "ctx", ring(peers, 1))

    product, state, mode_rate, head, weights, query, residue = pl.pallas_call(
        state_kernel,
        in_specs=[hbm_spec] * 4,
        out_shape=[
            bf16(rows, width),
            f32(MODES, width),
            f32(MODES, width),
            f32(2, 8, width),
            f32(*short_weight.shape),
            bf16(rows, width),
            f32(MODES, residues.shape[0]),
        ],
        scratch_shapes=[
            pltpu.VMEM((2, rows, width), BF16),
            pltpu.VMEM((wides, WIDE, rows), BF16),
            pltpu.VMEM((2 * rows, rows), BF16),
            pltpu.VMEM(short_weight.shape, BF16),
            pltpu.VMEM((MODES, rates.shape[0]), F32),
            pltpu.SemaphoreType.DMA((4,)),
            pltpu.SemaphoreType.DMA((2,)),
        ],
        compiler_params=params(),
        cost_estimate=cost(3),
        name="block_state",
    )(kept(projected), kept(short_weight), kept(rates.T), kept(residues.T))

    full_state, first = pl.pallas_call(
        lambda *refs: head_kernel(rows, *refs),
        in_specs=[smem_spec] + [vmem_spec] * 5,
        out_shape=[bf16(MODES, width), f32(8, width)],
        compiler_params=params(),
        cost_estimate=cost(0.2),
        name="head_tokens",
    )(place, before, head, weights, state, mode_rate)

    inner, entering, carry_table, gate, residual_here = pl.pallas_call(
        prepare_kernel,
        in_specs=[smem_spec, hbm_spec] + [vmem_spec] * 5,
        out_shape=[
            bf16(tiles, CHUNK + MODES, GROUPS * CHUNK),
            bf16(tiles, CHUNK, LANES),
            bf16(wides, rows, WIDE),
            f32(rows, width),
            bf16(rows, width),
        ],
        scratch_shapes=[pltpu.VMEM((2 * rows, rows), BF16), pltpu.SemaphoreType.DMA],
        compiler_params=params(),
        cost_estimate=cost(2),
        name="prepare",
    )(place, kept(residual), query, residue, before, weights, mode_rate)

    group, entry, stride = full_state, jnp.zeros((MODES, width), F32), 1
    levels = radices(peers)
    for level, radix in enumerate(levels):
        size = stride * radix
        if level == len(levels) - 1:
            break
        others = [lax.ppermute(group, "ctx", route) for route in routes(peers, stride, radix)[::-1]]
        if level == 0:
            others[0], inner = lax.optimization_barrier((others[0], inner))
        entry, group = pl.pallas_call(
            lambda *refs, radix=radix, stride=stride: join_kernel(rows, radix, stride, *refs),
            in_specs=[smem_spec] + [vmem_spec] * (2 + radix),
            out_shape=[f32(MODES, width), bf16(MODES, width)],
            compiler_params=params(),
            cost_estimate=cost(0.2),
            name="join",
        )(place, group, mode_rate, entry, *others)
        stride = size
    received = [lax.ppermute(group, "ctx", route) for route in routes(peers, stride, levels[-1])[::-1]]

    base = pl.pallas_call(
        local_kernel,
        out_shape=f32(rows, width),
        compiler_params=params(),
        cost_estimate=cost(5),
        name="local_conv",
    )(gate, residual_here, product, first, mode_rate, inner, entering, skip[None])

    count = lax.axis_size("fsdp")
    summed, squares = pl.pallas_call(
        lambda *refs: carry_kernel(stride, levels[-1], *refs),
        in_specs=[smem_spec] + [vmem_spec] * (5 + len(received)),
        out_shape=[f32(rows, width), f32(1, rows)],
        compiler_params=params(),
        cost_estimate=cost(1),
        name="add_carry",
    )(place, base, gate, carry_table, mode_rate, entry, *received)

    parts = [lax.ppermute(squares, "fsdp", route) for route in routes(count, 1, count)[::-1]]

    def write(kernel, operands, name):
        return pl.pallas_call(
            kernel,
            out_specs=hbm_spec,
            out_shape=bf16(rows, width),
            scratch_shapes=[pltpu.VMEM((rows, width), BF16), pltpu.SemaphoreType.DMA((max(8, wides),))],
            compiler_params=params(),
            cost_estimate=cost(1),
            name=name,
        )(*operands)

    new_residual = write(write_kernel, (summed,), "new_residual")
    normed = write(
        lambda *refs: norm_kernel(full_width, *refs), (summed, gain[None], squares, *parts), "normed"
    )
    return (new_residual, normed)


def solution(mesh):
    return jax.shard_map(
        per_device,
        mesh=mesh,
        in_specs=(
            P(None, "ctx", "fsdp"),
            P(None, None, "fsdp"),
            P("fsdp", None),
            P("fsdp", None),
            P("fsdp"),
            P("ctx", "fsdp"),
            P("fsdp"),
        ),
        out_specs=(P("ctx", "fsdp"), P("ctx", "fsdp")),
        check_vma=False,
    )
```

```python
import jax
import jax.numpy as jnp
from jax import lax
from jax.experimental import pallas as pl
from jax.experimental.pallas import tpu as pltpu
from jax.sharding import PartitionSpec as P

CHANNELS_PER_GRP = 16
MODES = 16
CHUNK = 32
LANES = 128
WIDE = 256
GROUPS = LANES // CHANNELS_PER_GRP
VMEM_LIMIT = 16 * 1024 * 1024
F32 = jnp.float32
BF16 = jnp.bfloat16


def index_of(shape, dim):
    return lax.broadcasted_iota(jnp.int32, shape, dim)


def pipelined(count, *stages):
    held = {}
    for step in range(count + len(stages) - 1):
        for k, stage in enumerate(stages):
            item = step - k
            if 0 <= item < count:
                held[item] = stage(item, *held.get(item, ()))


def lanes_of(tile, width=LANES):
    return slice(tile * width, (tile + 1) * width)


def selectors(groups):
    shape = (groups, WIDE)
    found = []
    for tile in range(groups * CHANNELS_PER_GRP // WIDE):
        own = index_of(shape, 0) == index_of(shape, 1) // CHANNELS_PER_GRP + tile * (WIDE // CHANNELS_PER_GRP)
        found.append(jnp.where(own, 1.0, 0.0).astype(BF16))
    return found


def per_channel(table, chosen):
    high = table.astype(BF16)
    rest = table - high.astype(F32)
    middle = rest.astype(BF16)
    low = (rest - middle.astype(F32)).astype(BF16)
    terms = jnp.concatenate([high, middle, low], axis=0)
    parts = []
    for selector in chosen:
        three = jnp.dot(terms, selector, preferred_element_type=F32)
        parts.append(three[:MODES] + three[MODES : 2 * MODES] + three[2 * MODES :])
    return jnp.concatenate(parts, axis=1)


def mode_row(channel_table):
    own = index_of(channel_table.shape, 0) == (index_of(channel_table.shape, 1) & (MODES - 1))
    return jnp.sum(jnp.where(own, channel_table, 0.0), axis=0, keepdims=True)


def as_column(row):
    return jnp.transpose(jnp.broadcast_to(row, (LANES, LANES)))


def own_mode(dtype):
    shape = (GROUPS, MODES, LANES)
    own = index_of(shape, 0) * MODES + index_of(shape, 1) == index_of(shape, 2)
    return jnp.where(own, 1.0, 0.0).astype(dtype)


def split(x):
    high = x.astype(BF16)
    return high, (x - high.astype(F32)).astype(BF16)


def group_mask(dtype):
    shape = (GROUPS, MODES, LANES)
    own = index_of(shape, 0) == index_of(shape, 2) // CHANNELS_PER_GRP
    return jnp.where(own, 1.0, 0.0).astype(dtype)


def spread(rows, mask):
    size = rows.shape[0]
    copies = rows.reshape(1, size // MODES, MODES, LANES) * mask.reshape(GROUPS, 1, MODES, LANES)
    return copies.reshape(GROUPS * size, LANES)


def shifted(block, before):
    one = pltpu.roll(block, 1, 0)
    two = pltpu.roll(block, 2, 0)
    first = index_of((8, block.shape[1]), 0)
    near, far = (0.0, 0.0) if before is None else (before[1:2], before[0:1])
    head_one = jnp.where(first == 0, near, one[:8])
    head_two = jnp.where(first == 0, far, jnp.where(first == 1, near, two[:8]))
    if block.shape[0] == 8:
        return head_one, head_two
    return jnp.concatenate([head_one, one[8:]], axis=0), jnp.concatenate([head_two, two[8:]], axis=0)


def short_conv(block, before, weights):
    one, two = shifted(block, before)
    return weights[0] * block + weights[1] * one + weights[2] * two


def shift_matrix(rows):
    shape = (2 * rows, rows)
    target = index_of(shape, 0)
    source = index_of(shape, 1)
    taken = jnp.where(target < rows, target - 1, target - (rows + 2))
    return jnp.where(source == taken, 1.0, 0.0).astype(BF16)


def earlier_tokens(shift, block):
    return jnp.dot(shift, block, preferred_element_type=F32)


def wide_conv(block, earlier, weights):
    rows = block.shape[0]
    wide = block.astype(F32)
    if earlier.shape[0] == rows:
        one = pltpu.roll(wide, 1, 0)
        head = jnp.where(index_of((8, wide.shape[1]), 0) == 0, 0.0, one[:8])
        one = jnp.concatenate([head, one[8:]], axis=0)
    else:
        one = earlier[:rows]
    return weights[0] * wide + weights[1] * one + weights[2] * earlier[-rows:]


def taps_of(weights, feature, lanes):
    return [weights[tap, feature : feature + 1, lanes] for tap in range(weights.shape[0])]


def state_kernel(
    projected_ref,
    weight_hbm,
    rate_hbm,
    residue_hbm,
    product_ref,
    state_ref,
    mode_rate_ref,
    head_ref,
    weight_ref,
    query_ref,
    residue_ref,
    shift_ref,
    buffer_ref,
    ending_ref,
    short_ref,
    rate_ref,
    sems,
    small_sems,
):
    rows, width = product_ref.shape
    wides = width // WIDE
    rate_copy = pltpu.make_async_copy(rate_hbm, rate_ref, small_sems.at[0])
    rate_copy.start()
    weight_copy = pltpu.make_async_copy(weight_hbm, short_ref, small_sems.at[1])
    copies = [pltpu.make_async_copy(projected_ref.at[pl.ds(1, 2)], buffer_ref, sems.at[0])]
    later = [
        pltpu.make_async_copy(residue_hbm, residue_ref, sems.at[2]),
        pltpu.make_async_copy(projected_ref.at[0], query_ref, sems.at[3]),
    ]
    for copy in copies:
        copy.start()
    weight_copy.start()
    shift_ref[...] = shift_matrix(rows)
    chosen = selectors(rate_ref.shape[1])
    eye = own_mode(BF16)
    mask = group_mask(F32)
    token = index_of((2 * LANES, rows), 1)
    left = jnp.where(token < 2, -1e30, (token - (rows - 1)).astype(F32)).astype(BF16)
    rate_copy.wait()
    mode_rate = per_channel(rate_ref[...], chosen)
    mode_rate_ref[...] = mode_rate

    def exponents(tile):
        high, low = split(mode_rate[:, lanes_of(tile)])
        diagonal = jnp.concatenate([spread(high, eye), spread(low, eye)], axis=1)
        return (jnp.dot(diagonal, left, preferred_element_type=F32),)

    def endings(tile, exponent):
        ending_ref[tile // 2, lanes_of(tile % 2), :] = jnp.exp(exponent).astype(BF16)

    pipelined(width // LANES, exponents, endings)
    weight_copy.wait()
    weights = short_ref[...].astype(F32)
    weight_ref[...] = weights
    for copy in copies:
        copy.wait()
    for copy in later:
        copy.start()

    def fetch(wide):
        here = lanes_of(wide, WIDE)
        return (
            earlier_tokens(shift_ref[...], buffer_ref[0, :, here]),
            earlier_tokens(shift_ref[rows:, :], buffer_ref[1, :, here]),
        )

    def multiply(wide, *earlier):
        here = lanes_of(wide, WIDE)
        parts = []
        for c in (0, 1):
            head_ref[c, :, here] = buffer_ref[c, 0:16, here].astype(F32)[:8]
            parts.append(wide_conv(buffer_ref[c, :, here], earlier[c], taps_of(weights, c + 1, here)))
        product = (parts[0] * parts[1]).astype(BF16)
        product_ref[:, here] = product
        return (jnp.dot(ending_ref[wide], product, preferred_element_type=F32),)

    def leave(wide, every):
        for half in range(WIDE // LANES):
            own = every[lanes_of(half), lanes_of(half)].reshape(GROUPS, MODES, LANES)
            state_ref[:, lanes_of((WIDE // LANES) * wide + half)] = jnp.sum(own * mask, axis=0)

    pipelined(wides, fetch, multiply, leave)
    for copy in later:
        copy.wait()


def halo(before_ref, place_ref):
    return jnp.where(place_ref[0] > 0, before_ref[...].astype(F32), 0.0)


def head_kernel(rows, place_ref, before_ref, head_ref, weight_ref, state_ref, mode_rate_ref, full_ref, first_ref):
    before = halo(before_ref, place_ref)
    everything = slice(0, head_ref.shape[2])
    parts = [short_conv(head_ref[c], before[c + 1], taps_of(weight_ref, c + 1, everything)) for c in (0, 1)]
    first = (parts[0] * parts[1]).astype(BF16).astype(F32)
    first_ref[...] = first
    rate = mode_rate_ref[...]
    early = jnp.exp(-float(rows - 1) * rate) * first[0:1] + jnp.exp(-float(rows - 2) * rate) * first[1:2]
    full_ref[...] = (state_ref[...] + early).astype(BF16)


def prepare_kernel(
    place_ref,
    residual_hbm,
    query_ref,
    residue_ref,
    before_ref,
    weight_ref,
    mode_rate_ref,
    shift_ref,
    inner_ref,
    entering_ref,
    carry_ref,
    gate_ref,
    residual_ref,
    sem,
):
    rows, width = gate_ref.shape
    residual_copy = pltpu.make_async_copy(residual_hbm, residual_ref, sem)
    residual_copy.start()
    residue = per_channel(residue_ref[...], selectors(residue_ref.shape[1]))
    wide = GROUPS * CHUNK
    step = index_of((CHUNK, LANES), 0).astype(F32)
    causal = (index_of((CHUNK, wide), 1) & (CHUNK - 1)) <= index_of((CHUNK, wide), 0)
    eye = own_mode(BF16)
    flat_eye = jnp.where((index_of((MODES, LANES), 1) & (MODES - 1)) == index_of((MODES, LANES), 0), 1.0, 0.0)
    flat_eye = flat_eye.astype(BF16)
    shape = (2 * LANES, wide)
    source = (index_of(shape, 1) & (CHUNK - 1)).astype(F32)
    own = (index_of(shape, 0) & (LANES - 1)) // MODES == index_of(shape, 1) // CHUNK
    own_chunk = jnp.where(own[:LANES], 1.0, 0.0).astype(BF16)
    risen = source[:, :LANES].astype(BF16)
    left = jnp.where(own, source - (CHUNK - 1), 0.0).astype(BF16)

    def exponents(tile):
        rate = mode_rate_ref[:, lanes_of(tile)]
        high, low = split(rate)
        diagonal = jnp.concatenate([spread(high, eye), spread(low, eye)], axis=1)
        each = jnp.concatenate([high * flat_eye, low * flat_eye], axis=1)
        return (
            jnp.dot(diagonal, risen, preferred_element_type=F32),
            jnp.dot(each, left, preferred_element_type=F32),
        )

    def products(tile, rise, end):
        here = lanes_of(tile)
        rise_high, rise_low = [
            jnp.concatenate([part] * (wide // LANES), axis=1) * own_chunk for part in split(jnp.exp(rise))
        ]
        rate_row = mode_row(mode_rate_ref[:, here])
        falling = mode_row(residue[:, here]) * jnp.exp(-rate_row * step)
        fall_high, fall_low = split(falling)
        half = tile % (WIDE // LANES)
        for chunk in range(rows // CHUNK):
            entering = (falling * jnp.exp(-float(CHUNK * chunk + 1) * rate_row)).astype(BF16)
            carry_ref[tile // (WIDE // LANES), chunk * CHUNK : (chunk + 1) * CHUNK, lanes_of(half)] = entering
            if chunk == 0:
                entering_ref[tile] = entering
        return (
            jnp.dot(jnp.concatenate([fall_high, fall_low], axis=0), rise_high, preferred_element_type=F32),
            jnp.dot(fall_high, rise_low, preferred_element_type=F32),
            jnp.exp(end),
        )

    def finish(tile, taps, rest, ending):
        taps = jnp.where(causal, taps[:CHUNK] + taps[CHUNK:] + rest, 0.0)
        inner_ref[tile] = jnp.concatenate([taps.astype(BF16), ending.astype(BF16)], axis=0)

    pipelined(width // LANES, exponents, products, finish)
    before = halo(before_ref, place_ref)

    def fetch(part):
        return (earlier_tokens(shift_ref[...], query_ref[:, lanes_of(part, WIDE)]),)

    def convolve(part, earlier):
        here = lanes_of(part, WIDE)
        weights = taps_of(weight_ref, 0, here)
        gate_ref[:, here] = wide_conv(query_ref[:, here], earlier, weights)
        head = query_ref[0:16, here].astype(F32)[:8]
        gate_ref[0:8, here] = short_conv(head, before[0, :, here], weights)

    pipelined(width // WIDE, fetch, convolve)
    residual_copy.wait()


def local_kernel(
    gate_ref,
    residual_ref,
    product_ref,
    first_ref,
    mode_rate_ref,
    inner_ref,
    entering_ref,
    skip_ref,
    base_ref,
):
    rows, width = product_ref.shape
    mask = group_mask(BF16)
    top = index_of((8, LANES), 0) < 2
    chunks = range(rows // CHUNK)

    def inside(tile):
        here = lanes_of(tile)
        pieces = []
        for chunk in chunks:
            piece = product_ref[chunk * CHUNK : (chunk + 1) * CHUNK, here]
            if chunk == 0:
                wide = piece.astype(F32)
                head = jnp.where(top, first_ref[:, here], wide[:8])
                piece = jnp.concatenate([head, wide[8:]], axis=0).astype(BF16)
            pieces.append(piece)
        found = []
        for pair in chunks[::2]:
            sources = jnp.concatenate([spread(pieces[pair + k], mask) for k in (0, 1)], axis=1)
            found.append(jnp.dot(inner_ref[tile], sources, preferred_element_type=F32))
        return found, pieces[0]

    def across(tile, inner, first):
        decay = jnp.exp(-float(CHUNK) * mode_rate_ref[:, lanes_of(tile)])
        state = jnp.zeros((MODES, LANES), F32)
        states = []
        for chunk in chunks:
            states.append(spread(state.astype(BF16), mask))
            state = decay * state + inner[chunk // 2][CHUNK:, lanes_of(chunk % 2)]
        outer = []
        for pair in chunks[::2]:
            two = jnp.concatenate(states[pair : pair + 2], axis=1)
            outer.append(jnp.dot(entering_ref[tile], two, preferred_element_type=F32))
        return [part[:CHUNK] for part in inner], outer, first

    def finish(tile, inner, outer, first):
        here = lanes_of(tile)
        skip = skip_ref[:, here]
        for chunk in chunks:
            span = slice(chunk * CHUNK, (chunk + 1) * CHUNK)
            piece = first if chunk == 0 else product_ref[span, here]
            conv = (inner[chunk // 2] + outer[chunk // 2])[:, lanes_of(chunk % 2)]
            whole = conv + skip * piece.astype(F32)
            base_ref[span, here] = residual_ref[span, here].astype(F32) + gate_ref[span, here] * whole

    pipelined(width // LANES, inside, across, finish)


def join_kernel(tokens, radix, stride, place_ref, own_ref, mode_rate_ref, entry_ref, *refs):
    others, (found_ref, group_ref) = refs[: radix - 1], refs[radix - 1 :]
    rate = mode_rate_ref[...]
    run = lax.rem(place_ref[0] // stride, radix)
    decay = jnp.exp(-float(tokens * stride) * rate)
    own = own_ref[...].astype(F32)
    values = [ref[...].astype(F32) for ref in others[::-1]]
    found = jnp.zeros_like(rate)
    total = jnp.zeros_like(rate)
    for position in range(radix):
        found = jnp.where(run == position, total, found)
        state = own
        for k, other in enumerate(values, 1):
            state = jnp.where(partner(run, k, radix) == position, other, state)
        total = decay * total + state
    if stride > 1:
        within = lax.rem(place_ref[0], stride).astype(F32) * float(tokens)
        found = jnp.exp(-within * rate) * found
    found_ref[...] = entry_ref[...] + found
    group_ref[...] = total.astype(BF16)


def carry_kernel(stride, radix, place_ref, base_ref, gate_ref, carry_ref, mode_rate_ref, inner_entry_ref, *refs):
    entry_refs, (summed_ref, squares_ref) = refs[:-2], refs[-2:]
    rows, width = base_ref.shape
    run = place_ref[0] // stride
    within = lax.rem(place_ref[0], stride).astype(F32) * float(rows)
    mask = group_mask(BF16)
    totals = [jnp.zeros((rows, LANES), F32)]
    nothing = jnp.zeros((LANES, LANES), BF16)

    def enter(tile):
        here = lanes_of(tile, WIDE)
        rate = mode_rate_ref[:, here]
        step = float(rows * stride)
        outer = jnp.zeros_like(rate)
        for k, ref in enumerate(entry_refs[::-1], 1):
            source = partner(run, k, radix)
            lag = jnp.maximum(run - 1 - source, 0).astype(F32) * step
            outer = outer + jnp.where(source < run, jnp.exp(-lag * rate) * ref[:, here].astype(F32), 0.0)
        entry = (inner_entry_ref[:, here] + jnp.exp(-within * rate) * outer).astype(BF16)
        left, right = spread(entry[:, :LANES], mask), spread(entry[:, LANES:], mask)
        both = jnp.concatenate(
            [jnp.concatenate([left, nothing], axis=1), jnp.concatenate([nothing, right], axis=1)], axis=0
        )
        return (jnp.dot(carry_ref[tile], both, preferred_element_type=F32),)

    def add(tile, carry):
        here = lanes_of(tile, WIDE)
        summed = base_ref[:, here] + gate_ref[:, here] * carry
        summed_ref[:, here] = summed
        square = summed * summed
        totals[0] = totals[0] + (square[:, :LANES] + square[:, LANES:])

    pipelined(width // WIDE, enter, add)
    total = totals[0]
    squares = lax.dot_general(
        jnp.ones((8, 2 * LANES), BF16),
        jnp.concatenate(split(total), axis=1),
        (((1,), (1,)), ((), ())),
        preferred_element_type=F32,
    )
    squares_ref[...] = squares[0:1]


def write_kernel(summed_ref, gain_ref, out_hbm, gained_ref, rounded_ref, sems):
    width = summed_ref.shape[1]
    copies = []
    for tile in range(width // WIDE):
        here = lanes_of(tile, WIDE)
        summed = summed_ref[:, here]
        rounded_ref[:, here] = summed.astype(BF16)
        span = pl.ds(tile * WIDE, WIDE)
        copies.append(pltpu.make_async_copy(rounded_ref.at[:, span], out_hbm.at[:, span], sems.at[tile]))
        copies[-1].start()
        gained_ref[:, here] = summed * gain_ref[:, here]
    for copy in copies:
        copy.wait()


def norm_kernel(full_width, gained_ref, *refs):
    squares_refs, (out_hbm, rounded_ref, sems) = refs[:-3], refs[-3:]
    rows, width = gained_ref.shape
    squares = squares_refs[0][...]
    for ref in squares_refs[1:]:
        squares = squares + ref[...]
    scale_row = lax.rsqrt(squares / full_width + 1e-05)
    scale = jnp.concatenate([as_column(scale_row[:, lanes_of(k)]) for k in range(rows // LANES)], axis=0)
    copies = []
    block = rows // 8
    for start in range(0, rows, block):
        span = slice(start, start + block)
        for tile in range(width // LANES):
            here = lanes_of(tile)
            rounded_ref[span, here] = (gained_ref[span, here] * scale[span]).astype(BF16)
        there = pl.ds(start, block)
        copies.append(pltpu.make_async_copy(rounded_ref.at[there, :], out_hbm.at[there, :], sems.at[start // block]))
        copies[-1].start()
    for copy in copies:
        copy.wait()


def params():
    return pltpu.CompilerParams(vmem_limit_bytes=VMEM_LIMIT)


def cost(microseconds):
    return pl.CostEstimate(flops=0, bytes_accessed=int(microseconds * 3.0e6), transcendentals=0)


def radices(count):
    found = []
    for radix in (4, 4, 4, 3, 3, 2, 5, 7):
        if count % radix == 0:
            found.append(radix)
            count //= radix
    return found + ([count] if count > 1 else [])


def partner(run, k, radix):
    if radix & (radix - 1) == 0:
        return run ^ k
    return (run - k + radix) % radix


def routes(count, stride, radix):
    found = []
    for k in range(1, radix):
        route = []
        for i in range(count):
            run = i // stride % radix
            route.append((i + (partner(run, k, radix) - run) * stride, i))
        found.append(route)
    return found


def ring(count, shift):
    return [(i, (i + shift) % count) for i in range(count)]


def per_device(projected, short_weight, rates, residues, skip, residual, gain):
    rows, width = projected.shape[1:]
    taps = short_weight.shape[0]
    peers = lax.axis_size("ctx")
    full_width = width * lax.axis_size("fsdp")
    place = lax.axis_index("ctx").astype(jnp.int32).reshape(1)
    hbm_spec = pl.BlockSpec(memory_space=pltpu.HBM)
    vmem_spec = pl.BlockSpec(memory_space=pltpu.VMEM)
    smem_spec = pl.BlockSpec(memory_space=pltpu.SMEM)
    tiles = width // LANES
    wides = width // WIDE

    def kept(array):
        return pltpu.with_memory_space_constraint(array, pltpu.HBM)

    def f32(*shape):
        return jax.ShapeDtypeStruct(shape, F32)

    def bf16(*shape):
        return jax.ShapeDtypeStruct(shape, BF16)

    before = lax.ppermute(projected[:, rows - (taps - 1) :, :], "ctx", ring(peers, 1))

    product, state, mode_rate, head, weights, query, residue, shift = pl.pallas_call(
        state_kernel,
        in_specs=[hbm_spec] * 4,
        out_shape=[
            bf16(rows, width),
            f32(MODES, width),
            f32(MODES, width),
            f32(2, 8, width),
            f32(*short_weight.shape),
            bf16(rows, width),
            f32(MODES, residues.shape[0]),
            bf16(2 * rows, rows),
        ],
        scratch_shapes=[
            pltpu.VMEM((2, rows, width), BF16),
            pltpu.VMEM((wides, WIDE, rows), BF16),
            pltpu.VMEM(short_weight.shape, BF16),
            pltpu.VMEM((MODES, rates.shape[0]), F32),
            pltpu.SemaphoreType.DMA((4,)),
            pltpu.SemaphoreType.DMA((2,)),
        ],
        compiler_params=params(),
        cost_estimate=cost(3),
        name="block_state",
    )(kept(projected), kept(short_weight), kept(rates.T), kept(residues.T))

    full_state, first = pl.pallas_call(
        lambda *refs: head_kernel(rows, *refs),
        in_specs=[smem_spec] + [vmem_spec] * 5,
        out_shape=[bf16(MODES, width), f32(8, width)],
        compiler_params=params(),
        cost_estimate=cost(0.2),
        name="head_tokens",
    )(place, before, head, weights, state, mode_rate)

    inner, entering, carry_table, gate, residual_here = pl.pallas_call(
        prepare_kernel,
        in_specs=[smem_spec, hbm_spec] + [vmem_spec] * 6,
        out_shape=[
            bf16(tiles, CHUNK + MODES, GROUPS * CHUNK),
            bf16(tiles, CHUNK, LANES),
            bf16(wides, rows, WIDE),
            f32(rows, width),
            bf16(rows, width),
        ],
        scratch_shapes=[pltpu.SemaphoreType.DMA],
        compiler_params=params(),
        cost_estimate=cost(2),
        name="prepare",
    )(place, kept(residual), query, residue, before, weights, mode_rate, shift)

    group, entry, stride = full_state, jnp.zeros((MODES, width), F32), 1
    levels = radices(peers)
    for level, radix in enumerate(levels):
        size = stride * radix
        if level == len(levels) - 1:
            break
        others = [lax.ppermute(group, "ctx", route) for route in routes(peers, stride, radix)[::-1]]
        if level == 0:
            others[0], inner = lax.optimization_barrier((others[0], inner))
        entry, group = pl.pallas_call(
            lambda *refs, radix=radix, stride=stride: join_kernel(rows, radix, stride, *refs),
            in_specs=[smem_spec] + [vmem_spec] * (2 + radix),
            out_shape=[f32(MODES, width), bf16(MODES, width)],
            compiler_params=params(),
            cost_estimate=cost(0.2),
            name="join",
        )(place, group, mode_rate, entry, *others)
        stride = size
    received = [lax.ppermute(group, "ctx", route) for route in routes(peers, stride, levels[-1])[::-1]]

    base = pl.pallas_call(
        local_kernel,
        out_shape=f32(rows, width),
        compiler_params=params(),
        cost_estimate=cost(5),
        name="local_conv",
    )(gate, residual_here, product, first, mode_rate, inner, entering, skip[None])

    count = lax.axis_size("fsdp")
    summed, squares = pl.pallas_call(
        lambda *refs: carry_kernel(stride, levels[-1], *refs),
        in_specs=[smem_spec] + [vmem_spec] * (5 + len(received)),
        out_shape=[f32(rows, width), f32(1, rows)],
        compiler_params=params(),
        cost_estimate=cost(1),
        name="add_carry",
    )(place, base, gate, carry_table, mode_rate, entry, *received)

    parts = [lax.ppermute(squares, "fsdp", route) for route in routes(count, 1, count)[::-1]]

    def write(kernel, operands, name, more_specs=(), more_shapes=()):
        return pl.pallas_call(
            kernel,
            out_specs=[hbm_spec, *more_specs],
            out_shape=[bf16(rows, width), *more_shapes],
            scratch_shapes=[pltpu.VMEM((rows, width), BF16), pltpu.SemaphoreType.DMA((max(8, wides),))],
            compiler_params=params(),
            cost_estimate=cost(1),
            name=name,
        )(*operands)

    new_residual, gained = write(
        write_kernel, (summed, gain[None]), "new_residual", [vmem_spec], [f32(rows, width)]
    )
    (normed,) = write(lambda *refs: norm_kernel(full_width, *refs), (gained, squares, *parts), "normed")
    return (new_residual, normed)


def solution(mesh):
    return jax.shard_map(
        per_device,
        mesh=mesh,
        in_specs=(
            P(None, "ctx", "fsdp"),
            P(None, None, "fsdp"),
            P("fsdp", None),
            P("fsdp", None),
            P("fsdp"),
            P("ctx", "fsdp"),
            P("fsdp"),
        ),
        out_specs=(P("ctx", "fsdp"), P("ctx", "fsdp")),
        check_vma=False,
    )
```

```python
import jax
import jax.numpy as jnp
from jax import lax
from jax.experimental import pallas as pl
from jax.experimental.pallas import tpu as pltpu
from jax.sharding import PartitionSpec as P

CHANNELS_PER_GRP = 16
MODES = 16
CHUNK = 32
LANES = 128
WIDE = 256
GROUPS = LANES // CHANNELS_PER_GRP
VMEM_LIMIT = 16 * 1024 * 1024
F32 = jnp.float32
BF16 = jnp.bfloat16


def index_of(shape, dim):
    return lax.broadcasted_iota(jnp.int32, shape, dim)


def pipelined(count, *stages):
    held = {}
    for step in range(count + len(stages) - 1):
        for k, stage in enumerate(stages):
            item = step - k
            if 0 <= item < count:
                held[item] = stage(item, *held.get(item, ()))


def lanes_of(tile, width=LANES):
    return slice(tile * width, (tile + 1) * width)


def selectors(groups):
    shape = (groups, WIDE)
    found = []
    for tile in range(groups * CHANNELS_PER_GRP // WIDE):
        own = index_of(shape, 0) == index_of(shape, 1) // CHANNELS_PER_GRP + tile * (WIDE // CHANNELS_PER_GRP)
        found.append(jnp.where(own, 1.0, 0.0).astype(BF16))
    return found


def per_channel(table, chosen):
    high = table.astype(BF16)
    rest = table - high.astype(F32)
    middle = rest.astype(BF16)
    low = (rest - middle.astype(F32)).astype(BF16)
    terms = jnp.concatenate([high, middle, low], axis=0)
    parts = []
    for selector in chosen:
        three = jnp.dot(terms, selector, preferred_element_type=F32)
        parts.append(three[:MODES] + three[MODES : 2 * MODES] + three[2 * MODES :])
    return jnp.concatenate(parts, axis=1)


def mode_row(channel_table):
    own = index_of(channel_table.shape, 0) == (index_of(channel_table.shape, 1) & (MODES - 1))
    return jnp.sum(jnp.where(own, channel_table, 0.0), axis=0, keepdims=True)


def as_column(row):
    return jnp.transpose(jnp.broadcast_to(row, (LANES, LANES)))


def own_mode(dtype):
    shape = (GROUPS, MODES, LANES)
    own = index_of(shape, 0) * MODES + index_of(shape, 1) == index_of(shape, 2)
    return jnp.where(own, 1.0, 0.0).astype(dtype)


def split(x):
    high = x.astype(BF16)
    return high, (x - high.astype(F32)).astype(BF16)


def group_mask(dtype):
    shape = (GROUPS, MODES, LANES)
    own = index_of(shape, 0) == index_of(shape, 2) // CHANNELS_PER_GRP
    return jnp.where(own, 1.0, 0.0).astype(dtype)


def spread(rows, mask):
    size = rows.shape[0]
    copies = rows.reshape(1, size // MODES, MODES, LANES) * mask.reshape(GROUPS, 1, MODES, LANES)
    return copies.reshape(GROUPS * size, LANES)


def shifted(block, before):
    one = pltpu.roll(block, 1, 0)
    two = pltpu.roll(block, 2, 0)
    first = index_of((8, block.shape[1]), 0)
    near, far = (0.0, 0.0) if before is None else (before[1:2], before[0:1])
    head_one = jnp.where(first == 0, near, one[:8])
    head_two = jnp.where(first == 0, far, jnp.where(first == 1, near, two[:8]))
    if block.shape[0] == 8:
        return head_one, head_two
    return jnp.concatenate([head_one, one[8:]], axis=0), jnp.concatenate([head_two, two[8:]], axis=0)


def short_conv(block, before, weights):
    one, two = shifted(block, before)
    return weights[0] * block + weights[1] * one + weights[2] * two


def shift_matrix(rows):
    shape = (2 * rows, rows)
    target = index_of(shape, 0)
    source = index_of(shape, 1)
    taken = jnp.where(target < rows, target - 1, target - (rows + 2))
    return jnp.where(source == taken, 1.0, 0.0).astype(BF16)


def earlier_tokens(shift, block):
    return jnp.dot(shift, block, preferred_element_type=F32)


def wide_conv(block, earlier, weights):
    rows = block.shape[0]
    wide = block.astype(F32)
    if earlier.shape[0] == rows:
        one = pltpu.roll(wide, 1, 0)
        head = jnp.where(index_of((8, wide.shape[1]), 0) == 0, 0.0, one[:8])
        one = jnp.concatenate([head, one[8:]], axis=0)
    else:
        one = earlier[:rows]
    return weights[0] * wide + weights[1] * one + weights[2] * earlier[-rows:]


def taps_of(weights, feature, lanes):
    return [weights[tap, feature : feature + 1, lanes] for tap in range(weights.shape[0])]


def state_kernel(
    projected_ref,
    weight_hbm,
    rate_hbm,
    residue_hbm,
    product_ref,
    state_ref,
    mode_rate_ref,
    head_ref,
    weight_ref,
    query_ref,
    residue_ref,
    shift_ref,
    buffer_ref,
    ending_ref,
    short_ref,
    rate_ref,
    sems,
    small_sems,
):
    rows, width = product_ref.shape
    wides = width // WIDE
    rate_copy = pltpu.make_async_copy(rate_hbm, rate_ref, small_sems.at[0])
    rate_copy.start()
    weight_copy = pltpu.make_async_copy(weight_hbm, short_ref, small_sems.at[1])
    copies = [pltpu.make_async_copy(projected_ref.at[pl.ds(1, 2)], buffer_ref, sems.at[0])]
    later = [
        pltpu.make_async_copy(residue_hbm, residue_ref, sems.at[2]),
        pltpu.make_async_copy(projected_ref.at[0], query_ref, sems.at[3]),
    ]
    for copy in copies:
        copy.start()
    weight_copy.start()
    shift_ref[...] = shift_matrix(rows)
    chosen = selectors(rate_ref.shape[1])
    eye = own_mode(BF16)
    mask = group_mask(F32)
    token = index_of((2 * LANES, rows), 1)
    left = jnp.where(token < 2, -1e30, (token - (rows - 1)).astype(F32)).astype(BF16)
    rate_copy.wait()
    mode_rate = per_channel(rate_ref[...], chosen)
    mode_rate_ref[...] = mode_rate

    def exponents(tile):
        high, low = split(mode_rate[:, lanes_of(tile)])
        diagonal = jnp.concatenate([spread(high, eye), spread(low, eye)], axis=1)
        return (jnp.dot(diagonal, left, preferred_element_type=F32),)

    def endings(tile, exponent):
        ending_ref[tile // 2, lanes_of(tile % 2), :] = jnp.exp(exponent).astype(BF16)

    pipelined(width // LANES, exponents, endings)
    weight_copy.wait()
    weights = short_ref[...].astype(F32)
    weight_ref[...] = weights
    for copy in copies:
        copy.wait()
    for copy in later:
        copy.start()

    def fetch(wide):
        here = lanes_of(wide, WIDE)
        return (
            earlier_tokens(shift_ref[...], buffer_ref[0, :, here]),
            earlier_tokens(shift_ref[rows:, :], buffer_ref[1, :, here]),
        )

    def multiply(wide, *earlier):
        here = lanes_of(wide, WIDE)
        parts = []
        for c in (0, 1):
            head_ref[c, :, here] = buffer_ref[c, 0:16, here].astype(F32)[:8]
            parts.append(wide_conv(buffer_ref[c, :, here], earlier[c], taps_of(weights, c + 1, here)))
        product = (parts[0] * parts[1]).astype(BF16)
        product_ref[:, here] = product
        return (product,)

    def reach(wide, product):
        return (jnp.dot(ending_ref[wide], product, preferred_element_type=F32),)

    def leave(wide, every):
        for half in range(WIDE // LANES):
            own = every[lanes_of(half), lanes_of(half)].reshape(GROUPS, MODES, LANES)
            state_ref[:, lanes_of((WIDE // LANES) * wide + half)] = jnp.sum(own * mask, axis=0)

    pipelined(wides, fetch, multiply, reach, leave)
    for copy in later:
        copy.wait()


def halo(before_ref, place_ref):
    return jnp.where(place_ref[0] > 0, before_ref[...].astype(F32), 0.0)


def head_kernel(rows, place_ref, before_ref, head_ref, weight_ref, state_ref, mode_rate_ref, full_ref, first_ref):
    before = halo(before_ref, place_ref)
    everything = slice(0, head_ref.shape[2])
    parts = [short_conv(head_ref[c], before[c + 1], taps_of(weight_ref, c + 1, everything)) for c in (0, 1)]
    first = (parts[0] * parts[1]).astype(BF16).astype(F32)
    first_ref[...] = first
    rate = mode_rate_ref[...]
    early = jnp.exp(-float(rows - 1) * rate) * first[0:1] + jnp.exp(-float(rows - 2) * rate) * first[1:2]
    full_ref[...] = (state_ref[...] + early).astype(BF16)


def prepare_kernel(
    place_ref,
    residual_hbm,
    query_ref,
    residue_ref,
    before_ref,
    weight_ref,
    mode_rate_ref,
    shift_ref,
    inner_ref,
    entering_ref,
    carry_ref,
    gate_ref,
    residual_ref,
    sem,
):
    rows, width = gate_ref.shape
    residual_copy = pltpu.make_async_copy(residual_hbm, residual_ref, sem)
    residual_copy.start()
    residue = per_channel(residue_ref[...], selectors(residue_ref.shape[1]))
    wide = GROUPS * CHUNK
    step = index_of((CHUNK, LANES), 0).astype(F32)
    causal = (index_of((CHUNK, wide), 1) & (CHUNK - 1)) <= index_of((CHUNK, wide), 0)
    eye = own_mode(BF16)
    flat_eye = jnp.where((index_of((MODES, LANES), 1) & (MODES - 1)) == index_of((MODES, LANES), 0), 1.0, 0.0)
    flat_eye = flat_eye.astype(BF16)
    shape = (2 * LANES, wide)
    source = (index_of(shape, 1) & (CHUNK - 1)).astype(F32)
    own = (index_of(shape, 0) & (LANES - 1)) // MODES == index_of(shape, 1) // CHUNK
    own_chunk = jnp.where(own[:LANES], 1.0, 0.0).astype(BF16)
    risen = source[:, :LANES].astype(BF16)
    left = jnp.where(own, source - (CHUNK - 1), 0.0).astype(BF16)

    def exponents(tile):
        rate = mode_rate_ref[:, lanes_of(tile)]
        high, low = split(rate)
        diagonal = jnp.concatenate([spread(high, eye), spread(low, eye)], axis=1)
        each = jnp.concatenate([high * flat_eye, low * flat_eye], axis=1)
        return (
            jnp.dot(diagonal, risen, preferred_element_type=F32),
            jnp.dot(each, left, preferred_element_type=F32),
        )

    def products(tile, rise, end):
        here = lanes_of(tile)
        rise_high, rise_low = [
            jnp.concatenate([part] * (wide // LANES), axis=1) * own_chunk for part in split(jnp.exp(rise))
        ]
        rate_row = mode_row(mode_rate_ref[:, here])
        falling = mode_row(residue[:, here]) * jnp.exp(-rate_row * step)
        fall_high, fall_low = split(falling)
        half = tile % (WIDE // LANES)
        for chunk in range(rows // CHUNK):
            entering = (falling * jnp.exp(-float(CHUNK * chunk + 1) * rate_row)).astype(BF16)
            carry_ref[tile // (WIDE // LANES), chunk * CHUNK : (chunk + 1) * CHUNK, lanes_of(half)] = entering
            if chunk == 0:
                entering_ref[tile] = entering
        return (
            jnp.dot(jnp.concatenate([fall_high, fall_low], axis=0), rise_high, preferred_element_type=F32),
            jnp.dot(fall_high, rise_low, preferred_element_type=F32),
            jnp.exp(end),
        )

    def finish(tile, taps, rest, ending):
        taps = jnp.where(causal, taps[:CHUNK] + taps[CHUNK:] + rest, 0.0)
        inner_ref[tile] = jnp.concatenate([taps.astype(BF16), ending.astype(BF16)], axis=0)

    pipelined(width // LANES, exponents, products, finish)
    before = halo(before_ref, place_ref)

    def fetch(part):
        return (earlier_tokens(shift_ref[...], query_ref[:, lanes_of(part, WIDE)]),)

    def convolve(part, earlier):
        here = lanes_of(part, WIDE)
        weights = taps_of(weight_ref, 0, here)
        gate_ref[:, here] = wide_conv(query_ref[:, here], earlier, weights)
        head = query_ref[0:16, here].astype(F32)[:8]
        gate_ref[0:8, here] = short_conv(head, before[0, :, here], weights)

    pipelined(width // WIDE, fetch, convolve)
    residual_copy.wait()


def local_kernel(
    gate_ref,
    residual_ref,
    product_ref,
    first_ref,
    mode_rate_ref,
    inner_ref,
    entering_ref,
    skip_ref,
    base_ref,
):
    rows, width = product_ref.shape
    mask = group_mask(BF16)
    top = index_of((8, LANES), 0) < 2
    chunks = range(rows // CHUNK)

    def inside(tile):
        here = lanes_of(tile)
        pieces = []
        for chunk in chunks:
            piece = product_ref[chunk * CHUNK : (chunk + 1) * CHUNK, here]
            if chunk == 0:
                wide = piece.astype(F32)
                head = jnp.where(top, first_ref[:, here], wide[:8])
                piece = jnp.concatenate([head, wide[8:]], axis=0).astype(BF16)
            pieces.append(piece)
        found = []
        for pair in chunks[::2]:
            sources = jnp.concatenate([spread(pieces[pair + k], mask) for k in (0, 1)], axis=1)
            found.append(jnp.dot(inner_ref[tile], sources, preferred_element_type=F32))
        return found, pieces[0]

    def across(tile, inner, first):
        decay = jnp.exp(-float(CHUNK) * mode_rate_ref[:, lanes_of(tile)])
        state = jnp.zeros((MODES, LANES), F32)
        states = []
        for chunk in chunks:
            states.append(spread(state.astype(BF16), mask))
            state = decay * state + inner[chunk // 2][CHUNK:, lanes_of(chunk % 2)]
        outer = []
        for pair in chunks[::2]:
            two = jnp.concatenate(states[pair : pair + 2], axis=1)
            outer.append(jnp.dot(entering_ref[tile], two, preferred_element_type=F32))
        return [part[:CHUNK] for part in inner], outer, first

    def finish(tile, inner, outer, first):
        here = lanes_of(tile)
        skip = skip_ref[:, here]
        for chunk in chunks:
            span = slice(chunk * CHUNK, (chunk + 1) * CHUNK)
            piece = first if chunk == 0 else product_ref[span, here]
            conv = (inner[chunk // 2] + outer[chunk // 2])[:, lanes_of(chunk % 2)]
            whole = conv + skip * piece.astype(F32)
            base_ref[span, here] = residual_ref[span, here].astype(F32) + gate_ref[span, here] * whole

    pipelined(width // LANES, inside, across, finish)


def join_kernel(tokens, radix, stride, place_ref, own_ref, mode_rate_ref, entry_ref, *refs):
    others, (found_ref, group_ref) = refs[: radix - 1], refs[radix - 1 :]
    rate = mode_rate_ref[...]
    run = lax.rem(place_ref[0] // stride, radix)
    decay = jnp.exp(-float(tokens * stride) * rate)
    own = own_ref[...].astype(F32)
    values = [ref[...].astype(F32) for ref in others[::-1]]
    found = jnp.zeros_like(rate)
    total = jnp.zeros_like(rate)
    for position in range(radix):
        found = jnp.where(run == position, total, found)
        state = own
        for k, other in enumerate(values, 1):
            state = jnp.where(partner(run, k, radix) == position, other, state)
        total = decay * total + state
    if stride > 1:
        within = lax.rem(place_ref[0], stride).astype(F32) * float(tokens)
        found = jnp.exp(-within * rate) * found
    found_ref[...] = entry_ref[...] + found
    group_ref[...] = total.astype(BF16)


def carry_kernel(stride, radix, place_ref, base_ref, gate_ref, carry_ref, mode_rate_ref, inner_entry_ref, *refs):
    entry_refs, (summed_ref, squares_ref) = refs[:-2], refs[-2:]
    rows, width = base_ref.shape
    run = place_ref[0] // stride
    within = lax.rem(place_ref[0], stride).astype(F32) * float(rows)
    mask = group_mask(BF16)
    totals = [jnp.zeros((rows, LANES), F32)]
    nothing = jnp.zeros((LANES, LANES), BF16)

    def enter(tile):
        here = lanes_of(tile, WIDE)
        rate = mode_rate_ref[:, here]
        step = float(rows * stride)
        outer = jnp.zeros_like(rate)
        for k, ref in enumerate(entry_refs[::-1], 1):
            source = partner(run, k, radix)
            lag = jnp.maximum(run - 1 - source, 0).astype(F32) * step
            outer = outer + jnp.where(source < run, jnp.exp(-lag * rate) * ref[:, here].astype(F32), 0.0)
        entry = (inner_entry_ref[:, here] + jnp.exp(-within * rate) * outer).astype(BF16)
        left, right = spread(entry[:, :LANES], mask), spread(entry[:, LANES:], mask)
        both = jnp.concatenate(
            [jnp.concatenate([left, nothing], axis=1), jnp.concatenate([nothing, right], axis=1)], axis=0
        )
        return (jnp.dot(carry_ref[tile], both, preferred_element_type=F32),)

    def add(tile, carry):
        here = lanes_of(tile, WIDE)
        summed = base_ref[:, here] + gate_ref[:, here] * carry
        summed_ref[:, here] = summed
        square = summed * summed
        totals[0] = totals[0] + (square[:, :LANES] + square[:, LANES:])

    pipelined(width // WIDE, enter, add)
    total = totals[0]
    squares = lax.dot_general(
        jnp.ones((8, 2 * LANES), BF16),
        jnp.concatenate(split(total), axis=1),
        (((1,), (1,)), ((), ())),
        preferred_element_type=F32,
    )
    squares_ref[...] = squares[0:1]


def write_kernel(summed_ref, gain_ref, out_hbm, gained_ref, rounded_ref, sems):
    width = summed_ref.shape[1]
    copies = []
    for tile in range(width // WIDE):
        here = lanes_of(tile, WIDE)
        summed = summed_ref[:, here]
        rounded_ref[:, here] = summed.astype(BF16)
        span = pl.ds(tile * WIDE, WIDE)
        copies.append(pltpu.make_async_copy(rounded_ref.at[:, span], out_hbm.at[:, span], sems.at[tile]))
        copies[-1].start()
        gained_ref[:, here] = summed * gain_ref[:, here]
    for copy in copies:
        copy.wait()


def norm_kernel(full_width, gained_ref, *refs):
    squares_refs, (out_hbm, rounded_ref, sems) = refs[:-3], refs[-3:]
    rows, width = gained_ref.shape
    squares = squares_refs[0][...]
    for ref in squares_refs[1:]:
        squares = squares + ref[...]
    scale_row = lax.rsqrt(squares / full_width + 1e-05)
    scale = jnp.concatenate([as_column(scale_row[:, lanes_of(k)]) for k in range(rows // LANES)], axis=0)
    copies = []
    block = rows // 8
    for start in range(0, rows, block):
        span = slice(start, start + block)
        for tile in range(width // LANES):
            here = lanes_of(tile)
            rounded_ref[span, here] = (gained_ref[span, here] * scale[span]).astype(BF16)
        there = pl.ds(start, block)
        copies.append(pltpu.make_async_copy(rounded_ref.at[there, :], out_hbm.at[there, :], sems.at[start // block]))
        copies[-1].start()
    for copy in copies:
        copy.wait()


def params():
    return pltpu.CompilerParams(vmem_limit_bytes=VMEM_LIMIT)


def cost(microseconds):
    return pl.CostEstimate(flops=0, bytes_accessed=int(microseconds * 3.0e6), transcendentals=0)


def radices(count):
    found = []
    for radix in (4, 4, 4, 3, 3, 2, 5, 7):
        if count % radix == 0:
            found.append(radix)
            count //= radix
    return found + ([count] if count > 1 else [])


def partner(run, k, radix):
    if radix & (radix - 1) == 0:
        return run ^ k
    return (run - k + radix) % radix


def routes(count, stride, radix):
    found = []
    for k in range(1, radix):
        route = []
        for i in range(count):
            run = i // stride % radix
            route.append((i + (partner(run, k, radix) - run) * stride, i))
        found.append(route)
    return found


def ring(count, shift):
    return [(i, (i + shift) % count) for i in range(count)]


def per_device(projected, short_weight, rates, residues, skip, residual, gain):
    rows, width = projected.shape[1:]
    taps = short_weight.shape[0]
    peers = lax.axis_size("ctx")
    full_width = width * lax.axis_size("fsdp")
    place = lax.axis_index("ctx").astype(jnp.int32).reshape(1)
    hbm_spec = pl.BlockSpec(memory_space=pltpu.HBM)
    vmem_spec = pl.BlockSpec(memory_space=pltpu.VMEM)
    smem_spec = pl.BlockSpec(memory_space=pltpu.SMEM)
    tiles = width // LANES
    wides = width // WIDE

    def kept(array):
        return pltpu.with_memory_space_constraint(array, pltpu.HBM)

    def f32(*shape):
        return jax.ShapeDtypeStruct(shape, F32)

    def bf16(*shape):
        return jax.ShapeDtypeStruct(shape, BF16)

    before = lax.ppermute(projected[:, rows - (taps - 1) :, :], "ctx", ring(peers, 1))

    product, state, mode_rate, head, weights, query, residue, shift = pl.pallas_call(
        state_kernel,
        in_specs=[hbm_spec] * 4,
        out_shape=[
            bf16(rows, width),
            f32(MODES, width),
            f32(MODES, width),
            f32(2, 8, width),
            f32(*short_weight.shape),
            bf16(rows, width),
            f32(MODES, residues.shape[0]),
            bf16(2 * rows, rows),
        ],
        scratch_shapes=[
            pltpu.VMEM((2, rows, width), BF16),
            pltpu.VMEM((wides, WIDE, rows), BF16),
            pltpu.VMEM(short_weight.shape, BF16),
            pltpu.VMEM((MODES, rates.shape[0]), F32),
            pltpu.SemaphoreType.DMA((4,)),
            pltpu.SemaphoreType.DMA((2,)),
        ],
        compiler_params=params(),
        cost_estimate=cost(3),
        name="block_state",
    )(kept(projected), kept(short_weight), kept(rates.T), kept(residues.T))

    full_state, first = pl.pallas_call(
        lambda *refs: head_kernel(rows, *refs),
        in_specs=[smem_spec] + [vmem_spec] * 5,
        out_shape=[bf16(MODES, width), f32(8, width)],
        compiler_params=params(),
        cost_estimate=cost(0.2),
        name="head_tokens",
    )(place, before, head, weights, state, mode_rate)

    inner, entering, carry_table, gate, residual_here = pl.pallas_call(
        prepare_kernel,
        in_specs=[smem_spec, hbm_spec] + [vmem_spec] * 6,
        out_shape=[
            bf16(tiles, CHUNK + MODES, GROUPS * CHUNK),
            bf16(tiles, CHUNK, LANES),
            bf16(wides, rows, WIDE),
            f32(rows, width),
            bf16(rows, width),
        ],
        scratch_shapes=[pltpu.SemaphoreType.DMA],
        compiler_params=params(),
        cost_estimate=cost(2),
        name="prepare",
    )(place, kept(residual), query, residue, before, weights, mode_rate, shift)

    group, entry, stride = full_state, jnp.zeros((MODES, width), F32), 1
    levels = radices(peers)
    for level, radix in enumerate(levels):
        size = stride * radix
        if level == len(levels) - 1:
            break
        others = [lax.ppermute(group, "ctx", route) for route in routes(peers, stride, radix)[::-1]]
        if level == 0:
            others[0], inner = lax.optimization_barrier((others[0], inner))
        entry, group = pl.pallas_call(
            lambda *refs, radix=radix, stride=stride: join_kernel(rows, radix, stride, *refs),
            in_specs=[smem_spec] + [vmem_spec] * (2 + radix),
            out_shape=[f32(MODES, width), bf16(MODES, width)],
            compiler_params=params(),
            cost_estimate=cost(0.2),
            name="join",
        )(place, group, mode_rate, entry, *others)
        stride = size
    received = [lax.ppermute(group, "ctx", route) for route in routes(peers, stride, levels[-1])[::-1]]

    base = pl.pallas_call(
        local_kernel,
        out_shape=f32(rows, width),
        compiler_params=params(),
        cost_estimate=cost(5),
        name="local_conv",
    )(gate, residual_here, product, first, mode_rate, inner, entering, skip[None])

    count = lax.axis_size("fsdp")
    summed, squares = pl.pallas_call(
        lambda *refs: carry_kernel(stride, levels[-1], *refs),
        in_specs=[smem_spec] + [vmem_spec] * (5 + len(received)),
        out_shape=[f32(rows, width), f32(1, rows)],
        compiler_params=params(),
        cost_estimate=cost(1),
        name="add_carry",
    )(place, base, gate, carry_table, mode_rate, entry, *received)

    parts = [lax.ppermute(squares, "fsdp", route) for route in routes(count, 1, count)[::-1]]

    def write(kernel, operands, name, more_specs=(), more_shapes=()):
        return pl.pallas_call(
            kernel,
            out_specs=[hbm_spec, *more_specs],
            out_shape=[bf16(rows, width), *more_shapes],
            scratch_shapes=[pltpu.VMEM((rows, width), BF16), pltpu.SemaphoreType.DMA((max(8, wides),))],
            compiler_params=params(),
            cost_estimate=cost(1),
            name=name,
        )(*operands)

    new_residual, gained = write(
        write_kernel, (summed, gain[None]), "new_residual", [vmem_spec], [f32(rows, width)]
    )
    (normed,) = write(lambda *refs: norm_kernel(full_width, *refs), (gained, squares, *parts), "normed")
    return (new_residual, normed)


def solution(mesh):
    return jax.shard_map(
        per_device,
        mesh=mesh,
        in_specs=(
            P(None, "ctx", "fsdp"),
            P(None, None, "fsdp"),
            P("fsdp", None),
            P("fsdp", None),
            P("fsdp"),
            P("ctx", "fsdp"),
            P("fsdp"),
        ),
        out_specs=(P("ctx", "fsdp"), P("ctx", "fsdp")),
        check_vma=False,
    )
```

```python
import jax
import jax.numpy as jnp
from jax import lax
from jax.experimental import pallas as pl
from jax.experimental.pallas import tpu as pltpu
from jax.sharding import PartitionSpec as P

CHANNELS_PER_GRP = 16
MODES = 16
CHUNK = 32
LANES = 128
WIDE = 256
GROUPS = LANES // CHANNELS_PER_GRP
VMEM_LIMIT = 16 * 1024 * 1024
F32 = jnp.float32
BF16 = jnp.bfloat16


def index_of(shape, dim):
    return lax.broadcasted_iota(jnp.int32, shape, dim)


def pipelined(count, *stages):
    held = {}
    for step in range(count + len(stages) - 1):
        for k, stage in enumerate(stages):
            item = step - k
            if 0 <= item < count:
                held[item] = stage(item, *held.get(item, ()))


def lanes_of(tile, width=LANES):
    return slice(tile * width, (tile + 1) * width)


def selectors(groups):
    shape = (groups, WIDE)
    found = []
    for tile in range(groups * CHANNELS_PER_GRP // WIDE):
        own = index_of(shape, 0) == index_of(shape, 1) // CHANNELS_PER_GRP + tile * (WIDE // CHANNELS_PER_GRP)
        found.append(jnp.where(own, 1.0, 0.0).astype(BF16))
    return found


def per_channel(table, chosen):
    high = table.astype(BF16)
    rest = table - high.astype(F32)
    middle = rest.astype(BF16)
    low = (rest - middle.astype(F32)).astype(BF16)
    terms = jnp.concatenate([high, middle, low], axis=0)
    parts = []
    for selector in chosen:
        three = jnp.dot(terms, selector, preferred_element_type=F32)
        parts.append(three[:MODES] + three[MODES : 2 * MODES] + three[2 * MODES :])
    return jnp.concatenate(parts, axis=1)


def mode_row(channel_table):
    own = index_of(channel_table.shape, 0) == (index_of(channel_table.shape, 1) & (MODES - 1))
    return jnp.sum(jnp.where(own, channel_table, 0.0), axis=0, keepdims=True)


def as_column(row):
    return jnp.transpose(jnp.broadcast_to(row, (LANES, LANES)))


def own_mode(dtype):
    shape = (GROUPS, MODES, LANES)
    own = index_of(shape, 0) * MODES + index_of(shape, 1) == index_of(shape, 2)
    return jnp.where(own, 1.0, 0.0).astype(dtype)


def split(x):
    high = x.astype(BF16)
    return high, (x - high.astype(F32)).astype(BF16)


def group_mask(dtype):
    shape = (GROUPS, MODES, LANES)
    own = index_of(shape, 0) == index_of(shape, 2) // CHANNELS_PER_GRP
    return jnp.where(own, 1.0, 0.0).astype(dtype)


def spread(rows, mask):
    size = rows.shape[0]
    copies = rows.reshape(1, size // MODES, MODES, LANES) * mask.reshape(GROUPS, 1, MODES, LANES)
    return copies.reshape(GROUPS * size, LANES)


def shifted(block, before):
    one = pltpu.roll(block, 1, 0)
    two = pltpu.roll(block, 2, 0)
    first = index_of((8, block.shape[1]), 0)
    near, far = (0.0, 0.0) if before is None else (before[1:2], before[0:1])
    head_one = jnp.where(first == 0, near, one[:8])
    head_two = jnp.where(first == 0, far, jnp.where(first == 1, near, two[:8]))
    if block.shape[0] == 8:
        return head_one, head_two
    return jnp.concatenate([head_one, one[8:]], axis=0), jnp.concatenate([head_two, two[8:]], axis=0)


def short_conv(block, before, weights):
    one, two = shifted(block, before)
    return weights[0] * block + weights[1] * one + weights[2] * two


def shift_matrix(rows):
    shape = (2 * rows, rows)
    target = index_of(shape, 0)
    source = index_of(shape, 1)
    taken = jnp.where(target < rows, target - 1, target - (rows + 2))
    return jnp.where(source == taken, 1.0, 0.0).astype(BF16)


def earlier_tokens(shift, block):
    return jnp.dot(shift, block, preferred_element_type=F32)


def wide_conv(block, earlier, weights):
    rows = block.shape[0]
    wide = block.astype(F32)
    if earlier.shape[0] == rows:
        one = pltpu.roll(wide, 1, 0)
        head = jnp.where(index_of((8, wide.shape[1]), 0) == 0, 0.0, one[:8])
        one = jnp.concatenate([head, one[8:]], axis=0)
    else:
        one = earlier[:rows]
    return weights[0] * wide + weights[1] * one + weights[2] * earlier[-rows:]


def taps_of(weights, feature, lanes):
    return [weights[tap, feature : feature + 1, lanes] for tap in range(weights.shape[0])]


def state_kernel(
    projected_ref,
    weight_hbm,
    rate_hbm,
    residue_hbm,
    product_ref,
    state_ref,
    mode_rate_ref,
    head_ref,
    weight_ref,
    query_ref,
    residue_ref,
    shift_ref,
    buffer_ref,
    ending_ref,
    short_ref,
    rate_ref,
    sems,
    small_sems,
):
    rows, width = product_ref.shape
    wides = width // WIDE
    rate_copy = pltpu.make_async_copy(rate_hbm, rate_ref, small_sems.at[0])
    rate_copy.start()
    weight_copy = pltpu.make_async_copy(weight_hbm, short_ref, small_sems.at[1])
    copies = [pltpu.make_async_copy(projected_ref.at[pl.ds(1, 2)], buffer_ref, sems.at[0])]
    later = [
        pltpu.make_async_copy(residue_hbm, residue_ref, sems.at[2]),
        pltpu.make_async_copy(projected_ref.at[0], query_ref, sems.at[3]),
    ]
    for copy in copies:
        copy.start()
    weight_copy.start()
    shift_ref[...] = shift_matrix(rows)
    chosen = selectors(rate_ref.shape[1])
    eye = own_mode(BF16)
    mask = group_mask(F32)
    token = index_of((2 * LANES, rows), 1)
    left = jnp.where(token < 2, -1e30, (token - (rows - 1)).astype(F32)).astype(BF16)
    rate_copy.wait()
    mode_rate = per_channel(rate_ref[...], chosen)
    mode_rate_ref[...] = mode_rate

    def exponents(tile):
        high, low = split(mode_rate[:, lanes_of(tile)])
        diagonal = jnp.concatenate([spread(high, eye), spread(low, eye)], axis=1)
        return (jnp.dot(diagonal, left, preferred_element_type=F32),)

    def endings(tile, exponent):
        ending_ref[tile // 2, lanes_of(tile % 2), :] = jnp.exp(exponent).astype(BF16)

    pipelined(width // LANES, exponents, endings)
    weight_copy.wait()
    weights = short_ref[...].astype(F32)
    weight_ref[...] = weights
    for copy in copies:
        copy.wait()
    for copy in later:
        copy.start()

    def fetch(wide):
        here = lanes_of(wide, WIDE)
        return (
            earlier_tokens(shift_ref[...], buffer_ref[0, :, here]),
            earlier_tokens(shift_ref[rows:, :], buffer_ref[1, :, here]),
        )

    def multiply(wide, *earlier):
        here = lanes_of(wide, WIDE)
        parts = []
        for c in (0, 1):
            head_ref[c, :, here] = buffer_ref[c, 0:16, here].astype(F32)[:8]
            parts.append(wide_conv(buffer_ref[c, :, here], earlier[c], taps_of(weights, c + 1, here)))
        product = (parts[0] * parts[1]).astype(BF16)
        product_ref[:, here] = product
        return (jnp.dot(ending_ref[wide], product, preferred_element_type=F32),)

    def leave(wide, every):
        for half in range(WIDE // LANES):
            own = every[lanes_of(half), lanes_of(half)].reshape(GROUPS, MODES, LANES)
            state_ref[:, lanes_of((WIDE // LANES) * wide + half)] = jnp.sum(own * mask, axis=0)

    pipelined(wides, fetch, multiply, leave)
    for copy in later:
        copy.wait()


def halo(before_ref, place_ref):
    return jnp.where(place_ref[0] > 0, before_ref[...].astype(F32), 0.0)


def head_kernel(rows, place_ref, before_ref, head_ref, weight_ref, state_ref, mode_rate_ref, full_ref, first_ref):
    before = halo(before_ref, place_ref)
    everything = slice(0, head_ref.shape[2])
    parts = [short_conv(head_ref[c], before[c + 1], taps_of(weight_ref, c + 1, everything)) for c in (0, 1)]
    first = (parts[0] * parts[1]).astype(BF16).astype(F32)
    first_ref[...] = first
    rate = mode_rate_ref[...]
    early = jnp.exp(-float(rows - 1) * rate) * first[0:1] + jnp.exp(-float(rows - 2) * rate) * first[1:2]
    full_ref[...] = (state_ref[...] + early).astype(BF16)


def prepare_kernel(
    place_ref,
    residual_hbm,
    query_ref,
    residue_ref,
    before_ref,
    weight_ref,
    mode_rate_ref,
    shift_ref,
    inner_ref,
    entering_ref,
    carry_ref,
    gate_ref,
    residual_ref,
    sem,
):
    rows, width = gate_ref.shape
    residual_copy = pltpu.make_async_copy(residual_hbm, residual_ref, sem)
    residual_copy.start()
    residue = per_channel(residue_ref[...], selectors(residue_ref.shape[1]))
    wide = GROUPS * CHUNK
    step = index_of((CHUNK, LANES), 0).astype(F32)
    causal = (index_of((CHUNK, wide), 1) & (CHUNK - 1)) <= index_of((CHUNK, wide), 0)
    eye = own_mode(BF16)
    flat_eye = jnp.where((index_of((MODES, LANES), 1) & (MODES - 1)) == index_of((MODES, LANES), 0), 1.0, 0.0)
    flat_eye = flat_eye.astype(BF16)
    shape = (2 * LANES, wide)
    source = (index_of(shape, 1) & (CHUNK - 1)).astype(F32)
    own = (index_of(shape, 0) & (LANES - 1)) // MODES == index_of(shape, 1) // CHUNK
    own_chunk = jnp.where(own[:LANES], 1.0, 0.0).astype(BF16)
    risen = source[:, :LANES].astype(BF16)
    left = jnp.where(own, source - (CHUNK - 1), 0.0).astype(BF16)

    def exponents(tile):
        rate = mode_rate_ref[:, lanes_of(tile)]
        high, low = split(rate)
        diagonal = jnp.concatenate([spread(high, eye), spread(low, eye)], axis=1)
        each = jnp.concatenate([high * flat_eye, low * flat_eye], axis=1)
        return (
            jnp.dot(diagonal, risen, preferred_element_type=F32),
            jnp.dot(each, left, preferred_element_type=F32),
        )

    def products(tile, rise, end):
        here = lanes_of(tile)
        rise_high, rise_low = [
            jnp.concatenate([part] * (wide // LANES), axis=1) * own_chunk for part in split(jnp.exp(rise))
        ]
        rate_row = mode_row(mode_rate_ref[:, here])
        falling = mode_row(residue[:, here]) * jnp.exp(-rate_row * step)
        fall_high, fall_low = split(falling)
        half = tile % (WIDE // LANES)
        for chunk in range(rows // CHUNK):
            entering = (falling * jnp.exp(-float(CHUNK * chunk + 1) * rate_row)).astype(BF16)
            carry_ref[tile // (WIDE // LANES), chunk * CHUNK : (chunk + 1) * CHUNK, lanes_of(half)] = entering
            if chunk == 0:
                entering_ref[tile] = entering
        return (
            jnp.dot(jnp.concatenate([fall_high, fall_low], axis=0), rise_high, preferred_element_type=F32),
            jnp.dot(fall_high, rise_low, preferred_element_type=F32),
            jnp.exp(end),
        )

    def finish(tile, taps, rest, ending):
        taps = jnp.where(causal, taps[:CHUNK] + taps[CHUNK:] + rest, 0.0)
        inner_ref[tile] = jnp.concatenate([taps.astype(BF16), ending.astype(BF16)], axis=0)

    pipelined(width // LANES, exponents, products, finish)
    before = halo(before_ref, place_ref)

    def fetch(part):
        return (earlier_tokens(shift_ref[...], query_ref[:, lanes_of(part, WIDE)]),)

    def convolve(part, earlier):
        here = lanes_of(part, WIDE)
        weights = taps_of(weight_ref, 0, here)
        gate_ref[:, here] = wide_conv(query_ref[:, here], earlier, weights)
        head = query_ref[0:16, here].astype(F32)[:8]
        gate_ref[0:8, here] = short_conv(head, before[0, :, here], weights)

    pipelined(width // WIDE, fetch, convolve)
    residual_copy.wait()


def local_kernel(
    gate_ref,
    residual_ref,
    product_ref,
    first_ref,
    mode_rate_ref,
    inner_ref,
    entering_ref,
    skip_ref,
    base_ref,
):
    rows, width = product_ref.shape
    mask = group_mask(BF16)
    top = index_of((8, LANES), 0) < 2
    chunks = range(rows // CHUNK)

    def inside(tile):
        here = lanes_of(tile)
        pieces = []
        for chunk in chunks:
            piece = product_ref[chunk * CHUNK : (chunk + 1) * CHUNK, here]
            if chunk == 0:
                wide = piece.astype(F32)
                head = jnp.where(top, first_ref[:, here], wide[:8])
                piece = jnp.concatenate([head, wide[8:]], axis=0).astype(BF16)
            pieces.append(piece)
        found = []
        for pair in chunks[::2]:
            sources = jnp.concatenate([spread(pieces[pair + k], mask) for k in (0, 1)], axis=1)
            found.append(jnp.dot(inner_ref[tile], sources, preferred_element_type=F32))
        return found, pieces[0]

    def across(tile, inner, first):
        decay = jnp.exp(-float(CHUNK) * mode_rate_ref[:, lanes_of(tile)])
        state = jnp.zeros((MODES, LANES), F32)
        states = []
        for chunk in chunks:
            states.append(spread(state.astype(BF16), mask))
            state = decay * state + inner[chunk // 2][CHUNK:, lanes_of(chunk % 2)]
        outer = []
        for pair in chunks[::2]:
            two = jnp.concatenate(states[pair : pair + 2], axis=1)
            outer.append(jnp.dot(entering_ref[tile], two, preferred_element_type=F32))
        return [part[:CHUNK] for part in inner], outer, first

    def finish(tile, inner, outer, first):
        here = lanes_of(tile)
        skip = skip_ref[:, here]
        for chunk in chunks:
            span = slice(chunk * CHUNK, (chunk + 1) * CHUNK)
            piece = first if chunk == 0 else product_ref[span, here]
            conv = (inner[chunk // 2] + outer[chunk // 2])[:, lanes_of(chunk % 2)]
            whole = conv + skip * piece.astype(F32)
            base_ref[span, here] = residual_ref[span, here].astype(F32) + gate_ref[span, here] * whole

    pipelined(width // LANES, inside, across, finish)


def join_kernel(tokens, radix, stride, place_ref, own_ref, mode_rate_ref, entry_ref, *refs):
    others, (found_ref, group_ref) = refs[: radix - 1], refs[radix - 1 :]
    rate = mode_rate_ref[...]
    run = lax.rem(place_ref[0] // stride, radix)
    decay = jnp.exp(-float(tokens * stride) * rate)
    own = own_ref[...].astype(F32)
    values = [ref[...].astype(F32) for ref in others[::-1]]
    found = jnp.zeros_like(rate)
    total = jnp.zeros_like(rate)
    for position in range(radix):
        found = jnp.where(run == position, total, found)
        state = own
        for k, other in enumerate(values, 1):
            state = jnp.where(partner(run, k, radix) == position, other, state)
        total = decay * total + state
    if stride > 1:
        within = lax.rem(place_ref[0], stride).astype(F32) * float(tokens)
        found = jnp.exp(-within * rate) * found
    found_ref[...] = entry_ref[...] + found
    group_ref[...] = total.astype(BF16)


def carry_kernel(stride, radix, place_ref, base_ref, gate_ref, carry_ref, mode_rate_ref, inner_entry_ref, *refs):
    entry_refs, (summed_ref, squares_ref) = refs[:-2], refs[-2:]
    rows, width = base_ref.shape
    run = place_ref[0] // stride
    within = lax.rem(place_ref[0], stride).astype(F32) * float(rows)
    mask = group_mask(BF16)
    totals = [jnp.zeros((rows, LANES), F32)]
    nothing = jnp.zeros((LANES, LANES), BF16)

    def enter(tile):
        here = lanes_of(tile, WIDE)
        rate = mode_rate_ref[:, here]
        step = float(rows * stride)
        outer = jnp.zeros_like(rate)
        for k, ref in enumerate(entry_refs[::-1], 1):
            source = partner(run, k, radix)
            lag = jnp.maximum(run - 1 - source, 0).astype(F32) * step
            outer = outer + jnp.where(source < run, jnp.exp(-lag * rate) * ref[:, here].astype(F32), 0.0)
        entry = (inner_entry_ref[:, here] + jnp.exp(-within * rate) * outer).astype(BF16)
        left, right = spread(entry[:, :LANES], mask), spread(entry[:, LANES:], mask)
        both = jnp.concatenate(
            [jnp.concatenate([left, nothing], axis=1), jnp.concatenate([nothing, right], axis=1)], axis=0
        )
        return (jnp.dot(carry_ref[tile], both, preferred_element_type=F32),)

    def add(tile, carry):
        here = lanes_of(tile, WIDE)
        summed = base_ref[:, here] + gate_ref[:, here] * carry
        summed_ref[:, here] = summed
        square = summed * summed
        totals[0] = totals[0] + (square[:, :LANES] + square[:, LANES:])

    pipelined(width // WIDE, enter, add)
    total = totals[0]
    squares = lax.dot_general(
        jnp.ones((8, 2 * LANES), BF16),
        jnp.concatenate(split(total), axis=1),
        (((1,), (1,)), ((), ())),
        preferred_element_type=F32,
    )
    squares_ref[...] = squares[0:1]


def write_kernel(summed_ref, gain_ref, out_hbm, gained_ref, rounded_ref, sems):
    width = summed_ref.shape[1]
    copies = []
    for tile in range(width // WIDE):
        here = lanes_of(tile, WIDE)
        summed = summed_ref[:, here]
        rounded_ref[:, here] = summed.astype(BF16)
        span = pl.ds(tile * WIDE, WIDE)
        copies.append(pltpu.make_async_copy(rounded_ref.at[:, span], out_hbm.at[:, span], sems.at[tile]))
        copies[-1].start()
        gained_ref[:, here] = summed * gain_ref[:, here]
    for copy in copies:
        copy.wait()


def norm_kernel(full_width, gained_ref, *refs):
    squares_refs, (out_hbm, rounded_ref, sems) = refs[:-3], refs[-3:]
    rows, width = gained_ref.shape
    squares = squares_refs[0][...]
    for ref in squares_refs[1:]:
        squares = squares + ref[...]
    scale_row = lax.rsqrt(squares / full_width + 1e-05)
    scale = jnp.concatenate([as_column(scale_row[:, lanes_of(k)]) for k in range(rows // LANES)], axis=0)
    copies = []
    block = rows // 4
    for start in range(0, rows, block):
        span = slice(start, start + block)
        for tile in range(width // LANES):
            here = lanes_of(tile)
            rounded_ref[span, here] = (gained_ref[span, here] * scale[span]).astype(BF16)
        there = pl.ds(start, block)
        copies.append(pltpu.make_async_copy(rounded_ref.at[there, :], out_hbm.at[there, :], sems.at[start // block]))
        copies[-1].start()
    for copy in copies:
        copy.wait()


def params():
    return pltpu.CompilerParams(vmem_limit_bytes=VMEM_LIMIT)


def cost(microseconds):
    return pl.CostEstimate(flops=0, bytes_accessed=int(microseconds * 3.0e6), transcendentals=0)


def radices(count):
    found = []
    for radix in (4, 4, 4, 3, 3, 2, 5, 7):
        if count % radix == 0:
            found.append(radix)
            count //= radix
    return found + ([count] if count > 1 else [])


def partner(run, k, radix):
    if radix & (radix - 1) == 0:
        return run ^ k
    return (run - k + radix) % radix


def routes(count, stride, radix):
    found = []
    for k in range(1, radix):
        route = []
        for i in range(count):
            run = i // stride % radix
            route.append((i + (partner(run, k, radix) - run) * stride, i))
        found.append(route)
    return found


def ring(count, shift):
    return [(i, (i + shift) % count) for i in range(count)]


def per_device(projected, short_weight, rates, residues, skip, residual, gain):
    rows, width = projected.shape[1:]
    taps = short_weight.shape[0]
    peers = lax.axis_size("ctx")
    full_width = width * lax.axis_size("fsdp")
    place = lax.axis_index("ctx").astype(jnp.int32).reshape(1)
    hbm_spec = pl.BlockSpec(memory_space=pltpu.HBM)
    vmem_spec = pl.BlockSpec(memory_space=pltpu.VMEM)
    smem_spec = pl.BlockSpec(memory_space=pltpu.SMEM)
    tiles = width // LANES
    wides = width // WIDE

    def kept(array):
        return pltpu.with_memory_space_constraint(array, pltpu.HBM)

    def f32(*shape):
        return jax.ShapeDtypeStruct(shape, F32)

    def bf16(*shape):
        return jax.ShapeDtypeStruct(shape, BF16)

    before = lax.ppermute(projected[:, rows - (taps - 1) :, :], "ctx", ring(peers, 1))

    product, state, mode_rate, head, weights, query, residue, shift = pl.pallas_call(
        state_kernel,
        in_specs=[hbm_spec] * 4,
        out_shape=[
            bf16(rows, width),
            f32(MODES, width),
            f32(MODES, width),
            f32(2, 8, width),
            f32(*short_weight.shape),
            bf16(rows, width),
            f32(MODES, residues.shape[0]),
            bf16(2 * rows, rows),
        ],
        scratch_shapes=[
            pltpu.VMEM((2, rows, width), BF16),
            pltpu.VMEM((wides, WIDE, rows), BF16),
            pltpu.VMEM(short_weight.shape, BF16),
            pltpu.VMEM((MODES, rates.shape[0]), F32),
            pltpu.SemaphoreType.DMA((4,)),
            pltpu.SemaphoreType.DMA((2,)),
        ],
        compiler_params=params(),
        cost_estimate=cost(3),
        name="block_state",
    )(kept(projected), kept(short_weight), kept(rates.T), kept(residues.T))

    full_state, first = pl.pallas_call(
        lambda *refs: head_kernel(rows, *refs),
        in_specs=[smem_spec] + [vmem_spec] * 5,
        out_shape=[bf16(MODES, width), f32(8, width)],
        compiler_params=params(),
        cost_estimate=cost(0.2),
        name="head_tokens",
    )(place, before, head, weights, state, mode_rate)

    inner, entering, carry_table, gate, residual_here = pl.pallas_call(
        prepare_kernel,
        in_specs=[smem_spec, hbm_spec] + [vmem_spec] * 6,
        out_shape=[
            bf16(tiles, CHUNK + MODES, GROUPS * CHUNK),
            bf16(tiles, CHUNK, LANES),
            bf16(wides, rows, WIDE),
            f32(rows, width),
            bf16(rows, width),
        ],
        scratch_shapes=[pltpu.SemaphoreType.DMA],
        compiler_params=params(),
        cost_estimate=cost(2),
        name="prepare",
    )(place, kept(residual), query, residue, before, weights, mode_rate, shift)

    group, entry, stride = full_state, jnp.zeros((MODES, width), F32), 1
    levels = radices(peers)
    for level, radix in enumerate(levels):
        size = stride * radix
        if level == len(levels) - 1:
            break
        others = [lax.ppermute(group, "ctx", route) for route in routes(peers, stride, radix)[::-1]]
        if level == 0:
            others[0], inner = lax.optimization_barrier((others[0], inner))
        entry, group = pl.pallas_call(
            lambda *refs, radix=radix, stride=stride: join_kernel(rows, radix, stride, *refs),
            in_specs=[smem_spec] + [vmem_spec] * (2 + radix),
            out_shape=[f32(MODES, width), bf16(MODES, width)],
            compiler_params=params(),
            cost_estimate=cost(0.2),
            name="join",
        )(place, group, mode_rate, entry, *others)
        stride = size
    received = [lax.ppermute(group, "ctx", route) for route in routes(peers, stride, levels[-1])[::-1]]

    base = pl.pallas_call(
        local_kernel,
        out_shape=f32(rows, width),
        compiler_params=params(),
        cost_estimate=cost(5),
        name="local_conv",
    )(gate, residual_here, product, first, mode_rate, inner, entering, skip[None])

    count = lax.axis_size("fsdp")
    summed, squares = pl.pallas_call(
        lambda *refs: carry_kernel(stride, levels[-1], *refs),
        in_specs=[smem_spec] + [vmem_spec] * (5 + len(received)),
        out_shape=[f32(rows, width), f32(1, rows)],
        compiler_params=params(),
        cost_estimate=cost(1),
        name="add_carry",
    )(place, base, gate, carry_table, mode_rate, entry, *received)

    parts = [lax.ppermute(squares, "fsdp", route) for route in routes(count, 1, count)[::-1]]

    def write(kernel, operands, name, more_specs=(), more_shapes=()):
        return pl.pallas_call(
            kernel,
            out_specs=[hbm_spec, *more_specs],
            out_shape=[bf16(rows, width), *more_shapes],
            scratch_shapes=[pltpu.VMEM((rows, width), BF16), pltpu.SemaphoreType.DMA((max(8, wides),))],
            compiler_params=params(),
            cost_estimate=cost(1),
            name=name,
        )(*operands)

    new_residual, gained = write(
        write_kernel, (summed, gain[None]), "new_residual", [vmem_spec], [f32(rows, width)]
    )
    (normed,) = write(lambda *refs: norm_kernel(full_width, *refs), (gained, squares, *parts), "normed")
    return (new_residual, normed)


def solution(mesh):
    return jax.shard_map(
        per_device,
        mesh=mesh,
        in_specs=(
            P(None, "ctx", "fsdp"),
            P(None, None, "fsdp"),
            P("fsdp", None),
            P("fsdp", None),
            P("fsdp"),
            P("ctx", "fsdp"),
            P("fsdp"),
        ),
        out_specs=(P("ctx", "fsdp"), P("ctx", "fsdp")),
        check_vma=False,
    )
```
